32 devices in a mesh: dp: 8 (over z, core), mp: 4 (over y, x).
Axes of the slice: x: 2, y: 2, z: 4, core: 2. Of those that a mesh axis runs over, the one named last changes fastest.
Arguments:
- inputs: bfloat16 [8192, 2048], P('dp'), may hold values from -6 to 6
- counts: int32 [8], P('dp'), may hold values from 1 to 1024, 4096 in all
- cotangent: bfloat16 [8192, 2048], P('dp'), may hold values from -6 to 6
- gain_attn: float32 [2048], P('dp'), may hold values from 0.5 to 1.5
- w_query: float32 [2048, 2048], P('dp', 'mp'), may hold values from -0.125 to 0.125
- w_key: float32 [2048, 2048], P('dp', 'mp'), may hold values from -0.125 to 0.125
- w_value: float32 [2048, 2048], P('dp', 'mp'), may hold values from -0.125 to 0.125
- w_output: float32 [2048, 2048], P('mp', 'dp'), may hold values from -0.5 to 0.5
- gain_ffn: float32 [2048], P('dp'), may hold values from 0.5 to 1.5
- w_gate: float32 [2048, 8192], P('dp', 'mp'), may hold values from -0.125 to 0.125
- w_up: float32 [2048, 8192], P('dp', 'mp'), may hold values from -0.125 to 0.125
- w_down: float32 [8192, 2048], P('mp', 'dp'), may hold values from -0.0625 to 0.0625
Outputs:
- layer_out: bfloat16 [8192, 2048], P('dp')
- input_grad: float32 [8192, 2048], P('dp')
- grad_gain_attn: float32 [2048], P('dp')
- grad_w_query: float32 [2048, 2048], P('dp', 'mp')
- grad_w_key: float32 [2048, 2048], P('dp', 'mp')
- grad_w_value: float32 [2048, 2048], P('dp', 'mp')
- grad_w_output: float32 [2048, 2048], P('mp', 'dp')
- grad_gain_ffn: float32 [2048], P('dp')
- grad_w_gate: float32 [2048, 8192], P('dp', 'mp')
- grad_w_up: float32 [2048, 8192], P('dp', 'mp')
- grad_w_down: float32 [8192, 2048], P('mp', 'dp')
The draws below stay inside these ranges and needn't reach their ends.
Inputs may be any that keep to these rules, and one draw needn't show every extreme that they name: `counts`: valid tokens of each sequence, the first ones of its row; one sequence has exactly 1024, and all together make half of the 8192 slots.
All inputs are finite; a program needn't handle non-finite values. No bound on the sum of `counts` on one device may be relied on, other than what follows from the above.
Results may differ from the reference program's by a relative error of at most 0.02.
Values may be sent and summed in bfloat16 or wider, within the bound.
A program may use at most 192 MiB of HBM per device.

```python
import math
from functools import partial
import jax
import jax.numpy as jnp
import numpy as np
from jax import lax

D = 2048
H = 16
HD = 128
FF = 8192
SEQ = 1024
TOKENS = 8192
N_DP = 8


def shard_levels(own_key, extent, cuts, low, top_value):
    level = 1.0
    for dim, parts in cuts:
        heights = jax.random.uniform(jax.random.fold_in(jax.random.fold_in(own_key, 6), dim), (parts,), jnp.float32, low / len(cuts), top_value / len(cuts))
        level = level * jnp.repeat(jnp.exp(heights), extent[dim] // parts).reshape((-1,) + (1,) * (len(extent) - 1 - dim))
    return level


def split_up(amount, total, reach, skew):
    loads = [(1 << 20) // math.isqrt(grade ** skew) + 1 for grade in range(2, amount + 1)]
    spare, holding = total - reach - (amount - 1), [1] * (amount - 1)
    while spare > 0:
        movable = [i for i in range(amount - 1) if holding[i] < reach]
        mass, left = sum([loads[i] for i in movable]), spare
        for i in movable:
            addition = min(reach - holding[i], max(1, left * loads[i] // mass), spare)
            holding[i] = holding[i] + addition
            spare = spare - addition
    return np.array([reach] + holding)


def uneven(stream_key, amount, total, bound, skew):
    if amount == 2:
        one = jax.random.randint(stream_key, (), max(1, total - bound), min(bound, total - 1) + 1)
        return jnp.stack([one, total - one])
    lengths = jnp.asarray(split_up(amount, total, bound, skew), jnp.int32)
    twos = (amount - 1) // 2
    giver, sink = lengths[1:1 + 2 * twos:2], lengths[2:2 + 2 * twos:2]
    slack = jnp.minimum(giver - 1, bound - sink)
    moved = jax.random.randint(jax.random.fold_in(stream_key, 1), (twos,), 0, 1 << 20) % (slack + 1)
    lengths = lengths.at[1:1 + 2 * twos:2].set(giver - moved).at[2:2 + 2 * twos:2].set(sink + moved)
    return lengths[jax.random.permutation(jax.random.fold_in(stream_key, 2), amount)]


def normal_values(rng, extent, spread, bound, shards=(), dtype=jnp.bfloat16):
    values = jax.random.normal(rng, extent, jnp.float32) * spread
    if len(shards) > 0:
        values = shard_levels(rng, extent, shards, -0.22, 0.18) * values
    return jnp.clip(values, min=-bound, max=bound).astype(dtype)


def setup_inputs(seed: int = 0) -> dict:
    splits = jax.random.split(jax.random.key(seed), 13)
    inputs = normal_values(splits[0], (TOKENS, D), 1.0, 6.0, ((0, 8),))
    counts = uneven(splits[1], N_DP, SEQ * N_DP // 2, SEQ, 2).astype(jnp.int32)
    cotangent = normal_values(splits[2], (TOKENS, D), 1.0, 6.0, ((0, 8),))
    gain_attn = jnp.clip(1.0 + 0.1 * jax.random.normal(splits[3], (D,), jnp.float32), 0.5, 1.5)
    w_query = normal_values(splits[4], (D, H * HD), D ** -0.5, 0.125, ((0, 8), (1, 4)), jnp.float32)
    w_key = normal_values(splits[5], (D, H * HD), D ** -0.5, 0.125, ((0, 8), (1, 4)), jnp.float32)
    w_value = normal_values(splits[6], (D, H * HD), D ** -0.5, 0.125, ((0, 8), (1, 4)), jnp.float32)
    w_output = normal_values(splits[7], (H * HD, D), (H * HD // 16) ** -0.5, 0.5, ((0, 4), (1, 8)), jnp.float32)
    gain_ffn = jnp.clip(1.0 + 0.1 * jax.random.normal(splits[8], (D,), jnp.float32), 0.5, 1.5)
    w_gate = normal_values(splits[9], (D, FF), D ** -0.5, 0.125, ((0, 8), (1, 4)), jnp.float32)
    w_up = normal_values(splits[10], (D, FF), D ** -0.5, 0.125, ((0, 8), (1, 4)), jnp.float32)
    w_down = normal_values(splits[11], (FF, D), FF ** -0.5, 0.0625, ((0, 4), (1, 8)), jnp.float32)
    return dict(inputs=inputs, counts=counts, cotangent=cotangent, gain_attn=gain_attn, w_query=w_query, w_key=w_key, w_value=w_value, w_output=w_output, gain_ffn=gain_ffn, w_gate=w_gate, w_up=w_up, w_down=w_down)


@jax.custom_vjp
def low(v):
    return lax.optimization_barrier(v.astype(jnp.bfloat16)).astype(jnp.float32)

@jax.custom_vjp
def low_back(v):
    return v

def low_keep(v):
    return (low(v), None)

def low_pass(kept, grad):
    return (grad,)

def back_keep(v):
    return (v, None)

def back_low(kept, grad):
    return (low(grad),)
low.defvjp(low_keep, low_pass)
low_back.defvjp(back_keep, back_low)
EPS = 1e-06
HIGH = lax.Precision.HIGHEST

def matmul(left, right):
    return jnp.dot(left, right, precision=HIGH, preferred_element_type=jnp.float32)

def rms_norm(field, gain):
    scale = lax.rsqrt(lax.optimization_barrier(jnp.mean(field * field, axis=-1, keepdims=True)) + EPS)
    return field * scale * gain

def attend_sequence(packed):
    queries, keys, values, count = packed
    raw = low_back(jnp.einsum('qhd,khd->hqk', queries, keys, precision=HIGH))
    logistic = jax.nn.sigmoid(raw * HD ** (-0.5) - math.log(SEQ))
    positions = jnp.arange(SEQ)
    allowed = ((positions[None, :] <= positions[:, None]) & (positions[None, :] < count)).astype(jnp.float32)
    attn_weight = low(logistic * allowed[None])
    return jnp.einsum('hqk,khd->qhd', attn_weight, values, precision=HIGH)

def forward_layer(counts, inputs, gain_attn, w_query, w_key, w_value, w_output, gain_ffn, w_gate, w_up, w_down):
    normed_in = low(rms_norm(inputs, low(gain_attn)))
    queries = low_back(low(matmul(normed_in, low(w_query))))
    keys = low_back(low(matmul(normed_in, low(w_key))))
    values = low_back(low(matmul(normed_in, low(w_value))))
    shape_four = (N_DP, SEQ, H, HD)
    attended = lax.map(jax.checkpoint(attend_sequence), (queries.reshape(shape_four), keys.reshape(shape_four), values.reshape(shape_four), counts))
    attended = low_back(low(attended.reshape(TOKENS, H * HD)))
    attn_branch = low_back(matmul(attended, low(w_output)))
    hidden_state = inputs + attn_branch
    normed_mid = low(rms_norm(hidden_state, low(gain_ffn)))
    gate_value = low_back(low(matmul(normed_mid, low(w_gate))))
    up_value = low_back(low(matmul(normed_mid, low(w_up))))
    inner = low(jax.nn.silu(gate_value) * up_value)
    ffn_branch = low_back(matmul(inner, low(w_down)))
    return hidden_state + ffn_branch

def reference(inputs, counts, cotangent, gain_attn, w_query, w_key, w_value, w_output, gain_ffn, w_gate, w_up, w_down):
    positions = jnp.arange(SEQ)
    valid = (positions[None, :] < counts[:, None]).astype(jnp.float32).reshape(TOKENS, 1)
    layer = partial(forward_layer, counts)
    result, pullback = jax.vjp(layer, inputs.astype(jnp.float32), gain_attn, w_query, w_key, w_value, w_output, gain_ffn, w_gate, w_up, w_down)
    grads = pullback(cotangent.astype(jnp.float32) * valid)
    return (result.astype(jnp.bfloat16), grads[0], grads[1], grads[2], grads[3], grads[4], grads[5], grads[6], grads[7], grads[8], grads[9])
```

```python
import functools
import math

import jax
import jax.numpy as jnp
from jax import lax
from jax.experimental import pallas as pl
from jax.experimental.pallas import tpu as pltpu
from jax.sharding import PartitionSpec as P

HD = 128
EPS = 1e-06
BF = jnp.bfloat16
F32 = jnp.float32
NT = (((1,), (1,)), ((), ()))
TN = (((0,), (0,)), ((), ()))
NN = (((1,), (0,)), ((), ()))


def dot(a, b, dims=NN):
    return lax.dot_general(a, b, dims, preferred_element_type=F32)


def logistic_block(q, k, seq):
    raw = dot(q, k, NT)
    shifted = math.log(seq) - raw * HD ** (-0.5)
    return 1.0 / (1.0 + jnp.exp(shifted))


def allowed_block(row0, rows, col0, cols, count):
    ri = row0 + lax.broadcasted_iota(jnp.int32, (rows, cols), 0)
    ci = col0 + lax.broadcasted_iota(jnp.int32, (rows, cols), 1)
    return (ci <= ri) & (ci < count)


def attn_fwd_kernel(seq, blk, count_ref, q_ref, k_ref, v_ref, o_ref):
    count = count_ref[0]
    for i in range(seq // blk):
        rows = pl.ds(i * blk, blk)
        width = (i + 1) * blk
        lg = logistic_block(q_ref[rows, :], k_ref[pl.ds(0, width), :], seq)
        w = jnp.where(allowed_block(i * blk, blk, 0, width, count), lg, 0.0).astype(BF)
        o_ref[rows, :] = dot(w, v_ref[pl.ds(0, width), :]).astype(BF)


def attn_fwd(qkv, count, seq):
    heads = qkv.shape[1] // (3 * HD)
    blk = min(256, seq)
    spec = lambda part: pl.BlockSpec((seq, HD), lambda h, c: (0, part * heads + h))
    return pl.pallas_call(
        functools.partial(attn_fwd_kernel, seq, blk),
        grid_spec=pltpu.PrefetchScalarGridSpec(
            num_scalar_prefetch=1,
            grid=(heads,),
            in_specs=[spec(0), spec(1), spec(2)],
            out_specs=pl.BlockSpec((seq, HD), lambda h, c: (0, h)),
        ),
        out_shape=jax.ShapeDtypeStruct((seq, heads * HD), BF),
        compiler_params=pltpu.CompilerParams(vmem_limit_bytes=48 * 1024 * 1024),
        name="attn_fwd",
    )(count, qkv, qkv, qkv)


def attn_bwd_kernel(seq, blk, count_ref, q_ref, k_ref, v_ref, g_ref, dq_ref, dk_ref, dv_ref, dka, dva):
    count = count_ref[0]
    n = seq // blk
    for i in range(n - 1, -1, -1):
        rows = pl.ds(i * blk, blk)
        width = (i + 1) * blk
        keys = pl.ds(0, width)
        q = q_ref[rows, :]
        g = g_ref[rows, :]
        k = k_ref[keys, :]
        lg = jnp.where(
            allowed_block(i * blk, blk, 0, width, count), logistic_block(q, k, seq), 0.0
        )
        w = lg.astype(BF)
        gw = dot(g, v_ref[keys, :], NT)
        gs = (gw * lg * (1.0 - lg) * HD ** (-0.5)).astype(BF)
        dq_ref[rows, :] = dot(gs, k).astype(BF)
        dk = dot(gs, q, TN)
        dv = dot(w, g, TN)
        if i == n - 1:
            dka[...] = dk
            dva[...] = dv
        else:
            dka[keys, :] += dk
            dva[keys, :] += dv
    dk_ref[...] = dka[...].astype(BF)
    dv_ref[...] = dva[...].astype(BF)


def attn_bwd(qkv, grad, count, seq):
    heads = qkv.shape[1] // (3 * HD)
    blk = min(256, seq)
    spec = lambda part: pl.BlockSpec((seq, HD), lambda h, c: (0, part * heads + h))
    out = jax.ShapeDtypeStruct((seq, heads * HD), BF)
    return pl.pallas_call(
        functools.partial(attn_bwd_kernel, seq, blk),
        grid_spec=pltpu.PrefetchScalarGridSpec(
            num_scalar_prefetch=1,
            grid=(heads,),
            in_specs=[spec(0), spec(1), spec(2), spec(0)],
            out_specs=[spec(0)] * 3,
            scratch_shapes=[pltpu.VMEM((seq, HD), F32), pltpu.VMEM((seq, HD), F32)],
        ),
        out_shape=[out, out, out],
        compiler_params=pltpu.CompilerParams(vmem_limit_bytes=48 * 1024 * 1024),
        name="attn_bwd",
    )(count, qkv, qkv, qkv, grad)


def norm_backward(grad_normed, field, scale, gain):
    unit = field * scale
    weighted = grad_normed * gain
    grad_field = scale * (weighted - unit * jnp.mean(weighted * unit, axis=1, keepdims=True))
    return (grad_field, jnp.sum(grad_normed * unit, axis=0))


def after(value, *deps):
    return lax.optimization_barrier((value,) + deps)[0]


def on_device(
    inputs,
    counts,
    cotangent,
    gain_attn,
    w_query,
    w_key,
    w_value,
    w_output,
    gain_ffn,
    w_gate,
    w_up,
    w_down,
):
    seq = inputs.shape[0]
    hh = w_query.shape[1]
    ff = w_gate.shape[1]
    mp = lax.axis_size("mp")
    me = lax.axis_index("mp")
    part = seq // mp
    gather = lambda x: lax.all_gather(x, "dp", axis=0, tiled=True)
    scatter = lambda x: lax.psum_scatter(x, "dp", scatter_dimension=0, tiled=True)
    mp_gather = lambda x: lax.all_gather(x, "mp", axis=0, tiled=True)
    mp_scatter = lambda x: lax.psum_scatter(x.astype(BF), "mp", scatter_dimension=0, tiled=True)
    mine = lambda x: lax.dynamic_slice_in_dim(x, me * part, part, 0)

    attn_shard = jnp.concatenate([w_query, w_key, w_value, w_output.T], axis=1).astype(BF)
    attn_w = gather(attn_shard)
    gu_shard = jnp.concatenate([w_gate, w_up], axis=1).astype(BF)
    gu_w = gather(after(gu_shard, attn_w))
    down_shard = w_down.T.astype(BF)
    down_w = gather(after(down_shard, gu_w))
    gains = lax.all_gather(jnp.stack([gain_attn, gain_ffn]).astype(BF), "dp", axis=1, tiled=True)
    gains = gains.astype(F32)
    gain_in, gain_mid = gains[0:1], gains[1:2]

    count = counts[0]
    valid = (jnp.arange(seq) < count)[:, None]
    source = inputs.astype(F32)
    scale_in = lax.rsqrt(jnp.mean(source * source, axis=1, keepdims=True) + EPS)
    normed_in = (source * scale_in * gain_in).astype(BF)
    qkv = dot(normed_in, attn_w[:, : 3 * hh]).astype(BF)
    attended = attn_fwd(qkv, counts, seq)
    out_wt = attn_w[:, 3 * hh :]
    attn_sum = mp_scatter(dot(attended, out_wt, NT))
    my_source = mine(inputs).astype(F32)
    hidden = my_source + attn_sum.astype(F32)
    scale_mid = lax.rsqrt(jnp.mean(hidden * hidden, axis=1, keepdims=True) + EPS)
    normed_mid = mp_gather((hidden * scale_mid * gain_mid).astype(BF))
    gate_w, up_w = gu_w[:, :ff], gu_w[:, ff:]
    gate = dot(normed_mid, gate_w).astype(BF)
    up = dot(normed_mid, up_w).astype(BF)
    gate_f = gate.astype(F32)
    up_f = up.astype(F32)
    sg = jax.nn.sigmoid(gate_f)
    silu = gate_f * sg
    inner = (silu * up_f).astype(BF)
    grad_ffn = jnp.where(valid, cotangent, jnp.zeros_like(cotangent))
    grad_down_t = dot(grad_ffn, inner, TN).astype(BF)
    grad_inner = dot(grad_ffn, down_w)
    grad_gate = (grad_inner * up_f * sg * (1.0 + gate_f * (1.0 - sg))).astype(BF)
    grad_up = (grad_inner * silu).astype(BF)
    mid_terms = dot(grad_gate, gate_w, NT) + dot(grad_up, up_w, NT)
    grad_mid = mp_scatter(mid_terms).astype(F32)
    rs_down = scatter(grad_down_t)
    grad_gu = jnp.concatenate(
        [dot(normed_mid, grad_gate, TN).astype(BF), dot(normed_mid, grad_up, TN).astype(BF)], axis=1
    )
    rs_gu = scatter(after(grad_gu, rs_down))
    ffn_sum = mp_scatter(dot(inner, down_w, NT))
    layer_out = mp_gather((hidden + ffn_sum.astype(F32)).astype(BF))

    g_norm, g_gain_mid = norm_backward(grad_mid, hidden, scale_mid, gain_mid)
    grad_hidden = mine(grad_ffn).astype(F32) + g_norm
    grad_low = mp_gather(grad_hidden.astype(BF))
    grad_attended = dot(grad_low, out_wt).astype(BF)
    dq, dk, dv = attn_bwd(qkv, grad_attended, counts, seq)
    grads = [dq, dk, dv]
    grad_attn = jnp.concatenate(
        [dot(normed_in, g, TN).astype(BF) for g in grads] + [dot(grad_low, attended, TN).astype(BF)],
        axis=1,
    )
    rs_attn = scatter(after(grad_attn, rs_gu))
    in_terms = sum(dot(g, attn_w[:, i * hh : (i + 1) * hh], NT) for i, g in enumerate(grads))
    grad_in = mp_scatter(in_terms).astype(F32)
    g_source, g_gain_in = norm_backward(grad_in, my_source, mine(scale_in), gain_in)
    input_grad = mp_gather((grad_hidden + g_source).astype(BF)).astype(F32)
    g_gains = lax.psum(jnp.stack([g_gain_in, g_gain_mid]), ("dp", "mp"))
    width = g_gains.shape[1] // lax.axis_size("dp")
    g_gains = lax.dynamic_slice_in_dim(g_gains, lax.axis_index("dp") * width, width, 1)
    rs_attn = rs_attn.astype(F32)
    rs_gu = rs_gu.astype(F32)
    return (
        layer_out,
        input_grad,
        g_gains[0],
        rs_attn[:, :hh],
        rs_attn[:, hh : 2 * hh],
        rs_attn[:, 2 * hh : 3 * hh],
        rs_attn[:, 3 * hh :].T,
        g_gains[1],
        rs_gu[:, :ff],
        rs_gu[:, ff:],
        rs_down.astype(F32).T,
    )


def solution(mesh):
    row, both, swapped = P("dp", None), P("dp", "mp"), P("mp", "dp")
    weights = (both, both, both, swapped)
    ffn = (both, both, swapped)
    return jax.shard_map(
        on_device,
        mesh=mesh,
        in_specs=(row, P("dp"), row, P("dp")) + weights + (P("dp"),) + ffn,
        out_specs=(row, row, P("dp")) + weights + (P("dp"),) + ffn,
        check_vma=False,
    )
```

```python
import functools
import math

import jax
import jax.numpy as jnp
from jax import lax
from jax.experimental import pallas as pl
from jax.experimental.pallas import tpu as pltpu
from jax.sharding import PartitionSpec as P

HD = 128
EPS = 1e-06
BF = jnp.bfloat16
F32 = jnp.float32
NT = (((1,), (1,)), ((), ()))
TN = (((0,), (0,)), ((), ()))
NN = (((1,), (0,)), ((), ()))


def dot(a, b, dims=NN):
    return lax.dot_general(a, b, dims, preferred_element_type=F32)


def logistic_block(q, k, seq):
    raw = dot(q, k, NT)
    shifted = math.log(seq) - raw * HD ** (-0.5)
    return 1.0 / (1.0 + jnp.exp(shifted))


def allowed_block(row0, rows, col0, cols, count):
    ri = row0 + lax.broadcasted_iota(jnp.int32, (rows, cols), 0)
    ci = col0 + lax.broadcasted_iota(jnp.int32, (rows, cols), 1)
    return (ci <= ri) & (ci < count)


def attn_fwd_kernel(seq, blk, count_ref, q_ref, k_ref, v_ref, o_ref):
    count = count_ref[0]
    for i in range(seq // blk):
        rows = pl.ds(i * blk, blk)
        width = (i + 1) * blk
        lg = logistic_block(q_ref[rows, :], k_ref[pl.ds(0, width), :], seq)
        w = jnp.where(allowed_block(i * blk, blk, 0, width, count), lg, 0.0).astype(BF)
        o_ref[rows, :] = dot(w, v_ref[pl.ds(0, width), :]).astype(BF)


def attn_fwd(qkv, count, seq):
    heads = qkv.shape[1] // (3 * HD)
    blk = min(256, seq)
    spec = lambda part: pl.BlockSpec((seq, HD), lambda h, c: (0, part * heads + h))
    return pl.pallas_call(
        functools.partial(attn_fwd_kernel, seq, blk),
        grid_spec=pltpu.PrefetchScalarGridSpec(
            num_scalar_prefetch=1,
            grid=(heads,),
            in_specs=[spec(0), spec(1), spec(2)],
            out_specs=pl.BlockSpec((seq, HD), lambda h, c: (0, h)),
        ),
        out_shape=jax.ShapeDtypeStruct((seq, heads * HD), BF),
        compiler_params=pltpu.CompilerParams(vmem_limit_bytes=48 * 1024 * 1024),
        name="attn_fwd",
    )(count, qkv, qkv, qkv)


def attn_bwd_kernel(seq, blk, count_ref, q_ref, k_ref, v_ref, g_ref, dq_ref, dk_ref, dv_ref, dka, dva):
    count = count_ref[0]
    n = seq // blk
    for i in range(n - 1, -1, -1):
        rows = pl.ds(i * blk, blk)
        width = (i + 1) * blk
        keys = pl.ds(0, width)
        q = q_ref[rows, :]
        g = g_ref[rows, :]
        k = k_ref[keys, :]
        lg = jnp.where(
            allowed_block(i * blk, blk, 0, width, count), logistic_block(q, k, seq), 0.0
        )
        w = lg.astype(BF)
        gw = dot(g, v_ref[keys, :], NT)
        gs = (gw * lg * (1.0 - lg) * HD ** (-0.5)).astype(BF)
        dq_ref[rows, :] = dot(gs, k).astype(BF)
        dk = dot(gs, q, TN)
        dv = dot(w, g, TN)
        if i == n - 1:
            dka[...] = dk
            dva[...] = dv
        else:
            dka[keys, :] += dk
            dva[keys, :] += dv
    dk_ref[...] = dka[...].astype(BF)
    dv_ref[...] = dva[...].astype(BF)


def attn_bwd(qkv, grad, count, seq):
    heads = qkv.shape[1] // (3 * HD)
    blk = min(256, seq)
    spec = lambda part: pl.BlockSpec((seq, HD), lambda h, c: (0, part * heads + h))
    out = jax.ShapeDtypeStruct((seq, heads * HD), BF)
    return pl.pallas_call(
        functools.partial(attn_bwd_kernel, seq, blk),
        grid_spec=pltpu.PrefetchScalarGridSpec(
            num_scalar_prefetch=1,
            grid=(heads,),
            in_specs=[spec(0), spec(1), spec(2), spec(0)],
            out_specs=[spec(0)] * 3,
            scratch_shapes=[pltpu.VMEM((seq, HD), F32), pltpu.VMEM((seq, HD), F32)],
        ),
        out_shape=[out, out, out],
        compiler_params=pltpu.CompilerParams(vmem_limit_bytes=48 * 1024 * 1024),
        name="attn_bwd",
    )(count, qkv, qkv, qkv, grad)


MESH = pl.DeviceIdType.MESH
VMEM_LIMIT = 60 * 1024 * 1024


class Place:
    def __init__(self, n_dp):
        self.n = n_dp // 2
        self.dp = lax.axis_index("dp")
        self.m = lax.axis_index("mp")
        self.p = lax.div(self.dp, 2)
        self.c = lax.rem(self.dp, 2)
        self.above = (self.dp + 2, self.m)
        self.below = (self.dp - 2, self.m)
        self.core = (self.dp + 1 - 2 * self.c, self.m)
        x = lax.rem(self.m, 2)
        y = lax.div(self.m, 2)
        self.qx = self.m + 1 - 2 * x
        self.qy = self.m + 2 - 4 * y
        self.qd = 3 - self.m
        self.xdev = (self.dp, self.qx)
        self.ydev = (self.dp, self.qy)
        self.has_above = self.p < self.n - 1
        self.has_below = self.p > 0

    def fold(self, bit):
        return (self.dp + bit - 2 * bit * lax.rem(lax.div(self.dp, bit), 2), self.m)


def signal(dev):
    pl.semaphore_signal(pltpu.get_barrier_semaphore(), inc=1, device_id=dev, device_id_type=MESH)


def enter(at, extra=()):
    always = [at.core, at.xdev, at.ydev] + list(extra)
    for dev in always:
        signal(dev)

    @pl.when(at.has_above)
    def _():
        signal(at.above)

    @pl.when(at.has_below)
    def _():
        signal(at.below)

    ends = at.has_above.astype(jnp.int32) + at.has_below.astype(jnp.int32)
    pl.semaphore_wait(pltpu.get_barrier_semaphore(), len(always) + ends)


def remote(src, dst, send, recv, dev):
    return pltpu.make_async_remote_copy(
        src_ref=src, dst_ref=dst, send_sem=send, recv_sem=recv, device_id=dev, device_id_type=MESH
    )


def order_of(k, at):
    n, p = at.n, at.p
    if k == n - 1:
        return p
    high = jnp.where(k < p, k, n - 1 - k + p)
    low = jnp.where(k < n - 1 - p, n - 1 - k, k - (n - 1 - p))
    return jnp.where(2 * p >= n, high, low)


class LineSum:
    def __init__(self, at, pout, own, din, uin, sems):
        self.at, self.pout, self.own, self.din, self.uin = at, pout, own, din, uin
        self.po_s, self.po_r, self.d_s, self.d_r, self.u_s, self.u_r = sems
        self.pieces = own.shape[1]

    def core_copy(self, k):
        j = order_of(k, self.at)
        return remote(
            self.pout.at[k % 2], self.own.at[j], self.po_s.at[k % 2], self.po_r.at[k], self.at.core
        )

    def down_copy(self, s, i):
        return remote(
            self.own.at[s, i], self.din.at[s, i], self.d_s.at[s, i], self.d_r.at[s, i], self.at.below
        )

    def up_copy(self, s, i):
        n = self.at.n
        return remote(
            self.own.at[n - 1 - s, i],
            self.uin.at[s, i],
            self.u_s.at[s, i],
            self.u_r.at[s, i],
            self.at.above,
        )

    def other(self, k, tile):
        if k >= 2:
            self.core_copy(k - 2).wait_send()
        j = order_of(k, self.at)
        tile(2 * j + 1 - self.at.c, lambda i, v: self.store(self.pout, (k % 2,), i, v, False))
        self.core_copy(k).start()

    def store(self, ref, lead, i, value, add):
        at = lead + (i,)
        if add:
            value = value + ref[at].astype(F32)
        ref[at] = value.astype(BF)

    def mine(self, k, tile):
        at = self.at
        j = order_of(k, at)
        self.core_copy(k).wait_recv()
        tile(2 * j + at.c, lambda i, v: self.store(self.own, (j,), i, v, True))
        if k < at.n - 1:

            @pl.when(at.p == at.n - 1)
            def _():
                for i in range(self.pieces):
                    self.down_copy(k, i).start()

            @pl.when(at.p == 0)
            def _():
                for i in range(self.pieces):
                    self.up_copy(k, i).start()

    def add(self, dst, src, i):
        rows = dst.shape[0]
        step = 64
        for r in range(0, rows, step):
            rs = pl.ds(r, step)
            dst[rs, :] = (dst[rs, :].astype(F32) + src[rs, :].astype(F32)).astype(BF)

    def slot(self, t):
        at = self.at
        n, p = at.n, at.p
        sd = t - (n - 2 - p)
        su = t - (p - 1)

        @pl.loop(0, self.pieces)
        def _(i):
            @pl.when((sd >= 0) & (sd < p) & at.has_above)
            def _():
                self.down_copy(sd, i).wait_recv()
                self.add(self.own.at[sd, i], self.din.at[sd, i], i)
                self.down_copy(sd, i).start()

            @pl.when((su >= 0) & (su < n - 1 - p) & at.has_below)
            def _():
                self.up_copy(su, i).wait_recv()
                self.add(self.own.at[n - 1 - su, i], self.uin.at[su, i], i)
                self.up_copy(su, i).start()

    def final(self, out):
        at = self.at
        n, p = at.n, at.p

        @pl.loop(0, self.pieces)
        def _(i):
            @pl.when(at.has_above)
            def _():
                self.down_copy(p, i).wait_recv()

            @pl.when(at.has_below)
            def _():
                self.up_copy(n - 1 - p, i).wait_recv()

            for r in range(0, out.shape[1], 64):
                rs = pl.ds(r, 64)
                out[i, rs, :] = self.own[p, i, rs, :].astype(F32)

                @pl.when(at.has_above)
                def _():
                    out[i, rs, :] += self.din[p, i, rs, :].astype(F32)

                @pl.when(at.has_below)
                def _():
                    out[i, rs, :] += self.uin[n - 1 - p, i, rs, :].astype(F32)

    def drain(self):
        at = self.at
        n, p = at.n, at.p
        for k in range(max(0, n - 2), n):
            self.core_copy(k).wait_send()
        for s in range(n - 1):

            @pl.when(s < p)
            def _():
                for i in range(self.pieces):
                    self.down_copy(s, i).wait_send()

            @pl.when(s < n - 1 - p)
            def _():
                for i in range(self.pieces):
                    self.up_copy(s, i).wait_send()


def line_sum_scratch(n, pieces, rows, cols):
    dma = pltpu.SemaphoreType.DMA
    return [
        pltpu.VMEM((2, pieces, rows, cols), BF),
        pltpu.VMEM((n, pieces, rows, cols), BF),
        pltpu.VMEM((n - 1, pieces, rows, cols), BF),
        pltpu.VMEM((n - 1, pieces, rows, cols), BF),
        dma((2,)),
        dma((n,)),
        dma((n - 1, pieces)),
        dma((n - 1, pieces)),
        dma((n - 1, pieces)),
        dma((n - 1, pieces)),
    ]


class QuadSum:
    def __init__(self, at, t, r1, r2, sems):
        self.at, self.t, self.r1, self.r2 = at, t, r1, r2
        self.s1, self.v1, self.s2, self.v2 = sems

    def first(self, half, turn):
        at = self.at
        dev, quarter = (at.xdev, at.qx) if half == 0 else (at.ydev, at.qy)
        q = at.qd if turn == 0 else quarter
        return remote(
            self.t.at[half, q],
            self.r1.at[half, turn],
            self.s1.at[half, turn],
            self.v1.at[half, turn],
            dev,
        )

    def second(self, half):
        at = self.at
        dev, q = (at.ydev, at.qy) if half == 0 else (at.xdev, at.qx)
        return remote(
            self.r1.at[half, 0], self.r2.at[half], self.s2.at[half], self.v2.at[half], dev
        )

    def turn(self):
        at = self.at
        for half in range(2):
            q = at.qy if half == 0 else at.qx
            self.first(half, 0).wait_recv()

            @pl.loop(0, self.t.shape[2] // 64)
            def _(b):
                rs = pl.ds(pl.multiple_of(b * 64, 64), 64)
                total = self.r1[half, 0, rs, :].astype(F32) + self.t[half, q, rs, :].astype(F32)
                self.r1[half, 0, rs, :] = total.astype(BF)

            self.second(half).start()

    def arrive(self):
        for half in range(2):
            self.first(half, 1).wait_recv()
            self.second(half).wait_recv()

    def total(self, half, rs):
        own = self.t[half, self.at.m, rs, :].astype(F32)
        return own + self.r1[half, 1, rs, :].astype(F32) + self.r2[half, rs, :].astype(F32)

    def drain(self):
        for half in range(2):
            self.first(half, 0).wait_send()
            self.first(half, 1).wait_send()
            self.second(half).wait_send()


def quad_sum_scratch(rows, cols):
    dma = pltpu.SemaphoreType.DMA
    return [
        pltpu.VMEM((2, 4, rows, cols), BF),
        pltpu.VMEM((2, 2, rows, cols), BF),
        pltpu.VMEM((2, rows, cols), BF),
        dma((2, 2)),
        dma((2, 2)),
        dma((2,)),
        dma((2,)),
    ]


class QuadGather:
    def __init__(self, at, own, out, sems):
        self.at, self.own, self.out = at, own, out
        self.s, self.v, self.s2, self.v2, self.here = sems

    def spot(self, q, half):
        rows, cols = self.own.shape[1], self.own.shape[2]
        rs = pl.ds(pl.multiple_of(q * rows, rows), rows)
        return self.out.at[rs, pl.ds(half * cols, cols)]

    def direct(self, half, way):
        at = self.at
        dev = at.xdev if way == 0 else at.ydev
        return remote(
            self.own.at[half],
            self.spot(at.m, half),
            self.s.at[half, way],
            self.v.at[half, way],
            dev,
        )

    def onward(self, half):
        at = self.at
        q, dev = (at.qy, at.xdev) if half == 0 else (at.qx, at.ydev)
        return remote(
            self.spot(q, half), self.spot(q, half), self.s2.at[half], self.v2.at[half], dev
        )

    def keep(self, half):
        return pltpu.make_async_copy(self.own.at[half], self.spot(self.at.m, half), self.here.at[half])

    def start(self):
        for way in ((0, 1), (1, 0), (0, 0), (1, 1)):
            self.direct(*way).start()
        for half in range(2):
            self.keep(half).start()

    def forward(self):
        self.direct(0, 1).wait_recv()
        self.onward(0).start()
        self.direct(1, 0).wait_recv()
        self.onward(1).start()

    def finish(self):
        for half in range(2):
            self.direct(half, half).wait_recv()
            self.onward(half).wait_recv()
            self.keep(half).wait()
            self.onward(half).wait_send()
            for way in range(2):
                self.direct(half, way).wait_send()


def quad_gather_scratch(rows, cols):
    dma = pltpu.SemaphoreType.DMA
    return [
        pltpu.VMEM((2, rows, cols), BF),
        dma((2, 2)),
        dma((2, 2)),
        dma((2,)),
        dma((2,)),
        dma((2,)),
    ]


def halves(fn):
    return [fn(0), fn(1)]


def last_kernel(
    n_dp,
    dqkv_hbm,
    aw_hbm,
    nt_hbm,
    gt_hbm,
    att_hbm,
    x_ref,
    gh_ref,
    gain_ref,
    gmid_ref,
    rs_ref,
    grad_ref,
    gains_ref,
    dqkv,
    aw,
    nt,
    gt,
    att,
    loads,
    pout,
    own,
    din,
    uin,
    po_s,
    po_r,
    d_s,
    d_r,
    u_s,
    u_r,
    t,
    r1,
    r2,
    q1,
    q2,
    q3,
    q4,
    gown,
    g1,
    g2,
    g3,
    g4,
    g5,
    fold_out,
    fold_in,
    fold_s,
    fold_r,
):
    at = Place(n_dp)
    hh = att_hbm.shape[1]
    part = t.shape[2]
    chunk = own.shape[2]
    half_cols = t.shape[3]
    copies = [
        pltpu.make_async_copy(src, dst, loads.at[i])
        for i, (src, dst) in enumerate(
            [
                (dqkv_hbm, dqkv),
                (aw_hbm.at[:, pl.ds(0, 3 * hh)], aw),
                (nt_hbm, nt),
                (att_hbm, att),
                (gt_hbm, gt),
            ]
        )
    ]
    for cp in copies:
        cp.start()
    bits = [b for b in (2, 4, 8, 16) if b < n_dp]
    enter(at, [at.fold(b) for b in bits[1:]])
    quad = QuadSum(at, t, r1, r2, (q1, q2, q3, q4))
    line = LineSum(at, pout, own, din, uin, (po_s, po_r, d_s, d_r, u_s, u_r))
    gather = QuadGather(at, gown, grad_ref, (g1, g2, g3, g4, g5))
    copies[0].wait()
    copies[1].wait()

    def terms(q):
        rs = pl.ds(pl.multiple_of(q * part, part), part)
        width = 512

        @pl.loop(0, half_cols // width)
        def _(i):
            for half in range(2):
                d0 = pl.multiple_of(half * half_cols + i * width, width)
                v = dot(dqkv[rs, :], aw[pl.ds(d0, width), :], NT)
                t[half, q, :, pl.ds(pl.multiple_of(i * width, width), width)] = v.astype(BF)

    terms(at.qd)
    quad.first(0, 0).start()
    quad.first(1, 0).start()
    terms(at.qx)
    quad.first(0, 1).start()
    terms(at.qy)
    quad.first(1, 1).start()
    for cp in copies[2:]:
        cp.wait()

    def tile(block, put):
        rs = pl.ds(pl.multiple_of(block * chunk, chunk), chunk)

        @pl.loop(0, 3)
        def _(i):
            put(i, dot(nt[rs, :], dqkv[:, pl.ds(pl.multiple_of(i * hh, hh), hh)]))

        put(3, dot(gt[rs, :], att[...]))

    n = at.n
    for k in range(n + 1):
        if k < n:
            line.other(k, tile)
        if k > 0:
            line.mine(k - 1, tile)
    terms(at.m)
    quad.turn()
    line.slot(0)
    quad.arrive()

    fold_out[...] = jnp.zeros_like(fold_out)

    @pl.loop(0, part // 32)
    def _(b):
        rs = pl.ds(pl.multiple_of(b * 32, 32), 32)
        x = x_ref[rs, :].astype(F32)
        scale = lax.rsqrt(jnp.mean(x * x, axis=1, keepdims=True) + EPS)
        g = jnp.concatenate([quad.total(0, rs), quad.total(1, rs)], axis=1)
        unit = x * scale
        weighted = g * gain_ref[...]
        field = scale * (weighted - unit * jnp.mean(weighted * unit, axis=1, keepdims=True))
        res = (gh_ref[rs, :] + field).astype(BF)
        gown[0, rs, :] = res[:, :half_cols]
        gown[1, rs, :] = res[:, half_cols:]
        fold_out[0, 0:1, :] += jnp.sum(g * unit, axis=0, keepdims=True)

    gather.start()
    fold_out[0, 1:2, :] = gmid_ref[...]
    devs = [at.core, at.xdev, at.ydev] + [at.fold(b) for b in bits]

    def fold_copy(b):
        return remote(fold_out.at[b], fold_in.at[b], fold_s.at[b], fold_r.at[b], devs[b])

    def fold_next(b):
        fold_copy(b).wait_recv()
        nxt = fold_out[b] + fold_in[b]
        if b + 1 < len(devs):
            fold_out[b + 1] = nxt
            fold_copy(b + 1).start()
        else:
            gains_ref[...] = nxt

    fold_copy(0).start()
    for s in range(1, n - 2):
        line.slot(s)
    gather.forward()
    for b in range(len(devs)):
        fold_next(b)
    line.final(rs_ref)
    gather.finish()
    line.drain()
    quad.drain()
    for b in range(len(devs)):
        fold_copy(b).wait_send()


def last_stage(n_dp, dqkv, aw, nt, gt, att, x, gh, gain, gmid):
    seq, hh = att.shape
    d = nt.shape[0]
    n, part, chunk = n_dp // 2, seq // 4, d // n_dp
    dma = pltpu.SemaphoreType.DMA
    anyspace = pl.BlockSpec(memory_space=pl.ANY)
    vm = pl.BlockSpec(memory_space=pltpu.VMEM)
    folds = 3 + len([b for b in (2, 4, 8, 16) if b < n_dp])
    return pl.pallas_call(
        functools.partial(last_kernel, n_dp),
        out_shape=[
            jax.ShapeDtypeStruct((4, chunk, hh), F32),
            jax.ShapeDtypeStruct((seq, d), BF),
            jax.ShapeDtypeStruct((8, d), F32),
        ],
        in_specs=[anyspace] * 5 + [vm] * 4,
        out_specs=[vm, anyspace, vm],
        scratch_shapes=[
            pltpu.VMEM((seq, 3 * hh), BF),
            pltpu.VMEM((d, 3 * hh), BF),
            pltpu.VMEM((d, seq), BF),
            pltpu.VMEM((d, seq), BF),
            pltpu.VMEM((seq, hh), BF),
            dma((5,)),
        ]
        + line_sum_scratch(n, 4, chunk, hh)
        + quad_sum_scratch(part, d // 2)
        + quad_gather_scratch(part, d // 2)
        + [
            pltpu.VMEM((folds, 8, d), F32),
            pltpu.VMEM((folds, 8, d), F32),
            dma((folds,)),
            dma((folds,)),
        ],
        compiler_params=pltpu.CompilerParams(
            collective_id=5, has_side_effects=True, vmem_limit_bytes=VMEM_LIMIT
        ),
        name="last_stage",
    )(dqkv, aw, nt, gt, att, x, gh, gain, gmid)


def norm_backward(grad_normed, field, scale, gain):
    unit = field * scale
    weighted = grad_normed * gain
    grad_field = scale * (weighted - unit * jnp.mean(weighted * unit, axis=1, keepdims=True))
    return (grad_field, jnp.sum(grad_normed * unit, axis=0))


def after(value, *deps):
    return lax.optimization_barrier((value,) + deps)[0]


def on_device(
    inputs,
    counts,
    cotangent,
    gain_attn,
    w_query,
    w_key,
    w_value,
    w_output,
    gain_ffn,
    w_gate,
    w_up,
    w_down,
):
    seq = inputs.shape[0]
    hh = w_query.shape[1]
    ff = w_gate.shape[1]
    mp = lax.axis_size("mp")
    me = lax.axis_index("mp")
    part = seq // mp
    gather = lambda x: lax.all_gather(x, "dp", axis=0, tiled=True)
    scatter = lambda x: lax.psum_scatter(x, "dp", scatter_dimension=0, tiled=True)
    mp_gather = lambda x: lax.all_gather(x, "mp", axis=0, tiled=True)
    mp_scatter = lambda x: lax.psum_scatter(x.astype(BF), "mp", scatter_dimension=0, tiled=True)
    mine = lambda x: lax.dynamic_slice_in_dim(x, me * part, part, 0)

    attn_shard = jnp.concatenate([w_query, w_key, w_value, w_output.T], axis=1).astype(BF)
    attn_w = gather(attn_shard)
    gu_shard = jnp.concatenate([w_gate, w_up], axis=1).astype(BF)
    gu_w = gather(after(gu_shard, attn_w))
    down_shard = w_down.T.astype(BF)
    down_w = gather(after(down_shard, gu_w))
    gains = lax.all_gather(jnp.stack([gain_attn, gain_ffn]).astype(BF), "dp", axis=1, tiled=True)
    gains = gains.astype(F32)
    gain_in, gain_mid = gains[0:1], gains[1:2]

    count = counts[0]
    valid = (jnp.arange(seq) < count)[:, None]
    source = inputs.astype(F32)
    scale_in = lax.rsqrt(jnp.mean(source * source, axis=1, keepdims=True) + EPS)
    normed_in = (source * scale_in * gain_in).astype(BF)
    qkv = dot(normed_in, attn_w[:, : 3 * hh]).astype(BF)
    attended = attn_fwd(qkv, counts, seq)
    out_wt = attn_w[:, 3 * hh :]
    attn_sum = mp_scatter(dot(attended, out_wt, NT))
    my_source = mine(inputs).astype(F32)
    hidden = my_source + attn_sum.astype(F32)
    scale_mid = lax.rsqrt(jnp.mean(hidden * hidden, axis=1, keepdims=True) + EPS)
    normed_mid = mp_gather((hidden * scale_mid * gain_mid).astype(BF))
    gate_w, up_w = gu_w[:, :ff], gu_w[:, ff:]
    gate = dot(normed_mid, gate_w).astype(BF)
    up = dot(normed_mid, up_w).astype(BF)
    gate_f = gate.astype(F32)
    up_f = up.astype(F32)
    sg = jax.nn.sigmoid(gate_f)
    silu = gate_f * sg
    inner = (silu * up_f).astype(BF)
    grad_ffn = jnp.where(valid, cotangent, jnp.zeros_like(cotangent))
    grad_down_t = dot(grad_ffn, inner, TN).astype(BF)
    grad_inner = dot(grad_ffn, down_w)
    grad_gate = (grad_inner * up_f * sg * (1.0 + gate_f * (1.0 - sg))).astype(BF)
    grad_up = (grad_inner * silu).astype(BF)
    mid_terms = dot(grad_gate, gate_w, NT) + dot(grad_up, up_w, NT)
    grad_mid = mp_scatter(mid_terms).astype(F32)
    rs_down = scatter(grad_down_t)
    grad_gu = jnp.concatenate(
        [dot(normed_mid, grad_gate, TN).astype(BF), dot(normed_mid, grad_up, TN).astype(BF)], axis=1
    )
    rs_gu = scatter(after(grad_gu, rs_down))
    ffn_sum = mp_scatter(dot(inner, down_w, NT))
    layer_out = mp_gather((hidden + ffn_sum.astype(F32)).astype(BF))

    g_norm, g_gain_mid = norm_backward(grad_mid, hidden, scale_mid, gain_mid)
    grad_hidden = mine(grad_ffn).astype(F32) + g_norm
    grad_low = mp_gather(grad_hidden.astype(BF))
    grad_attended = dot(grad_low, out_wt).astype(BF)
    dq, dk, dv = attn_bwd(qkv, grad_attended, counts, seq)
    rs_attn, grad_low_in, g_gains = last_stage(
        lax.axis_size("dp"),
        jnp.concatenate([dq, dk, dv], axis=1),
        attn_w,
        normed_in.T,
        grad_low.T,
        attended,
        mine(inputs),
        grad_hidden,
        gain_in,
        g_gain_mid[None],
    )
    input_grad = grad_low_in.astype(F32)
    width = g_gains.shape[1] // lax.axis_size("dp")
    g_gains = lax.dynamic_slice_in_dim(g_gains, lax.axis_index("dp") * width, width, 1)
    rs_gu = rs_gu.astype(F32)
    return (
        layer_out,
        input_grad,
        g_gains[0],
        rs_attn[0],
        rs_attn[1],
        rs_attn[2],
        rs_attn[3].T,
        g_gains[1],
        rs_gu[:, :ff],
        rs_gu[:, ff:],
        rs_down.astype(F32).T,
    )


def solution(mesh):
    row, both, swapped = P("dp", None), P("dp", "mp"), P("mp", "dp")
    weights = (both, both, both, swapped)
    ffn = (both, both, swapped)
    return jax.shard_map(
        on_device,
        mesh=mesh,
        in_specs=(row, P("dp"), row, P("dp")) + weights + (P("dp"),) + ffn,
        out_specs=(row, row, P("dp")) + weights + (P("dp"),) + ffn,
        check_vma=False,
    )
```

```python
import functools
import math

import jax
import jax.numpy as jnp
from jax import lax
from jax.experimental import pallas as pl
from jax.experimental.pallas import tpu as pltpu
from jax.sharding import PartitionSpec as P

HD = 128
EPS = 1e-06
BF = jnp.bfloat16
F32 = jnp.float32
NT = (((1,), (1,)), ((), ()))
TN = (((0,), (0,)), ((), ()))
NN = (((1,), (0,)), ((), ()))


def dot(a, b, dims=NN):
    return lax.dot_general(a, b, dims, preferred_element_type=F32)


def logistic_block(q, k, seq):
    raw = dot(q, k, NT)
    shifted = math.log(seq) - raw * HD ** (-0.5)
    return 1.0 / (1.0 + jnp.exp(shifted))


def allowed_block(row0, rows, col0, cols, count):
    ri = row0 + lax.broadcasted_iota(jnp.int32, (rows, cols), 0)
    ci = col0 + lax.broadcasted_iota(jnp.int32, (rows, cols), 1)
    return (ci <= ri) & (ci < count)


def attn_fwd_kernel(seq, blk, count_ref, q_ref, k_ref, v_ref, o_ref):
    count = count_ref[0]
    for i in range(seq // blk):
        rows = pl.ds(i * blk, blk)
        width = (i + 1) * blk
        lg = logistic_block(q_ref[rows, :], k_ref[pl.ds(0, width), :], seq)
        w = jnp.where(allowed_block(i * blk, blk, 0, width, count), lg, 0.0).astype(BF)
        o_ref[rows, :] = dot(w, v_ref[pl.ds(0, width), :]).astype(BF)


def attn_fwd(qkv, count, seq):
    heads = qkv.shape[1] // (3 * HD)
    blk = min(256, seq)
    spec = lambda part: pl.BlockSpec((seq, HD), lambda h, c: (0, part * heads + h))
    return pl.pallas_call(
        functools.partial(attn_fwd_kernel, seq, blk),
        grid_spec=pltpu.PrefetchScalarGridSpec(
            num_scalar_prefetch=1,
            grid=(heads,),
            in_specs=[spec(0), spec(1), spec(2)],
            out_specs=pl.BlockSpec((seq, HD), lambda h, c: (0, h)),
        ),
        out_shape=jax.ShapeDtypeStruct((seq, heads * HD), BF),
        compiler_params=pltpu.CompilerParams(vmem_limit_bytes=48 * 1024 * 1024),
        name="attn_fwd",
    )(count, qkv, qkv, qkv)


def attn_bwd_kernel(seq, blk, count_ref, q_ref, k_ref, v_ref, g_ref, dq_ref, dk_ref, dv_ref, dka, dva):
    count = count_ref[0]
    n = seq // blk
    for i in range(n - 1, -1, -1):
        rows = pl.ds(i * blk, blk)
        width = (i + 1) * blk
        keys = pl.ds(0, width)
        q = q_ref[rows, :]
        g = g_ref[rows, :]
        k = k_ref[keys, :]
        lg = jnp.where(
            allowed_block(i * blk, blk, 0, width, count), logistic_block(q, k, seq), 0.0
        )
        w = lg.astype(BF)
        gw = dot(g, v_ref[keys, :], NT)
        gs = (gw * lg * (1.0 - lg) * HD ** (-0.5)).astype(BF)
        dq_ref[rows, :] = dot(gs, k).astype(BF)
        dk = dot(gs, q, TN)
        dv = dot(w, g, TN)
        if i == n - 1:
            dka[...] = dk
            dva[...] = dv
        else:
            dka[keys, :] += dk
            dva[keys, :] += dv
    dk_ref[...] = dka[...].astype(BF)
    dv_ref[...] = dva[...].astype(BF)


def attn_bwd(qkv, grad, count, seq):
    heads = qkv.shape[1] // (3 * HD)
    blk = min(256, seq)
    spec = lambda part: pl.BlockSpec((seq, HD), lambda h, c: (0, part * heads + h))
    out = jax.ShapeDtypeStruct((seq, heads * HD), BF)
    return pl.pallas_call(
        functools.partial(attn_bwd_kernel, seq, blk),
        grid_spec=pltpu.PrefetchScalarGridSpec(
            num_scalar_prefetch=1,
            grid=(heads,),
            in_specs=[spec(0), spec(1), spec(2), spec(0)],
            out_specs=[spec(0)] * 3,
            scratch_shapes=[pltpu.VMEM((seq, HD), F32), pltpu.VMEM((seq, HD), F32)],
        ),
        out_shape=[out, out, out],
        compiler_params=pltpu.CompilerParams(vmem_limit_bytes=48 * 1024 * 1024),
        name="attn_bwd",
    )(count, qkv, qkv, qkv, grad)


MESH = pl.DeviceIdType.MESH
VMEM_LIMIT = 60 * 1024 * 1024


class Place:
    def __init__(self, n_dp):
        self.n = n_dp // 2
        self.dp = lax.axis_index("dp")
        self.m = lax.axis_index("mp")
        self.p = lax.div(self.dp, 2)
        self.c = lax.rem(self.dp, 2)
        self.above = (self.dp + 2, self.m)
        self.below = (self.dp - 2, self.m)
        self.core = (self.dp + 1 - 2 * self.c, self.m)
        x = lax.rem(self.m, 2)
        y = lax.div(self.m, 2)
        self.qx = self.m + 1 - 2 * x
        self.qy = self.m + 2 - 4 * y
        self.qd = 3 - self.m
        self.xdev = (self.dp, self.qx)
        self.ydev = (self.dp, self.qy)
        self.has_above = self.p < self.n - 1
        self.has_below = self.p > 0

    def fold(self, bit):
        return (self.dp + bit - 2 * bit * lax.rem(lax.div(self.dp, bit), 2), self.m)


def signal(dev):
    pl.semaphore_signal(pltpu.get_barrier_semaphore(), inc=1, device_id=dev, device_id_type=MESH)


def enter(at, extra=()):
    always = [at.core, at.xdev, at.ydev] + list(extra)
    for dev in always:
        signal(dev)

    @pl.when(at.has_above)
    def _():
        signal(at.above)

    @pl.when(at.has_below)
    def _():
        signal(at.below)

    ends = at.has_above.astype(jnp.int32) + at.has_below.astype(jnp.int32)
    pl.semaphore_wait(pltpu.get_barrier_semaphore(), len(always) + ends)


def remote(src, dst, send, recv, dev):
    return pltpu.make_async_remote_copy(
        src_ref=src, dst_ref=dst, send_sem=send, recv_sem=recv, device_id=dev, device_id_type=MESH
    )


def order_of(k, at):
    n, p = at.n, at.p
    if k == n - 1:
        return p
    high = jnp.where(k < p, k, n - 1 - k + p)
    low = jnp.where(k < n - 1 - p, n - 1 - k, k - (n - 1 - p))
    return jnp.where(2 * p >= n, high, low)


class LineSum:
    def __init__(self, at, pout, own, din, uin, sems):
        self.at, self.pout, self.own, self.din, self.uin = at, pout, own, din, uin
        self.po_s, self.po_r, self.d_s, self.d_r, self.u_s, self.u_r = sems
        self.slots, self.pieces = pout.shape[0], own.shape[1]

    def core_copy(self, k):
        j = order_of(k, self.at)
        return remote(
            self.pout.at[k % self.slots],
            self.own.at[j],
            self.po_s.at[k % self.slots],
            self.po_r.at[k],
            self.at.core,
        )

    def down_copy(self, s, i):
        return remote(
            self.own.at[s, i], self.din.at[s, i], self.d_s.at[s, i], self.d_r.at[s, i], self.at.below
        )

    def up_copy(self, s, i):
        n = self.at.n
        return remote(
            self.own.at[n - 1 - s, i],
            self.uin.at[s, i],
            self.u_s.at[s, i],
            self.u_r.at[s, i],
            self.at.above,
        )

    def other(self, k, tile):
        if k >= self.slots:
            self.core_copy(k - self.slots).wait_send()
        j = order_of(k, self.at)
        tile(2 * j + 1 - self.at.c, lambda i, v: self.store(self.pout, (k % self.slots,), i, v, False))
        self.core_copy(k).start()

    def store(self, ref, lead, i, value, add):
        at = lead + (i,)
        if add:
            value = value + ref[at].astype(F32)
        ref[at] = value.astype(BF)

    def mine(self, k, tile):
        at = self.at
        j = order_of(k, at)
        self.core_copy(k).wait_recv()
        tile(2 * j + at.c, lambda i, v: self.store(self.own, (j,), i, v, True))
        if k < at.n - 1:

            @pl.when(at.p == at.n - 1)
            def _():
                for i in range(self.pieces):
                    self.down_copy(k, i).start()

            @pl.when(at.p == 0)
            def _():
                for i in range(self.pieces):
                    self.up_copy(k, i).start()

    def add(self, dst, src):
        @pl.loop(0, dst.shape[0] // 64)
        def _(b):
            rs = pl.ds(pl.multiple_of(b * 64, 64), 64)
            dst[rs, :] = (dst[rs, :].astype(F32) + src[rs, :].astype(F32)).astype(BF)

    def slot(self, t):
        at = self.at
        n, p = at.n, at.p
        sd = t - (n - 2 - p)
        su = t - (p - 1)

        @pl.loop(0, self.pieces)
        def _(i):
            @pl.when((sd >= 0) & (sd < p) & at.has_above)
            def _():
                self.down_copy(sd, i).wait_recv()
                self.add(self.own.at[sd, i], self.din.at[sd, i])
                self.down_copy(sd, i).start()

            @pl.when((su >= 0) & (su < n - 1 - p) & at.has_below)
            def _():
                self.up_copy(su, i).wait_recv()
                self.add(self.own.at[n - 1 - su, i], self.uin.at[su, i])
                self.up_copy(su, i).start()

    def final(self, out):
        at = self.at
        n, p = at.n, at.p

        @pl.loop(0, self.pieces)
        def _(i):
            @pl.when(at.has_above)
            def _():
                self.down_copy(p, i).wait_recv()

            @pl.when(at.has_below)
            def _():
                self.up_copy(n - 1 - p, i).wait_recv()

            def close(parts):
                @pl.loop(0, out.shape[1] // 64)
                def _(b):
                    rs = pl.ds(pl.multiple_of(b * 64, 64), 64)
                    total = self.own[p, i, rs, :].astype(F32)
                    for ref, s in parts:
                        total = total + ref[s, i, rs, :].astype(F32)
                    out[i, rs, :] = total.astype(out.dtype)

            down, up = (self.din, p), (self.uin, n - 1 - p)

            @pl.when(at.has_above & at.has_below)
            def _():
                close([down, up])

            @pl.when(jnp.logical_not(at.has_below))
            def _():
                close([down])

            @pl.when(jnp.logical_not(at.has_above))
            def _():
                close([up])

    def drain(self):
        at = self.at
        n, p = at.n, at.p
        for k in range(n - self.slots, n):
            self.core_copy(k).wait_send()
        for s in range(n - 1):

            @pl.when(s < p)
            def _():
                for i in range(self.pieces):
                    self.down_copy(s, i).wait_send()

            @pl.when(s < n - 1 - p)
            def _():
                for i in range(self.pieces):
                    self.up_copy(s, i).wait_send()


def line_sum_scratch(n, pieces, rows, cols, slots=2):
    dma = pltpu.SemaphoreType.DMA
    return [
        pltpu.VMEM((slots, pieces, rows, cols), BF),
        pltpu.VMEM((n, pieces, rows, cols), BF),
        pltpu.VMEM((n - 1, pieces, rows, cols), BF),
        pltpu.VMEM((n - 1, pieces, rows, cols), BF),
        dma((slots,)),
        dma((n,)),
        dma((n - 1, pieces)),
        dma((n - 1, pieces)),
        dma((n - 1, pieces)),
        dma((n - 1, pieces)),
    ]


class QuadSum:
    def __init__(self, at, t, r1, r2, sems):
        self.at, self.t, self.r1, self.r2 = at, t, r1, r2
        self.s1, self.v1, self.s2, self.v2 = sems

    def source(self, half, q):
        return self.t.at[half, q]

    def mine(self, half, own, rs):
        q = self.at.m if own else (self.at.qy if half == 0 else self.at.qx)
        return self.t[half, q, rs, :].astype(F32)

    def first(self, half, turn):
        at = self.at
        dev, quarter = (at.xdev, at.qx) if half == 0 else (at.ydev, at.qy)
        q = at.qd if turn == 0 else quarter
        return remote(
            self.source(half, q),
            self.r1.at[half, turn],
            self.s1.at[half, turn],
            self.v1.at[half, turn],
            dev,
        )

    def second(self, half):
        at = self.at
        dev, q = (at.ydev, at.qy) if half == 0 else (at.xdev, at.qx)
        return remote(
            self.r1.at[half, 0], self.r2.at[half], self.s2.at[half], self.v2.at[half], dev
        )

    def turn(self):
        for half in range(2):
            self.first(half, 0).wait_recv()

            @pl.loop(0, self.r1.shape[2] // 64)
            def _(b):
                rs = pl.ds(pl.multiple_of(b * 64, 64), 64)
                total = self.r1[half, 0, rs, :].astype(F32) + self.mine(half, False, rs)
                self.r1[half, 0, rs, :] = total.astype(BF)

            self.second(half).start()

    def arrive(self):
        for half in range(2):
            self.first(half, 1).wait_recv()
            self.second(half).wait_recv()

    def total(self, half, rs):
        own = self.mine(half, True, rs)
        return own + self.r1[half, 1, rs, :].astype(F32) + self.r2[half, rs, :].astype(F32)

    def drain(self):
        for half in range(2):
            self.first(half, 0).wait_send()
            self.first(half, 1).wait_send()
            self.second(half).wait_send()


class QuadSumHbm(QuadSum):
    def __init__(self, at, hbm, t, r1, r2, sems):
        super().__init__(at, t, r1, r2, sems[:4])
        self.hbm = hbm
        rows, cols = t.shape[2], t.shape[3]
        self.loads = []
        for half in range(2):
            for own in range(2):
                q = at.m if own else (at.qy if half == 0 else at.qx)
                self.loads.append(
                    pltpu.make_async_copy(
                        self.source(half, q), t.at[half, own], sems[4].at[half, own]
                    )
                )

    def source(self, half, q):
        rows, cols = self.t.shape[2], self.t.shape[3]
        rs = pl.ds(pl.multiple_of(q * rows, rows), rows)
        return self.hbm.at[rs, pl.ds(half * cols, cols)]

    def mine(self, half, own, rs):
        return self.t[half, int(own), rs, :].astype(F32)


def quad_sum_scratch(rows, cols, quarters=4):
    dma = pltpu.SemaphoreType.DMA
    return [
        pltpu.VMEM((2, quarters, rows, cols), BF),
        pltpu.VMEM((2, 2, rows, cols), BF),
        pltpu.VMEM((2, rows, cols), BF),
        dma((2, 2)),
        dma((2, 2)),
        dma((2,)),
        dma((2,)),
    ]


class QuadGather:
    def __init__(self, at, own, out, sems):
        self.at, self.own, self.out = at, own, out
        self.s, self.v, self.s2, self.v2, self.here = sems

    def spot(self, q, half):
        rows, cols = self.own.shape[1], self.own.shape[2]
        rs = pl.ds(pl.multiple_of(q * rows, rows), rows)
        return self.out.at[rs, pl.ds(half * cols, cols)]

    def direct(self, half, way):
        at = self.at
        dev = at.xdev if way == 0 else at.ydev
        return remote(
            self.own.at[half],
            self.spot(at.m, half),
            self.s.at[half, way],
            self.v.at[half, way],
            dev,
        )

    def onward(self, half):
        at = self.at
        q, dev = (at.qy, at.xdev) if half == 0 else (at.qx, at.ydev)
        return remote(
            self.spot(q, half), self.spot(q, half), self.s2.at[half], self.v2.at[half], dev
        )

    def keep(self, half):
        return pltpu.make_async_copy(self.own.at[half], self.spot(self.at.m, half), self.here.at[half])

    def start(self):
        for way in ((0, 1), (1, 0), (0, 0), (1, 1)):
            self.direct(*way).start()
        for half in range(2):
            self.keep(half).start()

    def forward(self):
        self.direct(0, 1).wait_recv()
        self.onward(0).start()
        self.direct(1, 0).wait_recv()
        self.onward(1).start()

    def finish(self):
        for half in range(2):
            self.direct(half, half).wait_recv()
            self.onward(half).wait_recv()
            self.keep(half).wait()
            self.onward(half).wait_send()
            for way in range(2):
                self.direct(half, way).wait_send()


def quad_gather_scratch(rows, cols):
    dma = pltpu.SemaphoreType.DMA
    return [
        pltpu.VMEM((2, rows, cols), BF),
        dma((2, 2)),
        dma((2, 2)),
        dma((2,)),
        dma((2,)),
        dma((2,)),
    ]


def last_kernel(
    n_dp,
    dqkv_hbm,
    aw_hbm,
    nt_hbm,
    gt_hbm,
    att_hbm,
    x_ref,
    gh_ref,
    gain_ref,
    gmid_ref,
    rs_ref,
    grad_ref,
    gains_ref,
    dqkv,
    aw,
    nt,
    gt,
    att,
    loads,
    pout,
    own,
    din,
    uin,
    po_s,
    po_r,
    d_s,
    d_r,
    u_s,
    u_r,
    t,
    r1,
    r2,
    q1,
    q2,
    q3,
    q4,
    gown,
    g1,
    g2,
    g3,
    g4,
    g5,
    fold_out,
    fold_in,
    fold_s,
    fold_r,
):
    at = Place(n_dp)
    hh = att_hbm.shape[1]
    part = t.shape[2]
    chunk = own.shape[2]
    half_cols = t.shape[3]
    copies = [
        pltpu.make_async_copy(src, dst, loads.at[i])
        for i, (src, dst) in enumerate(
            [
                (dqkv_hbm, dqkv),
                (aw_hbm.at[:, pl.ds(0, 3 * hh)], aw),
                (nt_hbm, nt),
                (att_hbm, att),
                (gt_hbm, gt),
            ]
        )
    ]
    for cp in copies:
        cp.start()
    bits = [b for b in (2, 4, 8, 16) if b < n_dp]
    enter(at, [at.fold(b) for b in bits[1:]])
    quad = QuadSum(at, t, r1, r2, (q1, q2, q3, q4))
    line = LineSum(at, pout, own, din, uin, (po_s, po_r, d_s, d_r, u_s, u_r))
    gather = QuadGather(at, gown, grad_ref, (g1, g2, g3, g4, g5))
    copies[0].wait()
    copies[1].wait()

    def terms(q):
        rs = pl.ds(pl.multiple_of(q * part, part), part)
        width = 512

        @pl.loop(0, half_cols // width)
        def _(i):
            for half in range(2):
                d0 = pl.multiple_of(half * half_cols + i * width, width)
                v = dot(dqkv[rs, :], aw[pl.ds(d0, width), :], NT)
                t[half, q, :, pl.ds(pl.multiple_of(i * width, width), width)] = v.astype(BF)

    terms(at.qd)
    quad.first(0, 0).start()
    quad.first(1, 0).start()
    terms(at.qx)
    quad.first(0, 1).start()
    terms(at.qy)
    quad.first(1, 1).start()
    for cp in copies[2:]:
        cp.wait()

    def tile(block, put):
        rs = pl.ds(pl.multiple_of(block * chunk, chunk), chunk)

        @pl.loop(0, 3)
        def _(i):
            put(i, dot(nt[rs, :], dqkv[:, pl.ds(pl.multiple_of(i * hh, hh), hh)]))

        put(3, dot(gt[rs, :], att[...]))

    n = at.n
    for k in range(n + 1):
        if k < n:
            line.other(k, tile)
        if k > 0:
            line.mine(k - 1, tile)
    terms(at.m)
    quad.turn()
    line.slot(0)
    quad.arrive()

    fold_out[...] = jnp.zeros_like(fold_out)

    @pl.loop(0, part // 32)
    def _(b):
        rs = pl.ds(pl.multiple_of(b * 32, 32), 32)
        x = x_ref[rs, :].astype(F32)
        scale = lax.rsqrt(jnp.mean(x * x, axis=1, keepdims=True) + EPS)
        g = jnp.concatenate([quad.total(0, rs), quad.total(1, rs)], axis=1)
        unit = x * scale
        weighted = g * gain_ref[...]
        field = scale * (weighted - unit * jnp.mean(weighted * unit, axis=1, keepdims=True))
        res = (gh_ref[rs, :] + field).astype(BF)
        gown[0, rs, :] = res[:, :half_cols]
        gown[1, rs, :] = res[:, half_cols:]
        fold_out[0, 0:1, :] += jnp.sum(g * unit, axis=0, keepdims=True)

    gather.start()
    fold_out[0, 1:2, :] = gmid_ref[...]
    devs = [at.core, at.xdev, at.ydev] + [at.fold(b) for b in bits]

    def fold_copy(b):
        return remote(fold_out.at[b], fold_in.at[b], fold_s.at[b], fold_r.at[b], devs[b])

    def fold_next(b):
        fold_copy(b).wait_recv()
        nxt = fold_out[b] + fold_in[b]
        if b + 1 < len(devs):
            fold_out[b + 1] = nxt
            fold_copy(b + 1).start()
        else:
            gains_ref[...] = nxt

    fold_copy(0).start()
    for s in range(1, n - 2):
        line.slot(s)
    gather.forward()
    for b in range(len(devs)):
        fold_next(b)
    line.final(rs_ref)
    gather.finish()
    line.drain()
    quad.drain()
    for b in range(len(devs)):
        fold_copy(b).wait_send()


def last_stage(n_dp, dqkv, aw, nt, gt, att, x, gh, gain, gmid):
    seq, hh = att.shape
    d = nt.shape[0]
    n, part, chunk = n_dp // 2, seq // 4, d // n_dp
    dma = pltpu.SemaphoreType.DMA
    anyspace = pl.BlockSpec(memory_space=pl.ANY)
    vm = pl.BlockSpec(memory_space=pltpu.VMEM)
    folds = 3 + len([b for b in (2, 4, 8, 16) if b < n_dp])
    return pl.pallas_call(
        functools.partial(last_kernel, n_dp),
        out_shape=[
            jax.ShapeDtypeStruct((4, chunk, hh), F32),
            jax.ShapeDtypeStruct((seq, d), BF),
            jax.ShapeDtypeStruct((8, d), F32),
        ],
        in_specs=[anyspace] * 5 + [vm] * 4,
        out_specs=[vm, anyspace, vm],
        scratch_shapes=[
            pltpu.VMEM((seq, 3 * hh), BF),
            pltpu.VMEM((d, 3 * hh), BF),
            pltpu.VMEM((d, seq), BF),
            pltpu.VMEM((d, seq), BF),
            pltpu.VMEM((seq, hh), BF),
            dma((5,)),
        ]
        + line_sum_scratch(n, 4, chunk, hh)
        + quad_sum_scratch(part, d // 2)
        + quad_gather_scratch(part, d // 2)
        + [
            pltpu.VMEM((folds, 8, d), F32),
            pltpu.VMEM((folds, 8, d), F32),
            dma((folds,)),
            dma((folds,)),
        ],
        compiler_params=pltpu.CompilerParams(
            collective_id=5, has_side_effects=True, vmem_limit_bytes=VMEM_LIMIT
        ),
        name="last_stage",
    )(dqkv, aw, nt, gt, att, x, gh, gain, gmid)


def mid_kernel(
    n_dp,
    ggu_hbm,
    gw_hbm,
    nm_hbm,
    ft_hbm,
    hid_ref,
    cot_ref,
    gain_ref,
    rs_ref,
    low_ref,
    lay_ref,
    gh_ref,
    gg_ref,
    ggu,
    wt,
    wt_s,
    nm,
    nm_s,
    load_s,
    *rest,
):
    at = Place(n_dp)
    n = at.n
    line = LineSum(at, *rest[0:4], rest[4:10])
    mid = QuadSum(at, *rest[10:13], rest[13:17])
    lay = QuadSumHbm(at, ft_hbm, *rest[17:20], rest[20:25])
    gather_low = QuadGather(at, rest[25], low_ref, rest[26:31])
    gather_lay = QuadGather(at, rest[31], lay_ref, rest[32:37])
    part, half_cols = mid.t.shape[2], mid.t.shape[3]
    chunk, width = line.own.shape[2], line.own.shape[3]
    pieces = line.pieces
    drows = wt.shape[1]
    tiles = half_cols // drows

    load = pltpu.make_async_copy(ggu_hbm, ggu, load_s.at[0])
    load.start()

    def nm_copy(e):
        k, core = e // 2, e % 2
        block = 2 * order_of(k, at) + (1 - at.c if core == 0 else at.c)
        cols = pl.ds(pl.multiple_of(block * chunk, chunk), chunk)
        return pltpu.make_async_copy(nm_hbm.at[:, cols], nm.at[e % 2], nm_s.at[e % 2])

    def wt_copy(half, i, slot):
        rows = pl.ds(pl.multiple_of(half * half_cols + i * drows, drows), drows)
        return pltpu.make_async_copy(gw_hbm.at[rows, :], wt.at[slot], wt_s.at[slot])

    nm_copy(0).start()
    wt_copy(0, 0, 0).start()
    for cp in lay.loads:
        cp.start()
    enter(at)
    for way in ((0, 0), (1, 0), (0, 1), (1, 1)):
        lay.first(*way).start()
    load.wait()

    def run(e):
        if e + 1 < 2 * n:
            nm_copy(e + 1).start()
        nm_copy(e).wait()
        lhs = nm[e % 2].T

        def tile(block, put):
            @pl.loop(0, pieces)
            def _(i):
                put(i, dot(lhs, ggu[:, pl.ds(pl.multiple_of(i * width, width), width)]))

        if e % 2 == 0:
            line.other(e // 2, tile)
        else:
            line.mine(e // 2, tile)

    def terms(half):
        @pl.loop(0, tiles)
        def _(i):
            slot = lax.rem(i, 2)
            if half == 0:
                nxt = wt_copy(jnp.where(i + 1 < tiles, 0, 1), lax.rem(i + 1, tiles), 1 - slot)
                nxt.start()
            else:

                @pl.when(i + 1 < tiles)
                def _():
                    wt_copy(1, i + 1, 1 - slot).start()

            wt_copy(half, i, slot).wait()
            v = dot(ggu[...], wt[slot], NT).astype(BF)
            cols = pl.ds(pl.multiple_of(i * drows, drows), drows)
            for q in range(4):
                mid.t[half, q, :, cols] = v[q * part : (q + 1) * part]

        mid.first(half, 0).start()
        mid.first(half, 1).start()

    run(0)
    run(1)
    terms(0)
    run(2)
    run(3)
    terms(1)
    for cp in lay.loads:
        cp.wait()
    lay.turn()
    for e in range(4, 2 * n):
        run(e)
    lay.arrive()

    @pl.loop(0, part // 32)
    def _(b):
        rs = pl.ds(pl.multiple_of(b * 32, 32), 32)
        for half in range(2):
            h = hid_ref[rs, pl.ds(half * half_cols, half_cols)]
            gather_lay.own[half, rs, :] = (h + lay.total(half, rs)).astype(BF)

    gather_lay.start()
    line.slot(0)
    mid.turn()
    mid.arrive()
    gg_ref[...] = jnp.zeros_like(gg_ref)

    @pl.loop(0, part // 32)
    def _(b):
        rs = pl.ds(pl.multiple_of(b * 32, 32), 32)
        h = hid_ref[rs, :]
        scale = lax.rsqrt(jnp.mean(h * h, axis=1, keepdims=True) + EPS)
        g = jnp.concatenate([mid.total(0, rs), mid.total(1, rs)], axis=1)
        unit = h * scale
        weighted = g * gain_ref[...]
        field = scale * (weighted - unit * jnp.mean(weighted * unit, axis=1, keepdims=True))
        res = cot_ref[rs, :].astype(F32) + field
        gh_ref[rs, :] = res
        low = res.astype(BF)
        gather_low.own[0, rs, :] = low[:, :half_cols]
        gather_low.own[1, rs, :] = low[:, half_cols:]
        gg_ref[...] += jnp.sum(g * unit, axis=0, keepdims=True)

    gather_low.start()
    gather_lay.forward()
    for s in range(1, n - 2):
        line.slot(s)
    gather_low.forward()
    line.final(rs_ref)
    gather_lay.finish()
    gather_low.finish()
    line.drain()
    mid.drain()
    lay.drain()


def mid_stage(n_dp, ggu, gw, nm, ft, hid, cot, gain):
    seq, wide = ggu.shape
    d = gw.shape[0]
    n, part, chunk = n_dp // 2, seq // 4, d // n_dp
    dma = pltpu.SemaphoreType.DMA
    hbm = pl.BlockSpec(memory_space=pl.ANY)
    vm = pl.BlockSpec(memory_space=pltpu.VMEM)
    pieces = 4
    return pl.pallas_call(
        functools.partial(mid_kernel, n_dp),
        out_shape=[
            jax.ShapeDtypeStruct((pieces, chunk, wide // pieces), BF),
            jax.ShapeDtypeStruct((seq, d), BF),
            jax.ShapeDtypeStruct((seq, d), BF),
            jax.ShapeDtypeStruct((part, d), F32),
            jax.ShapeDtypeStruct((1, d), F32),
        ],
        in_specs=[hbm] * 4 + [vm] * 3,
        out_specs=[vm, hbm, hbm, vm, vm],
        scratch_shapes=[
            pltpu.VMEM((seq, wide), BF),
            pltpu.VMEM((2, 256, wide), BF),
            dma((2,)),
            pltpu.VMEM((2, seq, chunk), BF),
            dma((2,)),
            dma((1,)),
        ]
        + line_sum_scratch(n, pieces, chunk, wide // pieces, 1)
        + quad_sum_scratch(part, d // 2)
        + quad_sum_scratch(part, d // 2, 2)
        + [dma((2, 2))]
        + quad_gather_scratch(part, d // 2) * 2,
        compiler_params=pltpu.CompilerParams(
            collective_id=4, has_side_effects=True, vmem_limit_bytes=VMEM_LIMIT
        ),
        name="mid_stage",
    )(ggu, gw, nm, ft, hid, cot, gain)


def after(value, *deps):
    return lax.optimization_barrier((value,) + deps)[0]


def on_device(
    inputs,
    counts,
    cotangent,
    gain_attn,
    w_query,
    w_key,
    w_value,
    w_output,
    gain_ffn,
    w_gate,
    w_up,
    w_down,
):
    seq = inputs.shape[0]
    hh = w_query.shape[1]
    ff = w_gate.shape[1]
    mp = lax.axis_size("mp")
    me = lax.axis_index("mp")
    part = seq // mp
    gather = lambda x: lax.all_gather(x, "dp", axis=0, tiled=True)
    scatter = lambda x: lax.psum_scatter(x, "dp", scatter_dimension=0, tiled=True)
    mp_gather = lambda x: lax.all_gather(x, "mp", axis=0, tiled=True)
    mp_scatter = lambda x: lax.psum_scatter(x.astype(BF), "mp", scatter_dimension=0, tiled=True)
    mine = lambda x: lax.dynamic_slice_in_dim(x, me * part, part, 0)

    attn_shard = jnp.concatenate([w_query, w_key, w_value, w_output.T], axis=1).astype(BF)
    attn_w = gather(attn_shard)
    pieces = 4
    pack = lambda g, u: jnp.stack(
        [g.reshape(g.shape[0], pieces, -1), u.reshape(u.shape[0], pieces, -1)], axis=2
    ).reshape(g.shape[0], -1)
    gu_shard = pack(w_gate, w_up).astype(BF)
    gu_w = gather(after(gu_shard, attn_w))
    down_shard = w_down.T.astype(BF)
    down_w = gather(after(down_shard, gu_w))
    gains = lax.all_gather(jnp.stack([gain_attn, gain_ffn]).astype(BF), "dp", axis=1, tiled=True)
    gains = gains.astype(F32)
    gain_in, gain_mid = gains[0:1], gains[1:2]

    count = counts[0]
    valid = (jnp.arange(seq) < count)[:, None]
    source = inputs.astype(F32)
    scale_in = lax.rsqrt(jnp.mean(source * source, axis=1, keepdims=True) + EPS)
    normed_in = (source * scale_in * gain_in).astype(BF)
    qkv = dot(normed_in, attn_w[:, : 3 * hh]).astype(BF)
    attended = attn_fwd(qkv, counts, seq)
    out_wt = attn_w[:, 3 * hh :]
    attn_sum = mp_scatter(dot(attended, out_wt, NT))
    my_source = mine(inputs).astype(F32)
    hidden = my_source + attn_sum.astype(F32)
    scale_mid = lax.rsqrt(jnp.mean(hidden * hidden, axis=1, keepdims=True) + EPS)
    normed_mid = mp_gather((hidden * scale_mid * gain_mid).astype(BF))
    gu = dot(normed_mid, gu_w).astype(BF).reshape(seq, pieces, 2, -1)
    gate_f = gu[:, :, 0].reshape(seq, ff).astype(F32)
    up_f = gu[:, :, 1].reshape(seq, ff).astype(F32)
    sg = jax.nn.sigmoid(gate_f)
    silu = gate_f * sg
    inner = (silu * up_f).astype(BF)
    grad_ffn = jnp.where(valid, cotangent, jnp.zeros_like(cotangent))
    grad_down_t = dot(grad_ffn, inner, TN).astype(BF)
    grad_inner = dot(grad_ffn, down_w)
    grad_gate = (grad_inner * up_f * sg * (1.0 + gate_f * (1.0 - sg))).astype(BF)
    grad_up = (grad_inner * silu).astype(BF)
    rs_down = scatter(grad_down_t)
    ffn_terms = dot(inner, down_w, NT).astype(BF)
    rs_gu, grad_low, layer_out, grad_hidden, g_gain_mid = mid_stage(
        lax.axis_size("dp"),
        pack(grad_gate, grad_up),
        gu_w,
        normed_mid,
        ffn_terms,
        hidden,
        mine(grad_ffn),
        gain_mid,
    )
    grad_attended = dot(grad_low, out_wt).astype(BF)
    dq, dk, dv = attn_bwd(qkv, grad_attended, counts, seq)
    rs_attn, grad_low_in, g_gains = last_stage(
        lax.axis_size("dp"),
        jnp.concatenate([dq, dk, dv], axis=1),
        attn_w,
        normed_in.T,
        grad_low.T,
        attended,
        mine(inputs),
        grad_hidden,
        gain_in,
        g_gain_mid,
    )
    input_grad = grad_low_in.astype(F32)
    width = g_gains.shape[1] // lax.axis_size("dp")
    g_gains = lax.dynamic_slice_in_dim(g_gains, lax.axis_index("dp") * width, width, 1)
    half = ff // pieces
    unpack = lambda i: jnp.concatenate(
        [rs_gu[k, :, i * half : (i + 1) * half] for k in range(pieces)], axis=1
    ).astype(F32)
    return (
        layer_out,
        input_grad,
        g_gains[0],
        rs_attn[0],
        rs_attn[1],
        rs_attn[2],
        rs_attn[3].T,
        g_gains[1],
        unpack(0),
        unpack(1),
        rs_down.astype(F32).T,
    )


def solution(mesh):
    row, both, swapped = P("dp", None), P("dp", "mp"), P("mp", "dp")
    weights = (both, both, both, swapped)
    ffn = (both, both, swapped)
    return jax.shard_map(
        on_device,
        mesh=mesh,
        in_specs=(row, P("dp"), row, P("dp")) + weights + (P("dp"),) + ffn,
        out_specs=(row, row, P("dp")) + weights + (P("dp"),) + ffn,
        check_vma=False,
    )
```

```python
import functools
import math

import jax
import jax.numpy as jnp
from jax import lax
from jax.experimental import pallas as pl
from jax.experimental.pallas import tpu as pltpu
from jax.sharding import PartitionSpec as P

HD = 128
EPS = 1e-06
BF = jnp.bfloat16
F32 = jnp.float32
NT = (((1,), (1,)), ((), ()))
TN = (((0,), (0,)), ((), ()))
NN = (((1,), (0,)), ((), ()))


def dot(a, b, dims=NN):
    return lax.dot_general(a, b, dims, preferred_element_type=F32)


def logistic_block(q, k, seq):
    raw = dot(q, k, NT)
    shifted = math.log(seq) - raw * HD ** (-0.5)
    return 1.0 / (1.0 + jnp.exp(shifted))


def allowed_block(row0, rows, col0, cols, count):
    ri = row0 + lax.broadcasted_iota(jnp.int32, (rows, cols), 0)
    ci = col0 + lax.broadcasted_iota(jnp.int32, (rows, cols), 1)
    return (ci <= ri) & (ci < count)


def attn_fwd_kernel(seq, blk, count_ref, q_ref, k_ref, v_ref, o_ref):
    count = count_ref[0]
    for i in range(seq // blk):
        rows = pl.ds(i * blk, blk)
        width = (i + 1) * blk
        lg = logistic_block(q_ref[rows, :], k_ref[pl.ds(0, width), :], seq)
        w = jnp.where(allowed_block(i * blk, blk, 0, width, count), lg, 0.0).astype(BF)
        o_ref[rows, :] = dot(w, v_ref[pl.ds(0, width), :]).astype(BF)


def attn_fwd(qkv, count, seq):
    heads = qkv.shape[1] // (3 * HD)
    blk = min(256, seq)
    spec = lambda part: pl.BlockSpec((seq, HD), lambda h, c: (0, part * heads + h))
    return pl.pallas_call(
        functools.partial(attn_fwd_kernel, seq, blk),
        grid_spec=pltpu.PrefetchScalarGridSpec(
            num_scalar_prefetch=1,
            grid=(heads,),
            in_specs=[spec(0), spec(1), spec(2)],
            out_specs=pl.BlockSpec((seq, HD), lambda h, c: (0, h)),
        ),
        out_shape=jax.ShapeDtypeStruct((seq, heads * HD), BF),
        compiler_params=pltpu.CompilerParams(vmem_limit_bytes=48 * 1024 * 1024),
        name="attn_fwd",
    )(count, qkv, qkv, qkv)


def attn_bwd_kernel(seq, blk, count_ref, q_ref, k_ref, v_ref, g_ref, dq_ref, dk_ref, dv_ref, dka, dva):
    count = count_ref[0]
    n = seq // blk
    for i in range(n - 1, -1, -1):
        rows = pl.ds(i * blk, blk)
        width = (i + 1) * blk
        keys = pl.ds(0, width)
        q = q_ref[rows, :]
        g = g_ref[rows, :]
        k = k_ref[keys, :]
        lg = jnp.where(
            allowed_block(i * blk, blk, 0, width, count), logistic_block(q, k, seq), 0.0
        )
        w = lg.astype(BF)
        gw = dot(g, v_ref[keys, :], NT)
        gs = (gw * lg * (1.0 - lg) * HD ** (-0.5)).astype(BF)
        dq_ref[rows, :] = dot(gs, k).astype(BF)
        dk = dot(gs, q, TN)
        dv = dot(w, g, TN)
        if i == n - 1:
            dka[...] = dk
            dva[...] = dv
        else:
            dka[keys, :] += dk
            dva[keys, :] += dv
    dk_ref[...] = dka[...].astype(BF)
    dv_ref[...] = dva[...].astype(BF)


def attn_bwd(qkv, grad, count, seq):
    heads = qkv.shape[1] // (3 * HD)
    blk = min(256, seq)
    spec = lambda part: pl.BlockSpec((seq, HD), lambda h, c: (0, part * heads + h))
    out = jax.ShapeDtypeStruct((seq, heads * HD), BF)
    return pl.pallas_call(
        functools.partial(attn_bwd_kernel, seq, blk),
        grid_spec=pltpu.PrefetchScalarGridSpec(
            num_scalar_prefetch=1,
            grid=(heads,),
            in_specs=[spec(0), spec(1), spec(2), spec(0)],
            out_specs=[spec(0)] * 3,
            scratch_shapes=[pltpu.VMEM((seq, HD), F32), pltpu.VMEM((seq, HD), F32)],
        ),
        out_shape=[out, out, out],
        compiler_params=pltpu.CompilerParams(vmem_limit_bytes=48 * 1024 * 1024),
        name="attn_bwd",
    )(count, qkv, qkv, qkv, grad)


MESH = pl.DeviceIdType.MESH
VMEM_LIMIT = 60 * 1024 * 1024
PIECES = 4


class Place:
    def __init__(self, n_dp):
        self.n = n_dp // 2
        self.dp = lax.axis_index("dp")
        self.m = lax.axis_index("mp")
        self.p = lax.div(self.dp, 2)
        self.c = lax.rem(self.dp, 2)
        self.above = (self.dp + 2, self.m)
        self.below = (self.dp - 2, self.m)
        self.core = (self.dp + 1 - 2 * self.c, self.m)
        x = lax.rem(self.m, 2)
        y = lax.div(self.m, 2)
        self.qx = self.m + 1 - 2 * x
        self.qy = self.m + 2 - 4 * y
        self.qd = 3 - self.m
        self.xdev = (self.dp, self.qx)
        self.ydev = (self.dp, self.qy)
        self.has_above = self.p < self.n - 1
        self.has_below = self.p > 0

    def fold(self, bit):
        return (self.dp + bit - 2 * bit * lax.rem(lax.div(self.dp, bit), 2), self.m)


def signal(dev):
    pl.semaphore_signal(pltpu.get_barrier_semaphore(), inc=1, device_id=dev, device_id_type=MESH)


def enter(at, extra=()):
    always = [at.core, at.xdev, at.ydev] + list(extra)
    for dev in always:
        signal(dev)

    @pl.when(at.has_above)
    def _():
        signal(at.above)

    @pl.when(at.has_below)
    def _():
        signal(at.below)

    ends = at.has_above.astype(jnp.int32) + at.has_below.astype(jnp.int32)
    pl.semaphore_wait(pltpu.get_barrier_semaphore(), len(always) + ends)


def remote(src, dst, send, recv, dev):
    return pltpu.make_async_remote_copy(
        src_ref=src, dst_ref=dst, send_sem=send, recv_sem=recv, device_id=dev, device_id_type=MESH
    )


def order_of(k, at):
    n, p = at.n, at.p
    if k == n - 1:
        return p
    high = jnp.where(k < p, k, n - 1 - k + p)
    low = jnp.where(k < n - 1 - p, n - 1 - k, k - (n - 1 - p))
    return jnp.where(2 * p >= n, high, low)


class LineSum:
    def __init__(self, at, pout, own, din, uin, sems):
        self.at, self.pout, self.own, self.din, self.uin = at, pout, own, din, uin
        self.po_s, self.po_r, self.d_s, self.d_r, self.u_s, self.u_r = sems
        self.slots, self.pieces = pout.shape[0], own.shape[1]

    def core_copy(self, k):
        j = order_of(k, self.at)
        return remote(
            self.pout.at[k % self.slots],
            self.own.at[j],
            self.po_s.at[k % self.slots],
            self.po_r.at[k],
            self.at.core,
        )

    def down_copy(self, s, i):
        return remote(
            self.own.at[s, i], self.din.at[s, i], self.d_s.at[s, i], self.d_r.at[s, i], self.at.below
        )

    def up_copy(self, s, i):
        n = self.at.n
        return remote(
            self.own.at[n - 1 - s, i],
            self.uin.at[s, i],
            self.u_s.at[s, i],
            self.u_r.at[s, i],
            self.at.above,
        )

    def other(self, k, tile):
        if k >= self.slots:
            self.core_copy(k - self.slots).wait_send()
        j = order_of(k, self.at)
        tile(2 * j + 1 - self.at.c, lambda i, v: self.store(self.pout, (k % self.slots,), i, v, False))
        self.core_copy(k).start()

    def store(self, ref, lead, i, value, add):
        at = lead + (i,)
        if add:
            value = value + ref[at].astype(F32)
        ref[at] = value.astype(BF)

    def mine(self, k, tile):
        at = self.at
        j = order_of(k, at)
        self.core_copy(k).wait_recv()
        tile(2 * j + at.c, lambda i, v: self.store(self.own, (j,), i, v, True))
        if k < at.n - 1:

            @pl.when(at.p == at.n - 1)
            def _():
                for i in range(self.pieces):
                    self.down_copy(k, i).start()

            @pl.when(at.p == 0)
            def _():
                for i in range(self.pieces):
                    self.up_copy(k, i).start()

    def add(self, dst, src):
        @pl.loop(0, dst.shape[0] // 64)
        def _(b):
            rs = pl.ds(pl.multiple_of(b * 64, 64), 64)
            dst[rs, :] = (dst[rs, :].astype(F32) + src[rs, :].astype(F32)).astype(BF)

    def slot(self, t):
        at = self.at
        n, p = at.n, at.p
        sd = t - (n - 2 - p)
        su = t - (p - 1)

        @pl.loop(0, self.pieces)
        def _(i):
            @pl.when((sd >= 0) & (sd < p) & at.has_above)
            def _():
                self.down_copy(sd, i).wait_recv()
                self.add(self.own.at[sd, i], self.din.at[sd, i])
                self.down_copy(sd, i).start()

            @pl.when((su >= 0) & (su < n - 1 - p) & at.has_below)
            def _():
                self.up_copy(su, i).wait_recv()
                self.add(self.own.at[n - 1 - su, i], self.uin.at[su, i])
                self.up_copy(su, i).start()

    def final(self, out):
        at = self.at
        n, p = at.n, at.p

        @pl.loop(0, self.pieces)
        def _(i):
            @pl.when(at.has_above)
            def _():
                self.down_copy(p, i).wait_recv()

            @pl.when(at.has_below)
            def _():
                self.up_copy(n - 1 - p, i).wait_recv()

            def close(parts):
                @pl.loop(0, out.shape[1] // 64)
                def _(b):
                    rs = pl.ds(pl.multiple_of(b * 64, 64), 64)
                    total = self.own[p, i, rs, :].astype(F32)
                    for ref, s in parts:
                        total = total + ref[s, i, rs, :].astype(F32)
                    out[i, rs, :] = total.astype(out.dtype)

            down, up = (self.din, p), (self.uin, n - 1 - p)

            @pl.when(at.has_above & at.has_below)
            def _():
                close([down, up])

            @pl.when(jnp.logical_not(at.has_below))
            def _():
                close([down])

            @pl.when(jnp.logical_not(at.has_above))
            def _():
                close([up])

    def drain(self):
        at = self.at
        n, p = at.n, at.p
        for k in range(n - self.slots, n):
            self.core_copy(k).wait_send()
        for s in range(n - 1):

            @pl.when(s < p)
            def _():
                for i in range(self.pieces):
                    self.down_copy(s, i).wait_send()

            @pl.when(s < n - 1 - p)
            def _():
                for i in range(self.pieces):
                    self.up_copy(s, i).wait_send()


def line_sum_scratch(n, pieces, rows, cols, slots=2):
    dma = pltpu.SemaphoreType.DMA
    return [
        pltpu.VMEM((slots, pieces, rows, cols), BF),
        pltpu.VMEM((n, pieces, rows, cols), BF),
        pltpu.VMEM((n - 1, pieces, rows, cols), BF),
        pltpu.VMEM((n - 1, pieces, rows, cols), BF),
        dma((slots,)),
        dma((n,)),
        dma((n - 1, pieces)),
        dma((n - 1, pieces)),
        dma((n - 1, pieces)),
        dma((n - 1, pieces)),
    ]


class QuadSum:
    def __init__(self, at, t, r1, r2, sems):
        self.at, self.t, self.r1, self.r2 = at, t, r1, r2
        self.s1, self.v1, self.s2, self.v2 = sems

    def source(self, half, q):
        return self.t.at[half, q]

    def mine(self, half, own, rs):
        q = self.at.m if own else (self.at.qy if half == 0 else self.at.qx)
        return self.t[half, q, rs, :].astype(F32)

    def first(self, half, turn):
        at = self.at
        dev, quarter = (at.xdev, at.qx) if half == 0 else (at.ydev, at.qy)
        q = at.qd if turn == 0 else quarter
        return remote(
            self.source(half, q),
            self.r1.at[half, turn],
            self.s1.at[half, turn],
            self.v1.at[half, turn],
            dev,
        )

    def second(self, half):
        at = self.at
        dev, q = (at.ydev, at.qy) if half == 0 else (at.xdev, at.qx)
        return remote(
            self.r1.at[half, 0], self.r2.at[half], self.s2.at[half], self.v2.at[half], dev
        )

    def turn(self):
        for half in range(2):
            self.first(half, 0).wait_recv()

            @pl.loop(0, self.r1.shape[2] // 64)
            def _(b):
                rs = pl.ds(pl.multiple_of(b * 64, 64), 64)
                total = self.r1[half, 0, rs, :].astype(F32) + self.mine(half, False, rs)
                self.r1[half, 0, rs, :] = total.astype(BF)

            self.second(half).start()

    def arrive(self):
        for half in range(2):
            self.first(half, 1).wait_recv()
            self.second(half).wait_recv()

    def total(self, half, rs):
        own = self.mine(half, True, rs)
        return own + self.r1[half, 1, rs, :].astype(F32) + self.r2[half, rs, :].astype(F32)

    def drain(self):
        for half in range(2):
            self.first(half, 0).wait_send()
            self.first(half, 1).wait_send()
            self.second(half).wait_send()


class QuadSumHbm(QuadSum):
    def __init__(self, at, hbm, t, r1, r2, sems):
        super().__init__(at, t, r1, r2, sems[:4])
        self.hbm = hbm
        rows, cols = t.shape[2], t.shape[3]
        self.loads = []
        for half in range(2):
            for own in range(2):
                q = at.m if own else (at.qy if half == 0 else at.qx)
                self.loads.append(
                    pltpu.make_async_copy(
                        self.source(half, q), t.at[half, own], sems[4].at[half, own]
                    )
                )

    def source(self, half, q):
        rows, cols = self.t.shape[2], self.t.shape[3]
        rs = pl.ds(pl.multiple_of(q * rows, rows), rows)
        return self.hbm.at[rs, pl.ds(half * cols, cols)]

    def mine(self, half, own, rs):
        return self.t[half, int(own), rs, :].astype(F32)


def quad_sum_scratch(rows, cols, quarters=4):
    dma = pltpu.SemaphoreType.DMA
    return [
        pltpu.VMEM((2, quarters, rows, cols), BF),
        pltpu.VMEM((2, 2, rows, cols), BF),
        pltpu.VMEM((2, rows, cols), BF),
        dma((2, 2)),
        dma((2, 2)),
        dma((2,)),
        dma((2,)),
    ]


class QuadGather:
    def __init__(self, at, own, out, sems):
        self.at, self.own, self.out = at, own, out
        self.s, self.v, self.s2, self.v2, self.here = sems

    def spot(self, q, half):
        rows, cols = self.own.shape[1], self.own.shape[2]
        rs = pl.ds(pl.multiple_of(q * rows, rows), rows)
        return self.out.at[rs, pl.ds(half * cols, cols)]

    def direct(self, half, way):
        at = self.at
        dev = at.xdev if way == 0 else at.ydev
        return remote(
            self.own.at[half],
            self.spot(at.m, half),
            self.s.at[half, way],
            self.v.at[half, way],
            dev,
        )

    def onward(self, half):
        at = self.at
        q, dev = (at.qy, at.xdev) if half == 0 else (at.qx, at.ydev)
        return remote(
            self.spot(q, half), self.spot(q, half), self.s2.at[half], self.v2.at[half], dev
        )

    def keep(self, half):
        return pltpu.make_async_copy(self.own.at[half], self.spot(self.at.m, half), self.here.at[half])

    def start(self):
        for way in ((0, 1), (1, 0), (0, 0), (1, 1)):
            self.direct(*way).start()
        for half in range(2):
            self.keep(half).start()

    def forward(self):
        self.direct(0, 1).wait_recv()
        self.onward(0).start()
        self.direct(1, 0).wait_recv()
        self.onward(1).start()

    def finish(self):
        for half in range(2):
            self.direct(half, half).wait_recv()
            self.onward(half).wait_recv()
            self.keep(half).wait()
            self.onward(half).wait_send()
            for way in range(2):
                self.direct(half, way).wait_send()


def quad_gather_scratch(rows, cols):
    dma = pltpu.SemaphoreType.DMA
    return [
        pltpu.VMEM((2, rows, cols), BF),
        dma((2, 2)),
        dma((2, 2)),
        dma((2,)),
        dma((2,)),
        dma((2,)),
    ]


class LineGather:
    def __init__(self, at, pieces, shard, spot, sems):
        self.at, self.pieces, self.shard, self.spot = at, pieces, shard, spot
        self.d_s, self.d_r, self.u_s, self.u_r, self.c_s, self.c_r, self.here = sems

    def down_copy(self, h, i, own=False):
        b = 2 * (self.at.p + h) + self.at.c
        dst = self.spot(b, i)
        src = self.shard(i) if own else dst
        return remote(src, dst, self.d_s.at[h, i], self.d_r.at[h, i], self.at.below)

    def up_copy(self, h, i, own=False):
        b = 2 * (self.at.p - h) + self.at.c
        dst = self.spot(b, i)
        src = self.shard(i) if own else dst
        return remote(src, dst, self.u_s.at[h, i], self.u_r.at[h, i], self.at.above)

    def core_copy(self, z, i, own=False, incoming=False):
        b = 2 * z + (1 - self.at.c if incoming else self.at.c)
        dst = self.spot(b, i)
        src = self.shard(i) if own else dst
        return remote(src, dst, self.c_s.at[z, i], self.c_r.at[z, i], self.at.core)

    def keep(self, i):
        at = self.at
        return pltpu.make_async_copy(self.shard(i), self.spot(at.dp, i), self.here.at[i])

    def start(self):
        at = self.at
        for i in range(self.pieces):

            @pl.when(at.has_below)
            def _():
                self.down_copy(0, i, True).start()

            @pl.when(at.has_above)
            def _():
                self.up_copy(0, i, True).start()

        for i in range(self.pieces):
            self.core_copy(at.p, i, True).start()
            self.keep(i).start()

    def slot(self, h, i):
        at = self.at
        n, p = at.n, at.p

        @pl.when(p + h < n)
        def _():
            self.down_copy(h - 1, i).wait_recv()

            @pl.when(at.has_below)
            def _():
                self.down_copy(h, i).start()

            self.core_copy(p + h, i).start()

        @pl.when(p - h >= 0)
        def _():
            self.up_copy(h - 1, i).wait_recv()

            @pl.when(at.has_above)
            def _():
                self.up_copy(h, i).start()

            self.core_copy(p - h, i).start()

    def stage(self, h):
        @pl.loop(0, self.pieces)
        def _(i):
            self.slot(h, i)

    def ready(self, z, i):
        self.core_copy(z, i, incoming=True).wait_recv()

    def drain(self):
        at = self.at
        n, p = at.n, at.p

        @pl.loop(0, self.pieces)
        def _(i):
            for h in range(n):

                @pl.when((p + h < n) & at.has_below)
                def _():
                    self.down_copy(h, i, h == 0).wait_send()

                @pl.when((p - h >= 0) & at.has_above)
                def _():
                    self.up_copy(h, i, h == 0).wait_send()

            for z in range(n):
                self.core_copy(z, i).wait_send()


def line_gather_scratch(n, pieces):
    dma = pltpu.SemaphoreType.DMA
    return [dma((n, pieces))] * 6 + [dma((pieces,))]


def rows_spot(out, rows, width):
    def spot(b, i):
        rs = pl.ds(pl.multiple_of(b * rows, rows), rows)
        return out.at[rs, pl.ds(pl.multiple_of(i * width, width), width)]

    return spot


def cols_of(ref, width, base=0):
    return lambda i: ref.at[:, pl.ds(pl.multiple_of(base + i * width, width), width)]


def gate_kernel(
    n_dp,
    att_ref,
    aw_hbm,
    sh_hbm,
    x_ref,
    gain_ref,
    gw_ref,
    nm_ref,
    hid_ref,
    gu_ref,
    inner_ref,
    wo,
    nm,
    wbuf,
    gbuf,
    ibuf,
    load_s,
    wb_s,
    gb_s,
    ib_s,
    *rest,
):
    at = Place(n_dp)
    n = at.n
    quad = QuadSum(at, *rest[0:3], rest[3:7])
    gather_nm = QuadGather(at, rest[7], nm_ref, rest[8:13])
    sems = rest[13:20]
    hh = wo.shape[1]
    part, half_cols = quad.t.shape[2], quad.t.shape[3]
    chunk, wide = sh_hbm.shape
    pieces = sems[6].shape[0]
    width = wide // pieces
    line = LineGather(at, pieces, cols_of(sh_hbm, width), rows_spot(gw_ref, chunk, width), sems)

    load = pltpu.make_async_copy(aw_hbm.at[:, pl.ds(3 * hh, hh)], wo, load_s.at[0])
    load.start()
    enter(at)
    line.start()
    load.wait()

    def terms(q):
        rs = pl.ds(pl.multiple_of(q * part, part), part)
        for half in range(2):
            w = wo[half * half_cols : (half + 1) * half_cols, :]
            quad.t[half, q] = dot(att_ref[rs, :], w, NT).astype(BF)

    terms(at.qd)
    quad.first(0, 0).start()
    quad.first(1, 0).start()
    terms(at.qx)
    quad.first(0, 1).start()
    terms(at.qy)
    quad.first(1, 1).start()
    terms(at.m)
    quad.turn()
    quad.arrive()

    @pl.loop(0, part // 32)
    def _(b):
        rs = pl.ds(pl.multiple_of(b * 32, 32), 32)
        h = x_ref[rs, :].astype(F32) + jnp.concatenate(
            [quad.total(0, rs), quad.total(1, rs)], axis=1
        )
        hid_ref[rs, :] = h
        scale = lax.rsqrt(jnp.mean(h * h, axis=1, keepdims=True) + EPS)
        res = (h * scale * gain_ref[...]).astype(BF)
        gather_nm.own[0, rs, :] = res[:, :half_cols]
        gather_nm.own[1, rs, :] = res[:, half_cols:]

    gather_nm.start()
    line.stage(1)
    gather_nm.forward()
    gather_nm.finish()
    load = pltpu.make_async_copy(nm_ref, nm, load_s.at[0])
    load.start()
    for h in range(2, n - 1):
        line.stage(h)
    load.wait()

    def w_copy(i, slot):
        cols = pl.ds(pl.multiple_of(i * width, width), width)
        return pltpu.make_async_copy(gw_ref.at[:, cols], wbuf.at[slot], wb_s.at[slot])

    def g_copy(i, slot):
        cols = pl.ds(pl.multiple_of(i * width, width), width)
        return pltpu.make_async_copy(gbuf.at[slot], gu_ref.at[:, cols], gb_s.at[slot])

    def i_copy(i, slot):
        cols = pl.ds(pl.multiple_of(i * (width // 2), width // 2), width // 2)
        return pltpu.make_async_copy(ibuf.at[slot], inner_ref.at[:, cols], ib_s.at[slot])

    @pl.loop(0, pieces)
    def _(i):
        slot = lax.rem(i, 2)
        line.slot(n - 1, i)
        line.keep(i).wait()
        for z in range(n):
            line.ready(z, i)
        w_copy(i, slot).start()

        @pl.when(i >= 2)
        def _():
            g_copy(i - 2, slot).wait()
            i_copy(i - 2, slot).wait()

        w_copy(i, slot).wait()

        @pl.loop(0, nm.shape[0] // 256)
        def _(b):
            rs = pl.ds(pl.multiple_of(b * 256, 256), 256)
            v = dot(nm[rs, :], wbuf[slot]).astype(BF)
            gbuf[slot, rs, :] = v
            g = v[:, : width // 2].astype(F32)
            u = v[:, width // 2 :].astype(F32)
            ibuf[slot, rs, :] = (g / (1.0 + jnp.exp(-g)) * u).astype(BF)

        g_copy(i, slot).start()
        i_copy(i, slot).start()

    for i in range(max(0, pieces - 2), pieces):
        g_copy(i, i % 2).wait()
        i_copy(i, i % 2).wait()
    line.drain()
    quad.drain()


def gate_stage(n_dp, att, aw, shard, x, gain):
    seq, hh = att.shape
    d = aw.shape[0]
    chunk, wide = shard.shape
    n, part = n_dp // 2, seq // 4
    dma = pltpu.SemaphoreType.DMA
    hbm = pl.BlockSpec(memory_space=pl.ANY)
    vm = pl.BlockSpec(memory_space=pltpu.VMEM)
    width = wide // PIECES
    return pl.pallas_call(
        functools.partial(gate_kernel, n_dp),
        out_shape=[
            jax.ShapeDtypeStruct((d, wide), BF),
            jax.ShapeDtypeStruct((seq, d), BF),
            jax.ShapeDtypeStruct((part, d), F32),
            jax.ShapeDtypeStruct((seq, wide), BF),
            jax.ShapeDtypeStruct((seq, wide // 2), BF),
        ],
        in_specs=[vm, hbm, hbm, vm, vm],
        out_specs=[hbm, hbm, vm, hbm, hbm],
        scratch_shapes=[
            pltpu.VMEM((d, hh), BF),
            pltpu.VMEM((seq, d), BF),
            pltpu.VMEM((2, d, width), BF),
            pltpu.VMEM((2, seq, width), BF),
            pltpu.VMEM((2, seq, width // 2), BF),
            dma((1,)),
            dma((2,)),
            dma((2,)),
            dma((2,)),
        ]
        + quad_sum_scratch(part, d // 2)
        + quad_gather_scratch(part, d // 2)
        + line_gather_scratch(n, PIECES),
        compiler_params=pltpu.CompilerParams(
            collective_id=2, has_side_effects=True, vmem_limit_bytes=VMEM_LIMIT
        ),
        name="gate_stage",
    )(att, aw, shard, x, gain)


def down_kernel(
    n_dp,
    inner_hbm,
    gu_hbm,
    cot_hbm,
    sh_hbm,
    rs_ref,
    ft_ref,
    ggu_ref,
    dn_ref,
    inner,
    gu,
    cot,
    dn,
    acc,
    ftb,
    load_s,
    ft_s,
    dn_s,
    gg_s,
    *rest,
):
    at = Place(n_dp)
    n, p = at.n, at.p
    line = LineSum(at, *rest[0:4], rest[4:10])
    sems = rest[10:17]
    chunk, ff = sh_hbm.shape
    pieces = sems[6].shape[0]
    width = ff // pieces
    gather = LineGather(at, pieces, cols_of(sh_hbm, width), rows_spot(dn_ref, chunk, width), sems)
    pair = 2 * chunk
    loads = [
        pltpu.make_async_copy(src, dst, load_s.at[i])
        for i, (src, dst) in enumerate([(cot_hbm, cot), (inner_hbm, inner), (gu_hbm, gu)])
    ]
    for cp in loads:
        cp.start()
    enter(at)
    gather.start()
    loads[0].wait()
    loads[1].wait()

    def run(e):
        k, core = e // 2, e % 2
        block = 2 * order_of(k, at) + (1 - at.c if core == 0 else at.c)
        lhs = cot[:, pl.ds(pl.multiple_of(block * chunk, chunk), chunk)].T

        def tile(_, put):
            @pl.loop(0, pieces)
            def _(i):
                put(i, dot(lhs, inner[:, pl.ds(pl.multiple_of(i * width, width), width)]))

        if core == 0:
            line.other(k, tile)
        else:
            line.mine(k, tile)

    for e in range(2 * n):
        run(e)

    def ft_copy(z, slot):
        cols = pl.ds(pl.multiple_of(z * pair, pair), pair)
        return pltpu.make_async_copy(ftb.at[slot], ft_ref.at[:, cols], ft_s.at[slot])

    def work(z, fresh):
        rs = pl.ds(pl.multiple_of(z * pair, pair), pair)

        @pl.loop(0, pieces)
        def _(i):
            gather.ready(z, i)

        load = pltpu.make_async_copy(dn_ref.at[rs, :], dn, dn_s.at[0])
        load.start()
        load.wait()

        @pl.loop(0, ff // 512)
        def _(i):
            cols = pl.ds(pl.multiple_of(i * 512, 512), 512)
            v = dot(cot[:, rs], dn[:, cols])
            acc[:, cols] = v if fresh else acc[:, cols] + v

        if not fresh:
            ft_copy(z, 0).wait()
        ftb[0] = dot(inner[...], dn[...], NT).astype(BF)
        ft_copy(z, 0).start()

    for i in range(pieces):
        gather.keep(i).wait()
    work(p, True)
    loads[2].wait()

    @pl.loop(1, n)
    def _(h):
        gather.stage(h)
        line.slot(h - 1)

        @pl.when(p + h < n)
        def _():
            work(p + h, False)

        @pl.when(p - h >= 0)
        def _():
            work(p - h, False)

    half = width

    def gg_copy(i):
        cols = pl.ds(pl.multiple_of(i * 2 * half, 2 * half), 2 * half)
        return pltpu.make_async_copy(gu.at[:, cols], ggu_ref.at[:, cols], gg_s.at[i])

    @pl.loop(0, pieces)
    def _(i):
        gcols = pl.ds(pl.multiple_of(i * 2 * half, half), half)
        ucols = pl.ds(pl.multiple_of(i * 2 * half + half, half), half)
        acols = pl.ds(pl.multiple_of(i * half, half), half)

        @pl.loop(0, gu.shape[0] // 64)
        def _(b):
            rs = pl.ds(pl.multiple_of(b * 64, 64), 64)
            g = gu[rs, gcols].astype(F32)
            u = gu[rs, ucols].astype(F32)
            gi = acc[rs, acols]
            sg = 1.0 / (1.0 + jnp.exp(-g))
            gu[rs, gcols] = (gi * u * sg * (1.0 + g * (1.0 - sg))).astype(BF)
            gu[rs, ucols] = (gi * g * sg).astype(BF)

        gg_copy(i).start()

    line.final(rs_ref)
    for i in range(pieces):
        gg_copy(i).wait()
    ft_copy(p, 0).wait()
    line.drain()
    gather.drain()


def down_stage(n_dp, inner, gu, cot, shard):
    seq, d = cot.shape
    chunk, ff = shard.shape
    n = n_dp // 2
    dma = pltpu.SemaphoreType.DMA
    hbm = pl.BlockSpec(memory_space=pl.ANY)
    vm = pl.BlockSpec(memory_space=pltpu.VMEM)
    return pl.pallas_call(
        functools.partial(down_kernel, n_dp),
        out_shape=[
            jax.ShapeDtypeStruct((PIECES, chunk, ff // PIECES), BF),
            jax.ShapeDtypeStruct((seq, d), BF),
            jax.ShapeDtypeStruct((seq, 2 * ff), BF),
            jax.ShapeDtypeStruct((d, ff), BF),
        ],
        in_specs=[hbm] * 4,
        out_specs=[vm, hbm, hbm, hbm],
        scratch_shapes=[
            pltpu.VMEM((seq, ff), BF),
            pltpu.VMEM((seq, 2 * ff), BF),
            pltpu.VMEM((seq, d), BF),
            pltpu.VMEM((2 * chunk, ff), BF),
            pltpu.VMEM((seq, ff), F32),
            pltpu.VMEM((1, seq, 2 * chunk), BF),
            dma((3,)),
            dma((1,)),
            dma((1,)),
            dma((PIECES,)),
        ]
        + line_sum_scratch(n, PIECES, chunk, ff // PIECES)
        + line_gather_scratch(n, PIECES),
        compiler_params=pltpu.CompilerParams(
            collective_id=3, has_side_effects=True, vmem_limit_bytes=VMEM_LIMIT
        ),
        name="down_stage",
    )(inner, gu, cot, shard)[:3]


def mid_kernel(
    n_dp,
    ggu_hbm,
    gw_hbm,
    nm_hbm,
    ft_hbm,
    hid_ref,
    cot_ref,
    gain_ref,
    rs_ref,
    low_ref,
    lay_ref,
    gh_ref,
    gg_ref,
    ggu,
    wt,
    wt_s,
    nm,
    nm_s,
    load_s,
    *rest,
):
    at = Place(n_dp)
    n = at.n
    line = LineSum(at, *rest[0:4], rest[4:10])
    mid = QuadSum(at, *rest[10:13], rest[13:17])
    lay = QuadSumHbm(at, ft_hbm, *rest[17:20], rest[20:25])
    gather_low = QuadGather(at, rest[25], low_ref, rest[26:31])
    gather_lay = QuadGather(at, rest[31], lay_ref, rest[32:37])
    part, half_cols = mid.t.shape[2], mid.t.shape[3]
    chunk, width = line.own.shape[2], line.own.shape[3]
    pieces = line.pieces
    drows = wt.shape[1]
    tiles = half_cols // drows

    load = pltpu.make_async_copy(ggu_hbm, ggu, load_s.at[0])
    load.start()

    def nm_copy(e):
        k, core = e // 2, e % 2
        block = 2 * order_of(k, at) + (1 - at.c if core == 0 else at.c)
        cols = pl.ds(pl.multiple_of(block * chunk, chunk), chunk)
        return pltpu.make_async_copy(nm_hbm.at[:, cols], nm.at[e % 2], nm_s.at[e % 2])

    def wt_copy(half, i, slot):
        rows = pl.ds(pl.multiple_of(half * half_cols + i * drows, drows), drows)
        return pltpu.make_async_copy(gw_hbm.at[rows, :], wt.at[slot], wt_s.at[slot])

    nm_copy(0).start()
    wt_copy(0, 0, 0).start()
    for cp in lay.loads:
        cp.start()
    enter(at)
    for way in ((0, 0), (1, 0), (0, 1), (1, 1)):
        lay.first(*way).start()
    load.wait()

    def run(e):
        if e + 1 < 2 * n:
            nm_copy(e + 1).start()
        nm_copy(e).wait()
        lhs = nm[e % 2].T

        def tile(block, put):
            @pl.loop(0, pieces)
            def _(i):
                put(i, dot(lhs, ggu[:, pl.ds(pl.multiple_of(i * width, width), width)]))

        if e % 2 == 0:
            line.other(e // 2, tile)
        else:
            line.mine(e // 2, tile)

    def terms(half):
        @pl.loop(0, tiles)
        def _(i):
            slot = lax.rem(i, 2)
            if half == 0:
                nxt = wt_copy(jnp.where(i + 1 < tiles, 0, 1), lax.rem(i + 1, tiles), 1 - slot)
                nxt.start()
            else:

                @pl.when(i + 1 < tiles)
                def _():
                    wt_copy(1, i + 1, 1 - slot).start()

            wt_copy(half, i, slot).wait()
            v = dot(ggu[...], wt[slot], NT).astype(BF)
            cols = pl.ds(pl.multiple_of(i * drows, drows), drows)
            for q in range(4):
                mid.t[half, q, :, cols] = v[q * part : (q + 1) * part]

        mid.first(half, 0).start()
        mid.first(half, 1).start()

    run(0)
    run(1)
    terms(0)
    run(2)
    run(3)
    terms(1)
    for cp in lay.loads:
        cp.wait()
    lay.turn()
    for e in range(4, 2 * n):
        run(e)
    lay.arrive()

    @pl.loop(0, part // 32)
    def _(b):
        rs = pl.ds(pl.multiple_of(b * 32, 32), 32)
        for half in range(2):
            h = hid_ref[rs, pl.ds(half * half_cols, half_cols)]
            gather_lay.own[half, rs, :] = (h + lay.total(half, rs)).astype(BF)

    gather_lay.start()
    line.slot(0)
    mid.turn()
    mid.arrive()
    gg_ref[...] = jnp.zeros_like(gg_ref)

    @pl.loop(0, part // 32)
    def _(b):
        rs = pl.ds(pl.multiple_of(b * 32, 32), 32)
        h = hid_ref[rs, :]
        scale = lax.rsqrt(jnp.mean(h * h, axis=1, keepdims=True) + EPS)
        g = jnp.concatenate([mid.total(0, rs), mid.total(1, rs)], axis=1)
        unit = h * scale
        weighted = g * gain_ref[...]
        field = scale * (weighted - unit * jnp.mean(weighted * unit, axis=1, keepdims=True))
        res = cot_ref[rs, :].astype(F32) + field
        gh_ref[rs, :] = res
        low = res.astype(BF)
        gather_low.own[0, rs, :] = low[:, :half_cols]
        gather_low.own[1, rs, :] = low[:, half_cols:]
        gg_ref[...] += jnp.sum(g * unit, axis=0, keepdims=True)

    gather_low.start()
    gather_lay.forward()
    for s in range(1, n - 2):
        line.slot(s)
    gather_low.forward()
    line.final(rs_ref)
    gather_lay.finish()
    gather_low.finish()
    line.drain()
    mid.drain()
    lay.drain()


def mid_stage(n_dp, ggu, gw, nm, ft, hid, cot, gain):
    seq, wide = ggu.shape
    d = gw.shape[0]
    n, part, chunk = n_dp // 2, seq // 4, d // n_dp
    dma = pltpu.SemaphoreType.DMA
    hbm = pl.BlockSpec(memory_space=pl.ANY)
    vm = pl.BlockSpec(memory_space=pltpu.VMEM)
    pieces = 4
    return pl.pallas_call(
        functools.partial(mid_kernel, n_dp),
        out_shape=[
            jax.ShapeDtypeStruct((pieces, chunk, wide // pieces), BF),
            jax.ShapeDtypeStruct((seq, d), BF),
            jax.ShapeDtypeStruct((seq, d), BF),
            jax.ShapeDtypeStruct((part, d), F32),
            jax.ShapeDtypeStruct((1, d), F32),
        ],
        in_specs=[hbm] * 4 + [vm] * 3,
        out_specs=[vm, hbm, hbm, vm, vm],
        scratch_shapes=[
            pltpu.VMEM((seq, wide), BF),
            pltpu.VMEM((2, 256, wide), BF),
            dma((2,)),
            pltpu.VMEM((2, seq, chunk), BF),
            dma((2,)),
            dma((1,)),
        ]
        + line_sum_scratch(n, pieces, chunk, wide // pieces, 1)
        + quad_sum_scratch(part, d // 2)
        + quad_sum_scratch(part, d // 2, 2)
        + [dma((2, 2))]
        + quad_gather_scratch(part, d // 2) * 2,
        compiler_params=pltpu.CompilerParams(
            collective_id=4, has_side_effects=True, vmem_limit_bytes=VMEM_LIMIT
        ),
        name="mid_stage",
    )(ggu, gw, nm, ft, hid, cot, gain)


def last_kernel(
    n_dp,
    dqkv_hbm,
    aw_hbm,
    nt_hbm,
    gt_hbm,
    att_hbm,
    x_ref,
    gh_ref,
    gain_ref,
    gmid_ref,
    rs_ref,
    grad_ref,
    gains_ref,
    dqkv,
    aw,
    nt,
    gt,
    att,
    loads,
    pout,
    own,
    din,
    uin,
    po_s,
    po_r,
    d_s,
    d_r,
    u_s,
    u_r,
    t,
    r1,
    r2,
    q1,
    q2,
    q3,
    q4,
    gown,
    g1,
    g2,
    g3,
    g4,
    g5,
    fold_out,
    fold_in,
    fold_s,
    fold_r,
):
    at = Place(n_dp)
    hh = att_hbm.shape[1]
    part = t.shape[2]
    chunk = own.shape[2]
    half_cols = t.shape[3]
    copies = [
        pltpu.make_async_copy(src, dst, loads.at[i])
        for i, (src, dst) in enumerate(
            [
                (dqkv_hbm, dqkv),
                (aw_hbm.at[:, pl.ds(0, 3 * hh)], aw),
                (nt_hbm, nt),
                (att_hbm, att),
                (gt_hbm, gt),
            ]
        )
    ]
    for cp in copies:
        cp.start()
    bits = [b for b in (2, 4, 8, 16) if b < n_dp]
    enter(at, [at.fold(b) for b in bits[1:]])
    quad = QuadSum(at, t, r1, r2, (q1, q2, q3, q4))
    line = LineSum(at, pout, own, din, uin, (po_s, po_r, d_s, d_r, u_s, u_r))
    gather = QuadGather(at, gown, grad_ref, (g1, g2, g3, g4, g5))
    copies[0].wait()
    copies[1].wait()

    def terms(q):
        rs = pl.ds(pl.multiple_of(q * part, part), part)
        width = 512

        @pl.loop(0, half_cols // width)
        def _(i):
            for half in range(2):
                d0 = pl.multiple_of(half * half_cols + i * width, width)
                v = dot(dqkv[rs, :], aw[pl.ds(d0, width), :], NT)
                t[half, q, :, pl.ds(pl.multiple_of(i * width, width), width)] = v.astype(BF)

    terms(at.qd)
    quad.first(0, 0).start()
    quad.first(1, 0).start()
    terms(at.qx)
    quad.first(0, 1).start()
    terms(at.qy)
    quad.first(1, 1).start()
    for cp in copies[2:]:
        cp.wait()

    def tile(block, put):
        rs = pl.ds(pl.multiple_of(block * chunk, chunk), chunk)

        @pl.loop(0, 3)
        def _(i):
            put(i, dot(nt[rs, :], dqkv[:, pl.ds(pl.multiple_of(i * hh, hh), hh)]))

        put(3, dot(gt[rs, :], att[...]))

    n = at.n
    for k in range(n + 1):
        if k < n:
            line.other(k, tile)
        if k > 0:
            line.mine(k - 1, tile)
    terms(at.m)
    quad.turn()
    line.slot(0)
    quad.arrive()

    fold_out[...] = jnp.zeros_like(fold_out)

    @pl.loop(0, part // 32)
    def _(b):
        rs = pl.ds(pl.multiple_of(b * 32, 32), 32)
        x = x_ref[rs, :].astype(F32)
        scale = lax.rsqrt(jnp.mean(x * x, axis=1, keepdims=True) + EPS)
        g = jnp.concatenate([quad.total(0, rs), quad.total(1, rs)], axis=1)
        unit = x * scale
        weighted = g * gain_ref[...]
        field = scale * (weighted - unit * jnp.mean(weighted * unit, axis=1, keepdims=True))
        res = (gh_ref[rs, :] + field).astype(BF)
        gown[0, rs, :] = res[:, :half_cols]
        gown[1, rs, :] = res[:, half_cols:]
        fold_out[0, 0:1, :] += jnp.sum(g * unit, axis=0, keepdims=True)

    gather.start()
    fold_out[0, 1:2, :] = gmid_ref[...]
    devs = [at.core, at.xdev, at.ydev] + [at.fold(b) for b in bits]

    def fold_copy(b):
        return remote(fold_out.at[b], fold_in.at[b], fold_s.at[b], fold_r.at[b], devs[b])

    def fold_next(b):
        fold_copy(b).wait_recv()
        nxt = fold_out[b] + fold_in[b]
        if b + 1 < len(devs):
            fold_out[b + 1] = nxt
            fold_copy(b + 1).start()
        else:
            gains_ref[...] = nxt

    fold_copy(0).start()
    for s in range(1, n - 2):
        line.slot(s)
    gather.forward()
    for b in range(len(devs)):
        fold_next(b)
    line.final(rs_ref)
    gather.finish()
    line.drain()
    quad.drain()
    for b in range(len(devs)):
        fold_copy(b).wait_send()


def last_stage(n_dp, dqkv, aw, nt, gt, att, x, gh, gain, gmid):
    seq, hh = att.shape
    d = nt.shape[0]
    n, part, chunk = n_dp // 2, seq // 4, d // n_dp
    dma = pltpu.SemaphoreType.DMA
    anyspace = pl.BlockSpec(memory_space=pl.ANY)
    vm = pl.BlockSpec(memory_space=pltpu.VMEM)
    folds = 3 + len([b for b in (2, 4, 8, 16) if b < n_dp])
    return pl.pallas_call(
        functools.partial(last_kernel, n_dp),
        out_shape=[
            jax.ShapeDtypeStruct((4, chunk, hh), F32),
            jax.ShapeDtypeStruct((seq, d), BF),
            jax.ShapeDtypeStruct((8, d), F32),
        ],
        in_specs=[anyspace] * 5 + [vm] * 4,
        out_specs=[vm, anyspace, vm],
        scratch_shapes=[
            pltpu.VMEM((seq, 3 * hh), BF),
            pltpu.VMEM((d, 3 * hh), BF),
            pltpu.VMEM((d, seq), BF),
            pltpu.VMEM((d, seq), BF),
            pltpu.VMEM((seq, hh), BF),
            dma((5,)),
        ]
        + line_sum_scratch(n, 4, chunk, hh)
        + quad_sum_scratch(part, d // 2)
        + quad_gather_scratch(part, d // 2)
        + [
            pltpu.VMEM((folds, 8, d), F32),
            pltpu.VMEM((folds, 8, d), F32),
            dma((folds,)),
            dma((folds,)),
        ],
        compiler_params=pltpu.CompilerParams(
            collective_id=5, has_side_effects=True, vmem_limit_bytes=VMEM_LIMIT
        ),
        name="last_stage",
    )(dqkv, aw, nt, gt, att, x, gh, gain, gmid)


def after(value, *deps):
    return lax.optimization_barrier((value,) + deps)[0]


def on_device(
    inputs,
    counts,
    cotangent,
    gain_attn,
    w_query,
    w_key,
    w_value,
    w_output,
    gain_ffn,
    w_gate,
    w_up,
    w_down,
):
    seq = inputs.shape[0]
    hh = w_query.shape[1]
    ff = w_gate.shape[1]
    mp = lax.axis_size("mp")
    n_dp = lax.axis_size("dp")
    me = lax.axis_index("mp")
    part = seq // mp
    gather = lambda x: lax.all_gather(x, "dp", axis=0, tiled=True)
    scatter = lambda x: lax.psum_scatter(x, "dp", scatter_dimension=0, tiled=True)
    mp_gather = lambda x: lax.all_gather(x, "mp", axis=0, tiled=True)
    mp_scatter = lambda x: lax.psum_scatter(x.astype(BF), "mp", scatter_dimension=0, tiled=True)
    mine = lambda x: lax.dynamic_slice_in_dim(x, me * part, part, 0)

    attn_shard = jnp.concatenate([w_query, w_key, w_value, w_output.T], axis=1).astype(BF)
    attn_w = gather(attn_shard)
    pack = lambda g, u: jnp.stack(
        [g.reshape(g.shape[0], PIECES, -1), u.reshape(u.shape[0], PIECES, -1)], axis=2
    ).reshape(g.shape[0], -1)
    gu_shard = pack(w_gate, w_up).astype(BF)
    down_shard = w_down.T.astype(BF)
    gains = lax.all_gather(jnp.stack([gain_attn, gain_ffn]).astype(BF), "dp", axis=1, tiled=True)
    gains = gains.astype(F32)
    gain_in, gain_mid = gains[0:1], gains[1:2]

    count = counts[0]
    valid = (jnp.arange(seq) < count)[:, None]
    source = inputs.astype(F32)
    scale_in = lax.rsqrt(jnp.mean(source * source, axis=1, keepdims=True) + EPS)
    normed_in = (source * scale_in * gain_in).astype(BF)
    qkv = dot(normed_in, attn_w[:, : 3 * hh]).astype(BF)
    attended = attn_fwd(qkv, counts, seq)
    out_wt = attn_w[:, 3 * hh :]
    grad_ffn = jnp.where(valid, cotangent, jnp.zeros_like(cotangent))
    my_source = mine(inputs)
    gu_w, normed_mid, hidden, gu, inner = gate_stage(
        n_dp, attended, attn_w, gu_shard, my_source, gain_mid
    )
    rs_down, ffn_terms, ggu = down_stage(n_dp, inner, gu, grad_ffn, down_shard)
    rs_gu, grad_low, layer_out, grad_hidden, g_gain_mid = mid_stage(
        n_dp,
        ggu,
        gu_w,
        normed_mid,
        ffn_terms,
        hidden,
        mine(grad_ffn),
        gain_mid,
    )
    grad_attended = dot(grad_low, out_wt).astype(BF)
    dq, dk, dv = attn_bwd(qkv, grad_attended, counts, seq)
    rs_attn, grad_low_in, g_gains = last_stage(
        n_dp,
        jnp.concatenate([dq, dk, dv], axis=1),
        attn_w,
        normed_in.T,
        grad_low.T,
        attended,
        my_source,
        grad_hidden,
        gain_in,
        g_gain_mid,
    )
    input_grad = grad_low_in.astype(F32)
    width = g_gains.shape[1] // lax.axis_size("dp")
    g_gains = lax.dynamic_slice_in_dim(g_gains, lax.axis_index("dp") * width, width, 1)
    half = ff // PIECES
    unpack = lambda i: jnp.concatenate(
        [rs_gu[k, :, i * half : (i + 1) * half] for k in range(PIECES)], axis=1
    ).astype(F32)
    down_t = jnp.concatenate([rs_down[k] for k in range(PIECES)], axis=1)
    return (
        layer_out,
        input_grad,
        g_gains[0],
        rs_attn[0],
        rs_attn[1],
        rs_attn[2],
        rs_attn[3].T,
        g_gains[1],
        unpack(0),
        unpack(1),
        down_t.astype(F32).T,
    )


def solution(mesh):
    row, both, swapped = P("dp", None), P("dp", "mp"), P("mp", "dp")
    weights = (both, both, both, swapped)
    ffn = (both, both, swapped)
    return jax.shard_map(
        on_device,
        mesh=mesh,
        in_specs=(row, P("dp"), row, P("dp")) + weights + (P("dp"),) + ffn,
        out_specs=(row, row, P("dp")) + weights + (P("dp"),) + ffn,
        check_vma=False,
    )
```

```python
import functools
import math

import jax
import jax.numpy as jnp
from jax import lax
from jax.experimental import pallas as pl
from jax.experimental.pallas import tpu as pltpu
from jax.sharding import PartitionSpec as P

HD = 128
EPS = 1e-06
BF = jnp.bfloat16
F32 = jnp.float32
NT = (((1,), (1,)), ((), ()))
TN = (((0,), (0,)), ((), ()))
NN = (((1,), (0,)), ((), ()))


def dot(a, b, dims=NN):
    return lax.dot_general(a, b, dims, preferred_element_type=F32)


def logistic_block(q, k, seq):
    raw = dot(q, k, NT)
    shifted = math.log(seq) - raw * HD ** (-0.5)
    return 1.0 / (1.0 + jnp.exp(shifted))


def allowed_block(row0, rows, col0, cols, count):
    ri = row0 + lax.broadcasted_iota(jnp.int32, (rows, cols), 0)
    ci = col0 + lax.broadcasted_iota(jnp.int32, (rows, cols), 1)
    return (ci <= ri) & (ci < count)


MESH = pl.DeviceIdType.MESH
VMEM_LIMIT = 60 * 1024 * 1024
PIECES = 4


def flipped(index, bit):
    return index + bit - 2 * bit * lax.rem(lax.div(index, bit), 2)


def spread(j, bits):
    return sum(bit for i, bit in enumerate(bits) if j >> i & 1)


class Place:
    def __init__(self, n_dp, n_mp):
        self.n = n_dp // 2
        self.dp = lax.axis_index("dp")
        self.m = lax.axis_index("mp")
        self.p = lax.div(self.dp, 2)
        self.c = lax.rem(self.dp, 2)
        self.above = (self.dp + 2, self.m)
        self.below = (self.dp - 2, self.m)
        self.core = (self.dp + 1 - 2 * self.c, self.m)
        self.bits = [b for b in (1, 2, 4, 8, 16) if b < n_mp]
        self.has_above = self.p < self.n - 1
        self.has_below = self.p > 0

    def fold(self, bit):
        return (flipped(self.dp, bit), self.m)

    def peer(self, bit):
        return (self.dp, flipped(self.m, bit))

    def quarter(self, mask):
        q = self.m
        for bit in self.bits:
            if mask & bit:
                q = flipped(q, bit)
        return q


def signal(dev):
    pl.semaphore_signal(pltpu.get_barrier_semaphore(), inc=1, device_id=dev, device_id_type=MESH)


def enter(at, extra=()):
    always = [at.core] + [at.peer(bit) for bit in at.bits] + list(extra)
    for dev in always:
        signal(dev)

    @pl.when(at.has_above)
    def _():
        signal(at.above)

    @pl.when(at.has_below)
    def _():
        signal(at.below)

    ends = at.has_above.astype(jnp.int32) + at.has_below.astype(jnp.int32)
    pl.semaphore_wait(pltpu.get_barrier_semaphore(), len(always) + ends)


def remote(src, dst, send, recv, dev):
    return pltpu.make_async_remote_copy(
        src_ref=src, dst_ref=dst, send_sem=send, recv_sem=recv, device_id=dev, device_id_type=MESH
    )


def part_rows(at, part):
    return pl.ds(pl.multiple_of(at.m * part, part), part)


def order_of(k, at):
    n, p = at.n, at.p
    if k == n - 1:
        return p
    high = jnp.where(k < p, k, n - 1 - k + p)
    low = jnp.where(k < n - 1 - p, n - 1 - k, k - (n - 1 - p))
    return jnp.where(2 * p >= n, high, low)


class LineSum:
    def __init__(self, at, pout, own, din, uin, sems):
        self.at, self.pout, self.own, self.din, self.uin = at, pout, own, din, uin
        self.po_s, self.po_r, self.d_s, self.d_r, self.u_s, self.u_r = sems
        self.slots, self.pieces = pout.shape[0], own.shape[1]

    def core_copy(self, k, i):
        j = order_of(k, self.at)
        slot = k % self.slots
        return remote(
            self.pout.at[slot, i],
            self.own.at[j, i],
            self.po_s.at[slot, i],
            self.po_r.at[k, i],
            self.at.core,
        )

    def down_copy(self, s, i):
        return remote(
            self.own.at[s, i], self.din.at[s, i], self.d_s.at[s, i], self.d_r.at[s, i], self.at.below
        )

    def up_copy(self, s, i):
        n = self.at.n
        return remote(
            self.own.at[n - 1 - s, i],
            self.uin.at[s, i],
            self.u_s.at[s, i],
            self.u_r.at[s, i],
            self.at.above,
        )

    def other(self, k, tile):
        @pl.loop(0, self.pieces)
        def _(i):
            if k >= self.slots:
                self.core_copy(k - self.slots, i).wait_send()
            self.pout[k % self.slots, i] = tile(i).astype(BF)
            self.core_copy(k, i).start()

    def mine(self, k, tile):
        at = self.at
        j = order_of(k, at)

        @pl.loop(0, self.pieces)
        def _(i):
            value = tile(i)
            self.core_copy(k, i).wait_recv()
            self.own[j, i] = (value + self.own[j, i].astype(F32)).astype(BF)
            if k < at.n - 1:

                @pl.when(at.p == at.n - 1)
                def _():
                    self.down_copy(k, i).start()

                @pl.when(at.p == 0)
                def _():
                    self.up_copy(k, i).start()

    def add(self, dst, src):
        @pl.loop(0, dst.shape[0] // 64)
        def _(b):
            rs = pl.ds(pl.multiple_of(b * 64, 64), 64)
            dst[rs, :] = (dst[rs, :].astype(F32) + src[rs, :].astype(F32)).astype(BF)

    def slot(self, t):
        at = self.at
        n, p = at.n, at.p
        sd = t - (n - 2 - p)
        su = t - (p - 1)

        @pl.loop(0, self.pieces)
        def _(i):
            @pl.when((sd >= 0) & (sd < p) & at.has_above)
            def _():
                self.down_copy(sd, i).wait_recv()
                self.add(self.own.at[sd, i], self.din.at[sd, i])
                self.down_copy(sd, i).start()

            @pl.when((su >= 0) & (su < n - 1 - p) & at.has_below)
            def _():
                self.up_copy(su, i).wait_recv()
                self.add(self.own.at[n - 1 - su, i], self.uin.at[su, i])
                self.up_copy(su, i).start()

    def final(self, out):
        at = self.at
        n, p = at.n, at.p

        @pl.loop(0, self.pieces)
        def _(i):
            @pl.when(at.has_above)
            def _():
                self.down_copy(p, i).wait_recv()

            @pl.when(at.has_below)
            def _():
                self.up_copy(n - 1 - p, i).wait_recv()

            def close(parts):
                @pl.loop(0, out.shape[1] // 64)
                def _(b):
                    rs = pl.ds(pl.multiple_of(b * 64, 64), 64)
                    total = self.own[p, i, rs, :].astype(F32)
                    for ref, s in parts:
                        total = total + ref[s, i, rs, :].astype(F32)
                    out[i, rs, :] = total.astype(out.dtype)

            down, up = (self.din, p), (self.uin, n - 1 - p)

            @pl.when(at.has_above & at.has_below)
            def _():
                close([down, up])

            @pl.when(jnp.logical_not(at.has_below))
            def _():
                close([down])

            @pl.when(jnp.logical_not(at.has_above))
            def _():
                close([up])

    def drain(self):
        at = self.at
        n, p = at.n, at.p
        for k in range(n - self.slots, n):
            for i in range(self.pieces):
                self.core_copy(k, i).wait_send()
        for s in range(n - 1):

            @pl.when(s < p)
            def _():
                for i in range(self.pieces):
                    self.down_copy(s, i).wait_send()

            @pl.when(s < n - 1 - p)
            def _():
                for i in range(self.pieces):
                    self.up_copy(s, i).wait_send()


def line_sum_scratch(n, pieces, rows, cols, slots=2):
    dma = pltpu.SemaphoreType.DMA
    return [
        pltpu.VMEM((slots, pieces, rows, cols), BF),
        pltpu.VMEM((n, pieces, rows, cols), BF),
        pltpu.VMEM((n - 1, pieces, rows, cols), BF),
        pltpu.VMEM((n - 1, pieces, rows, cols), BF),
        dma((slots, pieces)),
        dma((n, pieces)),
        dma((n - 1, pieces)),
        dma((n - 1, pieces)),
        dma((n - 1, pieces)),
        dma((n - 1, pieces)),
    ]


class QuadSum:
    def __init__(self, at, t, r, sems):
        self.at, self.t, self.r = at, t, r
        self.s, self.v = sems
        self.order = [at.bits, at.bits[::-1]]
        self.levels = len(at.bits)
        self.seen = set()

    def count(self, k):
        return 1 << (self.levels - 1 - k)

    def slot(self, k, j):
        return sum(self.count(i) for i in range(k)) + j

    def rest(self, half, k):
        return self.order[half][k + 1 :]

    def index(self, half, k, mask):
        rest = self.rest(half, k)
        return self.slot(k, sum(1 << i for i, bit in enumerate(rest) if mask & bit))

    def source(self, half, mask):
        return self.t.at[half, self.at.quarter(mask)]

    def terms(self, half, mask, rs):
        return self.t[half, self.at.quarter(mask), rs, :].astype(F32)

    def copy(self, half, k, j):
        bit = self.order[half][k]
        mask = bit + spread(j, self.rest(half, k))
        src = self.source(half, mask) if k == 0 else self.r.at[half, self.index(half, k - 1, mask)]
        at = self.slot(k, j)
        return remote(
            src, self.r.at[half, at], self.s.at[half, at], self.v.at[half, at], self.at.peer(bit)
        )

    def offer(self, mask, only=(0, 1)):
        for half in only:
            if mask & self.order[half][0]:
                rest = self.rest(half, 0)
                self.copy(half, 0, sum(1 << i for i, b in enumerate(rest) if mask & b)).start()

    def masks(self):
        return sorted(range(1, 2 * self.count(0)), key=lambda m: -bin(m).count("1")) + [0]

    def come(self, half, k, mask):
        at = self.index(half, k, mask)
        if (half, at) not in self.seen:
            self.seen.add((half, at))
            self.copy(half, k, at - self.slot(k, 0)).wait_recv()
        return at

    def turn(self):
        for k in range(1, self.levels):
            for half in range(2):
                for j in range(self.count(k)):
                    mask = self.order[half][k] + spread(j, self.rest(half, k))
                    got = [self.come(half, i, mask) for i in range(k)]

                    @pl.loop(0, self.r.shape[2] // 64)
                    def _(b):
                        rs = pl.ds(pl.multiple_of(b * 64, 64), 64)
                        total = self.terms(half, mask, rs)
                        for i in got:
                            total = total + self.r[half, i, rs, :].astype(F32)
                        self.r[half, got[-1], rs, :] = total.astype(BF)

                    self.copy(half, k, j).start()

    def arrive(self):
        self.got = [[self.come(half, k, 0) for k in range(self.levels)] for half in range(2)]

    def total(self, half, rs):
        total = self.terms(half, 0, rs)
        for i in self.got[half]:
            total = total + self.r[half, i, rs, :].astype(F32)
        return total

    def drain(self):
        for half in range(2):
            for k in range(self.levels):
                for j in range(self.count(k)):
                    self.copy(half, k, j).wait_send()


class QuadSumHbm(QuadSum):
    def __init__(self, at, hbm, t, r, sems):
        super().__init__(at, t, r, sems[:2])
        self.hbm = hbm
        self.loads = [
            pltpu.make_async_copy(
                self.source(half, spread(j, self.rest(half, 0))), t.at[half, j], sems[2].at[half, j]
            )
            for half in range(2)
            for j in range(self.count(0))
        ]

    def source(self, half, mask):
        rows, cols = self.t.shape[2], self.t.shape[3]
        rs = pl.ds(pl.multiple_of(self.at.quarter(mask) * rows, rows), rows)
        return self.hbm.at[rs, pl.ds(half * cols, cols)]

    def terms(self, half, mask, rs):
        return self.t[half, self.index(half, 0, mask), rs, :].astype(F32)


def quad_sum_scratch(mp, rows, cols, parts=None):
    dma = pltpu.SemaphoreType.DMA
    return [
        pltpu.VMEM((2, parts or mp, rows, cols), BF),
        pltpu.VMEM((2, mp - 1, rows, cols), BF),
        dma((2, mp - 1)),
        dma((2, mp - 1)),
    ]


class QuadGather:
    def __init__(self, at, own, out, sems):
        self.at, self.own, self.out = at, own, out
        self.s, self.v, self.here = sems
        self.order = [at.bits[::-1], at.bits]
        self.levels = len(at.bits)
        self.seen = set()

    def spot(self, mask, half):
        rows, cols = self.own.shape[1], self.own.shape[2]
        rs = pl.ds(pl.multiple_of(self.at.quarter(mask) * rows, rows), rows)
        return self.out.at[rs, pl.ds(half * cols, cols)]

    def copy(self, half, k, j):
        mask = spread(j, self.order[half][:k])
        dst = self.spot(mask, half)
        src = self.own.at[half] if j == 0 else dst
        at = (1 << k) - 1 + j
        dev = self.at.peer(self.order[half][k])
        return remote(src, dst, self.s.at[half, at], self.v.at[half, at], dev)

    def come(self, half, k, j):
        if (half, k, j) not in self.seen:
            self.seen.add((half, k, j))
            self.copy(half, k, j).wait_recv()

    def keep(self, half):
        return pltpu.make_async_copy(self.own.at[half], self.spot(0, half), self.here.at[half])

    def start(self):
        for k in range(self.levels):
            for half in range(2):
                self.copy(half, k, 0).start()
        for half in range(2):
            self.keep(half).start()

    def forward(self):
        for k in range(1, self.levels):
            for half in range(2):
                for j in range(1, 1 << k):
                    top = j.bit_length() - 1
                    self.come(half, top, j - (1 << top))
                    self.copy(half, k, j).start()

    def finish(self):
        for half in range(2):
            for k in range(self.levels):
                for j in range(1 << k):
                    self.come(half, k, j)
                    self.copy(half, k, j).wait_send()
            self.keep(half).wait()


def quad_gather_scratch(mp, rows, cols):
    dma = pltpu.SemaphoreType.DMA
    return [pltpu.VMEM((2, rows, cols), BF), dma((2, mp - 1)), dma((2, mp - 1)), dma((2,))]


class LineGather:
    def __init__(self, at, pieces, shard, spot, sems):
        self.at, self.pieces, self.shard, self.spot = at, pieces, shard, spot
        self.d_s, self.d_r, self.u_s, self.u_r, self.c_s, self.c_r, self.here = sems

    def down_copy(self, h, i, own=False):
        b = 2 * (self.at.p + h) + self.at.c
        dst = self.spot(b, i)
        src = self.shard(i) if own else dst
        return remote(src, dst, self.d_s.at[h, i], self.d_r.at[h, i], self.at.below)

    def up_copy(self, h, i, own=False):
        b = 2 * (self.at.p - h) + self.at.c
        dst = self.spot(b, i)
        src = self.shard(i) if own else dst
        return remote(src, dst, self.u_s.at[h, i], self.u_r.at[h, i], self.at.above)

    def core_copy(self, z, i, own=False, incoming=False):
        b = 2 * z + (1 - self.at.c if incoming else self.at.c)
        dst = self.spot(b, i)
        src = self.shard(i) if own else dst
        return remote(src, dst, self.c_s.at[z, i], self.c_r.at[z, i], self.at.core)

    def keep(self, i):
        at = self.at
        return pltpu.make_async_copy(self.shard(i), self.spot(at.dp, i), self.here.at[i])

    def start(self):
        at = self.at
        for i in range(self.pieces):

            @pl.when(at.has_below)
            def _():
                self.down_copy(0, i, True).start()

            @pl.when(at.has_above)
            def _():
                self.up_copy(0, i, True).start()

        for i in range(self.pieces):
            self.core_copy(at.p, i, True).start()
            self.keep(i).start()

    def slot(self, h, i):
        at = self.at
        n, p = at.n, at.p

        @pl.when(p + h < n)
        def _():
            self.down_copy(h - 1, i).wait_recv()

            @pl.when(at.has_below)
            def _():
                self.down_copy(h, i).start()

            self.core_copy(p + h, i).start()

        @pl.when(p - h >= 0)
        def _():
            self.up_copy(h - 1, i).wait_recv()

            @pl.when(at.has_above)
            def _():
                self.up_copy(h, i).start()

            self.core_copy(p - h, i).start()

    def stage(self, h):
        @pl.loop(0, self.pieces)
        def _(i):
            self.slot(h, i)

    def ready(self, z, i):
        self.core_copy(z, i, incoming=True).wait_recv()

    def drain(self):
        at = self.at
        n, p = at.n, at.p

        @pl.loop(0, self.pieces)
        def _(i):
            for h in range(n):

                @pl.when((p + h < n) & at.has_below)
                def _():
                    self.down_copy(h, i, h == 0).wait_send()

                @pl.when((p - h >= 0) & at.has_above)
                def _():
                    self.up_copy(h, i, h == 0).wait_send()

            for z in range(n):
                self.core_copy(z, i).wait_send()


def line_gather_scratch(n, pieces):
    dma = pltpu.SemaphoreType.DMA
    return [dma((n, pieces))] * 6 + [dma((pieces,))]


def rows_spot(out, rows, width):
    def spot(b, i):
        rs = pl.ds(pl.multiple_of(b * rows, rows), rows)
        return out.at[rs, pl.ds(pl.multiple_of(i * width, width), width)]

    return spot


def cols_of(ref, width, base=0):
    return lambda i: ref.at[:, pl.ds(pl.multiple_of(base + i * width, width), width)]


def attend_rows(qkv, out, seq, hh, count, head):
    cols = lambda first: pl.ds(pl.multiple_of(first + head * HD, HD), HD)
    blk = 256
    for i in range(seq // blk):
        rows = pl.ds(i * blk, blk)
        span = (i + 1) * blk
        lg = logistic_block(qkv[rows, cols(0)], qkv[pl.ds(0, span), cols(hh)], seq)
        w = jnp.where(allowed_block(i * blk, blk, 0, span, count), lg, 0.0).astype(BF)
        out[rows, cols(0)] = dot(w, qkv[pl.ds(0, span), cols(2 * hh)]).astype(BF)


def attn_kernel(
    n_dp,
    n_mp,
    count_ref,
    gains_in,
    wq_hbm,
    wk_hbm,
    wv_hbm,
    wo_hbm,
    wg_hbm,
    wu_hbm,
    wd_hbm,
    x_hbm,
    cot_hbm,
    aw_ref,
    qkv_ref,
    att_ref,
    nin_ref,
    gains_ref,
    gush_ref,
    dnsh_ref,
    cotm_ref,
    w4,
    wo,
    shard,
    x,
    qkv,
    wbuf,
    wgu,
    wd,
    gush,
    dnsh,
    cot,
    load_s,
    wb_s,
    out_s,
    *rest,
):
    at = Place(n_dp, n_mp)
    n = at.n
    chunk, hh = wq_hbm.shape
    seq, d = x.shape
    ff = wgu.shape[2]
    loads = [
        pltpu.make_async_copy(src, dst, load_s.at[i])
        for i, (src, dst) in enumerate(
            [
                (wq_hbm, w4.at[0]),
                (wk_hbm, w4.at[1]),
                (wv_hbm, w4.at[2]),
                (wo_hbm, wo),
                (x_hbm, x),
                (wg_hbm, wgu.at[0]),
                (wu_hbm, wgu.at[1]),
                (wd_hbm, wd),
                (cot_hbm, cot),
            ]
        )
    ]
    for cp in loads:
        cp.start()
    spot = rows_spot(aw_ref, chunk, hh)
    three = LineGather(at, 3, cols_of(shard, hh), spot, rest[0:7])
    last = LineGather(
        at, 1, lambda i: shard.at[:, pl.ds(3 * hh, hh)], lambda b, i: spot(b, 3), rest[7:14]
    )
    small = LineGather(
        at,
        1,
        lambda i: gains_in,
        lambda b, i: gains_ref.at[:, pl.ds(pl.multiple_of(b * chunk, chunk), chunk)],
        rest[14:21],
    )
    enter(at)
    small.start()
    for i in range(3):
        loads[i].wait()
        shard[:, i * hh : (i + 1) * hh] = w4[i].astype(BF)
    three.start()
    loads[3].wait()
    shard[:, 3 * hh :] = wo[...].T.astype(BF)
    small.slot(1, 0)
    loads[5].wait()
    loads[6].wait()
    half = ff // PIECES

    @pl.loop(0, PIECES)
    def _(i):
        cols = pl.ds(pl.multiple_of(i * half, half), half)
        for k in range(2):
            to = pl.ds(pl.multiple_of((2 * i + k) * half, half), half)
            gush[:, to] = wgu[k, :, cols].astype(BF)

    outs = [pltpu.make_async_copy(gush, gush_ref, out_s.at[0])]
    outs[0].start()
    for h in range(2, n):
        small.slot(h, 0)
    small.keep(0).wait()
    for z in range(n):
        small.ready(z, 0)
    loads[4].wait()

    @pl.loop(0, seq // 32)
    def _(b):
        rs = pl.ds(pl.multiple_of(b * 32, 32), 32)
        v = x[rs, :].astype(F32)
        scale = lax.rsqrt(jnp.mean(v * v, axis=1, keepdims=True) + EPS)
        x[rs, :] = (v * scale * gains_ref[0:1, :]).astype(BF)

    outs.append(pltpu.make_async_copy(x, nin_ref, out_s.at[1]))
    outs[1].start()
    three.stage(1)
    loads[7].wait()

    @pl.loop(0, ff // 256)
    def _(i):
        rs = pl.ds(pl.multiple_of(i * 256, 256), 256)
        dnsh[:, rs] = wd[rs, :].T.astype(BF)

    outs.append(pltpu.make_async_copy(dnsh, dnsh_ref, out_s.at[2]))
    outs[2].start()
    loads[8].wait()
    count = count_ref[0]

    @pl.loop(0, seq // 32)
    def _(b):
        rs = pl.ds(pl.multiple_of(b * 32, 32), 32)
        row = b * 32 + lax.broadcasted_iota(jnp.int32, (32, d), 0)
        cot[rs, :] = jnp.where(row < count, cot[rs, :].astype(F32), 0.0).astype(BF)

    outs.append(pltpu.make_async_copy(cot, cotm_ref, out_s.at[3]))
    outs[3].start()
    for h in range(2, n - 1):
        three.stage(h)
    last.start()

    def w_copy(i):
        cols = pl.ds(pl.multiple_of(i * hh, hh), hh)
        return pltpu.make_async_copy(aw_ref.at[:, cols], wbuf.at[i], wb_s.at[i])

    for i in range(3):
        three.slot(n - 1, i)
        three.keep(i).wait()
        for z in range(n):
            three.ready(z, i)
        w_copy(i).start()
        if i == 1:
            last.slot(1, 0)
        w_copy(i).wait()

        @pl.loop(0, seq // 256)
        def _(b):
            rs = pl.ds(pl.multiple_of(b * 256, 256), 256)
            qkv[rs, i * hh : (i + 1) * hh] = dot(x[rs, :], wbuf[i]).astype(BF)

    outs.append(pltpu.make_async_copy(qkv, qkv_ref, out_s.at[4]))
    outs[4].start()
    for h in range(2, n - 1):
        last.slot(h, 0)
    heads = hh // HD

    @pl.loop(0, heads // 2)
    def _(head):
        attend_rows(qkv, att_ref, seq, hh, count, head)

    last.slot(n - 1, 0)

    @pl.loop(heads // 2, heads)
    def _(head):
        attend_rows(qkv, att_ref, seq, hh, count, head)

    last.keep(0).wait()
    for z in range(n):
        last.ready(z, 0)
    for cp in outs:
        cp.wait()
    small.drain()
    three.drain()
    last.drain()


def attn_stage(n_dp, n_mp, counts, gains, wq, wk, wv, wo, wg, wu, wd, x, cot):
    seq, d = x.shape
    chunk, hh = wq.shape
    ff = wg.shape[1]
    n = n_dp // 2
    dma = pltpu.SemaphoreType.DMA
    hbm = pl.BlockSpec(memory_space=pl.ANY)
    vm = pl.BlockSpec(memory_space=pltpu.VMEM)
    shapes = [
        ((d, 4 * hh), BF),
        ((seq, 3 * hh), BF),
        ((seq, hh), BF),
        ((seq, d), BF),
        ((8, d), F32),
        ((chunk, 2 * ff), BF),
        ((chunk, ff), BF),
        ((seq, d), BF),
    ]
    return pl.pallas_call(
        functools.partial(attn_kernel, n_dp, n_mp),
        out_shape=[jax.ShapeDtypeStruct(*s) for s in shapes],
        in_specs=[pl.BlockSpec(memory_space=pltpu.SMEM), vm] + [hbm] * 9,
        out_specs=[hbm, hbm, vm, hbm, vm, hbm, hbm, hbm],
        scratch_shapes=[
            pltpu.VMEM((3, chunk, hh), F32),
            pltpu.VMEM((hh, chunk), F32),
            pltpu.VMEM((chunk, 4 * hh), BF),
            pltpu.VMEM((seq, d), BF),
            pltpu.VMEM((seq, 3 * hh), BF),
            pltpu.VMEM((3, d, hh), BF),
            pltpu.VMEM((2, chunk, ff), F32),
            pltpu.VMEM((ff, chunk), F32),
            pltpu.VMEM((chunk, 2 * ff), BF),
            pltpu.VMEM((chunk, ff), BF),
            pltpu.VMEM((seq, d), BF),
            dma((9,)),
            dma((3,)),
            dma((5,)),
        ]
        + line_gather_scratch(n, 3)
        + line_gather_scratch(n, 1) * 2,
        compiler_params=pltpu.CompilerParams(
            collective_id=1, has_side_effects=True, vmem_limit_bytes=VMEM_LIMIT
        ),
        name="attn_stage",
    )(counts, gains, wq, wk, wv, wo, wg, wu, wd, x, cot)


def gate_kernel(
    n_dp,
    n_mp,
    att_ref,
    aw_hbm,
    sh_hbm,
    x_hbm,
    gain_ref,
    gw_ref,
    nm_ref,
    hid_ref,
    gu_ref,
    inner_ref,
    wo,
    xs,
    nm,
    wbuf,
    gbuf,
    ibuf,
    load_s,
    wb_s,
    gb_s,
    ib_s,
    *rest,
):
    at = Place(n_dp, n_mp)
    n = at.n
    quad = QuadSum(at, *rest[0:2], rest[2:4])
    gather_nm = QuadGather(at, rest[4], nm_ref, rest[5:8])
    sems = rest[8:15]
    hh = wo.shape[1]
    part, half_cols = quad.t.shape[2], quad.t.shape[3]
    chunk, wide = sh_hbm.shape
    pieces = sems[6].shape[0]
    width = wide // pieces
    line = LineGather(at, pieces, cols_of(sh_hbm, width), rows_spot(gw_ref, chunk, width), sems)

    load = pltpu.make_async_copy(aw_hbm.at[:, pl.ds(3 * hh, hh)], wo, load_s.at[0])
    load.start()
    load_x = pltpu.make_async_copy(x_hbm.at[part_rows(at, part), :], xs, load_s.at[1])
    load_x.start()
    enter(at)
    line.start()
    load.wait()

    def terms(q):
        rs = pl.ds(pl.multiple_of(q * part, part), part)
        for half in range(2):
            w = wo[half * half_cols : (half + 1) * half_cols, :]
            quad.t[half, q] = dot(att_ref[rs, :], w, NT).astype(BF)

    for mask in quad.masks():
        terms(at.quarter(mask))
        quad.offer(mask)
    quad.turn()
    quad.arrive()
    load_x.wait()

    @pl.loop(0, part // 32)
    def _(b):
        rs = pl.ds(pl.multiple_of(b * 32, 32), 32)
        h = xs[rs, :].astype(F32) + jnp.concatenate(
            [quad.total(0, rs), quad.total(1, rs)], axis=1
        )
        hid_ref[rs, :] = h
        scale = lax.rsqrt(jnp.mean(h * h, axis=1, keepdims=True) + EPS)
        res = (h * scale * gain_ref[1:2, :]).astype(BF)
        gather_nm.own[0, rs, :] = res[:, :half_cols]
        gather_nm.own[1, rs, :] = res[:, half_cols:]

    gather_nm.start()
    line.stage(1)
    gather_nm.forward()
    gather_nm.finish()
    load = pltpu.make_async_copy(nm_ref, nm, load_s.at[0])
    load.start()
    for h in range(2, n - 1):
        line.stage(h)
    load.wait()

    def w_copy(i, slot):
        cols = pl.ds(pl.multiple_of(i * width, width), width)
        return pltpu.make_async_copy(gw_ref.at[:, cols], wbuf.at[slot], wb_s.at[slot])

    def g_copy(i, slot):
        cols = pl.ds(pl.multiple_of(i * width, width), width)
        return pltpu.make_async_copy(gbuf.at[slot], gu_ref.at[:, cols], gb_s.at[slot])

    def i_copy(i, slot):
        cols = pl.ds(pl.multiple_of(i * (width // 2), width // 2), width // 2)
        return pltpu.make_async_copy(ibuf.at[slot], inner_ref.at[:, cols], ib_s.at[slot])

    @pl.loop(0, pieces)
    def _(i):
        slot = lax.rem(i, 2)
        line.slot(n - 1, i)
        line.keep(i).wait()
        for z in range(n):
            line.ready(z, i)
        w_copy(i, slot).start()

        @pl.when(i >= 2)
        def _():
            g_copy(i - 2, slot).wait()
            i_copy(i - 2, slot).wait()

        w_copy(i, slot).wait()

        @pl.loop(0, nm.shape[0] // 256)
        def _(b):
            rs = pl.ds(pl.multiple_of(b * 256, 256), 256)
            v = dot(nm[rs, :], wbuf[slot]).astype(BF)
            gbuf[slot, rs, :] = v
            g = v[:, : width // 2].astype(F32)
            u = v[:, width // 2 :].astype(F32)
            ibuf[slot, rs, :] = (g / (1.0 + jnp.exp(-g)) * u).astype(BF)

        g_copy(i, slot).start()
        i_copy(i, slot).start()

    for i in range(max(0, pieces - 2), pieces):
        g_copy(i, i % 2).wait()
        i_copy(i, i % 2).wait()
    line.drain()
    quad.drain()


def gate_stage(n_dp, n_mp, att, aw, shard, x, gain):
    seq, hh = att.shape
    d = aw.shape[0]
    chunk, wide = shard.shape
    n, part = n_dp // 2, seq // n_mp
    dma = pltpu.SemaphoreType.DMA
    hbm = pl.BlockSpec(memory_space=pl.ANY)
    vm = pl.BlockSpec(memory_space=pltpu.VMEM)
    width = wide // PIECES
    return pl.pallas_call(
        functools.partial(gate_kernel, n_dp, n_mp),
        out_shape=[
            jax.ShapeDtypeStruct((d, wide), BF),
            jax.ShapeDtypeStruct((seq, d), BF),
            jax.ShapeDtypeStruct((part, d), F32),
            jax.ShapeDtypeStruct((seq, wide), BF),
            jax.ShapeDtypeStruct((seq, wide // 2), BF),
        ],
        in_specs=[vm, hbm, hbm, hbm, vm],
        out_specs=[hbm, hbm, vm, hbm, hbm],
        scratch_shapes=[
            pltpu.VMEM((d, hh), BF),
            pltpu.VMEM((part, d), BF),
            pltpu.VMEM((seq, d), BF),
            pltpu.VMEM((2, d, width), BF),
            pltpu.VMEM((2, seq, width), BF),
            pltpu.VMEM((2, seq, width // 2), BF),
            dma((2,)),
            dma((2,)),
            dma((2,)),
            dma((2,)),
        ]
        + quad_sum_scratch(n_mp, part, d // 2)
        + quad_gather_scratch(n_mp, part, d // 2)
        + line_gather_scratch(n, PIECES),
        compiler_params=pltpu.CompilerParams(
            collective_id=2, has_side_effects=True, vmem_limit_bytes=VMEM_LIMIT
        ),
        name="gate_stage",
    )(att, aw, shard, x, gain)


def down_kernel(
    n_dp,
    n_mp,
    inner_hbm,
    gu_hbm,
    cot_hbm,
    sh_hbm,
    rs_ref,
    ft_ref,
    ggu_ref,
    dn_ref,
    inner,
    gu,
    cot,
    dn,
    acc,
    ftb,
    load_s,
    ft_s,
    dn_s,
    gg_s,
    *rest,
):
    at = Place(n_dp, n_mp)
    n, p = at.n, at.p
    line = LineSum(at, *rest[0:4], rest[4:10])
    sems = rest[10:17]
    chunk, ff = sh_hbm.shape
    pieces = sems[6].shape[0]
    width = ff // pieces
    gather = LineGather(at, pieces, cols_of(sh_hbm, width), rows_spot(dn_ref, chunk, width), sems)
    pair = 2 * chunk
    loads = [
        pltpu.make_async_copy(src, dst, load_s.at[i])
        for i, (src, dst) in enumerate([(cot_hbm, cot), (inner_hbm, inner), (gu_hbm, gu)])
    ]
    for cp in loads:
        cp.start()
    enter(at)
    gather.start()
    loads[0].wait()
    loads[1].wait()

    def run(e):
        k, core = e // 2, e % 2
        block = 2 * order_of(k, at) + (1 - at.c if core == 0 else at.c)
        lhs = cot[:, pl.ds(pl.multiple_of(block * chunk, chunk), chunk)].T

        def tile(i):
            return dot(lhs, inner[:, pl.ds(pl.multiple_of(i * width, width), width)])

        if core == 0:
            line.other(k, tile)
        else:
            line.mine(k, tile)

    for e in range(2 * n):
        run(e)

    def ft_copy(z, slot):
        cols = pl.ds(pl.multiple_of(z * pair, pair), pair)
        return pltpu.make_async_copy(ftb.at[slot], ft_ref.at[:, cols], ft_s.at[slot])

    def work(z, fresh):
        rs = pl.ds(pl.multiple_of(z * pair, pair), pair)

        @pl.loop(0, pieces)
        def _(i):
            gather.ready(z, i)

        load = pltpu.make_async_copy(dn_ref.at[rs, :], dn, dn_s.at[0])
        load.start()
        load.wait()

        @pl.loop(0, ff // 512)
        def _(i):
            cols = pl.ds(pl.multiple_of(i * 512, 512), 512)
            v = dot(cot[:, rs], dn[:, cols])
            acc[:, cols] = v if fresh else acc[:, cols] + v

        if not fresh:
            ft_copy(z, 0).wait()
        ftb[0] = dot(inner[...], dn[...], NT).astype(BF)
        ft_copy(z, 0).start()

    for i in range(pieces):
        gather.keep(i).wait()
    work(p, True)
    loads[2].wait()

    @pl.loop(1, n)
    def _(h):
        gather.stage(h)
        line.slot(h - 1)

        @pl.when(p + h < n)
        def _():
            work(p + h, False)

        @pl.when(p - h >= 0)
        def _():
            work(p - h, False)

    half = width

    def gg_copy(i):
        cols = pl.ds(pl.multiple_of(i * 2 * half, 2 * half), 2 * half)
        return pltpu.make_async_copy(gu.at[:, cols], ggu_ref.at[:, cols], gg_s.at[i])

    @pl.loop(0, pieces)
    def _(i):
        gcols = pl.ds(pl.multiple_of(i * 2 * half, half), half)
        ucols = pl.ds(pl.multiple_of(i * 2 * half + half, half), half)
        acols = pl.ds(pl.multiple_of(i * half, half), half)

        @pl.loop(0, gu.shape[0] // 64)
        def _(b):
            rs = pl.ds(pl.multiple_of(b * 64, 64), 64)
            g = gu[rs, gcols].astype(F32)
            u = gu[rs, ucols].astype(F32)
            gi = acc[rs, acols]
            sg = 1.0 / (1.0 + jnp.exp(-g))
            gu[rs, gcols] = (gi * u * sg * (1.0 + g * (1.0 - sg))).astype(BF)
            gu[rs, ucols] = (gi * g * sg).astype(BF)

        gg_copy(i).start()

    line.final(rs_ref)
    for i in range(pieces):
        gg_copy(i).wait()
    ft_copy(p, 0).wait()
    line.drain()
    gather.drain()


def down_stage(n_dp, n_mp, inner, gu, cot, shard):
    seq, d = cot.shape
    chunk, ff = shard.shape
    n = n_dp // 2
    dma = pltpu.SemaphoreType.DMA
    hbm = pl.BlockSpec(memory_space=pl.ANY)
    vm = pl.BlockSpec(memory_space=pltpu.VMEM)
    return pl.pallas_call(
        functools.partial(down_kernel, n_dp, n_mp),
        out_shape=[
            jax.ShapeDtypeStruct((PIECES, chunk, ff // PIECES), BF),
            jax.ShapeDtypeStruct((seq, d), BF),
            jax.ShapeDtypeStruct((seq, 2 * ff), BF),
            jax.ShapeDtypeStruct((d, ff), BF),
        ],
        in_specs=[hbm] * 4,
        out_specs=[vm, hbm, hbm, hbm],
        scratch_shapes=[
            pltpu.VMEM((seq, ff), BF),
            pltpu.VMEM((seq, 2 * ff), BF),
            pltpu.VMEM((seq, d), BF),
            pltpu.VMEM((2 * chunk, ff), BF),
            pltpu.VMEM((seq, ff), F32),
            pltpu.VMEM((1, seq, 2 * chunk), BF),
            dma((3,)),
            dma((1,)),
            dma((1,)),
            dma((PIECES,)),
        ]
        + line_sum_scratch(n, PIECES, chunk, ff // PIECES)
        + line_gather_scratch(n, PIECES),
        compiler_params=pltpu.CompilerParams(
            collective_id=3, has_side_effects=True, vmem_limit_bytes=VMEM_LIMIT
        ),
        name="down_stage",
    )(inner, gu, cot, shard)[:3]


def mid_kernel(
    n_dp,
    n_mp,
    ggu_hbm,
    gw_hbm,
    nm_hbm,
    ft_hbm,
    cot_hbm,
    qkv_hbm,
    aw_hbm,
    count_ref,
    hid_ref,
    gain_ref,
    rs_ref,
    low_ref,
    lay_ref,
    gh_ref,
    gg_ref,
    dq_ref,
    space,
    wt,
    wt_s,
    nm,
    nm_s,
    cot,
    dka,
    dva,
    load_s,
    *rest,
):
    at = Place(n_dp, n_mp)
    n = at.n
    line = LineSum(at, *rest[0:4], rest[4:10])
    mid = QuadSum(at, *rest[10:12], rest[12:14])
    lay = QuadSumHbm(at, ft_hbm, *rest[14:16], rest[16:19])
    gather_low = QuadGather(at, rest[19], low_ref, rest[20:23])
    gather_lay = QuadGather(at, rest[23], lay_ref, rest[24:27])
    part, half_cols = mid.t.shape[2], mid.t.shape[3]
    chunk, width = line.own.shape[2], line.own.shape[3]
    pieces = line.pieces
    hh = qkv_hbm.shape[1] // 3
    drows = wt.shape[1]
    tiles = half_cols // drows

    wide = ggu_hbm.shape[1]
    ggu = space.at[:, pl.ds(0, wide)]
    load = pltpu.make_async_copy(ggu_hbm, ggu, load_s.at[0])
    load.start()
    load_cot = pltpu.make_async_copy(cot_hbm.at[part_rows(at, part), :], cot, load_s.at[1])
    load_cot.start()

    def nm_copy(e):
        k, core = e // 2, e % 2
        block = 2 * order_of(k, at) + (1 - at.c if core == 0 else at.c)
        cols = pl.ds(pl.multiple_of(block * chunk, chunk), chunk)
        return pltpu.make_async_copy(nm_hbm.at[:, cols], nm.at[e % 2], nm_s.at[e % 2])

    def wt_copy(half, i, slot):
        rows = pl.ds(pl.multiple_of(half * half_cols + i * drows, drows), drows)
        return pltpu.make_async_copy(gw_hbm.at[rows, :], wt.at[slot], wt_s.at[slot])

    nm_copy(0).start()
    wt_copy(0, 0, 0).start()
    for cp in lay.loads:
        cp.start()
    enter(at)
    for mask in lay.masks():
        lay.offer(mask)
    load.wait()

    def run(e):
        if e + 1 < 2 * n:
            nm_copy(e + 1).start()
        nm_copy(e).wait()
        lhs = nm[e % 2].T

        def tile(i):
            return dot(lhs, ggu[:, pl.ds(pl.multiple_of(i * width, width), width)])

        if e % 2 == 0:
            line.other(e // 2, tile)
        else:
            line.mine(e // 2, tile)

    def terms(half):
        @pl.loop(0, tiles)
        def _(i):
            slot = lax.rem(i, 2)
            if half == 0:
                nxt = wt_copy(jnp.where(i + 1 < tiles, 0, 1), lax.rem(i + 1, tiles), 1 - slot)
                nxt.start()
            else:

                @pl.when(i + 1 < tiles)
                def _():
                    wt_copy(1, i + 1, 1 - slot).start()

            wt_copy(half, i, slot).wait()
            v = dot(ggu[...], wt[slot], NT).astype(BF)
            cols = pl.ds(pl.multiple_of(i * drows, drows), drows)
            for q in range(n_mp):
                mid.t[half, q, :, cols] = v[q * part : (q + 1) * part]

        for mask in mid.masks():
            mid.offer(mask, (half,))

    run(0)
    run(1)
    terms(0)
    run(2)
    run(3)
    terms(1)
    for cp in lay.loads:
        cp.wait()
    lay.turn()
    for e in range(4, 2 * n):
        run(e)
    lay.arrive()

    @pl.loop(0, part // 32)
    def _(b):
        rs = pl.ds(pl.multiple_of(b * 32, 32), 32)
        for half in range(2):
            h = hid_ref[rs, pl.ds(half * half_cols, half_cols)]
            gather_lay.own[half, rs, :] = (h + lay.total(half, rs)).astype(BF)

    line.slot(0)
    per = half_cols // hh
    blocks_d = 2 * half_cols // part
    wo_spot = [(e // per // (n_mp // 2), e // per % (n_mp // 2), e % per) for e in range(blocks_d)]
    wo_parts = [
        pltpu.make_async_copy(
            aw_hbm.at[pl.ds(e * part, part), pl.ds(3 * hh, hh)],
            lay.t.at[i, j, :, pl.ds(k * hh, hh)],
            load_s.at[4 + e],
        )
        for e, (i, j, k) in enumerate(wo_spot)
    ]
    for cp in wo_parts:
        cp.start()
    load_qkv = pltpu.make_async_copy(
        qkv_hbm, space.at[:, pl.ds(2 * half_cols, 3 * hh)], load_s.at[2]
    )
    load_qkv.start()
    mid.turn()
    mid.arrive()
    load_cot.wait()
    gg_ref[...] = jnp.zeros_like(gg_ref)

    @pl.loop(0, part // 32)
    def _(b):
        rs = pl.ds(pl.multiple_of(b * 32, 32), 32)
        h = hid_ref[rs, :]
        scale = lax.rsqrt(jnp.mean(h * h, axis=1, keepdims=True) + EPS)
        g = jnp.concatenate([mid.total(0, rs), mid.total(1, rs)], axis=1)
        unit = h * scale
        weighted = g * gain_ref[1:2, :]
        field = scale * (weighted - unit * jnp.mean(weighted * unit, axis=1, keepdims=True))
        res = cot[rs, :].astype(F32) + field
        gh_ref[rs, :] = res
        low = res.astype(BF)
        gather_low.own[0, rs, :] = low[:, :half_cols]
        gather_low.own[1, rs, :] = low[:, half_cols:]
        gg_ref[...] += jnp.sum(g * unit, axis=0, keepdims=True)

    gather_low.start()
    gather_low.forward()
    gather_lay.start()
    gather_low.finish()
    load_low = pltpu.make_async_copy(low_ref, space.at[:, pl.ds(0, 2 * half_cols)], load_s.at[3])
    load_low.start()
    for s in range(1, n - 2):
        line.slot(s)
    gather_lay.forward()
    load_low.wait()
    load_qkv.wait()
    for cp in wo_parts:
        cp.wait()
    seq = space.shape[0]
    base = 2 * half_cols
    gbase = base + 3 * hh

    @pl.loop(0, seq // 256)
    def _(b):
        rs = pl.ds(pl.multiple_of(b * 256, 256), 256)
        total = jnp.zeros((256, hh), F32)
        for e, (i, j, k) in enumerate(wo_spot):
            wo = lay.t[i, j, :, k * hh : (k + 1) * hh]
            total += dot(space[rs, e * part : (e + 1) * part], wo)
        space[rs, gbase : gbase + hh] = total.astype(BF)

    count = count_ref[0]
    blk = 256
    blocks = seq // blk

    @pl.loop(0, hh // HD)
    def _(head):
        at_cols = lambda first: pl.ds(pl.multiple_of(first + head * HD, HD), HD)
        for i in range(blocks - 1, -1, -1):
            rows = pl.ds(i * blk, blk)
            span = (i + 1) * blk
            keys = pl.ds(0, span)
            q = space[rows, at_cols(base)]
            g = space[rows, at_cols(gbase)]
            k = space[keys, at_cols(base + hh)]
            lg = jnp.where(
                allowed_block(i * blk, blk, 0, span, count), logistic_block(q, k, seq), 0.0
            )
            w = lg.astype(BF)
            gw = dot(g, space[keys, at_cols(base + 2 * hh)], NT)
            gs = (gw * lg * (1.0 - lg) * HD ** (-0.5)).astype(BF)
            wt[i // 2, :, at_cols((i % 2) * (wide // 2))] = dot(gs, k).astype(BF)
            dk = dot(gs, q, TN)
            dv = dot(w, g, TN)
            if i == blocks - 1:
                dka[...] = dk
                dva[...] = dv
            else:
                dka[keys, :] += dk
                dva[keys, :] += dv
        for i in range(blocks):
            rows = pl.ds(i * blk, blk)
            wt[i // 2, :, at_cols((i % 2) * (wide // 2) + hh)] = dka[rows, :].astype(BF)
            wt[i // 2, :, at_cols((i % 2) * (wide // 2) + 2 * hh)] = dva[rows, :].astype(BF)

    stores = [
        pltpu.make_async_copy(
            wt.at[i // 2, :, pl.ds((i % 2) * (wide // 2), 3 * hh)],
            dq_ref.at[pl.ds(i * blk, blk), :],
            load_s.at[4 + i],
        )
        for i in range(blocks)
    ]
    for cp in stores:
        cp.start()
    line.final(rs_ref)
    gather_lay.finish()
    for cp in stores:
        cp.wait()
    line.drain()
    mid.drain()
    lay.drain()


def mid_stage(n_dp, n_mp, ggu, gw, nm, ft, cot, qkv, aw, counts, hid, gain):
    seq, wide = ggu.shape
    hh = qkv.shape[1] // 3
    d = gw.shape[0]
    n, part, chunk = n_dp // 2, seq // n_mp, d // n_dp
    dma = pltpu.SemaphoreType.DMA
    hbm = pl.BlockSpec(memory_space=pl.ANY)
    vm = pl.BlockSpec(memory_space=pltpu.VMEM)
    pieces = PIECES
    return pl.pallas_call(
        functools.partial(mid_kernel, n_dp, n_mp),
        out_shape=[
            jax.ShapeDtypeStruct((pieces, chunk, wide // pieces), BF),
            jax.ShapeDtypeStruct((seq, d), BF),
            jax.ShapeDtypeStruct((seq, d), BF),
            jax.ShapeDtypeStruct((part, d), F32),
            jax.ShapeDtypeStruct((1, d), F32),
            jax.ShapeDtypeStruct((seq, 3 * hh), BF),
        ],
        in_specs=[hbm] * 7 + [pl.BlockSpec(memory_space=pltpu.SMEM)] + [vm] * 2,
        out_specs=[vm, hbm, hbm, vm, vm, hbm],
        scratch_shapes=[
            pltpu.VMEM((seq, max(wide, d + 4 * hh)), BF),
            pltpu.VMEM((2, 256, wide), BF),
            dma((2,)),
            pltpu.VMEM((2, seq, chunk), BF),
            dma((2,)),
            pltpu.VMEM((part, d), BF),
            pltpu.VMEM((seq, HD), F32),
            pltpu.VMEM((seq, HD), F32),
            dma((4 + max(d // part, seq // 256),)),
        ]
        + line_sum_scratch(n, pieces, chunk, wide // pieces, 1)
        + quad_sum_scratch(n_mp, part, d // 2)
        + quad_sum_scratch(n_mp, part, d // 2, n_mp // 2)
        + [dma((2, n_mp // 2))]
        + quad_gather_scratch(n_mp, part, d // 2) * 2,
        compiler_params=pltpu.CompilerParams(
            collective_id=4, has_side_effects=True, vmem_limit_bytes=VMEM_LIMIT
        ),
        name="mid_stage",
    )(ggu, gw, nm, ft, cot, qkv, aw, counts, hid, gain)


def last_kernel(
    n_dp,
    n_mp,
    dqkv_hbm,
    aw_hbm,
    nin_hbm,
    low_hbm,
    att_hbm,
    x_hbm,
    gh_ref,
    gain_ref,
    gmid_ref,
    rs_ref,
    grad_ref,
    gains_ref,
    rhs,
    aw,
    nin,
    low,
    lhs,
    x,
    loads,
    pout,
    own,
    din,
    uin,
    po_s,
    po_r,
    d_s,
    d_r,
    u_s,
    u_r,
    t,
    r,
    q1,
    q2,
    gown,
    g1,
    g2,
    g3,
    fold_out,
    fold_in,
    fold_s,
    fold_r,
):
    at = Place(n_dp, n_mp)
    hh = att_hbm.shape[1]
    part = t.shape[2]
    chunk = own.shape[2]
    half_cols = t.shape[3]
    copies = [
        pltpu.make_async_copy(src, dst, loads.at[i])
        for i, (src, dst) in enumerate(
            [
                (dqkv_hbm, rhs.at[:, pl.ds(0, 3 * hh)]),
                (aw_hbm.at[:, pl.ds(0, 3 * hh)], aw),
                (nin_hbm, nin),
                (att_hbm, rhs.at[:, pl.ds(3 * hh, hh)]),
                (low_hbm, low),
                (x_hbm.at[part_rows(at, part), :], x),
            ]
        )
    ]
    for cp in copies:
        cp.start()
    bits = [b for b in (2, 4, 8, 16) if b < n_dp]
    enter(at, [at.fold(b) for b in bits[1:]])
    quad = QuadSum(at, t, r, (q1, q2))
    line = LineSum(at, pout, own, din, uin, (po_s, po_r, d_s, d_r, u_s, u_r))
    gather = QuadGather(at, gown, grad_ref, (g1, g2, g3))
    copies[0].wait()
    copies[1].wait()

    def terms(q):
        rs = pl.ds(pl.multiple_of(q * part, part), part)
        width = 512

        @pl.loop(0, half_cols // width)
        def _(i):
            for half in range(2):
                d0 = pl.multiple_of(half * half_cols + i * width, width)
                v = dot(rhs[rs, 0 : 3 * hh], aw[pl.ds(d0, width), :], NT)
                t[half, q, :, pl.ds(pl.multiple_of(i * width, width), width)] = v.astype(BF)

    for mask in quad.masks()[:-1]:
        terms(at.quarter(mask))
        quad.offer(mask)
    for cp in copies[2:]:
        cp.wait()

    def run(k, core):
        block = 2 * order_of(k, at) + (at.c if core else 1 - at.c)
        cols = pl.ds(pl.multiple_of(block * chunk, chunk), chunk)
        lhs[0] = nin[:, cols].T
        lhs[1] = low[:, cols].T

        def tile(i):
            return dot(lhs[lax.div(i, 3)], rhs[:, pl.ds(pl.multiple_of(i * hh, hh), hh)])

        if core:
            line.mine(k, tile)
        else:
            line.other(k, tile)

    n = at.n
    for k in range(n + 1):
        if k < n:
            run(k, 0)
        if k > 0:
            run(k - 1, 1)
    terms(at.m)
    quad.turn()
    line.slot(0)
    quad.arrive()

    fold_out[...] = jnp.zeros_like(fold_out)

    @pl.loop(0, part // 32)
    def _(b):
        rs = pl.ds(pl.multiple_of(b * 32, 32), 32)
        v = x[rs, :].astype(F32)
        scale = lax.rsqrt(jnp.mean(v * v, axis=1, keepdims=True) + EPS)
        g = jnp.concatenate([quad.total(0, rs), quad.total(1, rs)], axis=1)
        unit = v * scale
        weighted = g * gain_ref[0:1, :]
        field = scale * (weighted - unit * jnp.mean(weighted * unit, axis=1, keepdims=True))
        res = (gh_ref[rs, :] + field).astype(BF)
        gown[0, rs, :] = res[:, :half_cols]
        gown[1, rs, :] = res[:, half_cols:]
        fold_out[0, 0:1, :] += jnp.sum(g * unit, axis=0, keepdims=True)

    gather.start()
    fold_out[0, 1:2, :] = gmid_ref[...]
    devs = [at.core] + [at.peer(b) for b in at.bits] + [at.fold(b) for b in bits]

    def fold_copy(b):
        return remote(fold_out.at[b], fold_in.at[b], fold_s.at[b], fold_r.at[b], devs[b])

    def fold_next(b):
        fold_copy(b).wait_recv()
        nxt = fold_out[b] + fold_in[b]
        if b + 1 < len(devs):
            fold_out[b + 1] = nxt
            fold_copy(b + 1).start()
        else:
            gains_ref[...] = nxt

    fold_copy(0).start()
    for s in range(1, n - 2):
        line.slot(s)
    gather.forward()
    for b in range(len(devs)):
        fold_next(b)
    line.final(rs_ref)
    gather.finish()
    line.drain()
    quad.drain()
    for b in range(len(devs)):
        fold_copy(b).wait_send()


def last_stage(n_dp, n_mp, dqkv, aw, nin, low, att, x, gh, gain, gmid):
    seq, hh = att.shape
    d = aw.shape[0]
    n, part, chunk = n_dp // 2, seq // n_mp, d // n_dp
    dma = pltpu.SemaphoreType.DMA
    anyspace = pl.BlockSpec(memory_space=pl.ANY)
    vm = pl.BlockSpec(memory_space=pltpu.VMEM)
    folds = 1 + len([b for b in (1, 2, 4, 8) if b < n_mp]) + len([b for b in (2, 4, 8, 16) if b < n_dp])
    return pl.pallas_call(
        functools.partial(last_kernel, n_dp, n_mp),
        out_shape=[
            jax.ShapeDtypeStruct((4, chunk, hh), BF),
            jax.ShapeDtypeStruct((seq, d), BF),
            jax.ShapeDtypeStruct((8, d), F32),
        ],
        in_specs=[anyspace] * 6 + [vm] * 3,
        out_specs=[vm, anyspace, vm],
        scratch_shapes=[
            pltpu.VMEM((seq, 4 * hh), BF),
            pltpu.VMEM((d, 3 * hh), BF),
            pltpu.VMEM((seq, d), BF),
            pltpu.VMEM((seq, d), BF),
            pltpu.VMEM((2, chunk, seq), BF),
            pltpu.VMEM((part, d), BF),
            dma((6,)),
        ]
        + line_sum_scratch(n, 4, chunk, hh)
        + quad_sum_scratch(n_mp, part, d // 2)
        + quad_gather_scratch(n_mp, part, d // 2)
        + [
            pltpu.VMEM((folds, 8, d), F32),
            pltpu.VMEM((folds, 8, d), F32),
            dma((folds,)),
            dma((folds,)),
        ],
        compiler_params=pltpu.CompilerParams(
            collective_id=5, has_side_effects=True, vmem_limit_bytes=VMEM_LIMIT
        ),
        name="last_stage",
    )(dqkv, aw, nin, low, att, x, gh, gain, gmid)


def on_device(
    inputs,
    counts,
    cotangent,
    gain_attn,
    w_query,
    w_key,
    w_value,
    w_output,
    gain_ffn,
    w_gate,
    w_up,
    w_down,
):
    ff = w_gate.shape[1]
    n_dp, n_mp = lax.axis_size("dp"), lax.axis_size("mp")
    gains = jnp.pad(jnp.stack([gain_attn, gain_ffn]), ((0, 6), (0, 0)))
    gains = gains.astype(BF).astype(F32)
    attn_w, qkv, attended, normed_in, gains, gu_shard, down_shard, grad_ffn = attn_stage(
        n_dp, n_mp, counts, gains, w_query, w_key, w_value, w_output, w_gate, w_up, w_down, inputs, cotangent
    )
    gu_w, normed_mid, hidden, gu, inner = gate_stage(
        n_dp, n_mp, attended, attn_w, gu_shard, inputs, gains
    )
    rs_down, ffn_terms, ggu = down_stage(n_dp, n_mp, inner, gu, grad_ffn, down_shard)
    rs_gu, grad_low, layer_out, grad_hidden, g_gain_mid, dqkv = mid_stage(
        n_dp, n_mp, ggu, gu_w, normed_mid, ffn_terms, grad_ffn, qkv, attn_w, counts, hidden, gains
    )
    rs_attn, grad_low_in, g_gains = last_stage(
        n_dp, n_mp, dqkv, attn_w, normed_in, grad_low, attended, inputs, grad_hidden, gains, g_gain_mid
    )
    input_grad = grad_low_in.astype(F32)
    width = g_gains.shape[1] // lax.axis_size("dp")
    g_gains = lax.dynamic_slice_in_dim(g_gains, lax.axis_index("dp") * width, width, 1)
    half = ff // PIECES
    unpack = lambda i: jnp.concatenate(
        [rs_gu[k, :, i * half : (i + 1) * half] for k in range(PIECES)], axis=1
    ).astype(F32)
    down_t = jnp.concatenate([rs_down[k] for k in range(PIECES)], axis=1)
    return (
        layer_out,
        input_grad,
        g_gains[0],
        rs_attn[0].astype(F32),
        rs_attn[1].astype(F32),
        rs_attn[2].astype(F32),
        rs_attn[3].astype(F32).T,
        g_gains[1],
        unpack(0),
        unpack(1),
        down_t.astype(F32).T,
    )


def solution(mesh):
    row, both, swapped = P("dp", None), P("dp", "mp"), P("mp", "dp")
    weights = (both, both, both, swapped)
    ffn = (both, both, swapped)
    return jax.shard_map(
        on_device,
        mesh=mesh,
        in_specs=(row, P("dp"), row, P("dp")) + weights + (P("dp"),) + ffn,
        out_specs=(row, row, P("dp")) + weights + (P("dp"),) + ffn,
        check_vma=False,
    )
```

```python
import functools
import math

import jax
import jax.numpy as jnp
from jax import lax
from jax.experimental import pallas as pl
from jax.experimental.pallas import tpu as pltpu
from jax.sharding import PartitionSpec as P

HD = 128
EPS = 1e-06
BF = jnp.bfloat16
F32 = jnp.float32
NT = (((1,), (1,)), ((), ()))
TN = (((0,), (0,)), ((), ()))
NN = (((1,), (0,)), ((), ()))


def dot(a, b, dims=NN):
    return lax.dot_general(a, b, dims, preferred_element_type=F32)


def logistic_block(q, k, seq):
    raw = dot(q, k, NT)
    shifted = math.log(seq) - raw * HD ** (-0.5)
    return 1.0 / (1.0 + jnp.exp(shifted))


def allowed_block(row0, rows, col0, cols, count):
    ri = row0 + lax.broadcasted_iota(jnp.int32, (rows, cols), 0)
    ci = col0 + lax.broadcasted_iota(jnp.int32, (rows, cols), 1)
    return (ci <= ri) & (ci < count)


MESH = pl.DeviceIdType.MESH
VMEM_LIMIT = 60 * 1024 * 1024
PIECES = 4


def flipped(index, bit):
    return index + bit - 2 * bit * lax.rem(lax.div(index, bit), 2)


def spread(j, bits):
    return sum(bit for i, bit in enumerate(bits) if j >> i & 1)


class Place:
    def __init__(self, n_dp, n_mp):
        self.n = n_dp // 2
        self.dp = lax.axis_index("dp")
        self.m = lax.axis_index("mp")
        self.p = lax.div(self.dp, 2)
        self.c = lax.rem(self.dp, 2)
        self.above = (self.dp + 2, self.m)
        self.below = (self.dp - 2, self.m)
        self.core = (self.dp + 1 - 2 * self.c, self.m)
        self.bits = [b for b in (1, 2, 4, 8, 16) if b < n_mp]
        self.has_above = self.p < self.n - 1
        self.has_below = self.p > 0

    def fold(self, bit):
        return (flipped(self.dp, bit), self.m)

    def peer(self, bit):
        return (self.dp, flipped(self.m, bit))

    def quarter(self, mask):
        q = self.m
        for bit in self.bits:
            if mask & bit:
                q = flipped(q, bit)
        return q


def signal(dev):
    pl.semaphore_signal(pltpu.get_barrier_semaphore(), inc=1, device_id=dev, device_id_type=MESH)


def enter(at, extra=()):
    always = [at.core] + [at.peer(bit) for bit in at.bits] + list(extra)
    for dev in always:
        signal(dev)

    @pl.when(at.has_above)
    def _():
        signal(at.above)

    @pl.when(at.has_below)
    def _():
        signal(at.below)

    ends = at.has_above.astype(jnp.int32) + at.has_below.astype(jnp.int32)
    pl.semaphore_wait(pltpu.get_barrier_semaphore(), len(always) + ends)


def remote(src, dst, send, recv, dev):
    return pltpu.make_async_remote_copy(
        src_ref=src, dst_ref=dst, send_sem=send, recv_sem=recv, device_id=dev, device_id_type=MESH
    )


def part_rows(at, part):
    return pl.ds(pl.multiple_of(at.m * part, part), part)


def order_of(k, at):
    n, p = at.n, at.p
    if k == n - 1:
        return p
    high = jnp.where(k < p, k, n - 1 - k + p)
    low = jnp.where(k < n - 1 - p, n - 1 - k, k - (n - 1 - p))
    return jnp.where(2 * p >= n, high, low)


class LineSum:
    def __init__(self, at, pout, own, din, uin, sems, paced=False):
        self.paced = paced
        self.at, self.pout, self.own, self.din, self.uin = at, pout, own, din, uin
        self.po_s, self.po_r, self.d_s, self.d_r, self.u_s, self.u_r = sems
        self.slots, self.pieces = pout.shape[0], own.shape[1]

    def core_copy(self, k, i):
        j = order_of(k, self.at)
        slot = k % self.slots
        return remote(
            self.pout.at[slot, i],
            self.own.at[j, i],
            self.po_s.at[slot, i],
            self.po_r.at[k, i],
            self.at.core,
        )

    def down_copy(self, s, i):
        return remote(
            self.own.at[s, i], self.din.at[s, i], self.d_s.at[s, i], self.d_r.at[s, i], self.at.below
        )

    def up_copy(self, s, i):
        n = self.at.n
        return remote(
            self.own.at[n - 1 - s, i],
            self.uin.at[s, i],
            self.u_s.at[s, i],
            self.u_r.at[s, i],
            self.at.above,
        )

    def other(self, k, tile):
        @pl.loop(0, self.pieces)
        def _(i):
            if k >= self.slots:
                self.core_copy(k - self.slots, i).wait_send()
            self.pout[k % self.slots, i] = tile(i).astype(BF)
            self.core_copy(k, i).start()

    def mine(self, k, tile):
        at = self.at
        j = order_of(k, at)

        @pl.loop(0, self.pieces)
        def _(i):
            value = tile(i)
            self.core_copy(k, i).wait_recv()
            self.own[j, i] = (value + self.own[j, i].astype(F32)).astype(BF)
            if k < (1 if self.paced else at.n - 1):

                @pl.when(at.p == at.n - 1)
                def _():
                    self.down_copy(k, i).start()

                @pl.when(at.p == 0)
                def _():
                    self.up_copy(k, i).start()

    def add(self, dst, src):
        @pl.loop(0, dst.shape[0] // 64)
        def _(b):
            rs = pl.ds(pl.multiple_of(b * 64, 64), 64)
            dst[rs, :] = (dst[rs, :].astype(F32) + src[rs, :].astype(F32)).astype(BF)

    def slot(self, t):
        at = self.at
        n, p = at.n, at.p
        sd = t - (n - 2 - p)
        su = t - (p - 1)

        @pl.loop(0, self.pieces)
        def _(i):
            @pl.when((sd >= 0) & (sd < p) & at.has_above)
            def _():
                self.down_copy(sd, i).wait_recv()
                self.add(self.own.at[sd, i], self.din.at[sd, i])
                self.down_copy(sd, i).start()

            @pl.when((su >= 0) & (su < n - 1 - p) & at.has_below)
            def _():
                self.up_copy(su, i).wait_recv()
                self.add(self.own.at[n - 1 - su, i], self.uin.at[su, i])
                self.up_copy(su, i).start()

            if self.paced:

                @pl.when(p == n - 1)
                def _():
                    self.down_copy(t, i).wait_send()
                    self.down_copy(t + 1, i).start()

                @pl.when(p == 0)
                def _():
                    self.up_copy(t, i).wait_send()
                    self.up_copy(t + 1, i).start()

    def final(self, out):
        at = self.at
        n, p = at.n, at.p

        @pl.loop(0, self.pieces)
        def _(i):
            @pl.when(at.has_above)
            def _():
                self.down_copy(p, i).wait_recv()

            @pl.when(at.has_below)
            def _():
                self.up_copy(n - 1 - p, i).wait_recv()

            def close(parts):
                @pl.loop(0, out.shape[1] // 64)
                def _(b):
                    rs = pl.ds(pl.multiple_of(b * 64, 64), 64)
                    total = self.own[p, i, rs, :].astype(F32)
                    for ref, s in parts:
                        total = total + ref[s, i, rs, :].astype(F32)
                    out[i, rs, :] = total.astype(out.dtype)

            down, up = (self.din, p), (self.uin, n - 1 - p)

            @pl.when(at.has_above & at.has_below)
            def _():
                close([down, up])

            @pl.when(jnp.logical_not(at.has_below))
            def _():
                close([down])

            @pl.when(jnp.logical_not(at.has_above))
            def _():
                close([up])

    def drain(self):
        at = self.at
        n, p = at.n, at.p
        for k in range(n - self.slots, n):
            for i in range(self.pieces):
                self.core_copy(k, i).wait_send()
        for s in range(n - 1):
            done = self.paced and s < n - 2

            @pl.when((s < p) & (at.has_above if done else at.has_below))
            def _():
                for i in range(self.pieces):
                    self.down_copy(s, i).wait_send()

            @pl.when((s < n - 1 - p) & (at.has_below if done else at.has_above))
            def _():
                for i in range(self.pieces):
                    self.up_copy(s, i).wait_send()


def line_sum_scratch(n, pieces, rows, cols, slots=2):
    dma = pltpu.SemaphoreType.DMA
    return [
        pltpu.VMEM((slots, pieces, rows, cols), BF),
        pltpu.VMEM((n, pieces, rows, cols), BF),
        pltpu.VMEM((n - 1, pieces, rows, cols), BF),
        pltpu.VMEM((n - 1, pieces, rows, cols), BF),
        dma((slots, pieces)),
        dma((n, pieces)),
        dma((n - 1, pieces)),
        dma((n - 1, pieces)),
        dma((n - 1, pieces)),
        dma((n - 1, pieces)),
    ]


class QuadSum:
    def __init__(self, at, t, r, sems):
        self.at, self.t, self.r = at, t, r
        self.s, self.v = sems
        self.order = [at.bits, at.bits[::-1]]
        self.levels = len(at.bits)
        self.seen = set()

    def count(self, k):
        return 1 << (self.levels - 1 - k)

    def slot(self, k, j):
        return sum(self.count(i) for i in range(k)) + j

    def rest(self, half, k):
        return self.order[half][k + 1 :]

    def index(self, half, k, mask):
        rest = self.rest(half, k)
        return self.slot(k, sum(1 << i for i, bit in enumerate(rest) if mask & bit))

    def source(self, half, mask):
        return self.t.at[half, self.at.quarter(mask)]

    def terms(self, half, mask, rs):
        return self.t[half, self.at.quarter(mask), rs, :].astype(F32)

    def copy(self, half, k, j):
        bit = self.order[half][k]
        mask = bit + spread(j, self.rest(half, k))
        src = self.source(half, mask) if k == 0 else self.r.at[half, self.index(half, k - 1, mask)]
        at = self.slot(k, j)
        return remote(
            src, self.r.at[half, at], self.s.at[half, at], self.v.at[half, at], self.at.peer(bit)
        )

    def offer(self, mask, only=(0, 1)):
        for half in only:
            if mask & self.order[half][0]:
                rest = self.rest(half, 0)
                self.copy(half, 0, sum(1 << i for i, b in enumerate(rest) if mask & b)).start()

    def masks(self):
        return sorted(range(1, 2 * self.count(0)), key=lambda m: -bin(m).count("1")) + [0]

    def come(self, half, k, mask):
        at = self.index(half, k, mask)
        if (half, at) not in self.seen:
            self.seen.add((half, at))
            self.copy(half, k, at - self.slot(k, 0)).wait_recv()
        return at

    def turn(self):
        for k in range(1, self.levels):
            for half in range(2):
                for j in range(self.count(k)):
                    mask = self.order[half][k] + spread(j, self.rest(half, k))
                    got = [self.come(half, i, mask) for i in range(k)]

                    @pl.loop(0, self.r.shape[2] // 64)
                    def _(b):
                        rs = pl.ds(pl.multiple_of(b * 64, 64), 64)
                        total = self.terms(half, mask, rs)
                        for i in got:
                            total = total + self.r[half, i, rs, :].astype(F32)
                        self.r[half, got[-1], rs, :] = total.astype(BF)

                    self.copy(half, k, j).start()

    def arrive(self):
        self.got = [[self.come(half, k, 0) for k in range(self.levels)] for half in range(2)]

    def total(self, half, rs):
        total = self.terms(half, 0, rs)
        for i in self.got[half]:
            total = total + self.r[half, i, rs, :].astype(F32)
        return total

    def drain(self):
        for half in range(2):
            for k in range(self.levels):
                for j in range(self.count(k)):
                    self.copy(half, k, j).wait_send()


class QuadSumHbm(QuadSum):
    def __init__(self, at, hbm, t, r, sems):
        super().__init__(at, t, r, sems[:2])
        self.hbm = hbm
        self.loads = [
            pltpu.make_async_copy(
                self.source(half, spread(j, self.rest(half, 0))), t.at[half, j], sems[2].at[half, j]
            )
            for half in range(2)
            for j in range(self.count(0))
        ]

    def source(self, half, mask):
        rows, cols = self.t.shape[2], self.t.shape[3]
        rs = pl.ds(pl.multiple_of(self.at.quarter(mask) * rows, rows), rows)
        return self.hbm.at[rs, pl.ds(half * cols, cols)]

    def terms(self, half, mask, rs):
        return self.t[half, self.index(half, 0, mask), rs, :].astype(F32)


def quad_sum_scratch(mp, rows, cols, parts=None):
    dma = pltpu.SemaphoreType.DMA
    return [
        pltpu.VMEM((2, parts or mp, rows, cols), BF),
        pltpu.VMEM((2, mp - 1, rows, cols), BF),
        dma((2, mp - 1)),
        dma((2, mp - 1)),
    ]


class QuadGather:
    def __init__(self, at, own, out, sems):
        self.at, self.own, self.out = at, own, out
        self.s, self.v, self.here = sems
        self.order = [at.bits[::-1], at.bits]
        self.levels = len(at.bits)
        self.seen = set()

    def spot(self, mask, half):
        rows, cols = self.own.shape[1], self.own.shape[2]
        rs = pl.ds(pl.multiple_of(self.at.quarter(mask) * rows, rows), rows)
        return self.out.at[rs, pl.ds(half * cols, cols)]

    def copy(self, half, k, j):
        mask = spread(j, self.order[half][:k])
        dst = self.spot(mask, half)
        src = self.own.at[half] if j == 0 else dst
        at = (1 << k) - 1 + j
        dev = self.at.peer(self.order[half][k])
        return remote(src, dst, self.s.at[half, at], self.v.at[half, at], dev)

    def come(self, half, k, j):
        if (half, k, j) not in self.seen:
            self.seen.add((half, k, j))
            self.copy(half, k, j).wait_recv()

    def keep(self, half):
        return pltpu.make_async_copy(self.own.at[half], self.spot(0, half), self.here.at[half])

    def start(self):
        for k in range(self.levels):
            for half in range(2):
                self.copy(half, k, 0).start()
        for half in range(2):
            self.keep(half).start()

    def forward(self):
        for k in range(1, self.levels):
            for half in range(2):
                for j in range(1, 1 << k):
                    top = j.bit_length() - 1
                    self.come(half, top, j - (1 << top))
                    self.copy(half, k, j).start()

    def finish(self):
        for half in range(2):
            for k in range(self.levels):
                for j in range(1 << k):
                    self.come(half, k, j)
                    self.copy(half, k, j).wait_send()
            self.keep(half).wait()


def quad_gather_scratch(mp, rows, cols):
    dma = pltpu.SemaphoreType.DMA
    return [pltpu.VMEM((2, rows, cols), BF), dma((2, mp - 1)), dma((2, mp - 1)), dma((2,))]


class LineGather:
    def __init__(self, at, pieces, shard, spot, sems):
        self.at, self.pieces, self.shard, self.spot = at, pieces, shard, spot
        self.d_s, self.d_r, self.u_s, self.u_r, self.c_s, self.c_r, self.here = sems

    def down_copy(self, h, i, own=False):
        b = 2 * (self.at.p + h) + self.at.c
        dst = self.spot(b, i)
        src = self.shard(i) if own and self.shard else dst
        return remote(src, dst, self.d_s.at[h, i], self.d_r.at[h, i], self.at.below)

    def up_copy(self, h, i, own=False):
        b = 2 * (self.at.p - h) + self.at.c
        dst = self.spot(b, i)
        src = self.shard(i) if own and self.shard else dst
        return remote(src, dst, self.u_s.at[h, i], self.u_r.at[h, i], self.at.above)

    def core_copy(self, z, i, own=False, incoming=False):
        b = 2 * z + (1 - self.at.c if incoming else self.at.c)
        dst = self.spot(b, i)
        src = self.shard(i) if own and self.shard else dst
        return remote(src, dst, self.c_s.at[z, i], self.c_r.at[z, i], self.at.core)

    def keep(self, i):
        at = self.at
        return pltpu.make_async_copy(self.shard(i), self.spot(at.dp, i), self.here.at[i])

    def start(self):
        at = self.at
        for i in range(self.pieces):

            @pl.when(at.has_below)
            def _():
                self.down_copy(0, i, True).start()

            @pl.when(at.has_above)
            def _():
                self.up_copy(0, i, True).start()

        for i in range(self.pieces):
            self.core_copy(at.p, i, True).start()
            if self.shard:
                self.keep(i).start()

    def slot(self, h, i):
        at = self.at
        n, p = at.n, at.p

        @pl.when(p + h < n)
        def _():
            self.down_copy(h - 1, i).wait_recv()

            @pl.when(at.has_below)
            def _():
                self.down_copy(h, i).start()

            self.core_copy(p + h, i).start()

        @pl.when(p - h >= 0)
        def _():
            self.up_copy(h - 1, i).wait_recv()

            @pl.when(at.has_above)
            def _():
                self.up_copy(h, i).start()

            self.core_copy(p - h, i).start()

    def stage(self, h):
        @pl.loop(0, self.pieces)
        def _(i):
            self.slot(h, i)

    def ready(self, z, i):
        self.core_copy(z, i, incoming=True).wait_recv()

    def drain(self):
        at = self.at
        n, p = at.n, at.p

        @pl.loop(0, self.pieces)
        def _(i):
            for h in range(n):

                @pl.when((p + h < n) & at.has_below)
                def _():
                    self.down_copy(h, i, h == 0).wait_send()

                @pl.when((p - h >= 0) & at.has_above)
                def _():
                    self.up_copy(h, i, h == 0).wait_send()

            for z in range(n):
                self.core_copy(z, i).wait_send()


def line_gather_scratch(n, pieces):
    dma = pltpu.SemaphoreType.DMA
    return [dma((n, pieces))] * 6 + [dma((pieces,))]


def rows_spot(out, rows, width):
    def spot(b, i):
        rs = pl.ds(pl.multiple_of(b * rows, rows), rows)
        return out.at[rs, pl.ds(pl.multiple_of(i * width, width), width)]

    return spot


def cols_of(ref, width, base=0):
    return lambda i: ref.at[:, pl.ds(pl.multiple_of(base + i * width, width), width)]


def attend_rows(qkv, out, seq, hh, count, head):
    cols = lambda first: pl.ds(pl.multiple_of(first + head * HD, HD), HD)
    blk = 256
    for i in range(seq // blk):
        rows = pl.ds(i * blk, blk)
        span = (i + 1) * blk
        lg = logistic_block(qkv[rows, cols(0)], qkv[pl.ds(0, span), cols(hh)], seq)
        w = jnp.where(allowed_block(i * blk, blk, 0, span, count), lg, 0.0).astype(BF)
        out[rows, cols(0)] = dot(w, qkv[pl.ds(0, span), cols(2 * hh)]).astype(BF)


def attn_kernel(
    n_dp,
    n_mp,
    count_ref,
    gains_in,
    wq_hbm,
    wk_hbm,
    wv_hbm,
    wo_hbm,
    wg_hbm,
    wu_hbm,
    wd_hbm,
    x_hbm,
    cot_hbm,
    aw_ref,
    qkv_ref,
    att_ref,
    nin_ref,
    gains_ref,
    gush_ref,
    dnsh_ref,
    cotm_ref,
    w4,
    wo,
    shard,
    x,
    qkv,
    wbuf,
    wgu,
    wd,
    gush,
    dnsh,
    cot,
    load_s,
    wb_s,
    out_s,
    *rest,
):
    at = Place(n_dp, n_mp)
    n = at.n
    chunk, hh = wq_hbm.shape
    seq, d = x.shape
    ff = wgu.shape[2]
    loads = [
        pltpu.make_async_copy(src, dst, load_s.at[i])
        for i, (src, dst) in enumerate(
            [
                (wq_hbm, w4.at[0]),
                (wk_hbm, w4.at[1]),
                (wv_hbm, w4.at[2]),
                (wo_hbm, wo),
                (x_hbm, x),
                (wg_hbm, wgu.at[0]),
                (wu_hbm, wgu.at[1]),
                (wd_hbm, wd),
                (cot_hbm, cot),
            ]
        )
    ]
    for cp in loads:
        cp.start()
    spot = rows_spot(aw_ref, chunk, hh)
    three = LineGather(at, 3, cols_of(shard, hh), spot, rest[0:7])
    last = LineGather(
        at, 1, lambda i: shard.at[:, pl.ds(3 * hh, hh)], lambda b, i: spot(b, 3), rest[7:14]
    )
    small = LineGather(
        at,
        1,
        lambda i: gains_in,
        lambda b, i: gains_ref.at[:, pl.ds(pl.multiple_of(b * chunk, chunk), chunk)],
        rest[14:21],
    )
    enter(at)
    small.start()
    for i in range(3):
        loads[i].wait()
        shard[:, i * hh : (i + 1) * hh] = w4[i].astype(BF)
    three.start()
    loads[3].wait()
    shard[:, 3 * hh :] = wo[...].T.astype(BF)
    small.slot(1, 0)
    loads[5].wait()
    loads[6].wait()
    half = ff // PIECES

    @pl.loop(0, PIECES)
    def _(i):
        cols = pl.ds(pl.multiple_of(i * half, half), half)
        for k in range(2):
            to = pl.ds(pl.multiple_of((2 * i + k) * half, half), half)
            gush[:, to] = wgu[k, :, cols].astype(BF)

    outs = [pltpu.make_async_copy(gush, gush_ref, out_s.at[0])]
    outs[0].start()
    for h in range(2, n):
        small.slot(h, 0)
    small.keep(0).wait()
    for z in range(n):
        small.ready(z, 0)
    loads[4].wait()

    @pl.loop(0, seq // 32)
    def _(b):
        rs = pl.ds(pl.multiple_of(b * 32, 32), 32)
        v = x[rs, :].astype(F32)
        scale = lax.rsqrt(jnp.mean(v * v, axis=1, keepdims=True) + EPS)
        x[rs, :] = (v * scale * gains_ref[0:1, :]).astype(BF)

    outs.append(pltpu.make_async_copy(x, nin_ref, out_s.at[1]))
    outs[1].start()
    three.stage(1)
    loads[7].wait()

    @pl.loop(0, ff // 256)
    def _(i):
        rs = pl.ds(pl.multiple_of(i * 256, 256), 256)
        dnsh[:, rs] = wd[rs, :].T.astype(BF)

    outs.append(pltpu.make_async_copy(dnsh, dnsh_ref, out_s.at[2]))
    outs[2].start()
    loads[8].wait()
    count = count_ref[0]

    @pl.loop(0, seq // 32)
    def _(b):
        rs = pl.ds(pl.multiple_of(b * 32, 32), 32)
        row = b * 32 + lax.broadcasted_iota(jnp.int32, (32, d), 0)
        cot[rs, :] = jnp.where(row < count, cot[rs, :].astype(F32), 0.0).astype(BF)

    outs.append(pltpu.make_async_copy(cot, cotm_ref, out_s.at[3]))
    outs[3].start()
    for h in range(2, n - 1):
        three.stage(h)
    last.start()

    def w_copy(i):
        cols = pl.ds(pl.multiple_of(i * hh, hh), hh)
        return pltpu.make_async_copy(aw_ref.at[:, cols], wbuf.at[i], wb_s.at[i])

    for i in range(3):
        three.slot(n - 1, i)
        three.keep(i).wait()
        for z in range(n):
            three.ready(z, i)
        w_copy(i).start()
        if i == 1:
            last.slot(1, 0)
        w_copy(i).wait()

        @pl.loop(0, seq // 256)
        def _(b):
            rs = pl.ds(pl.multiple_of(b * 256, 256), 256)
            qkv[rs, i * hh : (i + 1) * hh] = dot(x[rs, :], wbuf[i]).astype(BF)

    outs.append(pltpu.make_async_copy(qkv, qkv_ref, out_s.at[4]))
    outs[4].start()
    for h in range(2, n - 1):
        last.slot(h, 0)
    heads = hh // HD

    @pl.loop(0, heads // 2)
    def _(head):
        attend_rows(qkv, att_ref, seq, hh, count, head)

    last.slot(n - 1, 0)

    @pl.loop(heads // 2, heads)
    def _(head):
        attend_rows(qkv, att_ref, seq, hh, count, head)

    last.keep(0).wait()
    for z in range(n):
        last.ready(z, 0)
    for cp in outs:
        cp.wait()
    small.drain()
    three.drain()
    last.drain()


def attn_stage(n_dp, n_mp, counts, gains, wq, wk, wv, wo, wg, wu, wd, x, cot):
    seq, d = x.shape
    chunk, hh = wq.shape
    ff = wg.shape[1]
    n = n_dp // 2
    dma = pltpu.SemaphoreType.DMA
    hbm = pl.BlockSpec(memory_space=pl.ANY)
    vm = pl.BlockSpec(memory_space=pltpu.VMEM)
    shapes = [
        ((d, 4 * hh), BF),
        ((seq, 3 * hh), BF),
        ((seq, hh), BF),
        ((seq, d), BF),
        ((8, d), F32),
        ((chunk, 2 * ff), BF),
        ((chunk, ff), BF),
        ((seq, d), BF),
    ]
    return pl.pallas_call(
        functools.partial(attn_kernel, n_dp, n_mp),
        out_shape=[jax.ShapeDtypeStruct(*s) for s in shapes],
        in_specs=[pl.BlockSpec(memory_space=pltpu.SMEM), vm] + [hbm] * 9,
        out_specs=[hbm, hbm, vm, hbm, vm, hbm, hbm, hbm],
        scratch_shapes=[
            pltpu.VMEM((3, chunk, hh), F32),
            pltpu.VMEM((hh, chunk), F32),
            pltpu.VMEM((chunk, 4 * hh), BF),
            pltpu.VMEM((seq, d), BF),
            pltpu.VMEM((seq, 3 * hh), BF),
            pltpu.VMEM((3, d, hh), BF),
            pltpu.VMEM((2, chunk, ff), F32),
            pltpu.VMEM((ff, chunk), F32),
            pltpu.VMEM((chunk, 2 * ff), BF),
            pltpu.VMEM((chunk, ff), BF),
            pltpu.VMEM((seq, d), BF),
            dma((9,)),
            dma((3,)),
            dma((5,)),
        ]
        + line_gather_scratch(n, 3)
        + line_gather_scratch(n, 1) * 2,
        compiler_params=pltpu.CompilerParams(
            collective_id=1, has_side_effects=True, vmem_limit_bytes=VMEM_LIMIT
        ),
        name="attn_stage",
    )(counts, gains, wq, wk, wv, wo, wg, wu, wd, x, cot)


def gate_kernel(
    n_dp,
    n_mp,
    att_ref,
    aw_hbm,
    sh_hbm,
    x_hbm,
    gain_ref,
    gw_ref,
    nm_ref,
    hid_ref,
    gu_ref,
    inner_ref,
    wo,
    sh,
    xs,
    nm,
    wbuf,
    gbuf,
    ibuf,
    load_s,
    wb_s,
    gb_s,
    ib_s,
    *rest,
):
    at = Place(n_dp, n_mp)
    n = at.n
    quad = QuadSum(at, *rest[0:2], rest[2:4])
    gather_nm = QuadGather(at, rest[4], nm_ref, rest[5:8])
    sems = rest[8:15]
    hh = wo.shape[1]
    part, half_cols = quad.t.shape[2], quad.t.shape[3]
    chunk, wide = sh_hbm.shape
    pieces = sems[6].shape[0]
    width = wide // pieces
    line = LineGather(at, pieces, cols_of(sh, width), rows_spot(gw_ref, chunk, width), sems)

    load_sh = pltpu.make_async_copy(sh_hbm, sh, load_s.at[2])
    load_sh.start()
    load = pltpu.make_async_copy(aw_hbm.at[:, pl.ds(3 * hh, hh)], wo, load_s.at[0])
    load.start()
    load_x = pltpu.make_async_copy(x_hbm.at[part_rows(at, part), :], xs, load_s.at[1])
    load_x.start()
    enter(at)
    load_sh.wait()
    line.start()
    load.wait()

    def terms(q):
        rs = pl.ds(pl.multiple_of(q * part, part), part)
        for half in range(2):
            w = wo[half * half_cols : (half + 1) * half_cols, :]
            quad.t[half, q] = dot(att_ref[rs, :], w, NT).astype(BF)

    for mask in quad.masks():
        terms(at.quarter(mask))
        quad.offer(mask)
    quad.turn()
    quad.arrive()
    load_x.wait()

    @pl.loop(0, part // 32)
    def _(b):
        rs = pl.ds(pl.multiple_of(b * 32, 32), 32)
        h = xs[rs, :].astype(F32) + jnp.concatenate(
            [quad.total(0, rs), quad.total(1, rs)], axis=1
        )
        hid_ref[rs, :] = h
        scale = lax.rsqrt(jnp.mean(h * h, axis=1, keepdims=True) + EPS)
        res = (h * scale * gain_ref[1:2, :]).astype(BF)
        gather_nm.own[0, rs, :] = res[:, :half_cols]
        gather_nm.own[1, rs, :] = res[:, half_cols:]

    gather_nm.start()
    line.stage(1)
    gather_nm.forward()
    gather_nm.finish()
    load = pltpu.make_async_copy(nm_ref, nm, load_s.at[0])
    load.start()
    for h in range(2, n - 1):
        line.stage(h)
    load.wait()

    def w_copy(i, slot):
        cols = pl.ds(pl.multiple_of(i * width, width), width)
        return pltpu.make_async_copy(gw_ref.at[:, cols], wbuf.at[slot], wb_s.at[slot])

    def g_copy(i, slot):
        cols = pl.ds(pl.multiple_of(i * width, width), width)
        return pltpu.make_async_copy(gbuf.at[slot], gu_ref.at[:, cols], gb_s.at[slot])

    def i_copy(i, slot):
        cols = pl.ds(pl.multiple_of(i * (width // 2), width // 2), width // 2)
        return pltpu.make_async_copy(ibuf.at[slot], inner_ref.at[:, cols], ib_s.at[slot])

    @pl.loop(0, pieces)
    def _(i):
        slot = lax.rem(i, 2)
        line.slot(n - 1, i)
        line.keep(i).wait()
        for z in range(n):
            line.ready(z, i)
        w_copy(i, slot).start()

        @pl.when(i >= 2)
        def _():
            g_copy(i - 2, slot).wait()
            i_copy(i - 2, slot).wait()

        w_copy(i, slot).wait()

        @pl.loop(0, nm.shape[0] // 256)
        def _(b):
            rs = pl.ds(pl.multiple_of(b * 256, 256), 256)
            v = dot(nm[rs, :], wbuf[slot]).astype(BF)
            gbuf[slot, rs, :] = v
            g = v[:, : width // 2].astype(F32)
            u = v[:, width // 2 :].astype(F32)
            ibuf[slot, rs, :] = (g / (1.0 + jnp.exp(-g)) * u).astype(BF)

        g_copy(i, slot).start()
        i_copy(i, slot).start()

    for i in range(max(0, pieces - 2), pieces):
        g_copy(i, i % 2).wait()
        i_copy(i, i % 2).wait()
    line.drain()
    quad.drain()


def gate_stage(n_dp, n_mp, att, aw, shard, x, gain):
    seq, hh = att.shape
    d = aw.shape[0]
    chunk, wide = shard.shape
    n, part = n_dp // 2, seq // n_mp
    dma = pltpu.SemaphoreType.DMA
    hbm = pl.BlockSpec(memory_space=pl.ANY)
    vm = pl.BlockSpec(memory_space=pltpu.VMEM)
    width = wide // PIECES
    return pl.pallas_call(
        functools.partial(gate_kernel, n_dp, n_mp),
        out_shape=[
            jax.ShapeDtypeStruct((d, wide), BF),
            jax.ShapeDtypeStruct((seq, d), BF),
            jax.ShapeDtypeStruct((part, d), F32),
            jax.ShapeDtypeStruct((seq, wide), BF),
            jax.ShapeDtypeStruct((seq, wide // 2), BF),
        ],
        in_specs=[vm, hbm, hbm, hbm, vm],
        out_specs=[hbm, hbm, vm, hbm, hbm],
        scratch_shapes=[
            pltpu.VMEM((d, hh), BF),
            pltpu.VMEM((chunk, wide), BF),
            pltpu.VMEM((part, d), BF),
            pltpu.VMEM((seq, d), BF),
            pltpu.VMEM((2, d, width), BF),
            pltpu.VMEM((2, seq, width), BF),
            pltpu.VMEM((2, seq, width // 2), BF),
            dma((3,)),
            dma((2,)),
            dma((2,)),
            dma((2,)),
        ]
        + quad_sum_scratch(n_mp, part, d // 2)
        + quad_gather_scratch(n_mp, part, d // 2)
        + line_gather_scratch(n, PIECES),
        compiler_params=pltpu.CompilerParams(
            collective_id=2, has_side_effects=True, vmem_limit_bytes=VMEM_LIMIT
        ),
        name="gate_stage",
    )(att, aw, shard, x, gain)


def down_kernel(
    n_dp,
    n_mp,
    inner_hbm,
    gu_hbm,
    cot_hbm,
    sh_hbm,
    rs_ref,
    ft_ref,
    ggu_ref,
    inner,
    gu,
    cot,
    dn,
    acc,
    ftb,
    load_s,
    ft_s,
    dn_s,
    gg_s,
    *rest,
):
    at = Place(n_dp, n_mp)
    n, p = at.n, at.p
    line = LineSum(at, *rest[0:4], rest[4:10])
    sems = rest[10:17]
    chunk, ff = sh_hbm.shape
    pieces = sems[6].shape[0]
    width = ff // pieces
    gather = LineGather(at, pieces, None, rows_spot(dn, chunk, width), sems)
    pair = 2 * chunk
    loads = [
        pltpu.make_async_copy(src, dst, load_s.at[i])
        for i, (src, dst) in enumerate([(cot_hbm, cot), (inner_hbm, inner), (gu_hbm, gu)])
    ]
    own = pltpu.make_async_copy(
        sh_hbm, dn.at[pl.ds(pl.multiple_of(at.dp * chunk, chunk), chunk), :], dn_s.at[0]
    )
    own.start()
    for cp in loads:
        cp.start()
    enter(at)
    own.wait()
    gather.start()
    loads[0].wait()
    loads[1].wait()

    def run(e):
        k, core = e // 2, e % 2
        block = 2 * order_of(k, at) + (1 - at.c if core == 0 else at.c)
        lhs = cot[:, pl.ds(pl.multiple_of(block * chunk, chunk), chunk)].T

        def tile(i):
            return dot(lhs, inner[:, pl.ds(pl.multiple_of(i * width, width), width)])

        if core == 0:
            line.other(k, tile)
        else:
            line.mine(k, tile)

    for e in range(2 * n):
        run(e)

    def ft_copy(z, slot):
        cols = pl.ds(pl.multiple_of(z * pair, pair), pair)
        return pltpu.make_async_copy(ftb.at[slot], ft_ref.at[:, cols], ft_s.at[slot])

    def rows_of(z):
        return pl.ds(pl.multiple_of(z * pair, pair), pair)

    def grads(z, fresh):
        @pl.loop(0, pieces)
        def _(i):
            gather.ready(z, i)

        @pl.loop(0, ff // 512)
        def _(i):
            cols = pl.ds(pl.multiple_of(i * 512, 512), 512)
            v = dot(cot[:, rows_of(z)], dn[rows_of(z), cols])
            acc[:, cols] = v if fresh else acc[:, cols] + v

    def branch(z, fresh):
        if not fresh:
            ft_copy(z, 0).wait()
        ftb[0] = dot(inner[...], dn[rows_of(z), :], NT).astype(BF)
        ft_copy(z, 0).start()

    grads(p, True)
    branch(p, True)
    loads[2].wait()
    half = width

    def cols_at(i):
        g = pl.ds(pl.multiple_of(i * 2 * half, half), half)
        u = pl.ds(pl.multiple_of(i * 2 * half + half, half), half)
        return g, u, pl.ds(pl.multiple_of(i * half, half), half)

    @pl.loop(0, pieces)
    def _(i):
        gcols, ucols, _ = cols_at(i)

        @pl.loop(0, gu.shape[0] // 64)
        def _(b):
            rs = pl.ds(pl.multiple_of(b * 64, 64), 64)
            g = gu[rs, gcols].astype(F32)
            u = gu[rs, ucols].astype(F32)
            sg = 1.0 / (1.0 + jnp.exp(-g))
            gu[rs, gcols] = (u * sg * (1.0 + g * (1.0 - sg))).astype(BF)
            gu[rs, ucols] = (g * sg).astype(BF)

    @pl.loop(1, n - 1)
    def _(h):
        gather.stage(h)

        @pl.when(p + h < n)
        def _():
            grads(p + h, False)
            branch(p + h, False)

        @pl.when(p - h >= 0)
        def _():
            grads(p - h, False)
            branch(p - h, False)

        line.slot(h - 1)

    gather.stage(n - 1)

    @pl.when(jnp.logical_not(at.has_below))
    def _():
        grads(n - 1, False)

    @pl.when(jnp.logical_not(at.has_above))
    def _():
        grads(0, False)

    def gg_copy(i):
        cols = pl.ds(pl.multiple_of(i * 2 * half, 2 * half), 2 * half)
        return pltpu.make_async_copy(gu.at[:, cols], ggu_ref.at[:, cols], gg_s.at[i])

    @pl.loop(0, pieces)
    def _(i):
        gcols, ucols, acols = cols_at(i)

        @pl.loop(0, gu.shape[0] // 64)
        def _(b):
            rs = pl.ds(pl.multiple_of(b * 64, 64), 64)
            gi = acc[rs, acols]
            gu[rs, gcols] = (gi * gu[rs, gcols].astype(F32)).astype(BF)
            gu[rs, ucols] = (gi * gu[rs, ucols].astype(F32)).astype(BF)

        gg_copy(i).start()

    @pl.when(jnp.logical_not(at.has_below))
    def _():
        branch(n - 1, False)

    @pl.when(jnp.logical_not(at.has_above))
    def _():
        branch(0, False)

    line.final(rs_ref)
    for i in range(pieces):
        gg_copy(i).wait()
    ft_copy(p, 0).wait()
    line.drain()
    gather.drain()


def down_stage(n_dp, n_mp, inner, gu, cot, shard):
    seq, d = cot.shape
    chunk, ff = shard.shape
    n = n_dp // 2
    dma = pltpu.SemaphoreType.DMA
    hbm = pl.BlockSpec(memory_space=pl.ANY)
    vm = pl.BlockSpec(memory_space=pltpu.VMEM)
    return pl.pallas_call(
        functools.partial(down_kernel, n_dp, n_mp),
        out_shape=[
            jax.ShapeDtypeStruct((PIECES, chunk, ff // PIECES), BF),
            jax.ShapeDtypeStruct((seq, d), BF),
            jax.ShapeDtypeStruct((seq, 2 * ff), BF),
        ],
        in_specs=[hbm] * 4,
        out_specs=[vm, hbm, hbm],
        scratch_shapes=[
            pltpu.VMEM((seq, ff), BF),
            pltpu.VMEM((seq, 2 * ff), BF),
            pltpu.VMEM((seq, d), BF),
            pltpu.VMEM((d, ff), BF),
            pltpu.VMEM((seq, ff), F32),
            pltpu.VMEM((1, seq, 2 * chunk), BF),
            dma((3,)),
            dma((1,)),
            dma((1,)),
            dma((PIECES,)),
        ]
        + line_sum_scratch(n, PIECES, chunk, ff // PIECES)
        + line_gather_scratch(n, PIECES),
        compiler_params=pltpu.CompilerParams(
            collective_id=3, has_side_effects=True, vmem_limit_bytes=VMEM_LIMIT
        ),
        name="down_stage",
    )(inner, gu, cot, shard)


def mid_kernel(
    n_dp,
    n_mp,
    ggu_hbm,
    gw_hbm,
    nm_hbm,
    ft_hbm,
    cot_hbm,
    qkv_hbm,
    aw_hbm,
    count_ref,
    hid_ref,
    gain_ref,
    rs_ref,
    low_ref,
    lay_ref,
    gh_ref,
    gg_ref,
    dq_ref,
    space,
    wt,
    wt_s,
    nm,
    nm_s,
    cot,
    dka,
    dva,
    load_s,
    *rest,
):
    at = Place(n_dp, n_mp)
    n = at.n
    line = LineSum(at, *rest[0:4], rest[4:10])
    mid = QuadSum(at, *rest[10:12], rest[12:14])
    lay = QuadSumHbm(at, ft_hbm, *rest[14:16], rest[16:19])
    gather_low = QuadGather(at, rest[19], low_ref, rest[20:23])
    gather_lay = QuadGather(at, rest[23], lay_ref, rest[24:27])
    part, half_cols = mid.t.shape[2], mid.t.shape[3]
    chunk, width = line.own.shape[2], line.own.shape[3]
    pieces = line.pieces
    hh = qkv_hbm.shape[1] // 3
    drows = wt.shape[1]
    tiles = half_cols // drows

    wide = ggu_hbm.shape[1]
    ggu = space.at[:, pl.ds(0, wide)]
    load = pltpu.make_async_copy(ggu_hbm, ggu, load_s.at[0])
    load.start()
    load_cot = pltpu.make_async_copy(cot_hbm.at[part_rows(at, part), :], cot, load_s.at[1])
    load_cot.start()

    def nm_copy(e):
        k, core = e // 2, e % 2
        block = 2 * order_of(k, at) + (1 - at.c if core == 0 else at.c)
        cols = pl.ds(pl.multiple_of(block * chunk, chunk), chunk)
        return pltpu.make_async_copy(nm_hbm.at[:, cols], nm.at[e % 2], nm_s.at[e % 2])

    def wt_copy(half, i, slot):
        rows = pl.ds(pl.multiple_of(half * half_cols + i * drows, drows), drows)
        return pltpu.make_async_copy(gw_hbm.at[rows, :], wt.at[slot], wt_s.at[slot])

    nm_copy(0).start()
    wt_copy(0, 0, 0).start()
    for cp in lay.loads:
        cp.start()
    enter(at)
    for mask in lay.masks():
        lay.offer(mask)
    load.wait()

    def run(e):
        if e + 1 < 2 * n:
            nm_copy(e + 1).start()
        nm_copy(e).wait()
        lhs = nm[e % 2].T

        def tile(i):
            return dot(lhs, ggu[:, pl.ds(pl.multiple_of(i * width, width), width)])

        if e % 2 == 0:
            line.other(e // 2, tile)
        else:
            line.mine(e // 2, tile)

    def terms(half):
        @pl.loop(0, tiles)
        def _(i):
            slot = lax.rem(i, 2)
            if half == 0:
                nxt = wt_copy(jnp.where(i + 1 < tiles, 0, 1), lax.rem(i + 1, tiles), 1 - slot)
                nxt.start()
            else:

                @pl.when(i + 1 < tiles)
                def _():
                    wt_copy(1, i + 1, 1 - slot).start()

            wt_copy(half, i, slot).wait()
            v = dot(ggu[...], wt[slot], NT).astype(BF)
            cols = pl.ds(pl.multiple_of(i * drows, drows), drows)
            for q in range(n_mp):
                mid.t[half, q, :, cols] = v[q * part : (q + 1) * part]

        for mask in mid.masks():
            mid.offer(mask, (half,))

    run(0)
    run(1)
    terms(0)
    run(2)
    run(3)
    for cp in lay.loads:
        cp.wait()
    lay.turn()
    terms(1)
    for e in range(4, 2 * n):
        run(e)
    lay.arrive()

    @pl.loop(0, part // 32)
    def _(b):
        rs = pl.ds(pl.multiple_of(b * 32, 32), 32)
        for half in range(2):
            h = hid_ref[rs, pl.ds(half * half_cols, half_cols)]
            gather_lay.own[half, rs, :] = (h + lay.total(half, rs)).astype(BF)

    line.slot(0)
    per = half_cols // hh
    blocks_d = 2 * half_cols // part
    wo_spot = [(e // per // (n_mp // 2), e // per % (n_mp // 2), e % per) for e in range(blocks_d)]
    wo_parts = [
        pltpu.make_async_copy(
            aw_hbm.at[pl.ds(e * part, part), pl.ds(3 * hh, hh)],
            lay.t.at[i, j, :, pl.ds(k * hh, hh)],
            load_s.at[4 + e],
        )
        for e, (i, j, k) in enumerate(wo_spot)
    ]
    for cp in wo_parts:
        cp.start()
    load_qkv = pltpu.make_async_copy(
        qkv_hbm, space.at[:, pl.ds(2 * half_cols, 3 * hh)], load_s.at[2]
    )
    load_qkv.start()
    mid.turn()
    mid.arrive()
    load_cot.wait()
    gg_ref[...] = jnp.zeros_like(gg_ref)

    @pl.loop(0, part // 32)
    def _(b):
        rs = pl.ds(pl.multiple_of(b * 32, 32), 32)
        h = hid_ref[rs, :]
        scale = lax.rsqrt(jnp.mean(h * h, axis=1, keepdims=True) + EPS)
        g = jnp.concatenate([mid.total(0, rs), mid.total(1, rs)], axis=1)
        unit = h * scale
        weighted = g * gain_ref[1:2, :]
        field = scale * (weighted - unit * jnp.mean(weighted * unit, axis=1, keepdims=True))
        res = cot[rs, :].astype(F32) + field
        gh_ref[rs, :] = res
        low = res.astype(BF)
        gather_low.own[0, rs, :] = low[:, :half_cols]
        gather_low.own[1, rs, :] = low[:, half_cols:]
        gg_ref[...] += jnp.sum(g * unit, axis=0, keepdims=True)

    gather_low.start()
    for s in range(1, n - 2):
        line.slot(s)
    gather_low.forward()
    gather_lay.start()
    gather_low.finish()
    load_low = pltpu.make_async_copy(low_ref, space.at[:, pl.ds(0, 2 * half_cols)], load_s.at[3])
    load_low.start()
    load_low.wait()
    load_qkv.wait()
    for cp in wo_parts:
        cp.wait()
    seq = space.shape[0]
    base = 2 * half_cols
    gbase = base + 3 * hh

    @pl.loop(0, seq // 256)
    def _(b):
        rs = pl.ds(pl.multiple_of(b * 256, 256), 256)
        total = jnp.zeros((256, hh), F32)
        for e, (i, j, k) in enumerate(wo_spot):
            wo = lay.t[i, j, :, k * hh : (k + 1) * hh]
            total += dot(space[rs, e * part : (e + 1) * part], wo)
        space[rs, gbase : gbase + hh] = total.astype(BF)

    count = count_ref[0]
    blk = 256
    blocks = seq // blk

    @pl.loop(0, hh // HD)
    def _(head):
        at_cols = lambda first: pl.ds(pl.multiple_of(first + head * HD, HD), HD)
        for i in range(blocks - 1, -1, -1):
            rows = pl.ds(i * blk, blk)
            span = (i + 1) * blk
            keys = pl.ds(0, span)
            q = space[rows, at_cols(base)]
            g = space[rows, at_cols(gbase)]
            k = space[keys, at_cols(base + hh)]
            lg = jnp.where(
                allowed_block(i * blk, blk, 0, span, count), logistic_block(q, k, seq), 0.0
            )
            w = lg.astype(BF)
            gw = dot(g, space[keys, at_cols(base + 2 * hh)], NT)
            gs = (gw * lg * (1.0 - lg) * HD ** (-0.5)).astype(BF)
            wt[i // 2, :, at_cols((i % 2) * (wide // 2))] = dot(gs, k).astype(BF)
            dk = dot(gs, q, TN)
            dv = dot(w, g, TN)
            if i == blocks - 1:
                dka[...] = dk
                dva[...] = dv
            else:
                dka[keys, :] += dk
                dva[keys, :] += dv
        for i in range(blocks):
            rows = pl.ds(i * blk, blk)
            wt[i // 2, :, at_cols((i % 2) * (wide // 2) + hh)] = dka[rows, :].astype(BF)
            wt[i // 2, :, at_cols((i % 2) * (wide // 2) + 2 * hh)] = dva[rows, :].astype(BF)

    gather_lay.forward()
    stores = [
        pltpu.make_async_copy(
            wt.at[i // 2, :, pl.ds((i % 2) * (wide // 2), 3 * hh)],
            dq_ref.at[pl.ds(i * blk, blk), :],
            load_s.at[4 + i],
        )
        for i in range(blocks)
    ]
    for cp in stores:
        cp.start()
    line.final(rs_ref)
    gather_lay.finish()
    for cp in stores:
        cp.wait()
    line.drain()
    mid.drain()
    lay.drain()


def mid_stage(n_dp, n_mp, ggu, gw, nm, ft, cot, qkv, aw, counts, hid, gain):
    seq, wide = ggu.shape
    hh = qkv.shape[1] // 3
    d = gw.shape[0]
    n, part, chunk = n_dp // 2, seq // n_mp, d // n_dp
    dma = pltpu.SemaphoreType.DMA
    hbm = pl.BlockSpec(memory_space=pl.ANY)
    vm = pl.BlockSpec(memory_space=pltpu.VMEM)
    pieces = PIECES
    return pl.pallas_call(
        functools.partial(mid_kernel, n_dp, n_mp),
        out_shape=[
            jax.ShapeDtypeStruct((pieces, chunk, wide // pieces), BF),
            jax.ShapeDtypeStruct((seq, d), BF),
            jax.ShapeDtypeStruct((seq, d), BF),
            jax.ShapeDtypeStruct((part, d), F32),
            jax.ShapeDtypeStruct((1, d), F32),
            jax.ShapeDtypeStruct((seq, 3 * hh), BF),
        ],
        in_specs=[hbm] * 7 + [pl.BlockSpec(memory_space=pltpu.SMEM)] + [vm] * 2,
        out_specs=[vm, hbm, hbm, vm, vm, hbm],
        scratch_shapes=[
            pltpu.VMEM((seq, max(wide, d + 4 * hh)), BF),
            pltpu.VMEM((2, 256, wide), BF),
            dma((2,)),
            pltpu.VMEM((2, seq, chunk), BF),
            dma((2,)),
            pltpu.VMEM((part, d), BF),
            pltpu.VMEM((seq, HD), F32),
            pltpu.VMEM((seq, HD), F32),
            dma((4 + max(d // part, seq // 256),)),
        ]
        + line_sum_scratch(n, pieces, chunk, wide // pieces, 1)
        + quad_sum_scratch(n_mp, part, d // 2)
        + quad_sum_scratch(n_mp, part, d // 2, n_mp // 2)
        + [dma((2, n_mp // 2))]
        + quad_gather_scratch(n_mp, part, d // 2) * 2,
        compiler_params=pltpu.CompilerParams(
            collective_id=4, has_side_effects=True, vmem_limit_bytes=VMEM_LIMIT
        ),
        name="mid_stage",
    )(ggu, gw, nm, ft, cot, qkv, aw, counts, hid, gain)


def last_kernel(
    n_dp,
    n_mp,
    dqkv_hbm,
    aw_hbm,
    nin_hbm,
    low_hbm,
    att_hbm,
    x_hbm,
    gh_ref,
    gain_ref,
    gmid_ref,
    rs_ref,
    grad_ref,
    gains_ref,
    rhs,
    aw,
    nin,
    low,
    lhs,
    x,
    loads,
    pout,
    own,
    din,
    uin,
    po_s,
    po_r,
    d_s,
    d_r,
    u_s,
    u_r,
    t,
    r,
    q1,
    q2,
    gown,
    g1,
    g2,
    g3,
    gsum,
    fold_out,
    fold_in,
    fold_s,
    fold_r,
):
    at = Place(n_dp, n_mp)
    hh = att_hbm.shape[1]
    part = t.shape[2]
    chunk = own.shape[2]
    half_cols = t.shape[3]
    copies = [
        pltpu.make_async_copy(src, dst, loads.at[i])
        for i, (src, dst) in enumerate(
            [
                (dqkv_hbm, rhs.at[:, pl.ds(0, 3 * hh)]),
                (aw_hbm.at[:, pl.ds(0, 3 * hh)], aw),
                (nin_hbm, nin),
                (att_hbm, rhs.at[:, pl.ds(3 * hh, hh)]),
                (low_hbm, low),
                (x_hbm.at[part_rows(at, part), :], x),
            ]
        )
    ]
    for cp in copies:
        cp.start()
    bits = [b for b in (2, 4, 8, 16) if b < n_dp]
    enter(at, [at.fold(b) for b in bits[1:]])
    quad = QuadSum(at, t, r, (q1, q2))
    line = LineSum(at, pout, own, din, uin, (po_s, po_r, d_s, d_r, u_s, u_r), True)
    gather = QuadGather(at, gown, grad_ref, (g1, g2, g3))
    copies[0].wait()
    copies[1].wait()

    d = aw.shape[0]
    fold = fold_out.shape[2]
    per_row = d // fold

    def terms(q):
        rs = pl.ds(pl.multiple_of(q * part, part), part)
        width = 512

        @pl.loop(0, half_cols // width)
        def _(i):
            for half in range(2):
                d0 = pl.multiple_of(half * half_cols + i * width, width)
                v = dot(rhs[rs, 0 : 3 * hh], aw[pl.ds(d0, width), :], NT)
                t[half, q, :, pl.ds(pl.multiple_of(i * width, width), width)] = v.astype(BF)
                u = v * nin[rs, pl.ds(d0, width)].astype(F32)
                gsum[0:1, pl.ds(d0, width)] += jnp.sum(u, axis=0, keepdims=True)

    gsum[...] = jnp.zeros_like(gsum)
    copies[2].wait()
    masks = quad.masks()
    terms(at.quarter(masks[0]))
    quad.offer(masks[0])
    for cp in copies[3:5]:
        cp.wait()
    load_x = copies[5]

    def run(k, core):
        block = 2 * order_of(k, at) + (at.c if core else 1 - at.c)
        cols = pl.ds(pl.multiple_of(block * chunk, chunk), chunk)
        lhs[0] = nin[:, cols].T
        lhs[1] = low[:, cols].T

        def tile(i):
            return dot(lhs[lax.div(i, 3)], rhs[:, pl.ds(pl.multiple_of(i * hh, hh), hh)])

        if core:
            line.mine(k, tile)
        else:
            line.other(k, tile)

    n = at.n
    devs = [at.core] + [at.fold(b) for b in bits] + [at.peer(b) for b in at.bits]

    def fold_copy(b):
        return remote(fold_out.at[b], fold_in.at[b], fold_s.at[b], fold_r.at[b], devs[b])

    def fold_next(b):
        fold_copy(b).wait_recv()
        fold_out[b + 1] = fold_out[b] + fold_in[b]
        if b + 1 < len(devs):
            fold_copy(b + 1).start()

    run(0, 0)
    run(0, 1)
    for mask in masks[1:]:
        terms(at.quarter(mask))
        quad.offer(mask)
    gsum[0:1, :] = gsum[0:1, :] / gain_ref[0:1, :]
    gsum[1:2, :] = gmid_ref[...]
    for i in range(2):
        for j in range(per_row):
            fold_out[0, i * per_row + j] = gsum[i, j * fold : (j + 1) * fold]
    fold_copy(0).start()
    run(1, 0)
    run(1, 1)
    fold_next(0)
    for k in range(2, n):
        run(k, 0)
        run(k, 1)
    quad.turn()
    for b in range(1, len(bits)):
        fold_next(b)
    line.slot(0)
    quad.arrive()
    load_x.wait()
    fold_next(len(bits))
    @pl.loop(0, part // 32)
    def _(b):
        rs = pl.ds(pl.multiple_of(b * 32, 32), 32)
        v = x[rs, :].astype(F32)
        scale = lax.rsqrt(jnp.mean(v * v, axis=1, keepdims=True) + EPS)
        g = jnp.concatenate([quad.total(0, rs), quad.total(1, rs)], axis=1)
        unit = v * scale
        weighted = g * gain_ref[0:1, :]
        field = scale * (weighted - unit * jnp.mean(weighted * unit, axis=1, keepdims=True))
        res = (gh_ref[rs, :] + field).astype(BF)
        gown[0, rs, :] = res[:, :half_cols]
        gown[1, rs, :] = res[:, half_cols:]

    for b in range(len(bits) + 1, len(devs) - 1):
        fold_next(b)
    gather.start()
    for s in range(1, n - 2):
        line.slot(s)
    fold_next(len(devs) - 1)
    gather.forward()
    for i in range(2):
        for j in range(per_row):
            gsum[i, j * fold : (j + 1) * fold] = fold_out[len(devs), i * per_row + j]
    gains_ref[...] = gsum[:, pl.ds(pl.multiple_of(at.dp * chunk, chunk), chunk)]
    line.final(rs_ref)
    gather.finish()
    line.drain()
    quad.drain()
    for b in range(len(devs)):
        fold_copy(b).wait_send()


def last_stage(n_dp, n_mp, dqkv, aw, nin, low, att, x, gh, gain, gmid):
    seq, hh = att.shape
    d = aw.shape[0]
    n, part, chunk = n_dp // 2, seq // n_mp, d // n_dp
    dma = pltpu.SemaphoreType.DMA
    anyspace = pl.BlockSpec(memory_space=pl.ANY)
    vm = pl.BlockSpec(memory_space=pltpu.VMEM)
    folds = 1 + len([b for b in (1, 2, 4, 8) if b < n_mp]) + len([b for b in (2, 4, 8, 16) if b < n_dp])
    return pl.pallas_call(
        functools.partial(last_kernel, n_dp, n_mp),
        out_shape=[
            jax.ShapeDtypeStruct((4, chunk, hh), BF),
            jax.ShapeDtypeStruct((seq, d), BF),
            jax.ShapeDtypeStruct((8, chunk), F32),
        ],
        in_specs=[anyspace] * 6 + [vm] * 3,
        out_specs=[vm, anyspace, vm],
        scratch_shapes=[
            pltpu.VMEM((seq, 4 * hh), BF),
            pltpu.VMEM((d, 3 * hh), BF),
            pltpu.VMEM((seq, d), BF),
            pltpu.VMEM((seq, d), BF),
            pltpu.VMEM((2, chunk, seq), BF),
            pltpu.VMEM((part, d), BF),
            dma((6,)),
        ]
        + line_sum_scratch(n, 4, chunk, hh)
        + quad_sum_scratch(n_mp, part, d // 2)
        + quad_gather_scratch(n_mp, part, d // 2)
        + [
            pltpu.VMEM((8, d), F32),
            pltpu.VMEM((folds + 1, 8, d // 4), F32),
            pltpu.VMEM((folds, 8, d // 4), F32),
            dma((folds,)),
            dma((folds,)),
        ],
        compiler_params=pltpu.CompilerParams(
            collective_id=5, has_side_effects=True, vmem_limit_bytes=VMEM_LIMIT
        ),
        name="last_stage",
    )(dqkv, aw, nin, low, att, x, gh, gain, gmid)


def finish_kernel(
    low_ref,
    lay_ref,
    gu_ref,
    down_ref,
    attn_ref,
    gains_ref,
    lay_out,
    in_out,
    gate_out,
    up_out,
    down_out,
    q_out,
    k_out,
    v_out,
    o_out,
    g1_out,
    g2_out,
):
    lay_out[...] = lay_ref[...]
    in_out[...] = low_ref[...].astype(F32)
    half = gate_out.shape[1]
    gate_out[...] = gu_ref[0, :, :half].astype(F32)
    up_out[...] = gu_ref[0, :, half:].astype(F32)
    down_out[...] = down_ref[0].T.astype(F32)

    @pl.when(pl.program_id(0) == 0)
    def _():
        for i, ref in enumerate((q_out, k_out, v_out)):
            ref[...] = attn_ref[i].astype(F32)
        o_out[...] = attn_ref[3].T.astype(F32)
        g1_out[...] = gains_ref[0]
        g2_out[...] = gains_ref[1]


def finish_stage(low, lay, gu, down, attn, gains):
    seq, d = low.shape
    steps, chunk, wide = gu.shape
    width, hh = down.shape[2], attn.shape[2]
    row = pl.BlockSpec((seq // steps, d), lambda i: (i, 0))
    fixed = lambda *shape: pl.BlockSpec(shape, lambda i: (0,) * len(shape))
    piece = lambda w: pl.BlockSpec((1, chunk, w), lambda i: (i, 0, 0))
    cols = pl.BlockSpec((chunk, wide // 2), lambda i: (0, i))
    f32 = lambda *shape: jax.ShapeDtypeStruct(shape, F32)
    return pl.pallas_call(
        finish_kernel,
        grid=(steps,),
        in_specs=[row, row, piece(wide), piece(width), fixed(4, chunk, hh), fixed(*gains.shape)],
        out_specs=[row, row, cols, cols, pl.BlockSpec((width, chunk), lambda i: (i, 0))]
        + [fixed(chunk, hh)] * 3
        + [fixed(hh, chunk)]
        + [fixed(chunk)] * 2,
        out_shape=[
            jax.ShapeDtypeStruct((seq, d), BF),
            f32(seq, d),
            f32(chunk, steps * wide // 2),
            f32(chunk, steps * wide // 2),
            f32(steps * width, chunk),
        ]
        + [f32(chunk, hh)] * 3
        + [f32(hh, chunk)]
        + [f32(chunk)] * 2,
        compiler_params=pltpu.CompilerParams(vmem_limit_bytes=VMEM_LIMIT),
        name="finish_stage",
    )(low, lay, gu, down, attn, gains)


def on_device(
    inputs,
    counts,
    cotangent,
    gain_attn,
    w_query,
    w_key,
    w_value,
    w_output,
    gain_ffn,
    w_gate,
    w_up,
    w_down,
):
    n_dp, n_mp = lax.axis_size("dp"), lax.axis_size("mp")
    gains = jnp.pad(jnp.stack([gain_attn, gain_ffn]), ((0, 6), (0, 0)))
    gains = gains.astype(BF).astype(F32)
    attn_w, qkv, attended, normed_in, gains, gu_shard, down_shard, grad_ffn = attn_stage(
        n_dp, n_mp, counts, gains, w_query, w_key, w_value, w_output, w_gate, w_up, w_down, inputs, cotangent
    )
    gu_w, normed_mid, hidden, gu, inner = gate_stage(
        n_dp, n_mp, attended, attn_w, gu_shard, inputs, gains
    )
    rs_down, ffn_terms, ggu = down_stage(n_dp, n_mp, inner, gu, grad_ffn, down_shard)
    rs_gu, grad_low, layer_out, grad_hidden, g_gain_mid, dqkv = mid_stage(
        n_dp, n_mp, ggu, gu_w, normed_mid, ffn_terms, grad_ffn, qkv, attn_w, counts, hidden, gains
    )
    rs_attn, grad_low_in, g_gains = last_stage(
        n_dp, n_mp, dqkv, attn_w, normed_in, grad_low, attended, inputs, grad_hidden, gains, g_gain_mid
    )
    lay, grad_x, g_gate, g_up, g_down, g_q, g_k, g_v, g_o, g_attn, g_ffn = finish_stage(
        grad_low_in, layer_out, rs_gu, rs_down, rs_attn, g_gains
    )
    return (lay, grad_x, g_attn, g_q, g_k, g_v, g_o, g_ffn, g_gate, g_up, g_down)


def solution(mesh):
    row, both, swapped = P("dp", None), P("dp", "mp"), P("mp", "dp")
    weights = (both, both, both, swapped)
    ffn = (both, both, swapped)
    return jax.shard_map(
        on_device,
        mesh=mesh,
        in_specs=(row, P("dp"), row, P("dp")) + weights + (P("dp"),) + ffn,
        out_specs=(row, row, P("dp")) + weights + (P("dp"),) + ffn,
        check_vma=False,
    )
```

```python
import functools
import math

import jax
import jax.numpy as jnp
from jax import lax
from jax.experimental import pallas as pl
from jax.experimental.pallas import tpu as pltpu
from jax.sharding import PartitionSpec as P

HD = 128
EPS = 1e-06
BF = jnp.bfloat16
F32 = jnp.float32
NT = (((1,), (1,)), ((), ()))
TN = (((0,), (0,)), ((), ()))
NN = (((1,), (0,)), ((), ()))


def dot(a, b, dims=NN):
    return lax.dot_general(a, b, dims, preferred_element_type=F32)


def logistic_block(q, k, seq):
    raw = dot(q, k, NT)
    shifted = math.log(seq) - raw * HD ** (-0.5)
    return 1.0 / (1.0 + jnp.exp(shifted))


def allowed_block(row0, rows, col0, cols, count):
    ri = row0 + lax.broadcasted_iota(jnp.int32, (rows, cols), 0)
    ci = col0 + lax.broadcasted_iota(jnp.int32, (rows, cols), 1)
    return (ci <= ri) & (ci < count)


MESH = pl.DeviceIdType.MESH
VMEM_LIMIT = 60 * 1024 * 1024
PIECES = 4


def flipped(index, bit):
    return index + bit - 2 * bit * lax.rem(lax.div(index, bit), 2)


def spread(j, bits):
    return sum(bit for i, bit in enumerate(bits) if j >> i & 1)


class Place:
    def __init__(self, n_dp, n_mp):
        self.n = n_dp // 2
        self.dp = lax.axis_index("dp")
        self.m = lax.axis_index("mp")
        self.p = lax.div(self.dp, 2)
        self.c = lax.rem(self.dp, 2)
        self.above = (self.dp + 2, self.m)
        self.below = (self.dp - 2, self.m)
        self.core = (self.dp + 1 - 2 * self.c, self.m)
        self.bits = [b for b in (1, 2, 4, 8, 16) if b < n_mp]
        self.has_above = self.p < self.n - 1
        self.has_below = self.p > 0

    def fold(self, bit):
        return (flipped(self.dp, bit), self.m)

    def peer(self, bit):
        return (self.dp, flipped(self.m, bit))

    def quarter(self, mask):
        q = self.m
        for bit in self.bits:
            if mask & bit:
                q = flipped(q, bit)
        return q


def signal(dev):
    pl.semaphore_signal(pltpu.get_barrier_semaphore(), inc=1, device_id=dev, device_id_type=MESH)


def enter(at, extra=()):
    always = [at.core] + [at.peer(bit) for bit in at.bits] + list(extra)
    for dev in always:
        signal(dev)

    @pl.when(at.has_above)
    def _():
        signal(at.above)

    @pl.when(at.has_below)
    def _():
        signal(at.below)

    ends = at.has_above.astype(jnp.int32) + at.has_below.astype(jnp.int32)
    pl.semaphore_wait(pltpu.get_barrier_semaphore(), len(always) + ends)


def remote(src, dst, send, recv, dev):
    return pltpu.make_async_remote_copy(
        src_ref=src, dst_ref=dst, send_sem=send, recv_sem=recv, device_id=dev, device_id_type=MESH
    )


def part_rows(at, part):
    return pl.ds(pl.multiple_of(at.m * part, part), part)


def order_of(k, at):
    n, p = at.n, at.p
    if k == n - 1:
        return p
    high = jnp.where(k < p, k, n - 1 - k + p)
    low = jnp.where(k < n - 1 - p, n - 1 - k, k - (n - 1 - p))
    return jnp.where(2 * p >= n, high, low)


class LineSum:
    def __init__(self, at, pout, own, din, uin, sems, paced=False):
        self.paced = paced
        self.at, self.pout, self.own, self.din, self.uin = at, pout, own, din, uin
        self.po_s, self.po_r, self.d_s, self.d_r, self.u_s, self.u_r = sems
        self.slots, self.pieces = pout.shape[0], own.shape[1]

    def core_copy(self, k, i):
        j = order_of(k, self.at)
        slot = k % self.slots
        return remote(
            self.pout.at[slot, i],
            self.own.at[j, i],
            self.po_s.at[slot, i],
            self.po_r.at[k, i],
            self.at.core,
        )

    def down_copy(self, s, i):
        return remote(
            self.own.at[s, i], self.din.at[s, i], self.d_s.at[s, i], self.d_r.at[s, i], self.at.below
        )

    def up_copy(self, s, i):
        n = self.at.n
        return remote(
            self.own.at[n - 1 - s, i],
            self.uin.at[s, i],
            self.u_s.at[s, i],
            self.u_r.at[s, i],
            self.at.above,
        )

    def other(self, k, tile):
        @pl.loop(0, self.pieces)
        def _(i):
            if k >= self.slots:
                self.core_copy(k - self.slots, i).wait_send()
            self.pout[k % self.slots, i] = tile(i).astype(BF)
            self.core_copy(k, i).start()

    def mine(self, k, tile):
        at = self.at
        j = order_of(k, at)

        @pl.loop(0, self.pieces)
        def _(i):
            value = tile(i)
            self.core_copy(k, i).wait_recv()
            self.own[j, i] = (value + self.own[j, i].astype(F32)).astype(BF)
            if k < (1 if self.paced else at.n - 1):

                @pl.when(at.p == at.n - 1)
                def _():
                    self.down_copy(k, i).start()

                @pl.when(at.p == 0)
                def _():
                    self.up_copy(k, i).start()

    def add(self, dst, src):
        @pl.loop(0, dst.shape[0] // 64)
        def _(b):
            rs = pl.ds(pl.multiple_of(b * 64, 64), 64)
            dst[rs, :] = (dst[rs, :].astype(F32) + src[rs, :].astype(F32)).astype(BF)

    def slot(self, t):
        at = self.at
        n, p = at.n, at.p
        sd = t - (n - 2 - p)
        su = t - (p - 1)

        @pl.loop(0, self.pieces)
        def _(i):
            @pl.when((sd >= 0) & (sd < p) & at.has_above)
            def _():
                self.down_copy(sd, i).wait_recv()
                self.add(self.own.at[sd, i], self.din.at[sd, i])
                self.down_copy(sd, i).start()

            @pl.when((su >= 0) & (su < n - 1 - p) & at.has_below)
            def _():
                self.up_copy(su, i).wait_recv()
                self.add(self.own.at[n - 1 - su, i], self.uin.at[su, i])
                self.up_copy(su, i).start()

            if self.paced:

                @pl.when(p == n - 1)
                def _():
                    self.down_copy(t, i).wait_send()
                    self.down_copy(t + 1, i).start()

                @pl.when(p == 0)
                def _():
                    self.up_copy(t, i).wait_send()
                    self.up_copy(t + 1, i).start()

    def final(self, out, sink, sems):
        at = self.at
        n, p = at.n, at.p

        @pl.loop(0, self.pieces)
        def _(i):
            @pl.when(at.has_above)
            def _():
                self.down_copy(p, i).wait_recv()

            @pl.when(at.has_below)
            def _():
                self.up_copy(n - 1 - p, i).wait_recv()

            def close(parts):
                @pl.loop(0, out.shape[1] // 64)
                def _(b):
                    rs = pl.ds(pl.multiple_of(b * 64, 64), 64)
                    total = self.own[p, i, rs, :].astype(F32)
                    for ref, s in parts:
                        total = total + ref[s, i, rs, :].astype(F32)
                    out[i, rs, :] = total.astype(out.dtype)

            down, up = (self.din, p), (self.uin, n - 1 - p)

            @pl.when(at.has_above & at.has_below)
            def _():
                close([down, up])

            @pl.when(jnp.logical_not(at.has_below))
            def _():
                close([down])

            @pl.when(jnp.logical_not(at.has_above))
            def _():
                close([up])

            pltpu.make_async_copy(out.at[i], sink.at[i], sems.at[i]).start()

        return [
            pltpu.make_async_copy(out.at[i], sink.at[i], sems.at[i]) for i in range(self.pieces)
        ]

    def drain(self):
        at = self.at
        n, p = at.n, at.p
        for k in range(n - self.slots, n):
            for i in range(self.pieces):
                self.core_copy(k, i).wait_send()
        for s in range(n - 1):
            done = self.paced and s < n - 2

            @pl.when((s < p) & (at.has_above if done else at.has_below))
            def _():
                for i in range(self.pieces):
                    self.down_copy(s, i).wait_send()

            @pl.when((s < n - 1 - p) & (at.has_below if done else at.has_above))
            def _():
                for i in range(self.pieces):
                    self.up_copy(s, i).wait_send()


def line_sum_scratch(n, pieces, rows, cols, slots=2):
    dma = pltpu.SemaphoreType.DMA
    return [
        pltpu.VMEM((slots, pieces, rows, cols), BF),
        pltpu.VMEM((n, pieces, rows, cols), BF),
        pltpu.VMEM((n - 1, pieces, rows, cols), BF),
        pltpu.VMEM((n - 1, pieces, rows, cols), BF),
        dma((slots, pieces)),
        dma((n, pieces)),
        dma((n - 1, pieces)),
        dma((n - 1, pieces)),
        dma((n - 1, pieces)),
        dma((n - 1, pieces)),
    ]


class QuadSum:
    def __init__(self, at, t, r, sems):
        self.at, self.t, self.r = at, t, r
        self.s, self.v = sems
        self.order = [at.bits, at.bits[::-1]]
        self.levels = len(at.bits)
        self.seen = set()

    def count(self, k):
        return 1 << (self.levels - 1 - k)

    def slot(self, k, j):
        return sum(self.count(i) for i in range(k)) + j

    def rest(self, half, k):
        return self.order[half][k + 1 :]

    def index(self, half, k, mask):
        rest = self.rest(half, k)
        return self.slot(k, sum(1 << i for i, bit in enumerate(rest) if mask & bit))

    def source(self, half, mask):
        return self.t.at[half, self.at.quarter(mask)]

    def terms(self, half, mask, rs):
        return self.t[half, self.at.quarter(mask), rs, :].astype(F32)

    def copy(self, half, k, j):
        bit = self.order[half][k]
        mask = bit + spread(j, self.rest(half, k))
        src = self.source(half, mask) if k == 0 else self.r.at[half, self.index(half, k - 1, mask)]
        at = self.slot(k, j)
        return remote(
            src, self.r.at[half, at], self.s.at[half, at], self.v.at[half, at], self.at.peer(bit)
        )

    def offer(self, mask, only=(0, 1)):
        for half in only:
            if mask & self.order[half][0]:
                rest = self.rest(half, 0)
                self.copy(half, 0, sum(1 << i for i, b in enumerate(rest) if mask & b)).start()

    def masks(self):
        return sorted(range(1, 2 * self.count(0)), key=lambda m: -bin(m).count("1")) + [0]

    def come(self, half, k, mask):
        at = self.index(half, k, mask)
        if (half, at) not in self.seen:
            self.seen.add((half, at))
            self.copy(half, k, at - self.slot(k, 0)).wait_recv()
        return at

    def turn(self):
        for k in range(1, self.levels):
            for half in range(2):
                for j in range(self.count(k)):
                    mask = self.order[half][k] + spread(j, self.rest(half, k))
                    got = [self.come(half, i, mask) for i in range(k)]

                    @pl.loop(0, self.r.shape[2] // 64)
                    def _(b):
                        rs = pl.ds(pl.multiple_of(b * 64, 64), 64)
                        total = self.terms(half, mask, rs)
                        for i in got:
                            total = total + self.r[half, i, rs, :].astype(F32)
                        self.r[half, got[-1], rs, :] = total.astype(BF)

                    self.copy(half, k, j).start()

    def arrive(self):
        self.got = [[self.come(half, k, 0) for k in range(self.levels)] for half in range(2)]

    def total(self, half, rs):
        total = self.terms(half, 0, rs)
        for i in self.got[half]:
            total = total + self.r[half, i, rs, :].astype(F32)
        return total

    def drain(self):
        for half in range(2):
            for k in range(self.levels):
                for j in range(self.count(k)):
                    self.copy(half, k, j).wait_send()


class QuadSumHbm(QuadSum):
    def __init__(self, at, hbm, t, r, sems):
        super().__init__(at, t, r, sems[:2])
        self.hbm = hbm
        self.loads = [
            pltpu.make_async_copy(
                self.source(half, spread(j, self.rest(half, 0))), t.at[half, j], sems[2].at[half, j]
            )
            for half in range(2)
            for j in range(self.count(0))
        ]

    def source(self, half, mask):
        rows, cols = self.t.shape[2], self.t.shape[3]
        rs = pl.ds(pl.multiple_of(self.at.quarter(mask) * rows, rows), rows)
        return self.hbm.at[rs, pl.ds(half * cols, cols)]

    def terms(self, half, mask, rs):
        return self.t[half, self.index(half, 0, mask), rs, :].astype(F32)


def quad_sum_scratch(mp, rows, cols, parts=None):
    dma = pltpu.SemaphoreType.DMA
    return [
        pltpu.VMEM((2, parts or mp, rows, cols), BF),
        pltpu.VMEM((2, mp - 1, rows, cols), BF),
        dma((2, mp - 1)),
        dma((2, mp - 1)),
    ]


class QuadGather:
    def __init__(self, at, own, out, sems):
        self.at, self.own, self.out = at, own, out
        self.s, self.v, self.here = sems
        self.order = [at.bits[::-1], at.bits]
        self.levels = len(at.bits)
        self.seen = set()

    def spot(self, mask, half):
        rows, cols = self.own.shape[1], self.own.shape[2]
        rs = pl.ds(pl.multiple_of(self.at.quarter(mask) * rows, rows), rows)
        return self.out.at[rs, pl.ds(half * cols, cols)]

    def copy(self, half, k, j):
        mask = spread(j, self.order[half][:k])
        dst = self.spot(mask, half)
        src = self.own.at[half] if j == 0 else dst
        at = (1 << k) - 1 + j
        dev = self.at.peer(self.order[half][k])
        return remote(src, dst, self.s.at[half, at], self.v.at[half, at], dev)

    def come(self, half, k, j):
        if (half, k, j) not in self.seen:
            self.seen.add((half, k, j))
            self.copy(half, k, j).wait_recv()

    def keep(self, half):
        return pltpu.make_async_copy(self.own.at[half], self.spot(0, half), self.here.at[half])

    def start(self, levels=None):
        for k in range(self.levels) if levels is None else levels:
            for half in range(2):
                self.copy(half, k, 0).start()
                if k == 0:
                    self.keep(half).start()

    def forward(self):
        for k in range(1, self.levels):
            for half in range(2):
                for j in range(1, 1 << k):
                    top = j.bit_length() - 1
                    self.come(half, top, j - (1 << top))
                    self.copy(half, k, j).start()

    def finish(self):
        for half in range(2):
            for k in range(self.levels):
                for j in range(1 << k):
                    self.come(half, k, j)
                    self.copy(half, k, j).wait_send()
            self.keep(half).wait()


def quad_gather_scratch(mp, rows, cols):
    dma = pltpu.SemaphoreType.DMA
    return [pltpu.VMEM((2, rows, cols), BF), dma((2, mp - 1)), dma((2, mp - 1)), dma((2,))]


class LineGather:
    def __init__(self, at, pieces, shard, spot, sems):
        self.at, self.pieces, self.shard, self.spot = at, pieces, shard, spot
        self.d_s, self.d_r, self.u_s, self.u_r, self.c_s, self.c_r, self.here = sems

    def down_copy(self, h, i, own=False):
        b = 2 * (self.at.p + h) + self.at.c
        dst = self.spot(b, i)
        src = self.shard(i) if own and self.shard else dst
        return remote(src, dst, self.d_s.at[h, i], self.d_r.at[h, i], self.at.below)

    def up_copy(self, h, i, own=False):
        b = 2 * (self.at.p - h) + self.at.c
        dst = self.spot(b, i)
        src = self.shard(i) if own and self.shard else dst
        return remote(src, dst, self.u_s.at[h, i], self.u_r.at[h, i], self.at.above)

    def core_copy(self, z, i, own=False, incoming=False):
        b = 2 * z + (1 - self.at.c if incoming else self.at.c)
        dst = self.spot(b, i)
        src = self.shard(i) if own and self.shard else dst
        return remote(src, dst, self.c_s.at[z, i], self.c_r.at[z, i], self.at.core)

    def keep(self, i):
        at = self.at
        return pltpu.make_async_copy(self.shard(i), self.spot(at.dp, i), self.here.at[i])

    def start(self):
        at = self.at
        for i in range(self.pieces):

            @pl.when(at.has_below)
            def _():
                self.down_copy(0, i, True).start()

            @pl.when(at.has_above)
            def _():
                self.up_copy(0, i, True).start()

        for i in range(self.pieces):
            self.core_copy(at.p, i, True).start()
            if self.shard:
                self.keep(i).start()

    def slot(self, h, i):
        at = self.at
        n, p = at.n, at.p

        @pl.when(p + h < n)
        def _():
            self.down_copy(h - 1, i).wait_recv()

            @pl.when(at.has_below)
            def _():
                self.down_copy(h, i).start()

            self.core_copy(p + h, i).start()

        @pl.when(p - h >= 0)
        def _():
            self.up_copy(h - 1, i).wait_recv()

            @pl.when(at.has_above)
            def _():
                self.up_copy(h, i).start()

            self.core_copy(p - h, i).start()

    def stage(self, h):
        @pl.loop(0, self.pieces)
        def _(i):
            self.slot(h, i)

    def ready(self, z, i):
        self.core_copy(z, i, incoming=True).wait_recv()

    def drain(self):
        at = self.at
        n, p = at.n, at.p

        @pl.loop(0, self.pieces)
        def _(i):
            for h in range(n):

                @pl.when((p + h < n) & at.has_below)
                def _():
                    self.down_copy(h, i, h == 0).wait_send()

                @pl.when((p - h >= 0) & at.has_above)
                def _():
                    self.up_copy(h, i, h == 0).wait_send()

            for z in range(n):
                self.core_copy(z, i).wait_send()


def line_gather_scratch(n, pieces):
    dma = pltpu.SemaphoreType.DMA
    return [dma((n, pieces))] * 6 + [dma((pieces,))]


def rows_spot(out, rows, width):
    def spot(b, i):
        rs = pl.ds(pl.multiple_of(b * rows, rows), rows)
        return out.at[rs, pl.ds(pl.multiple_of(i * width, width), width)]

    return spot


def cols_of(ref, width, base=0):
    return lambda i: ref.at[:, pl.ds(pl.multiple_of(base + i * width, width), width)]


def attend_rows(qkv, out, seq, hh, count, head):
    cols = lambda first: pl.ds(pl.multiple_of(first + head * HD, HD), HD)
    blk = 256
    for i in range(seq // blk):
        rows = pl.ds(i * blk, blk)
        span = (i + 1) * blk
        lg = logistic_block(qkv[rows, cols(0)], qkv[pl.ds(0, span), cols(hh)], seq)
        w = jnp.where(allowed_block(i * blk, blk, 0, span, count), lg, 0.0).astype(BF)
        out[rows, cols(0)] = dot(w, qkv[pl.ds(0, span), cols(2 * hh)]).astype(BF)


def attn_kernel(
    n_dp,
    n_mp,
    count_ref,
    gains_in,
    wq_hbm,
    wk_hbm,
    wv_hbm,
    wo_hbm,
    wg_hbm,
    wu_hbm,
    wd_hbm,
    x_hbm,
    cot_hbm,
    aw_ref,
    qkv_ref,
    att_ref,
    nin_ref,
    gains_ref,
    gush_ref,
    dnsh_ref,
    cotm_ref,
    w4,
    wo,
    shard,
    x,
    qkv,
    wbuf,
    wgu,
    wd,
    gush,
    dnsh,
    cot,
    load_s,
    wb_s,
    out_s,
    *rest,
):
    at = Place(n_dp, n_mp)
    n = at.n
    chunk, hh = wq_hbm.shape
    seq, d = x.shape
    ff = wgu.shape[2]
    loads = [
        pltpu.make_async_copy(src, dst, load_s.at[i])
        for i, (src, dst) in enumerate(
            [
                (wq_hbm, w4.at[0]),
                (wk_hbm, w4.at[1]),
                (wv_hbm, w4.at[2]),
                (wo_hbm, wo),
                (x_hbm, x),
                (wg_hbm, wgu.at[0]),
                (wu_hbm, wgu.at[1]),
                (wd_hbm, wd),
                (cot_hbm, cot),
            ]
        )
    ]
    for cp in loads:
        cp.start()
    spot = rows_spot(aw_ref, chunk, hh)
    three = LineGather(at, 3, cols_of(shard, hh), spot, rest[0:7])
    last = LineGather(
        at, 1, lambda i: shard.at[:, pl.ds(3 * hh, hh)], lambda b, i: spot(b, 3), rest[7:14]
    )
    small = LineGather(
        at,
        1,
        lambda i: gains_in,
        lambda b, i: gains_ref.at[:, pl.ds(pl.multiple_of(b * chunk, chunk), chunk)],
        rest[14:21],
    )
    enter(at)
    small.start()
    for i in range(3):
        loads[i].wait()
        shard[:, i * hh : (i + 1) * hh] = w4[i].astype(BF)
    three.start()
    loads[3].wait()
    shard[:, 3 * hh :] = wo[...].T.astype(BF)
    small.slot(1, 0)
    loads[5].wait()
    loads[6].wait()
    half = ff // PIECES

    @pl.loop(0, PIECES)
    def _(i):
        cols = pl.ds(pl.multiple_of(i * half, half), half)
        for k in range(2):
            to = pl.ds(pl.multiple_of((2 * i + k) * half, half), half)
            gush[:, to] = wgu[k, :, cols].astype(BF)

    outs = [pltpu.make_async_copy(gush, gush_ref, out_s.at[0])]
    outs[0].start()
    loads[7].wait()

    @pl.loop(0, ff // 256)
    def _(i):
        rs = pl.ds(pl.multiple_of(i * 256, 256), 256)
        dnsh[:, rs] = wd[rs, :].T.astype(BF)

    outs.append(pltpu.make_async_copy(dnsh, dnsh_ref, out_s.at[2]))
    outs[-1].start()
    loads[8].wait()
    count = count_ref[0]

    @pl.loop(0, seq // 32)
    def _(b):
        rs = pl.ds(pl.multiple_of(b * 32, 32), 32)
        row = b * 32 + lax.broadcasted_iota(jnp.int32, (32, d), 0)
        cot[rs, :] = jnp.where(row < count, cot[rs, :].astype(F32), 0.0).astype(BF)

    outs.append(pltpu.make_async_copy(cot, cotm_ref, out_s.at[3]))
    outs[-1].start()
    for h in range(1, n - 1):
        small.slot(h + 1, 0)
        three.stage(h)
        if h == n - 2:
            last.start()
    small.keep(0).wait()
    for z in range(n):
        small.ready(z, 0)
    loads[4].wait()

    @pl.loop(0, seq // 32)
    def _(b):
        rs = pl.ds(pl.multiple_of(b * 32, 32), 32)
        v = x[rs, :].astype(F32)
        scale = lax.rsqrt(jnp.mean(v * v, axis=1, keepdims=True) + EPS)
        x[rs, :] = (v * scale * gains_ref[0:1, :]).astype(BF)

    outs.append(pltpu.make_async_copy(x, nin_ref, out_s.at[1]))
    outs[-1].start()

    def w_copy(i):
        cols = pl.ds(pl.multiple_of(i * hh, hh), hh)
        return pltpu.make_async_copy(aw_ref.at[:, cols], wbuf.at[i], wb_s.at[i])

    for i in range(3):
        three.slot(n - 1, i)
        three.keep(i).wait()
        for z in range(n):
            three.ready(z, i)
        w_copy(i).start()
        if i == 1:
            last.slot(1, 0)
        w_copy(i).wait()

        @pl.loop(0, seq // 256)
        def _(b):
            rs = pl.ds(pl.multiple_of(b * 256, 256), 256)
            qkv[rs, i * hh : (i + 1) * hh] = dot(x[rs, :], wbuf[i]).astype(BF)

    outs.append(pltpu.make_async_copy(qkv, qkv_ref, out_s.at[4]))
    outs[-1].start()
    for h in range(2, n - 1):
        last.slot(h, 0)
    heads = hh // HD

    @pl.loop(0, heads // 2)
    def _(head):
        attend_rows(qkv, att_ref, seq, hh, count, head)

    last.slot(n - 1, 0)

    @pl.loop(heads // 2, heads)
    def _(head):
        attend_rows(qkv, att_ref, seq, hh, count, head)

    last.keep(0).wait()
    for z in range(n):
        last.ready(z, 0)
    for cp in outs:
        cp.wait()
    small.drain()
    three.drain()
    last.drain()


def attn_stage(n_dp, n_mp, counts, gains, wq, wk, wv, wo, wg, wu, wd, x, cot):
    seq, d = x.shape
    chunk, hh = wq.shape
    ff = wg.shape[1]
    n = n_dp // 2
    dma = pltpu.SemaphoreType.DMA
    hbm = pl.BlockSpec(memory_space=pl.ANY)
    vm = pl.BlockSpec(memory_space=pltpu.VMEM)
    shapes = [
        ((d, 4 * hh), BF),
        ((seq, 3 * hh), BF),
        ((seq, hh), BF),
        ((seq, d), BF),
        ((8, d), F32),
        ((chunk, 2 * ff), BF),
        ((chunk, ff), BF),
        ((seq, d), BF),
    ]
    return pl.pallas_call(
        functools.partial(attn_kernel, n_dp, n_mp),
        out_shape=[jax.ShapeDtypeStruct(*s) for s in shapes],
        in_specs=[pl.BlockSpec(memory_space=pltpu.SMEM), vm] + [hbm] * 9,
        out_specs=[hbm, hbm, vm, hbm, vm, hbm, hbm, hbm],
        scratch_shapes=[
            pltpu.VMEM((3, chunk, hh), F32),
            pltpu.VMEM((hh, chunk), F32),
            pltpu.VMEM((chunk, 4 * hh), BF),
            pltpu.VMEM((seq, d), BF),
            pltpu.VMEM((seq, 3 * hh), BF),
            pltpu.VMEM((3, d, hh), BF),
            pltpu.VMEM((2, chunk, ff), F32),
            pltpu.VMEM((ff, chunk), F32),
            pltpu.VMEM((chunk, 2 * ff), BF),
            pltpu.VMEM((chunk, ff), BF),
            pltpu.VMEM((seq, d), BF),
            dma((9,)),
            dma((3,)),
            dma((5,)),
        ]
        + line_gather_scratch(n, 3)
        + line_gather_scratch(n, 1) * 2,
        compiler_params=pltpu.CompilerParams(
            collective_id=1, has_side_effects=True, vmem_limit_bytes=VMEM_LIMIT
        ),
        name="attn_stage",
    )(counts, gains, wq, wk, wv, wo, wg, wu, wd, x, cot)


def gate_kernel(
    n_dp,
    n_mp,
    att_ref,
    aw_hbm,
    sh_hbm,
    x_hbm,
    gain_ref,
    gw_ref,
    nm_ref,
    hid_hbm,
    gu_ref,
    inner_ref,
    wo,
    sh,
    xs,
    hid,
    acc,
    nm,
    wbuf,
    gbuf,
    ibuf,
    load_s,
    wb_s,
    gb_s,
    ib_s,
    *rest,
):
    at = Place(n_dp, n_mp)
    n = at.n
    quad = QuadSum(at, *rest[0:2], rest[2:4])
    gather_nm = QuadGather(at, rest[4], nm_ref, rest[5:8])
    sems = rest[8:15]
    hh = wo.shape[1]
    part, half_cols = quad.t.shape[2], quad.t.shape[3]
    chunk, wide = sh_hbm.shape
    pieces = sems[6].shape[0]
    width = wide // pieces
    line = LineGather(at, pieces, cols_of(sh, width), rows_spot(gw_ref, chunk, width), sems)

    load_sh = pltpu.make_async_copy(sh_hbm, sh, load_s.at[2])
    load_sh.start()
    load = pltpu.make_async_copy(aw_hbm.at[:, pl.ds(3 * hh, hh)], wo, load_s.at[0])
    load.start()
    load_x = pltpu.make_async_copy(x_hbm.at[part_rows(at, part), :], xs, load_s.at[1])
    load_x.start()
    enter(at)
    load_sh.wait()
    line.start()
    load.wait()

    def terms(q):
        rs = pl.ds(pl.multiple_of(q * part, part), part)
        for half in range(2):
            w = wo[half * half_cols : (half + 1) * half_cols, :]
            quad.t[half, q] = dot(att_ref[rs, :], w, NT).astype(BF)

    for mask in quad.masks():
        terms(at.quarter(mask))
        quad.offer(mask)
    quad.turn()
    quad.arrive()
    load_x.wait()

    @pl.loop(0, part // 32)
    def _(b):
        rs = pl.ds(pl.multiple_of(b * 32, 32), 32)
        h = xs[rs, :].astype(F32) + jnp.concatenate(
            [quad.total(0, rs), quad.total(1, rs)], axis=1
        )
        hid[rs, :] = h
        scale = lax.rsqrt(jnp.mean(h * h, axis=1, keepdims=True) + EPS)
        res = (h * scale * gain_ref[1:2, :]).astype(BF)
        gather_nm.own[0, rs, :] = res[:, :half_cols]
        gather_nm.own[1, rs, :] = res[:, half_cols:]

    gather_nm.start()
    store_hid = pltpu.make_async_copy(hid, hid_hbm, load_s.at[1])
    store_hid.start()
    line.stage(1)
    gather_nm.forward()
    gather_nm.finish()
    load = pltpu.make_async_copy(nm_ref, nm, load_s.at[0])
    load.start()
    for h in range(2, n - 1):
        line.stage(h)
    load.wait()

    pair = 2 * chunk
    near = jnp.where(2 * at.p < n, 0, 1)
    far = jnp.where(2 * at.p < n, n - 1, 0)
    most = (n - 1) * pair
    most_rows = pl.ds(pl.multiple_of(near * pair, pair), most)
    far_rows = pl.ds(pl.multiple_of(far * pair, pair), pair)

    def w_copy(i, slot, rows):
        cols = pl.ds(pl.multiple_of(i * width, width), width)
        return pltpu.make_async_copy(
            gw_ref.at[rows, cols], wbuf.at[slot, rows, :], wb_s.at[slot]
        )

    def first_part(i, slot):
        line.keep(i).wait()

        @pl.loop(0, n - 1)
        def _(z):
            line.ready(near + z, i)

        w_copy(i, slot, most_rows).start()
        w_copy(i, slot, most_rows).wait()

        @pl.loop(0, nm.shape[0] // 256)
        def _(b):
            rs = pl.ds(pl.multiple_of(b * 256, 256), 256)
            acc[rs, :] = dot(nm[rs, most_rows], wbuf[slot, most_rows, :])

    def g_copy(i, slot):
        cols = pl.ds(pl.multiple_of(i * width, width), width)
        return pltpu.make_async_copy(gbuf.at[slot], gu_ref.at[:, cols], gb_s.at[slot])

    def i_copy(i, slot):
        cols = pl.ds(pl.multiple_of(i * (width // 2), width // 2), width // 2)
        return pltpu.make_async_copy(ibuf.at[slot], inner_ref.at[:, cols], ib_s.at[slot])

    @pl.loop(0, pieces)
    def _(i):
        slot = lax.rem(i, 2)
        first_part(i, slot)
        line.slot(n - 1, i)
        line.ready(far, i)
        w_copy(i, slot, far_rows).start()

        @pl.when(i >= 2)
        def _():
            g_copy(i - 2, slot).wait()
            i_copy(i - 2, slot).wait()

        w_copy(i, slot, far_rows).wait()

        @pl.loop(0, nm.shape[0] // 256)
        def _(b):
            rs = pl.ds(pl.multiple_of(b * 256, 256), 256)
            v = (acc[rs, :] + dot(nm[rs, far_rows], wbuf[slot, far_rows, :])).astype(BF)
            gbuf[slot, rs, :] = v
            g = v[:, : width // 2].astype(F32)
            u = v[:, width // 2 :].astype(F32)
            ibuf[slot, rs, :] = (g / (1.0 + jnp.exp(-g)) * u).astype(BF)

        g_copy(i, slot).start()
        i_copy(i, slot).start()

    for i in range(max(0, pieces - 2), pieces):
        g_copy(i, i % 2).wait()
        i_copy(i, i % 2).wait()
    store_hid.wait()
    line.drain()
    quad.drain()


def gate_stage(n_dp, n_mp, att, aw, shard, x, gain):
    seq, hh = att.shape
    d = aw.shape[0]
    chunk, wide = shard.shape
    n, part = n_dp // 2, seq // n_mp
    dma = pltpu.SemaphoreType.DMA
    hbm = pl.BlockSpec(memory_space=pl.ANY)
    vm = pl.BlockSpec(memory_space=pltpu.VMEM)
    width = wide // PIECES
    return pl.pallas_call(
        functools.partial(gate_kernel, n_dp, n_mp),
        out_shape=[
            jax.ShapeDtypeStruct((d, wide), BF),
            jax.ShapeDtypeStruct((seq, d), BF),
            jax.ShapeDtypeStruct((part, d), F32),
            jax.ShapeDtypeStruct((seq, wide), BF),
            jax.ShapeDtypeStruct((seq, wide // 2), BF),
        ],
        in_specs=[vm, hbm, hbm, hbm, vm],
        out_specs=[hbm] * 5,
        scratch_shapes=[
            pltpu.VMEM((d, hh), BF),
            pltpu.VMEM((chunk, wide), BF),
            pltpu.VMEM((part, d), BF),
            pltpu.VMEM((part, d), F32),
            pltpu.VMEM((seq, width), F32),
            pltpu.VMEM((seq, d), BF),
            pltpu.VMEM((2, d, width), BF),
            pltpu.VMEM((2, seq, width), BF),
            pltpu.VMEM((2, seq, width // 2), BF),
            dma((3,)),
            dma((2,)),
            dma((2,)),
            dma((2,)),
        ]
        + quad_sum_scratch(n_mp, part, d // 2)
        + quad_gather_scratch(n_mp, part, d // 2)
        + line_gather_scratch(n, PIECES),
        compiler_params=pltpu.CompilerParams(
            collective_id=2, has_side_effects=True, vmem_limit_bytes=VMEM_LIMIT
        ),
        name="gate_stage",
    )(att, aw, shard, x, gain)


def down_kernel(
    n_dp,
    n_mp,
    inner_hbm,
    gu_hbm,
    cot_hbm,
    sh_hbm,
    rs_ref,
    ft_ref,
    ggu_ref,
    inner,
    gu,
    cot,
    dn,
    acc,
    ftb,
    res,
    load_s,
    cot_s,
    in_s,
    rs_s,
    ft_s,
    dn_s,
    gg_s,
    *rest,
):
    at = Place(n_dp, n_mp)
    n, p = at.n, at.p
    line = LineSum(at, *rest[0:4], rest[4:10])
    sems = rest[10:17]
    chunk, ff = sh_hbm.shape
    pieces = sems[6].shape[0]
    width = ff // pieces
    gather = LineGather(at, pieces, None, rows_spot(dn, chunk, width), sems)
    pair = 2 * chunk
    def cot_copy(k):
        cols = pl.ds(pl.multiple_of(order_of(k, at) * pair, pair), pair)
        return pltpu.make_async_copy(cot_hbm.at[:, cols], cot.at[:, cols], cot_s.at[k])

    def in_copy(i):
        cols = pl.ds(pl.multiple_of(i * width, width), width)
        return pltpu.make_async_copy(inner_hbm.at[:, cols], inner.at[:, cols], in_s.at[i])

    load_gu = pltpu.make_async_copy(gu_hbm, gu, load_s.at[0])
    own = pltpu.make_async_copy(
        sh_hbm, dn.at[pl.ds(pl.multiple_of(at.dp * chunk, chunk), chunk), :], dn_s.at[0]
    )
    own.start()
    cot_copy(0).start()
    for i in range(pieces):
        in_copy(i).start()
    for k in range(1, n):
        cot_copy(k).start()
    load_gu.start()
    enter(at)
    own.wait()
    gather.start()

    def run(e):
        k, core = e // 2, e % 2
        block = 2 * order_of(k, at) + (1 - at.c if core == 0 else at.c)
        if core == 0:
            cot_copy(k).wait()
        lhs = cot[:, pl.ds(pl.multiple_of(block * chunk, chunk), chunk)].T

        def tile(i):
            if e == 0:
                in_copy(i).wait()
            return dot(lhs, inner[:, pl.ds(pl.multiple_of(i * width, width), width)])

        if core == 0:
            line.other(k, tile)
        else:
            line.mine(k, tile)

    for e in range(2 * n):
        run(e)

    def ft_copy(z, slot):
        cols = pl.ds(pl.multiple_of(z * pair, pair), pair)
        return pltpu.make_async_copy(ftb.at[slot], ft_ref.at[:, cols], ft_s.at[slot])

    def rows_of(z):
        return pl.ds(pl.multiple_of(z * pair, pair), pair)

    def grads(z, fresh):
        @pl.loop(0, pieces)
        def _(i):
            gather.ready(z, i)

        @pl.loop(0, ff // 512)
        def _(i):
            cols = pl.ds(pl.multiple_of(i * 512, 512), 512)
            v = dot(cot[:, rows_of(z)], dn[rows_of(z), cols])
            acc[:, cols] = v if fresh else acc[:, cols] + v

    def branch(z, fresh):
        if not fresh:
            ft_copy(z, 0).wait()
        ftb[0] = dot(inner[...], dn[rows_of(z), :], NT).astype(BF)
        ft_copy(z, 0).start()

    grads(p, True)
    branch(p, True)
    load_gu.wait()
    half = width

    def cols_at(i):
        g = pl.ds(pl.multiple_of(i * 2 * half, half), half)
        u = pl.ds(pl.multiple_of(i * 2 * half + half, half), half)
        return g, u, pl.ds(pl.multiple_of(i * half, half), half)

    @pl.loop(0, pieces)
    def _(i):
        gcols, ucols, _ = cols_at(i)

        @pl.loop(0, gu.shape[0] // 64)
        def _(b):
            rs = pl.ds(pl.multiple_of(b * 64, 64), 64)
            g = gu[rs, gcols].astype(F32)
            u = gu[rs, ucols].astype(F32)
            sg = 1.0 / (1.0 + jnp.exp(-g))
            gu[rs, gcols] = (u * sg * (1.0 + g * (1.0 - sg))).astype(BF)
            gu[rs, ucols] = (g * sg).astype(BF)

    @pl.loop(1, n - 1)
    def _(h):
        gather.stage(h)

        @pl.when(p + h < n)
        def _():
            grads(p + h, False)
            branch(p + h, False)

        @pl.when(p - h >= 0)
        def _():
            grads(p - h, False)
            branch(p - h, False)

        line.slot(h - 1)

    gather.stage(n - 1)

    @pl.when(jnp.logical_not(at.has_below))
    def _():
        grads(n - 1, False)

    @pl.when(jnp.logical_not(at.has_above))
    def _():
        grads(0, False)

    def gg_copy(i):
        cols = pl.ds(pl.multiple_of(i * 2 * half, 2 * half), 2 * half)
        return pltpu.make_async_copy(gu.at[:, cols], ggu_ref.at[:, cols], gg_s.at[i])

    @pl.loop(0, pieces)
    def _(i):
        gcols, ucols, acols = cols_at(i)

        @pl.loop(0, gu.shape[0] // 64)
        def _(b):
            rs = pl.ds(pl.multiple_of(b * 64, 64), 64)
            gi = acc[rs, acols]
            gu[rs, gcols] = (gi * gu[rs, gcols].astype(F32)).astype(BF)
            gu[rs, ucols] = (gi * gu[rs, ucols].astype(F32)).astype(BF)

        gg_copy(i).start()

    @pl.when(jnp.logical_not(at.has_below))
    def _():
        branch(n - 1, False)

    @pl.when(jnp.logical_not(at.has_above))
    def _():
        branch(0, False)

    stores = line.final(res, rs_ref, rs_s)
    for i in range(pieces):
        gg_copy(i).wait()
    ft_copy(p, 0).wait()
    for cp in stores:
        cp.wait()
    line.drain()
    gather.drain()


def down_stage(n_dp, n_mp, inner, gu, cot, shard):
    seq, d = cot.shape
    chunk, ff = shard.shape
    n = n_dp // 2
    dma = pltpu.SemaphoreType.DMA
    hbm = pl.BlockSpec(memory_space=pl.ANY)
    return pl.pallas_call(
        functools.partial(down_kernel, n_dp, n_mp),
        out_shape=[
            jax.ShapeDtypeStruct((PIECES, chunk, ff // PIECES), BF),
            jax.ShapeDtypeStruct((seq, d), BF),
            jax.ShapeDtypeStruct((seq, 2 * ff), BF),
        ],
        in_specs=[hbm] * 4,
        out_specs=[hbm] * 3,
        scratch_shapes=[
            pltpu.VMEM((seq, ff), BF),
            pltpu.VMEM((seq, 2 * ff), BF),
            pltpu.VMEM((seq, d), BF),
            pltpu.VMEM((d, ff), BF),
            pltpu.VMEM((seq, ff), F32),
            pltpu.VMEM((1, seq, 2 * chunk), BF),
            pltpu.VMEM((PIECES, chunk, ff // PIECES), BF),
            dma((1,)),
            dma((n,)),
            dma((PIECES,)),
            dma((PIECES,)),
            dma((1,)),
            dma((1,)),
            dma((PIECES,)),
        ]
        + line_sum_scratch(n, PIECES, chunk, ff // PIECES)
        + line_gather_scratch(n, PIECES),
        compiler_params=pltpu.CompilerParams(
            collective_id=3, has_side_effects=True, vmem_limit_bytes=VMEM_LIMIT
        ),
        name="down_stage",
    )(inner, gu, cot, shard)


def mid_kernel(
    n_dp,
    n_mp,
    ggu_hbm,
    gw_hbm,
    nm_hbm,
    ft_hbm,
    cot_hbm,
    qkv_hbm,
    aw_hbm,
    count_ref,
    hid_hbm,
    gain_ref,
    rs_ref,
    low_ref,
    lay_ref,
    gh_hbm,
    gg_ref,
    dq_ref,
    space,
    wt,
    wt_s,
    nm,
    nm_s,
    cot,
    hid,
    gh,
    res,
    gg_s,
    rs_s,
    dka,
    dva,
    load_s,
    *rest,
):
    at = Place(n_dp, n_mp)
    n = at.n
    line = LineSum(at, *rest[0:4], rest[4:10])
    mid = QuadSum(at, *rest[10:12], rest[12:14])
    lay = QuadSumHbm(at, ft_hbm, *rest[14:16], rest[16:19])
    gather_low = QuadGather(at, rest[19], low_ref, rest[20:23])
    gather_lay = QuadGather(at, rest[23], lay_ref, rest[24:27])
    part, half_cols = mid.t.shape[2], mid.t.shape[3]
    chunk, width = line.own.shape[2], line.own.shape[3]
    pieces = line.pieces
    hh = qkv_hbm.shape[1] // 3
    drows = wt.shape[1]
    tiles = half_cols // drows

    wide = ggu_hbm.shape[1]
    ggu = space.at[:, pl.ds(0, wide)]

    def gg_copy(i):
        cols = pl.ds(pl.multiple_of(i * width, width), width)
        return pltpu.make_async_copy(ggu_hbm.at[:, cols], ggu.at[:, cols], gg_s.at[i])

    load_cot = pltpu.make_async_copy(cot_hbm.at[part_rows(at, part), :], cot, load_s.at[1])

    def nm_copy(e):
        k, core = e // 2, e % 2
        block = 2 * order_of(k, at) + (1 - at.c if core == 0 else at.c)
        cols = pl.ds(pl.multiple_of(block * chunk, chunk), chunk)
        return pltpu.make_async_copy(nm_hbm.at[:, cols], nm.at[e % 2], nm_s.at[e % 2])

    def wt_copy(half, i, slot):
        rows = pl.ds(pl.multiple_of(half * half_cols + i * drows, drows), drows)
        return pltpu.make_async_copy(gw_hbm.at[rows, :], wt.at[slot], wt_s.at[slot])

    nm_copy(0).start()
    for i in range(pieces):
        gg_copy(i).start()
    wt_copy(0, 0, 0).start()
    load_cot.start()
    load_hid = pltpu.make_async_copy(hid_hbm, hid, load_s.at[0])
    load_hid.start()
    for cp in lay.loads:
        cp.start()
    enter(at)
    for mask in lay.masks():
        lay.offer(mask)

    def run(e):
        if e + 1 < 2 * n:
            nm_copy(e + 1).start()
        nm_copy(e).wait()
        lhs = nm[e % 2].T

        def tile(i):
            if e == 0:
                gg_copy(i).wait()
            return dot(lhs, ggu[:, pl.ds(pl.multiple_of(i * width, width), width)])

        if e % 2 == 0:
            line.other(e // 2, tile)
        else:
            line.mine(e // 2, tile)

    def terms(half):
        @pl.loop(0, tiles)
        def _(i):
            slot = lax.rem(i, 2)
            if half == 0:
                nxt = wt_copy(jnp.where(i + 1 < tiles, 0, 1), lax.rem(i + 1, tiles), 1 - slot)
                nxt.start()
            else:

                @pl.when(i + 1 < tiles)
                def _():
                    wt_copy(1, i + 1, 1 - slot).start()

            wt_copy(half, i, slot).wait()
            v = dot(ggu[...], wt[slot], NT).astype(BF)
            cols = pl.ds(pl.multiple_of(i * drows, drows), drows)
            for q in range(n_mp):
                mid.t[half, q, :, cols] = v[q * part : (q + 1) * part]

        for mask in mid.masks():
            mid.offer(mask, (half,))

    run(0)
    run(1)
    terms(0)
    run(2)
    run(3)
    for cp in lay.loads:
        cp.wait()
    lay.turn()
    terms(1)
    for e in range(4, 2 * n):
        run(e)
    lay.arrive()
    load_hid.wait()

    @pl.loop(0, part // 32)
    def _(b):
        rs = pl.ds(pl.multiple_of(b * 32, 32), 32)
        for half in range(2):
            h = hid[rs, pl.ds(half * half_cols, half_cols)]
            gather_lay.own[half, rs, :] = (h + lay.total(half, rs)).astype(BF)

    gather_lay.start([0])
    line.slot(0)
    per = half_cols // hh
    blocks_d = 2 * half_cols // part
    wo_spot = [(e // per // (n_mp // 2), e // per % (n_mp // 2), e % per) for e in range(blocks_d)]
    wo_parts = [
        pltpu.make_async_copy(
            aw_hbm.at[pl.ds(e * part, part), pl.ds(3 * hh, hh)],
            lay.t.at[i, j, :, pl.ds(k * hh, hh)],
            load_s.at[4 + e],
        )
        for e, (i, j, k) in enumerate(wo_spot)
    ]
    for cp in wo_parts:
        cp.start()
    load_qkv = pltpu.make_async_copy(
        qkv_hbm, space.at[:, pl.ds(2 * half_cols, 3 * hh)], load_s.at[2]
    )
    load_qkv.start()
    mid.turn()
    mid.arrive()
    load_cot.wait()
    gg_ref[...] = jnp.zeros_like(gg_ref)

    @pl.loop(0, part // 32)
    def _(b):
        rs = pl.ds(pl.multiple_of(b * 32, 32), 32)
        h = hid[rs, :]
        scale = lax.rsqrt(jnp.mean(h * h, axis=1, keepdims=True) + EPS)
        g = jnp.concatenate([mid.total(0, rs), mid.total(1, rs)], axis=1)
        unit = h * scale
        weighted = g * gain_ref[1:2, :]
        field = scale * (weighted - unit * jnp.mean(weighted * unit, axis=1, keepdims=True))
        out = cot[rs, :].astype(F32) + field
        gh[rs, :] = out
        low = out.astype(BF)
        gather_low.own[0, rs, :] = low[:, :half_cols]
        gather_low.own[1, rs, :] = low[:, half_cols:]
        gg_ref[...] += jnp.sum(g * unit, axis=0, keepdims=True)

    gather_low.start()
    store_gh = pltpu.make_async_copy(gh, gh_hbm, load_s.at[1])
    store_gh.start()
    for s in range(1, n - 2):
        line.slot(s)
    gather_low.forward()
    gather_lay.start(range(1, gather_lay.levels))
    gather_low.finish()
    load_low = pltpu.make_async_copy(low_ref, space.at[:, pl.ds(0, 2 * half_cols)], load_s.at[3])
    load_low.start()
    load_low.wait()
    load_qkv.wait()
    for cp in wo_parts:
        cp.wait()
    seq = space.shape[0]
    base = 2 * half_cols
    gbase = base + 3 * hh

    @pl.loop(0, seq // 256)
    def _(b):
        rs = pl.ds(pl.multiple_of(b * 256, 256), 256)
        total = jnp.zeros((256, hh), F32)
        for e, (i, j, k) in enumerate(wo_spot):
            wo = lay.t[i, j, :, k * hh : (k + 1) * hh]
            total += dot(space[rs, e * part : (e + 1) * part], wo)
        space[rs, gbase : gbase + hh] = total.astype(BF)

    count = count_ref[0]
    blk = 256
    blocks = seq // blk

    def back(head):
        at_cols = lambda first: pl.ds(pl.multiple_of(first + head * HD, HD), HD)
        for i in range(blocks - 1, -1, -1):
            rows = pl.ds(i * blk, blk)
            span = (i + 1) * blk
            keys = pl.ds(0, span)
            q = space[rows, at_cols(base)]
            g = space[rows, at_cols(gbase)]
            k = space[keys, at_cols(base + hh)]
            lg = jnp.where(
                allowed_block(i * blk, blk, 0, span, count), logistic_block(q, k, seq), 0.0
            )
            w = lg.astype(BF)
            gw = dot(g, space[keys, at_cols(base + 2 * hh)], NT)
            gs = (gw * lg * (1.0 - lg) * HD ** (-0.5)).astype(BF)
            wt[i // 2, :, at_cols((i % 2) * (wide // 2))] = dot(gs, k).astype(BF)
            dk = dot(gs, q, TN)
            dv = dot(w, g, TN)
            if i == blocks - 1:
                dka[...] = dk
                dva[...] = dv
            else:
                dka[keys, :] += dk
                dva[keys, :] += dv
        for i in range(blocks):
            rows = pl.ds(i * blk, blk)
            wt[i // 2, :, at_cols((i % 2) * (wide // 2) + hh)] = dka[rows, :].astype(BF)
            wt[i // 2, :, at_cols((i % 2) * (wide // 2) + 2 * hh)] = dva[rows, :].astype(BF)

    heads = hh // HD
    pl.loop(0, heads // 2)(back)
    gather_lay.forward()
    pl.loop(heads // 2, heads)(back)
    stores = [
        pltpu.make_async_copy(
            wt.at[i // 2, :, pl.ds((i % 2) * (wide // 2), 3 * hh)],
            dq_ref.at[pl.ds(i * blk, blk), :],
            load_s.at[4 + i],
        )
        for i in range(blocks)
    ]
    for cp in stores:
        cp.start()
    stores += line.final(res, rs_ref, rs_s) + [store_gh]
    gather_lay.finish()
    for cp in stores:
        cp.wait()
    line.drain()
    mid.drain()
    lay.drain()


def mid_stage(n_dp, n_mp, ggu, gw, nm, ft, cot, qkv, aw, counts, hid, gain):
    seq, wide = ggu.shape
    hh = qkv.shape[1] // 3
    d = gw.shape[0]
    n, part, chunk = n_dp // 2, seq // n_mp, d // n_dp
    dma = pltpu.SemaphoreType.DMA
    hbm = pl.BlockSpec(memory_space=pl.ANY)
    vm = pl.BlockSpec(memory_space=pltpu.VMEM)
    pieces = PIECES
    return pl.pallas_call(
        functools.partial(mid_kernel, n_dp, n_mp),
        out_shape=[
            jax.ShapeDtypeStruct((pieces, chunk, wide // pieces), BF),
            jax.ShapeDtypeStruct((seq, d), BF),
            jax.ShapeDtypeStruct((seq, d), BF),
            jax.ShapeDtypeStruct((part, d), F32),
            jax.ShapeDtypeStruct((1, d), F32),
            jax.ShapeDtypeStruct((seq, 3 * hh), BF),
        ],
        in_specs=[hbm] * 7 + [pl.BlockSpec(memory_space=pltpu.SMEM), hbm, vm],
        out_specs=[hbm, hbm, hbm, hbm, vm, hbm],
        scratch_shapes=[
            pltpu.VMEM((seq, max(wide, d + 4 * hh)), BF),
            pltpu.VMEM((2, 256, wide), BF),
            dma((2,)),
            pltpu.VMEM((2, seq, chunk), BF),
            dma((2,)),
            pltpu.VMEM((part, d), BF),
            pltpu.VMEM((part, d), F32),
            pltpu.VMEM((part, d), F32),
            pltpu.VMEM((pieces, chunk, wide // pieces), BF),
            dma((pieces,)),
            dma((pieces,)),
            pltpu.VMEM((seq, HD), F32),
            pltpu.VMEM((seq, HD), F32),
            dma((4 + max(d // part, seq // 256),)),
        ]
        + line_sum_scratch(n, pieces, chunk, wide // pieces, 1)
        + quad_sum_scratch(n_mp, part, d // 2)
        + quad_sum_scratch(n_mp, part, d // 2, n_mp // 2)
        + [dma((2, n_mp // 2))]
        + quad_gather_scratch(n_mp, part, d // 2) * 2,
        compiler_params=pltpu.CompilerParams(
            collective_id=4, has_side_effects=True, vmem_limit_bytes=VMEM_LIMIT
        ),
        name="mid_stage",
    )(ggu, gw, nm, ft, cot, qkv, aw, counts, hid, gain)


def last_kernel(
    n_dp,
    n_mp,
    dqkv_hbm,
    aw_hbm,
    nin_hbm,
    low_hbm,
    att_hbm,
    x_hbm,
    gh_hbm,
    gain_ref,
    gmid_ref,
    rs_ref,
    grad_ref,
    gains_ref,
    rhs,
    aw,
    nin,
    low,
    lhs,
    x,
    gh,
    res,
    rs_s,
    loads,
    pout,
    own,
    din,
    uin,
    po_s,
    po_r,
    d_s,
    d_r,
    u_s,
    u_r,
    t,
    r,
    q1,
    q2,
    gown,
    g1,
    g2,
    g3,
    gsum,
    fold_out,
    fold_in,
    fold_s,
    fold_r,
):
    at = Place(n_dp, n_mp)
    hh = att_hbm.shape[1]
    part = t.shape[2]
    chunk = own.shape[2]
    half_cols = t.shape[3]
    copies = [
        pltpu.make_async_copy(src, dst, loads.at[i])
        for i, (src, dst) in enumerate(
            [
                (dqkv_hbm, rhs.at[:, pl.ds(0, 3 * hh)]),
                (aw_hbm.at[:, pl.ds(0, 3 * hh)], aw),
                (nin_hbm, nin),
                (att_hbm, rhs.at[:, pl.ds(3 * hh, hh)]),
                (low_hbm, low),
                (x_hbm.at[part_rows(at, part), :], x),
                (gh_hbm, gh),
            ]
        )
    ]
    for cp in copies:
        cp.start()
    bits = [b for b in (2, 4, 8, 16) if b < n_dp]
    enter(at, [at.fold(b) for b in bits[1:]])
    quad = QuadSum(at, t, r, (q1, q2))
    line = LineSum(at, pout, own, din, uin, (po_s, po_r, d_s, d_r, u_s, u_r), True)
    gather = QuadGather(at, gown, grad_ref, (g1, g2, g3))
    copies[0].wait()
    copies[1].wait()

    d = aw.shape[0]
    fold = fold_out.shape[2]
    per_row = d // fold

    def terms(q):
        rs = pl.ds(pl.multiple_of(q * part, part), part)
        width = 512

        @pl.loop(0, half_cols // width)
        def _(i):
            for half in range(2):
                d0 = pl.multiple_of(half * half_cols + i * width, width)
                v = dot(rhs[rs, 0 : 3 * hh], aw[pl.ds(d0, width), :], NT)
                t[half, q, :, pl.ds(pl.multiple_of(i * width, width), width)] = v.astype(BF)
                u = v * nin[rs, pl.ds(d0, width)].astype(F32)
                gsum[0:1, pl.ds(d0, width)] += jnp.sum(u, axis=0, keepdims=True)

    gsum[...] = jnp.zeros_like(gsum)
    copies[2].wait()
    masks = quad.masks()
    terms(at.quarter(masks[0]))
    quad.offer(masks[0])
    for cp in copies[3:5]:
        cp.wait()
    load_x = copies[5]

    def run(k, core):
        block = 2 * order_of(k, at) + (at.c if core else 1 - at.c)
        cols = pl.ds(pl.multiple_of(block * chunk, chunk), chunk)
        lhs[0] = nin[:, cols].T
        lhs[1] = low[:, cols].T

        def tile(i):
            return dot(lhs[lax.div(i, 3)], rhs[:, pl.ds(pl.multiple_of(i * hh, hh), hh)])

        if core:
            line.mine(k, tile)
        else:
            line.other(k, tile)

    n = at.n
    devs = [at.core] + [at.fold(b) for b in bits] + [at.peer(b) for b in at.bits]

    def fold_copy(b):
        return remote(fold_out.at[b], fold_in.at[b], fold_s.at[b], fold_r.at[b], devs[b])

    def fold_next(b):
        fold_copy(b).wait_recv()
        fold_out[b + 1] = fold_out[b] + fold_in[b]
        if b + 1 < len(devs):
            fold_copy(b + 1).start()

    run(0, 0)
    run(0, 1)
    for mask in masks[1:]:
        terms(at.quarter(mask))
        quad.offer(mask)
    gsum[0:1, :] = gsum[0:1, :] / gain_ref[0:1, :]
    gsum[1:2, :] = gmid_ref[...]
    for i in range(2):
        for j in range(per_row):
            fold_out[0, i * per_row + j] = gsum[i, j * fold : (j + 1) * fold]
    fold_copy(0).start()
    run(1, 0)
    run(1, 1)
    fold_next(0)
    for k in range(2, n):
        run(k, 0)
        run(k, 1)
    quad.turn()
    for b in range(1, len(bits)):
        fold_next(b)
    line.slot(0)
    quad.arrive()
    load_x.wait()
    copies[6].wait()
    fold_next(len(bits))
    @pl.loop(0, part // 32)
    def _(b):
        rs = pl.ds(pl.multiple_of(b * 32, 32), 32)
        v = x[rs, :].astype(F32)
        scale = lax.rsqrt(jnp.mean(v * v, axis=1, keepdims=True) + EPS)
        g = jnp.concatenate([quad.total(0, rs), quad.total(1, rs)], axis=1)
        unit = v * scale
        weighted = g * gain_ref[0:1, :]
        field = scale * (weighted - unit * jnp.mean(weighted * unit, axis=1, keepdims=True))
        total = (gh[rs, :] + field).astype(BF)
        gown[0, rs, :] = total[:, :half_cols]
        gown[1, rs, :] = total[:, half_cols:]

    for b in range(len(bits) + 1, len(devs) - 1):
        fold_next(b)
    gather.start()
    for s in range(1, n - 2):
        line.slot(s)
    fold_next(len(devs) - 1)
    gather.forward()
    for i in range(2):
        for j in range(per_row):
            gsum[i, j * fold : (j + 1) * fold] = fold_out[len(devs), i * per_row + j]
    gains_ref[...] = gsum[:, pl.ds(pl.multiple_of(at.dp * chunk, chunk), chunk)]
    stores = line.final(res, rs_ref, rs_s)
    gather.finish()
    for cp in stores:
        cp.wait()
    line.drain()
    quad.drain()
    for b in range(len(devs)):
        fold_copy(b).wait_send()


def last_stage(n_dp, n_mp, dqkv, aw, nin, low, att, x, gh, gain, gmid):
    seq, hh = att.shape
    d = aw.shape[0]
    n, part, chunk = n_dp // 2, seq // n_mp, d // n_dp
    dma = pltpu.SemaphoreType.DMA
    anyspace = pl.BlockSpec(memory_space=pl.ANY)
    vm = pl.BlockSpec(memory_space=pltpu.VMEM)
    folds = 1 + len([b for b in (1, 2, 4, 8) if b < n_mp]) + len([b for b in (2, 4, 8, 16) if b < n_dp])
    return pl.pallas_call(
        functools.partial(last_kernel, n_dp, n_mp),
        out_shape=[
            jax.ShapeDtypeStruct((4, chunk, hh), BF),
            jax.ShapeDtypeStruct((seq, d), BF),
            jax.ShapeDtypeStruct((8, chunk), F32),
        ],
        in_specs=[anyspace] * 7 + [vm] * 2,
        out_specs=[anyspace, anyspace, vm],
        scratch_shapes=[
            pltpu.VMEM((seq, 4 * hh), BF),
            pltpu.VMEM((d, 3 * hh), BF),
            pltpu.VMEM((seq, d), BF),
            pltpu.VMEM((seq, d), BF),
            pltpu.VMEM((2, chunk, seq), BF),
            pltpu.VMEM((part, d), BF),
            pltpu.VMEM((part, d), F32),
            pltpu.VMEM((4, chunk, hh), BF),
            dma((4,)),
            dma((7,)),
        ]
        + line_sum_scratch(n, 4, chunk, hh)
        + quad_sum_scratch(n_mp, part, d // 2)
        + quad_gather_scratch(n_mp, part, d // 2)
        + [
            pltpu.VMEM((8, d), F32),
            pltpu.VMEM((folds + 1, 8, d // 4), F32),
            pltpu.VMEM((folds, 8, d // 4), F32),
            dma((folds,)),
            dma((folds,)),
        ],
        compiler_params=pltpu.CompilerParams(
            collective_id=5, has_side_effects=True, vmem_limit_bytes=VMEM_LIMIT
        ),
        name="last_stage",
    )(dqkv, aw, nin, low, att, x, gh, gain, gmid)


def finish_kernel(
    low_ref,
    lay_ref,
    gu_ref,
    down_ref,
    attn_ref,
    gains_ref,
    lay_out,
    in_out,
    gate_out,
    up_out,
    down_out,
    q_out,
    k_out,
    v_out,
    o_out,
    g1_out,
    g2_out,
):
    lay_out[...] = lay_ref[...]
    in_out[...] = low_ref[...].astype(F32)
    half = gate_out.shape[1]
    gate_out[...] = gu_ref[0, :, :half].astype(F32)
    up_out[...] = gu_ref[0, :, half:].astype(F32)
    step = pl.program_id(0)

    @pl.when(lax.rem(step, 2) == 0)
    def _():
        down_out[...] = down_ref[0].T.astype(F32)

    @pl.when(step == 0)
    def _():
        for i, ref in enumerate((q_out, k_out, v_out)):
            ref[...] = attn_ref[i].astype(F32)
        o_out[...] = attn_ref[3].T.astype(F32)
        g1_out[...] = gains_ref[0]
        g2_out[...] = gains_ref[1]


def finish_stage(low, lay, gu, down, attn, gains):
    seq, d = low.shape
    steps, chunk, wide = gu.shape
    width, hh = down.shape[2], attn.shape[2]
    row = pl.BlockSpec((seq // (2 * steps), d), lambda i: (i, 0))
    fixed = lambda *shape: pl.BlockSpec(shape, lambda i: (0,) * len(shape))
    two = pl.BlockSpec((1, chunk // 2, wide), lambda i: (i // 2, i % 2, 0))
    piece = pl.BlockSpec((1, chunk, width), lambda i: (i // 2, 0, 0))
    cols = pl.BlockSpec((chunk // 2, wide // 2), lambda i: (i % 2, i // 2))
    f32 = lambda *shape: jax.ShapeDtypeStruct(shape, F32)
    return pl.pallas_call(
        finish_kernel,
        grid=(2 * steps,),
        in_specs=[row, row, two, piece, fixed(4, chunk, hh), fixed(*gains.shape)],
        out_specs=[row, row, cols, cols, pl.BlockSpec((width, chunk), lambda i: (i // 2, 0))]
        + [fixed(chunk, hh)] * 3
        + [fixed(hh, chunk)]
        + [fixed(chunk)] * 2,
        out_shape=[
            jax.ShapeDtypeStruct((seq, d), BF),
            f32(seq, d),
            f32(chunk, steps * wide // 2),
            f32(chunk, steps * wide // 2),
            f32(steps * width, chunk),
        ]
        + [f32(chunk, hh)] * 3
        + [f32(hh, chunk)]
        + [f32(chunk)] * 2,
        compiler_params=pltpu.CompilerParams(vmem_limit_bytes=VMEM_LIMIT),
        name="finish_stage",
    )(low, lay, gu, down, attn, gains)


def on_device(
    inputs,
    counts,
    cotangent,
    gain_attn,
    w_query,
    w_key,
    w_value,
    w_output,
    gain_ffn,
    w_gate,
    w_up,
    w_down,
):
    n_dp, n_mp = lax.axis_size("dp"), lax.axis_size("mp")
    gains = jnp.pad(jnp.stack([gain_attn, gain_ffn]), ((0, 6), (0, 0)))
    gains = gains.astype(BF).astype(F32)
    attn_w, qkv, attended, normed_in, gains, gu_shard, down_shard, grad_ffn = attn_stage(
        n_dp, n_mp, counts, gains, w_query, w_key, w_value, w_output, w_gate, w_up, w_down, inputs, cotangent
    )
    gu_w, normed_mid, hidden, gu, inner = gate_stage(
        n_dp, n_mp, attended, attn_w, gu_shard, inputs, gains
    )
    rs_down, ffn_terms, ggu = down_stage(n_dp, n_mp, inner, gu, grad_ffn, down_shard)
    rs_gu, grad_low, layer_out, grad_hidden, g_gain_mid, dqkv = mid_stage(
        n_dp, n_mp, ggu, gu_w, normed_mid, ffn_terms, grad_ffn, qkv, attn_w, counts, hidden, gains
    )
    rs_attn, grad_low_in, g_gains = last_stage(
        n_dp, n_mp, dqkv, attn_w, normed_in, grad_low, attended, inputs, grad_hidden, gains, g_gain_mid
    )
    lay, grad_x, g_gate, g_up, g_down, g_q, g_k, g_v, g_o, g_attn, g_ffn = finish_stage(
        grad_low_in, layer_out, rs_gu, rs_down, rs_attn, g_gains
    )
    return (lay, grad_x, g_attn, g_q, g_k, g_v, g_o, g_ffn, g_gate, g_up, g_down)


def solution(mesh):
    row, both, swapped = P("dp", None), P("dp", "mp"), P("mp", "dp")
    weights = (both, both, both, swapped)
    ffn = (both, both, swapped)
    return jax.shard_map(
        on_device,
        mesh=mesh,
        in_specs=(row, P("dp"), row, P("dp")) + weights + (P("dp"),) + ffn,
        out_specs=(row, row, P("dp")) + weights + (P("dp"),) + ffn,
        check_vma=False,
    )
```

```python
import functools
import math

import jax
import jax.numpy as jnp
from jax import lax
from jax.experimental import pallas as pl
from jax.experimental.pallas import tpu as pltpu
from jax.sharding import PartitionSpec as P

HD = 128
EPS = 1e-06
BF = jnp.bfloat16
F32 = jnp.float32
NT = (((1,), (1,)), ((), ()))
TN = (((0,), (0,)), ((), ()))
NN = (((1,), (0,)), ((), ()))


def dot(a, b, dims=NN):
    return lax.dot_general(a, b, dims, preferred_element_type=F32)


def logistic_block(q, k, seq):
    raw = dot(q, k, NT)
    shifted = math.log(seq) - raw * HD ** (-0.5)
    return 1.0 / (1.0 + jnp.exp(shifted))


def allowed_block(row0, rows, col0, cols, count):
    ri = row0 + lax.broadcasted_iota(jnp.int32, (rows, cols), 0)
    ci = col0 + lax.broadcasted_iota(jnp.int32, (rows, cols), 1)
    return (ci <= ri) & (ci < count)


MESH = pl.DeviceIdType.MESH
VMEM_LIMIT = 60 * 1024 * 1024
PIECES = 4
AHEAD = 1
DOWN_AHEAD = 2


def flipped(index, bit):
    return index + bit - 2 * bit * lax.rem(lax.div(index, bit), 2)


def spread(j, bits):
    return sum(bit for i, bit in enumerate(bits) if j >> i & 1)


class Place:
    def __init__(self, n_dp, n_mp):
        self.n = n_dp // 2
        self.dp = lax.axis_index("dp")
        self.m = lax.axis_index("mp")
        self.p = lax.div(self.dp, 2)
        self.c = lax.rem(self.dp, 2)
        self.above = (self.dp + 2, self.m)
        self.below = (self.dp - 2, self.m)
        self.core = (self.dp + 1 - 2 * self.c, self.m)
        self.bits = [b for b in (1, 2, 4, 8, 16) if b < n_mp]
        self.has_above = self.p < self.n - 1
        self.has_below = self.p > 0

    def fold(self, bit):
        return (flipped(self.dp, bit), self.m)

    def peer(self, bit):
        return (self.dp, flipped(self.m, bit))

    def quarter(self, mask):
        q = self.m
        for bit in self.bits:
            if mask & bit:
                q = flipped(q, bit)
        return q


def signal(dev):
    pl.semaphore_signal(pltpu.get_barrier_semaphore(), inc=1, device_id=dev, device_id_type=MESH)


def enter(at, extra=()):
    always = [at.core] + [at.peer(bit) for bit in at.bits] + list(extra)
    for dev in always:
        signal(dev)

    @pl.when(at.has_above)
    def _():
        signal(at.above)

    @pl.when(at.has_below)
    def _():
        signal(at.below)

    ends = at.has_above.astype(jnp.int32) + at.has_below.astype(jnp.int32)
    pl.semaphore_wait(pltpu.get_barrier_semaphore(), len(always) + ends)


def remote(src, dst, send, recv, dev):
    return pltpu.make_async_remote_copy(
        src_ref=src, dst_ref=dst, send_sem=send, recv_sem=recv, device_id=dev, device_id_type=MESH
    )


def part_rows(at, part):
    return pl.ds(pl.multiple_of(at.m * part, part), part)


def order_of(k, at):
    n, p = at.n, at.p
    if k == n - 1:
        return p
    high = jnp.where(k < p, k, n - 1 - k + p)
    low = jnp.where(k < n - 1 - p, n - 1 - k, k - (n - 1 - p))
    return jnp.where(2 * p >= n, high, low)


class LineSum:
    def __init__(self, at, pout, own, din, uin, sems, paced=False):
        self.paced = paced
        self.at, self.pout, self.own, self.din, self.uin = at, pout, own, din, uin
        self.po_s, self.po_r, self.d_s, self.d_r, self.u_s, self.u_r = sems
        self.slots, self.pieces = pout.shape[0], own.shape[1]

    def core_copy(self, k, i):
        j = order_of(k, self.at)
        slot = k % self.slots
        return remote(
            self.pout.at[slot, i],
            self.own.at[j, i],
            self.po_s.at[slot, i],
            self.po_r.at[k, i],
            self.at.core,
        )

    def down_copy(self, s, i):
        return remote(
            self.own.at[s, i], self.din.at[s, i], self.d_s.at[s, i], self.d_r.at[s, i], self.at.below
        )

    def up_copy(self, s, i):
        n = self.at.n
        return remote(
            self.own.at[n - 1 - s, i],
            self.uin.at[s, i],
            self.u_s.at[s, i],
            self.u_r.at[s, i],
            self.at.above,
        )

    def other(self, k, tile):
        @pl.loop(0, self.pieces)
        def _(i):
            if k >= self.slots:
                self.core_copy(k - self.slots, i).wait_send()
            self.pout[k % self.slots, i] = tile(i).astype(BF)
            self.core_copy(k, i).start()

    def mine(self, k, tile):
        at = self.at
        j = order_of(k, at)

        @pl.loop(0, self.pieces)
        def _(i):
            value = tile(i)
            self.core_copy(k, i).wait_recv()
            self.own[j, i] = (value + self.own[j, i].astype(F32)).astype(BF)
            if k < (1 if self.paced else at.n - 1):

                @pl.when(at.p == at.n - 1)
                def _():
                    self.down_copy(k, i).start()

                @pl.when(at.p == 0)
                def _():
                    self.up_copy(k, i).start()

    def add(self, dst, src):
        @pl.loop(0, dst.shape[0] // 64)
        def _(b):
            rs = pl.ds(pl.multiple_of(b * 64, 64), 64)
            dst[rs, :] = (dst[rs, :].astype(F32) + src[rs, :].astype(F32)).astype(BF)

    def slot(self, t):
        at = self.at
        n, p = at.n, at.p
        sd = t - (n - 2 - p)
        su = t - (p - 1)

        @pl.loop(0, self.pieces)
        def _(i):
            @pl.when((sd >= 0) & (sd < p) & at.has_above)
            def _():
                self.down_copy(sd, i).wait_recv()
                self.add(self.own.at[sd, i], self.din.at[sd, i])
                self.down_copy(sd, i).start()

            @pl.when((su >= 0) & (su < n - 1 - p) & at.has_below)
            def _():
                self.up_copy(su, i).wait_recv()
                self.add(self.own.at[n - 1 - su, i], self.uin.at[su, i])
                self.up_copy(su, i).start()

            if self.paced:

                @pl.when(p == n - 1)
                def _():
                    self.down_copy(t, i).wait_send()
                    self.down_copy(t + 1, i).start()

                @pl.when(p == 0)
                def _():
                    self.up_copy(t, i).wait_send()
                    self.up_copy(t + 1, i).start()

    def final(self, out, sink, sems):
        at = self.at
        n, p = at.n, at.p

        @pl.loop(0, self.pieces)
        def _(i):
            @pl.when(at.has_above)
            def _():
                self.down_copy(p, i).wait_recv()

            @pl.when(at.has_below)
            def _():
                self.up_copy(n - 1 - p, i).wait_recv()

            def close(parts):
                @pl.loop(0, out.shape[1] // 64)
                def _(b):
                    rs = pl.ds(pl.multiple_of(b * 64, 64), 64)
                    total = self.own[p, i, rs, :].astype(F32)
                    for ref, s in parts:
                        total = total + ref[s, i, rs, :].astype(F32)
                    out[i, rs, :] = total.astype(out.dtype)

            down, up = (self.din, p), (self.uin, n - 1 - p)

            @pl.when(at.has_above & at.has_below)
            def _():
                close([down, up])

            @pl.when(jnp.logical_not(at.has_below))
            def _():
                close([down])

            @pl.when(jnp.logical_not(at.has_above))
            def _():
                close([up])

            pltpu.make_async_copy(out.at[i], sink.at[i], sems.at[i]).start()

        return [
            pltpu.make_async_copy(out.at[i], sink.at[i], sems.at[i]) for i in range(self.pieces)
        ]

    def drain(self):
        at = self.at
        n, p = at.n, at.p
        for k in range(n - self.slots, n):
            for i in range(self.pieces):
                self.core_copy(k, i).wait_send()
        for s in range(n - 1):
            done = self.paced and s < n - 2

            @pl.when((s < p) & (at.has_above if done else at.has_below))
            def _():
                for i in range(self.pieces):
                    self.down_copy(s, i).wait_send()

            @pl.when((s < n - 1 - p) & (at.has_below if done else at.has_above))
            def _():
                for i in range(self.pieces):
                    self.up_copy(s, i).wait_send()


def line_sum_scratch(n, pieces, rows, cols, slots=2):
    dma = pltpu.SemaphoreType.DMA
    return [
        pltpu.VMEM((slots, pieces, rows, cols), BF),
        pltpu.VMEM((n, pieces, rows, cols), BF),
        pltpu.VMEM((n - 1, pieces, rows, cols), BF),
        pltpu.VMEM((n - 1, pieces, rows, cols), BF),
        dma((slots, pieces)),
        dma((n, pieces)),
        dma((n - 1, pieces)),
        dma((n - 1, pieces)),
        dma((n - 1, pieces)),
        dma((n - 1, pieces)),
    ]


class QuadSum:
    def __init__(self, at, t, r, sems):
        self.at, self.t, self.r = at, t, r
        self.s, self.v = sems
        self.blocks = self.s.shape[2]
        self.step = r.shape[2] // self.blocks
        self.order = [at.bits, at.bits[::-1]]
        self.levels = len(at.bits)
        self.seen = set()

    def count(self, k):
        return 1 << (self.levels - 1 - k)

    def slot(self, k, j):
        return sum(self.count(i) for i in range(k)) + j

    def rest(self, half, k):
        return self.order[half][k + 1 :]

    def index(self, half, k, mask):
        rest = self.rest(half, k)
        return self.slot(k, sum(1 << i for i, bit in enumerate(rest) if mask & bit))

    def source(self, half, mask):
        return self.t.at[half, self.at.quarter(mask)]

    def terms(self, half, mask, rs):
        return self.t[half, self.at.quarter(mask), rs, :].astype(F32)

    def split(self, k):
        return self.blocks if k == self.levels - 1 else 1

    def copy(self, half, k, j, block=0):
        bit = self.order[half][k]
        mask = bit + spread(j, self.rest(half, k))
        src = self.source(half, mask) if k == 0 else self.r.at[half, self.index(half, k - 1, mask)]
        at = self.slot(k, j)
        dst = self.r.at[half, at]
        if self.split(k) > 1:
            rows = pl.ds(block * self.step, self.step)
            src, dst = src.at[rows, :], dst.at[rows, :]
        send, recv = self.s.at[half, at, block], self.v.at[half, at, block]
        return remote(src, dst, send, recv, self.at.peer(bit))

    def offer(self, mask, only=(0, 1)):
        for half in only:
            if mask & self.order[half][0]:
                rest = self.rest(half, 0)
                self.copy(half, 0, sum(1 << i for i, b in enumerate(rest) if mask & b)).start()

    def masks(self):
        return sorted(range(1, 2 * self.count(0)), key=lambda m: -bin(m).count("1")) + [0]

    def come(self, half, k, mask, block=0):
        at = self.index(half, k, mask)
        block = min(block, self.split(k) - 1)
        if (half, at, block) not in self.seen:
            self.seen.add((half, at, block))
            self.copy(half, k, at - self.slot(k, 0), block).wait_recv()
        return at

    def turn(self):
        for k in range(1, self.levels):
            for block in range(self.split(k)):
                for half in range(2):
                    for j in range(self.count(k)):
                        self.pass_on(half, k, j, block)

    def pass_on(self, half, k, j, block):
        mask = self.order[half][k] + spread(j, self.rest(half, k))
        got = [self.come(half, i, mask) for i in range(k)]
        rows = self.r.shape[2] // self.split(k)

        @pl.loop(0, rows // 64)
        def _(b):
            rs = pl.ds(pl.multiple_of(block * rows + b * 64, 64), 64)
            total = self.terms(half, mask, rs)
            for i in got:
                total = total + self.r[half, i, rs, :].astype(F32)
            self.r[half, got[-1], rs, :] = total.astype(BF)

        self.copy(half, k, j, block).start()

    def arrive(self, block=0):
        self.got = [
            [self.come(half, k, 0, block) for k in range(self.levels)] for half in range(2)
        ]

    def total(self, half, rs):
        total = self.terms(half, 0, rs)
        for i in self.got[half]:
            total = total + self.r[half, i, rs, :].astype(F32)
        return total

    def drain(self):
        for half in range(2):
            for k in range(self.levels):
                for j in range(self.count(k)):
                    for block in range(self.split(k)):
                        self.copy(half, k, j, block).wait_send()


class QuadSumHbm(QuadSum):
    def __init__(self, at, hbm, t, r, sems):
        super().__init__(at, t, r, sems[:2])
        self.hbm = hbm
        self.loads = [
            pltpu.make_async_copy(
                self.source(half, spread(j, self.rest(half, 0))), t.at[half, j], sems[2].at[half, j]
            )
            for half in range(2)
            for j in range(self.count(0))
        ]

    def source(self, half, mask):
        rows, cols = self.t.shape[2], self.t.shape[3]
        rs = pl.ds(pl.multiple_of(self.at.quarter(mask) * rows, rows), rows)
        return self.hbm.at[rs, pl.ds(half * cols, cols)]

    def terms(self, half, mask, rs):
        return self.t[half, self.index(half, 0, mask), rs, :].astype(F32)


def quad_sum_scratch(mp, rows, cols, parts=None, blocks=1):
    dma = pltpu.SemaphoreType.DMA
    return [
        pltpu.VMEM((2, parts or mp, rows, cols), BF),
        pltpu.VMEM((2, mp - 1, rows, cols), BF),
        dma((2, mp - 1, blocks)),
        dma((2, mp - 1, blocks)),
    ]


class QuadGather:
    def __init__(self, at, own, out, sems):
        self.at, self.own, self.out = at, own, out
        self.s, self.v, self.here = sems
        self.blocks = self.s.shape[2]
        self.order = [at.bits[::-1], at.bits]
        self.levels = len(at.bits)
        self.seen = set()

    def mine(self, half, block):
        step = self.own.shape[1] // self.blocks
        return self.own.at[half, pl.ds(block * step, step), :]

    def spot(self, mask, half, block):
        rows, cols = self.own.shape[1], self.own.shape[2]
        step = rows // self.blocks
        rs = pl.ds(pl.multiple_of(self.at.quarter(mask) * rows + block * step, step), step)
        return self.out.at[rs, pl.ds(half * cols, cols)]

    def copy(self, half, k, j, block):
        mask = spread(j, self.order[half][:k])
        dst = self.spot(mask, half, block)
        src = self.mine(half, block) if j == 0 else dst
        at = (1 << k) - 1 + j
        dev = self.at.peer(self.order[half][k])
        return remote(src, dst, self.s.at[half, at, block], self.v.at[half, at, block], dev)

    def come(self, half, k, j, block):
        if (half, k, j, block) not in self.seen:
            self.seen.add((half, k, j, block))
            self.copy(half, k, j, block).wait_recv()

    def keep(self, half, block):
        return pltpu.make_async_copy(
            self.mine(half, block), self.spot(0, half, block), self.here.at[half, block]
        )

    def start(self, levels=None, block=0):
        for k in range(self.levels) if levels is None else levels:
            for half in range(2):
                self.copy(half, k, 0, block).start()
                if k == 0:
                    self.keep(half, block).start()

    def forward(self, block=0):
        for k in range(1, self.levels):
            for half in range(2):
                for j in range(1, 1 << k):
                    top = j.bit_length() - 1
                    self.come(half, top, j - (1 << top), block)
                    self.copy(half, k, j, block).start()

    def finish(self):
        for half in range(2):
            for block in range(self.blocks):
                for k in range(self.levels):
                    for j in range(1 << k):
                        self.come(half, k, j, block)
                        self.copy(half, k, j, block).wait_send()
                self.keep(half, block).wait()


def quad_gather_scratch(mp, rows, cols, blocks=1):
    dma = pltpu.SemaphoreType.DMA
    return [
        pltpu.VMEM((2, rows, cols), BF),
        dma((2, mp - 1, blocks)),
        dma((2, mp - 1, blocks)),
        dma((2, blocks)),
    ]


class LineGather:
    def __init__(self, at, pieces, shard, spot, sems, pre=0):
        self.pre = pre
        self.at, self.pieces, self.shard, self.spot = at, pieces, shard, spot
        self.d_s, self.d_r, self.u_s, self.u_r, self.c_s, self.c_r, self.here = sems

    def down_copy(self, h, i, own=False):
        b = 2 * (self.at.p + h) + self.at.c
        dst = self.spot(b, i)
        src = self.shard(i) if own and self.shard else dst
        return remote(src, dst, self.d_s.at[h, i], self.d_r.at[h, i], self.at.below)

    def up_copy(self, h, i, own=False):
        b = 2 * (self.at.p - h) + self.at.c
        dst = self.spot(b, i)
        src = self.shard(i) if own and self.shard else dst
        return remote(src, dst, self.u_s.at[h, i], self.u_r.at[h, i], self.at.above)

    def core_copy(self, z, i, own=False, incoming=False):
        b = 2 * z + (1 - self.at.c if incoming else self.at.c)
        dst = self.spot(b, i)
        src = self.shard(i) if own and self.shard else dst
        return remote(src, dst, self.c_s.at[z, i], self.c_r.at[z, i], self.at.core)

    def keep(self, i):
        at = self.at
        return pltpu.make_async_copy(self.shard(i), self.spot(at.dp, i), self.here.at[i])

    def start(self):
        at = self.at
        for i in range(self.pre, self.pieces):

            @pl.when(at.has_below)
            def _():
                self.down_copy(0, i, True).start()

            @pl.when(at.has_above)
            def _():
                self.up_copy(0, i, True).start()

        for i in range(self.pieces):
            self.core_copy(at.p, i, True).start()
            if self.shard:
                self.keep(i).start()

    def slot(self, h, i):
        at = self.at
        n, p = at.n, at.p

        @pl.when(p + h < n)
        def _():
            self.down_copy(h - 1, i).wait_recv()

            @pl.when(at.has_below)
            def _():
                self.down_copy(h, i).start()

            self.core_copy(p + h, i).start()

        @pl.when(p - h >= 0)
        def _():
            self.up_copy(h - 1, i).wait_recv()

            @pl.when(at.has_above)
            def _():
                self.up_copy(h, i).start()

            self.core_copy(p - h, i).start()

    def stage(self, h):
        @pl.loop(self.pre if h == 1 else 0, self.pieces)
        def _(i):
            self.slot(h, i)

    def early(self, i, above, below):
        at = self.at

        @pl.when(at.has_above)
        def _():
            b = 2 * at.p + 2 + at.c
            dst = self.spot(b, i)

            @pl.when(at.has_below)
            def _():
                remote(above, dst, self.d_s.at[1, i], self.d_r.at[1, i], at.below).start()

            z = at.p + 1
            remote(above, dst, self.c_s.at[z, i], self.c_r.at[z, i], at.core).start()

        @pl.when(at.has_below)
        def _():
            b = 2 * at.p - 2 + at.c
            dst = self.spot(b, i)

            @pl.when(at.has_above)
            def _():
                remote(below, dst, self.u_s.at[1, i], self.u_r.at[1, i], at.above).start()

            z = at.p - 1
            remote(below, dst, self.c_s.at[z, i], self.c_r.at[z, i], at.core).start()

    def ready(self, z, i):
        self.core_copy(z, i, incoming=True).wait_recv()

    def drain(self):
        at = self.at
        n, p = at.n, at.p

        @pl.loop(0, self.pieces)
        def _(i):
            for h in range(n):

                sent = (i >= self.pre) if h == 0 else True

                @pl.when((p + h < n) & at.has_below & sent)
                def _():
                    self.down_copy(h, i, h == 0).wait_send()

                @pl.when((p - h >= 0) & at.has_above & sent)
                def _():
                    self.up_copy(h, i, h == 0).wait_send()

            for z in range(n):
                self.core_copy(z, i).wait_send()


def line_gather_scratch(n, pieces):
    dma = pltpu.SemaphoreType.DMA
    return [dma((n, pieces))] * 6 + [dma((pieces,))]


def rows_spot(out, rows, width):
    def spot(b, i):
        rs = pl.ds(pl.multiple_of(b * rows, rows), rows)
        return out.at[rs, pl.ds(pl.multiple_of(i * width, width), width)]

    return spot


def cols_of(ref, width, base=0):
    return lambda i: ref.at[:, pl.ds(pl.multiple_of(base + i * width, width), width)]


class Presend:
    def __init__(self, at, src, got, sems):
        s, r = sems
        self.at = at
        self.down = remote(src, got.at[0], s.at[0], r.at[0], at.below)
        self.up = remote(src, got.at[1], s.at[1], r.at[1], at.above)

    def start(self):
        pl.when(self.at.has_below)(self.down.start)
        pl.when(self.at.has_above)(self.up.start)

    def finish(self):
        pl.when(self.at.has_above)(self.down.wait_recv)
        pl.when(self.at.has_below)(self.up.wait_recv)
        pl.when(self.at.has_below)(self.down.wait_send)
        pl.when(self.at.has_above)(self.up.wait_send)


def attend_rows(qkv, out, seq, hh, count, head):
    cols = lambda first: pl.ds(pl.multiple_of(first + head * HD, HD), HD)
    blk = 256
    for i in range(seq // blk):
        rows = pl.ds(i * blk, blk)
        span = (i + 1) * blk
        lg = logistic_block(qkv[rows, cols(0)], qkv[pl.ds(0, span), cols(hh)], seq)
        w = jnp.where(allowed_block(i * blk, blk, 0, span, count), lg, 0.0).astype(BF)
        out[rows, cols(0)] = dot(w, qkv[pl.ds(0, span), cols(2 * hh)]).astype(BF)


def attn_kernel(
    n_dp,
    n_mp,
    count_ref,
    ga_ref,
    gf_ref,
    wq_hbm,
    wk_hbm,
    wv_hbm,
    wo_hbm,
    wg_hbm,
    wu_hbm,
    wd_hbm,
    x_hbm,
    cot_hbm,
    aw_ref,
    qkv_ref,
    att_ref,
    nin_ref,
    gains_ref,
    gush_ref,
    dnsh_ref,
    cotm_ref,
    gpre_ref,
    gains_in,
    w4,
    wo,
    shard,
    x,
    qkv,
    wbuf,
    wgu,
    wd,
    gush,
    dnsh,
    cot,
    load_s,
    wb_s,
    out_s,
    *rest,
):
    at = Place(n_dp, n_mp)
    n = at.n
    chunk, hh = wq_hbm.shape
    seq, d = x.shape
    ff = wgu.shape[2]
    loads = [
        pltpu.make_async_copy(src, dst, load_s.at[i])
        for i, (src, dst) in enumerate(
            [
                (wq_hbm, w4.at[0]),
                (wk_hbm, w4.at[1]),
                (wv_hbm, w4.at[2]),
                (wo_hbm, wo),
                (x_hbm, x),
                (wg_hbm, wgu.at[0]),
                (wu_hbm, wgu.at[1]),
                (wd_hbm, wd),
                (cot_hbm, cot),
            ]
        )
    ]
    for cp in loads:
        cp.start()
    spot = rows_spot(aw_ref, chunk, hh)
    three = LineGather(at, 3, cols_of(shard, hh), spot, rest[0:7])
    last = LineGather(
        at, 1, lambda i: shard.at[:, pl.ds(3 * hh, hh)], lambda b, i: spot(b, 3), rest[7:14]
    )
    small = LineGather(
        at,
        1,
        lambda i: gains_in,
        lambda b, i: gains_ref.at[:, pl.ds(pl.multiple_of(b * chunk, chunk), chunk)],
        rest[14:21],
    )
    for i, ref in enumerate((ga_ref, gf_ref)):
        gains_in[i, :] = ref[...].astype(BF).astype(F32)
    enter(at)
    small.start()
    for i in range(3):
        loads[i].wait()
        shard[:, i * hh : (i + 1) * hh] = w4[i].astype(BF)
    three.start()
    loads[3].wait()
    shard[:, 3 * hh :] = wo[...].T.astype(BF)
    small.slot(1, 0)
    loads[5].wait()
    loads[6].wait()
    half = ff // PIECES

    @pl.loop(0, PIECES)
    def _(i):
        cols = pl.ds(pl.multiple_of(i * half, half), half)
        for k in range(2):
            to = pl.ds(pl.multiple_of((2 * i + k) * half, half), half)
            gush[:, to] = wgu[k, :, cols].astype(BF)

    outs = [pltpu.make_async_copy(gush, gush_ref, out_s.at[0])]
    outs[0].start()
    loads[7].wait()

    @pl.loop(0, ff // 256)
    def _(i):
        rs = pl.ds(pl.multiple_of(i * 256, 256), 256)
        dnsh[:, rs] = wd[rs, :].T.astype(BF)

    outs.append(pltpu.make_async_copy(dnsh, dnsh_ref, out_s.at[2]))
    outs[-1].start()
    loads[8].wait()
    count = count_ref[0]

    @pl.loop(0, seq // 32)
    def _(b):
        rs = pl.ds(pl.multiple_of(b * 32, 32), 32)
        row = b * 32 + lax.broadcasted_iota(jnp.int32, (32, d), 0)
        cot[rs, :] = jnp.where(row < count, cot[rs, :].astype(F32), 0.0).astype(BF)

    outs.append(pltpu.make_async_copy(cot, cotm_ref, out_s.at[3]))
    outs[-1].start()
    for h in range(1, n - 1):
        small.slot(h + 1, 0)
        three.stage(h)
        if h == n - 2:
            last.start()
    small.keep(0).wait()
    for z in range(n):
        small.ready(z, 0)
    loads[4].wait()

    @pl.loop(0, seq // 32)
    def _(b):
        rs = pl.ds(pl.multiple_of(b * 32, 32), 32)
        v = x[rs, :].astype(F32)
        scale = lax.rsqrt(jnp.mean(v * v, axis=1, keepdims=True) + EPS)
        x[rs, :] = (v * scale * gains_ref[0:1, :]).astype(BF)

    outs.append(pltpu.make_async_copy(x, nin_ref, out_s.at[1]))
    outs[-1].start()

    def w_copy(i):
        cols = pl.ds(pl.multiple_of(i * hh, hh), hh)
        return pltpu.make_async_copy(aw_ref.at[:, cols], wbuf.at[i], wb_s.at[i])

    for i in range(3):
        three.slot(n - 1, i)
        three.keep(i).wait()
        for z in range(n):
            three.ready(z, i)
        w_copy(i).start()
        if i == 1:
            last.slot(1, 0)
        w_copy(i).wait()

        @pl.loop(0, seq // 256)
        def _(b):
            rs = pl.ds(pl.multiple_of(b * 256, 256), 256)
            qkv[rs, i * hh : (i + 1) * hh] = dot(x[rs, :], wbuf[i]).astype(BF)

    outs.append(pltpu.make_async_copy(qkv, qkv_ref, out_s.at[4]))
    outs[-1].start()
    for h in range(2, n - 1):
        last.slot(h, 0)
    ahead = Presend(at, gush.at[:, pl.ds(0, 2 * half * AHEAD)], gpre_ref, rest[21:23])
    ahead.start()
    heads = hh // HD

    @pl.loop(0, heads // 2)
    def _(head):
        attend_rows(qkv, att_ref, seq, hh, count, head)

    last.slot(n - 1, 0)

    @pl.loop(heads // 2, heads)
    def _(head):
        attend_rows(qkv, att_ref, seq, hh, count, head)

    last.keep(0).wait()
    for z in range(n):
        last.ready(z, 0)
    for cp in outs:
        cp.wait()
    ahead.finish()
    small.drain()
    three.drain()
    last.drain()


def attn_stage(n_dp, n_mp, counts, ga, gf, wq, wk, wv, wo, wg, wu, wd, x, cot):
    seq, d = x.shape
    chunk, hh = wq.shape
    ff = wg.shape[1]
    n = n_dp // 2
    dma = pltpu.SemaphoreType.DMA
    hbm = pl.BlockSpec(memory_space=pl.ANY)
    vm = pl.BlockSpec(memory_space=pltpu.VMEM)
    shapes = [
        ((d, 4 * hh), BF),
        ((seq, 3 * hh), BF),
        ((seq, hh), BF),
        ((seq, d), BF),
        ((8, d), F32),
        ((chunk, 2 * ff), BF),
        ((chunk, ff), BF),
        ((seq, d), BF),
        ((2, chunk, 2 * ff * AHEAD // PIECES), BF),
    ]
    return pl.pallas_call(
        functools.partial(attn_kernel, n_dp, n_mp),
        out_shape=[jax.ShapeDtypeStruct(*s) for s in shapes],
        in_specs=[pl.BlockSpec(memory_space=pltpu.SMEM), vm, vm] + [hbm] * 9,
        out_specs=[hbm, hbm, vm, hbm, vm, hbm, hbm, hbm, hbm],
        scratch_shapes=[
            pltpu.VMEM((8, chunk), F32),
            pltpu.VMEM((3, chunk, hh), F32),
            pltpu.VMEM((hh, chunk), F32),
            pltpu.VMEM((chunk, 4 * hh), BF),
            pltpu.VMEM((seq, d), BF),
            pltpu.VMEM((seq, 3 * hh), BF),
            pltpu.VMEM((3, d, hh), BF),
            pltpu.VMEM((2, chunk, ff), F32),
            pltpu.VMEM((ff, chunk), F32),
            pltpu.VMEM((chunk, 2 * ff), BF),
            pltpu.VMEM((chunk, ff), BF),
            pltpu.VMEM((seq, d), BF),
            dma((9,)),
            dma((3,)),
            dma((5,)),
        ]
        + line_gather_scratch(n, 3)
        + line_gather_scratch(n, 1) * 2
        + [dma((2,))] * 2,
        compiler_params=pltpu.CompilerParams(
            collective_id=1, has_side_effects=True, vmem_limit_bytes=VMEM_LIMIT
        ),
        name="attn_stage",
    )(counts, ga, gf, wq, wk, wv, wo, wg, wu, wd, x, cot)


def gate_kernel(
    n_dp,
    n_mp,
    att_ref,
    aw_hbm,
    sh_hbm,
    gpre_hbm,
    dnsh_hbm,
    x_hbm,
    gain_ref,
    gw_ref,
    nm_ref,
    hid_hbm,
    gu_ref,
    inner_ref,
    dpre_ref,
    wo,
    gp,
    sh,
    xs,
    hid,
    acc,
    nm,
    wbuf,
    gbuf,
    ibuf,
    gp_s,
    load_s,
    wb_s,
    gb_s,
    ib_s,
    *rest,
):
    at = Place(n_dp, n_mp)
    n = at.n
    quad = QuadSum(at, *rest[0:2], rest[2:4])
    gather_nm = QuadGather(at, rest[4], nm_ref, rest[5:8])
    sems = rest[8:15]
    hh = wo.shape[1]
    part, half_cols = quad.t.shape[2], quad.t.shape[3]
    chunk, wide = sh_hbm.shape
    pieces = sems[6].shape[0]
    width = wide // pieces
    line = LineGather(at, pieces, cols_of(sh, width), rows_spot(gw_ref, chunk, width), sems, AHEAD)

    load_sh = pltpu.make_async_copy(sh_hbm, sh, load_s.at[2])
    load_sh.start()
    load_gp = pltpu.make_async_copy(gpre_hbm, gp, load_s.at[3])
    load_gp.start()
    load = pltpu.make_async_copy(aw_hbm.at[:, pl.ds(3 * hh, hh)], wo, load_s.at[0])
    load.start()
    load_x = pltpu.make_async_copy(x_hbm.at[part_rows(at, part), :], xs, load_s.at[1])
    load_x.start()
    enter(at)
    load_sh.wait()
    line.start()
    load_gp.wait()

    def place(side, i):
        b = at.dp + (2 if side == 0 else -2)
        piece = gp.at[side, :, pl.ds(i * width, width)]
        return pltpu.make_async_copy(piece, line.spot(b, i), gp_s.at[side, i])

    for i in range(AHEAD):
        line.early(i, *[gp.at[side, :, pl.ds(i * width, width)] for side in range(2)])
        pl.when(at.has_above)(place(0, i).start)
        pl.when(at.has_below)(place(1, i).start)
    load.wait()

    def terms(q):
        rs = pl.ds(pl.multiple_of(q * part, part), part)
        for half in range(2):
            w = wo[half * half_cols : (half + 1) * half_cols, :]
            quad.t[half, q] = dot(att_ref[rs, :], w, NT).astype(BF)

    for mask in quad.masks():
        terms(at.quarter(mask))
        quad.offer(mask)
    quad.turn()
    quad.arrive()
    load_x.wait()

    @pl.loop(0, part // 32)
    def _(b):
        rs = pl.ds(pl.multiple_of(b * 32, 32), 32)
        h = xs[rs, :].astype(F32) + jnp.concatenate(
            [quad.total(0, rs), quad.total(1, rs)], axis=1
        )
        hid[rs, :] = h
        scale = lax.rsqrt(jnp.mean(h * h, axis=1, keepdims=True) + EPS)
        res = (h * scale * gain_ref[1:2, :]).astype(BF)
        gather_nm.own[0, rs, :] = res[:, :half_cols]
        gather_nm.own[1, rs, :] = res[:, half_cols:]

    gather_nm.start()
    store_hid = pltpu.make_async_copy(hid, hid_hbm, load_s.at[1])
    store_hid.start()
    line.stage(1)
    gather_nm.forward()
    gather_nm.finish()
    load = pltpu.make_async_copy(nm_ref, nm, load_s.at[0])
    load.start()
    for h in range(2, n - 1):
        line.stage(h)
    load.wait()

    for i in range(AHEAD):
        pl.when(at.has_above)(place(0, i).wait)
        pl.when(at.has_below)(place(1, i).wait)
    ahead = Presend(
        at, dnsh_hbm.at[:, pl.ds(0, width // 2 * DOWN_AHEAD)], dpre_ref, rest[15:17]
    )
    ahead.start()

    pair = 2 * chunk
    near = jnp.where(2 * at.p < n, 0, 1)
    far = jnp.where(2 * at.p < n, n - 1, 0)
    most = (n - 1) * pair
    most_rows = pl.ds(pl.multiple_of(near * pair, pair), most)
    far_rows = pl.ds(pl.multiple_of(far * pair, pair), pair)

    def w_copy(i, slot, rows):
        cols = pl.ds(pl.multiple_of(i * width, width), width)
        return pltpu.make_async_copy(
            gw_ref.at[rows, cols], wbuf.at[slot, rows, :], wb_s.at[slot]
        )

    def first_part(i, slot):
        line.keep(i).wait()

        @pl.loop(0, n - 1)
        def _(z):
            line.ready(near + z, i)

        w_copy(i, slot, most_rows).start()
        w_copy(i, slot, most_rows).wait()

        @pl.loop(0, nm.shape[0] // 256)
        def _(b):
            rs = pl.ds(pl.multiple_of(b * 256, 256), 256)
            acc[rs, :] = dot(nm[rs, most_rows], wbuf[slot, most_rows, :])

    def g_copy(i, slot):
        cols = pl.ds(pl.multiple_of(i * width, width), width)
        return pltpu.make_async_copy(gbuf.at[slot], gu_ref.at[:, cols], gb_s.at[slot])

    def i_copy(i, slot):
        cols = pl.ds(pl.multiple_of(i * (width // 2), width // 2), width // 2)
        return pltpu.make_async_copy(ibuf.at[slot], inner_ref.at[:, cols], ib_s.at[slot])

    @pl.loop(0, pieces)
    def _(i):
        slot = lax.rem(i, 2)
        first_part(i, slot)
        line.slot(n - 1, i)
        line.ready(far, i)
        w_copy(i, slot, far_rows).start()

        @pl.when(i >= 2)
        def _():
            g_copy(i - 2, slot).wait()
            i_copy(i - 2, slot).wait()

        w_copy(i, slot, far_rows).wait()

        @pl.loop(0, nm.shape[0] // 256)
        def _(b):
            rs = pl.ds(pl.multiple_of(b * 256, 256), 256)
            v = (acc[rs, :] + dot(nm[rs, far_rows], wbuf[slot, far_rows, :])).astype(BF)
            gbuf[slot, rs, :] = v
            g = v[:, : width // 2].astype(F32)
            u = v[:, width // 2 :].astype(F32)
            ibuf[slot, rs, :] = (g / (1.0 + jnp.exp(-g)) * u).astype(BF)

        g_copy(i, slot).start()
        i_copy(i, slot).start()

    for i in range(max(0, pieces - 2), pieces):
        g_copy(i, i % 2).wait()
        i_copy(i, i % 2).wait()
    store_hid.wait()
    ahead.finish()
    line.drain()
    quad.drain()


def gate_stage(n_dp, n_mp, att, aw, shard, gpre, dnsh, x, gain):
    seq, hh = att.shape
    d = aw.shape[0]
    chunk, wide = shard.shape
    n, part = n_dp // 2, seq // n_mp
    dma = pltpu.SemaphoreType.DMA
    hbm = pl.BlockSpec(memory_space=pl.ANY)
    vm = pl.BlockSpec(memory_space=pltpu.VMEM)
    width = wide // PIECES
    return pl.pallas_call(
        functools.partial(gate_kernel, n_dp, n_mp),
        out_shape=[
            jax.ShapeDtypeStruct((d, wide), BF),
            jax.ShapeDtypeStruct((seq, d), BF),
            jax.ShapeDtypeStruct((part, d), F32),
            jax.ShapeDtypeStruct((seq, wide), BF),
            jax.ShapeDtypeStruct((seq, wide // 2), BF),
            jax.ShapeDtypeStruct((2, chunk, width // 2 * DOWN_AHEAD), BF),
        ],
        in_specs=[vm, hbm, hbm, hbm, hbm, hbm, vm],
        out_specs=[hbm] * 6,
        scratch_shapes=[
            pltpu.VMEM((d, hh), BF),
            pltpu.VMEM((2, chunk, width * AHEAD), BF),
            pltpu.VMEM((chunk, wide), BF),
            pltpu.VMEM((part, d), BF),
            pltpu.VMEM((part, d), F32),
            pltpu.VMEM((seq, width), F32),
            pltpu.VMEM((seq, d), BF),
            pltpu.VMEM((2, d, width), BF),
            pltpu.VMEM((2, seq, width), BF),
            pltpu.VMEM((2, seq, width // 2), BF),
            dma((2, AHEAD)),
            dma((4,)),
            dma((2,)),
            dma((2,)),
            dma((2,)),
        ]
        + quad_sum_scratch(n_mp, part, d // 2)
        + quad_gather_scratch(n_mp, part, d // 2)
        + line_gather_scratch(n, PIECES)
        + [dma((2,))] * 2,
        compiler_params=pltpu.CompilerParams(
            collective_id=2, has_side_effects=True, vmem_limit_bytes=VMEM_LIMIT
        ),
        name="gate_stage",
    )(att, aw, shard, gpre, dnsh, x, gain)


def down_kernel(
    n_dp,
    n_mp,
    inner_hbm,
    gu_hbm,
    cot_hbm,
    sh_hbm,
    dpre_hbm,
    rs_ref,
    ft_ref,
    ggu_ref,
    inner,
    gu,
    cot,
    dn,
    acc,
    ftb,
    res,
    dp_s,
    load_s,
    cot_s,
    in_s,
    rs_s,
    ft_s,
    dn_s,
    gg_s,
    *rest,
):
    at = Place(n_dp, n_mp)
    n, p = at.n, at.p
    line = LineSum(at, *rest[0:4], rest[4:10])
    sems = rest[10:17]
    chunk, ff = sh_hbm.shape
    pieces = sems[6].shape[0]
    width = ff // pieces
    gather = LineGather(at, pieces, None, rows_spot(dn, chunk, width), sems, DOWN_AHEAD)
    pair = 2 * chunk
    def cot_copy(k):
        cols = pl.ds(pl.multiple_of(order_of(k, at) * pair, pair), pair)
        return pltpu.make_async_copy(cot_hbm.at[:, cols], cot.at[:, cols], cot_s.at[k])

    def in_copy(i):
        cols = pl.ds(pl.multiple_of(i * width, width), width)
        return pltpu.make_async_copy(inner_hbm.at[:, cols], inner.at[:, cols], in_s.at[i])

    load_gu = pltpu.make_async_copy(gu_hbm, gu, load_s.at[0])
    own = pltpu.make_async_copy(
        sh_hbm, dn.at[pl.ds(pl.multiple_of(at.dp * chunk, chunk), chunk), :], dn_s.at[0]
    )
    own.start()

    def pre_copy(side):
        b = at.dp + (2 if side == 0 else -2)
        rows = pl.ds(pl.multiple_of(b * chunk, chunk), chunk)
        dst = dn.at[rows, pl.ds(0, width * DOWN_AHEAD)]
        return pltpu.make_async_copy(dpre_hbm.at[side], dst, dp_s.at[side])

    pl.when(at.has_above)(pre_copy(0).start)
    pl.when(at.has_below)(pre_copy(1).start)
    cot_copy(0).start()
    for i in range(pieces):
        in_copy(i).start()
    for k in range(1, n):
        cot_copy(k).start()
    load_gu.start()
    enter(at)
    own.wait()
    gather.start()
    pl.when(at.has_above)(pre_copy(0).wait)
    pl.when(at.has_below)(pre_copy(1).wait)
    for i in range(DOWN_AHEAD):
        gather.early(i, gather.spot(at.dp + 2, i), gather.spot(at.dp - 2, i))

    def run(e):
        k, core = e // 2, e % 2
        block = 2 * order_of(k, at) + (1 - at.c if core == 0 else at.c)
        if core == 0:
            cot_copy(k).wait()
        lhs = cot[:, pl.ds(pl.multiple_of(block * chunk, chunk), chunk)].T

        def tile(i):
            if e == 0:
                in_copy(i).wait()
            return dot(lhs, inner[:, pl.ds(pl.multiple_of(i * width, width), width)])

        if core == 0:
            line.other(k, tile)
        else:
            line.mine(k, tile)

    for e in range(2 * n):
        run(e)

    def ft_copy(z, slot):
        cols = pl.ds(pl.multiple_of(z * pair, pair), pair)
        return pltpu.make_async_copy(ftb.at[slot], ft_ref.at[:, cols], ft_s.at[slot])

    def rows_of(z):
        return pl.ds(pl.multiple_of(z * pair, pair), pair)

    def grads(z, fresh):
        @pl.loop(0, pieces)
        def _(i):
            gather.ready(z, i)

        @pl.loop(0, ff // 512)
        def _(i):
            cols = pl.ds(pl.multiple_of(i * 512, 512), 512)
            v = dot(cot[:, rows_of(z)], dn[rows_of(z), cols])
            acc[:, cols] = v if fresh else acc[:, cols] + v

    def branch(z, fresh):
        if not fresh:
            ft_copy(z, 0).wait()
        ftb[0] = dot(inner[...], dn[rows_of(z), :], NT).astype(BF)
        ft_copy(z, 0).start()

    grads(p, True)
    branch(p, True)
    load_gu.wait()
    half = width

    def cols_at(i):
        g = pl.ds(pl.multiple_of(i * 2 * half, half), half)
        u = pl.ds(pl.multiple_of(i * 2 * half + half, half), half)
        return g, u, pl.ds(pl.multiple_of(i * half, half), half)

    @pl.loop(0, pieces)
    def _(i):
        gcols, ucols, _ = cols_at(i)

        @pl.loop(0, gu.shape[0] // 64)
        def _(b):
            rs = pl.ds(pl.multiple_of(b * 64, 64), 64)
            g = gu[rs, gcols].astype(F32)
            u = gu[rs, ucols].astype(F32)
            sg = 1.0 / (1.0 + jnp.exp(-g))
            gu[rs, gcols] = (u * sg * (1.0 + g * (1.0 - sg))).astype(BF)
            gu[rs, ucols] = (g * sg).astype(BF)

    for h in range(1, n - 1):
        gather.stage(h)

        @pl.when(p + h < n)
        def _():
            grads(p + h, False)
            branch(p + h, False)

        @pl.when(p - h >= 0)
        def _():
            grads(p - h, False)
            branch(p - h, False)

        line.slot(h - 1)

    gather.stage(n - 1)

    @pl.when(jnp.logical_not(at.has_below))
    def _():
        grads(n - 1, False)

    @pl.when(jnp.logical_not(at.has_above))
    def _():
        grads(0, False)

    def gg_copy(i):
        cols = pl.ds(pl.multiple_of(i * 2 * half, 2 * half), 2 * half)
        return pltpu.make_async_copy(gu.at[:, cols], ggu_ref.at[:, cols], gg_s.at[i])

    @pl.loop(0, pieces)
    def _(i):
        gcols, ucols, acols = cols_at(i)

        @pl.loop(0, gu.shape[0] // 64)
        def _(b):
            rs = pl.ds(pl.multiple_of(b * 64, 64), 64)
            gi = acc[rs, acols]
            gu[rs, gcols] = (gi * gu[rs, gcols].astype(F32)).astype(BF)
            gu[rs, ucols] = (gi * gu[rs, ucols].astype(F32)).astype(BF)

        gg_copy(i).start()

    @pl.when(jnp.logical_not(at.has_below))
    def _():
        branch(n - 1, False)

    @pl.when(jnp.logical_not(at.has_above))
    def _():
        branch(0, False)

    stores = line.final(res, rs_ref, rs_s)
    for i in range(pieces):
        gg_copy(i).wait()
    ft_copy(p, 0).wait()
    for cp in stores:
        cp.wait()
    line.drain()
    gather.drain()


def down_stage(n_dp, n_mp, inner, gu, cot, shard, dpre):
    seq, d = cot.shape
    chunk, ff = shard.shape
    n = n_dp // 2
    dma = pltpu.SemaphoreType.DMA
    hbm = pl.BlockSpec(memory_space=pl.ANY)
    return pl.pallas_call(
        functools.partial(down_kernel, n_dp, n_mp),
        out_shape=[
            jax.ShapeDtypeStruct((PIECES, chunk, ff // PIECES), BF),
            jax.ShapeDtypeStruct((seq, d), BF),
            jax.ShapeDtypeStruct((seq, 2 * ff), BF),
        ],
        in_specs=[hbm] * 5,
        out_specs=[hbm] * 3,
        scratch_shapes=[
            pltpu.VMEM((seq, ff), BF),
            pltpu.VMEM((seq, 2 * ff), BF),
            pltpu.VMEM((seq, d), BF),
            pltpu.VMEM((d, ff), BF),
            pltpu.VMEM((seq, ff), F32),
            pltpu.VMEM((1, seq, 2 * chunk), BF),
            pltpu.VMEM((PIECES, chunk, ff // PIECES), BF),
            dma((2,)),
            dma((1,)),
            dma((n,)),
            dma((PIECES,)),
            dma((PIECES,)),
            dma((1,)),
            dma((1,)),
            dma((PIECES,)),
        ]
        + line_sum_scratch(n, PIECES, chunk, ff // PIECES)
        + line_gather_scratch(n, PIECES),
        compiler_params=pltpu.CompilerParams(
            collective_id=3, has_side_effects=True, vmem_limit_bytes=VMEM_LIMIT
        ),
        name="down_stage",
    )(inner, gu, cot, shard, dpre)


def mid_kernel(
    n_dp,
    n_mp,
    ggu_hbm,
    gw_hbm,
    nm_hbm,
    ft_hbm,
    cot_hbm,
    qkv_hbm,
    aw_hbm,
    count_ref,
    hid_hbm,
    gain_ref,
    rs_ref,
    low_ref,
    lay_ref,
    gh_hbm,
    gg_ref,
    dq_ref,
    space,
    wt,
    wt_s,
    nm,
    nm_s,
    cot,
    hid,
    gh,
    res,
    gg_s,
    rs_s,
    dka,
    dva,
    load_s,
    *rest,
):
    at = Place(n_dp, n_mp)
    n = at.n
    line = LineSum(at, *rest[0:4], rest[4:10])
    mid = QuadSum(at, *rest[10:12], rest[12:14])
    lay = QuadSumHbm(at, ft_hbm, *rest[14:16], rest[16:19])
    gather_low = QuadGather(at, rest[19], low_ref, rest[20:23])
    gather_lay = QuadGather(at, rest[23], lay_ref, rest[24:27])
    part, half_cols = mid.t.shape[2], mid.t.shape[3]
    chunk, width = line.own.shape[2], line.own.shape[3]
    pieces = line.pieces
    hh = qkv_hbm.shape[1] // 3
    drows = wt.shape[1]
    tiles = half_cols // drows

    wide = ggu_hbm.shape[1]
    ggu = space.at[:, pl.ds(0, wide)]

    def gg_copy(i):
        cols = pl.ds(pl.multiple_of(i * width, width), width)
        return pltpu.make_async_copy(ggu_hbm.at[:, cols], ggu.at[:, cols], gg_s.at[i])

    load_cot = pltpu.make_async_copy(cot_hbm.at[part_rows(at, part), :], cot, load_s.at[1])

    def nm_copy(e):
        k, core = e // 2, e % 2
        block = 2 * order_of(k, at) + (1 - at.c if core == 0 else at.c)
        cols = pl.ds(pl.multiple_of(block * chunk, chunk), chunk)
        return pltpu.make_async_copy(nm_hbm.at[:, cols], nm.at[e % 2], nm_s.at[e % 2])

    def wt_copy(half, i, slot):
        rows = pl.ds(pl.multiple_of(half * half_cols + i * drows, drows), drows)
        return pltpu.make_async_copy(gw_hbm.at[rows, :], wt.at[slot], wt_s.at[slot])

    nm_copy(0).start()
    for i in range(pieces):
        gg_copy(i).start()
    wt_copy(0, 0, 0).start()
    load_cot.start()
    load_hid = pltpu.make_async_copy(hid_hbm, hid, load_s.at[0])
    load_hid.start()
    for cp in lay.loads:
        cp.start()
    enter(at)
    for mask in lay.masks():
        lay.offer(mask)

    def run(e):
        if e + 1 < 2 * n:
            nm_copy(e + 1).start()
        nm_copy(e).wait()
        lhs = nm[e % 2].T

        def tile(i):
            if e == 0:
                gg_copy(i).wait()
            return dot(lhs, ggu[:, pl.ds(pl.multiple_of(i * width, width), width)])

        if e % 2 == 0:
            line.other(e // 2, tile)
        else:
            line.mine(e // 2, tile)

    def terms(half):
        @pl.loop(0, tiles)
        def _(i):
            slot = lax.rem(i, 2)
            if half == 0:
                nxt = wt_copy(jnp.where(i + 1 < tiles, 0, 1), lax.rem(i + 1, tiles), 1 - slot)
                nxt.start()
            else:

                @pl.when(i + 1 < tiles)
                def _():
                    wt_copy(1, i + 1, 1 - slot).start()

            wt_copy(half, i, slot).wait()
            v = dot(ggu[...], wt[slot], NT).astype(BF)
            cols = pl.ds(pl.multiple_of(i * drows, drows), drows)
            for q in range(n_mp):
                mid.t[half, q, :, cols] = v[q * part : (q + 1) * part]

        for mask in mid.masks():
            mid.offer(mask, (half,))

    run(0)
    run(1)
    terms(0)
    run(2)
    run(3)
    for cp in lay.loads:
        cp.wait()
    lay.turn()
    terms(1)
    for e in range(4, 2 * n):
        run(e)
    lay.arrive()
    load_hid.wait()

    @pl.loop(0, part // 32)
    def _(b):
        rs = pl.ds(pl.multiple_of(b * 32, 32), 32)
        for half in range(2):
            h = hid[rs, pl.ds(half * half_cols, half_cols)]
            gather_lay.own[half, rs, :] = (h + lay.total(half, rs)).astype(BF)

    gather_lay.start([0])
    line.slot(0)
    per = half_cols // hh
    blocks_d = 2 * half_cols // part
    wo_spot = [(e // per // (n_mp // 2), e // per % (n_mp // 2), e % per) for e in range(blocks_d)]
    wo_parts = [
        pltpu.make_async_copy(
            aw_hbm.at[pl.ds(e * part, part), pl.ds(3 * hh, hh)],
            lay.t.at[i, j, :, pl.ds(k * hh, hh)],
            load_s.at[4 + e],
        )
        for e, (i, j, k) in enumerate(wo_spot)
    ]
    for cp in wo_parts:
        cp.start()
    load_qkv = pltpu.make_async_copy(
        qkv_hbm, space.at[:, pl.ds(2 * half_cols, 3 * hh)], load_s.at[2]
    )
    load_qkv.start()
    mid.turn()
    mid.arrive()
    load_cot.wait()
    gg_ref[...] = jnp.zeros_like(gg_ref)

    @pl.loop(0, part // 32)
    def _(b):
        rs = pl.ds(pl.multiple_of(b * 32, 32), 32)
        h = hid[rs, :]
        scale = lax.rsqrt(jnp.mean(h * h, axis=1, keepdims=True) + EPS)
        g = jnp.concatenate([mid.total(0, rs), mid.total(1, rs)], axis=1)
        unit = h * scale
        weighted = g * gain_ref[1:2, :]
        field = scale * (weighted - unit * jnp.mean(weighted * unit, axis=1, keepdims=True))
        out = cot[rs, :].astype(F32) + field
        gh[rs, :] = out
        low = out.astype(BF)
        gather_low.own[0, rs, :] = low[:, :half_cols]
        gather_low.own[1, rs, :] = low[:, half_cols:]
        gg_ref[...] += jnp.sum(g * unit, axis=0, keepdims=True)

    gather_low.start()
    store_gh = pltpu.make_async_copy(gh, gh_hbm, load_s.at[1])
    store_gh.start()
    for s in range(1, n - 2):
        line.slot(s)
    gather_low.forward()
    gather_lay.start(range(1, gather_lay.levels))
    gather_low.finish()
    load_low = pltpu.make_async_copy(low_ref, space.at[:, pl.ds(0, 2 * half_cols)], load_s.at[3])
    load_low.start()
    load_low.wait()
    load_qkv.wait()
    for cp in wo_parts:
        cp.wait()
    seq = space.shape[0]
    base = 2 * half_cols
    gbase = base + 3 * hh

    @pl.loop(0, seq // 256)
    def _(b):
        rs = pl.ds(pl.multiple_of(b * 256, 256), 256)
        total = jnp.zeros((256, hh), F32)
        for e, (i, j, k) in enumerate(wo_spot):
            wo = lay.t[i, j, :, k * hh : (k + 1) * hh]
            total += dot(space[rs, e * part : (e + 1) * part], wo)
        space[rs, gbase : gbase + hh] = total.astype(BF)

    count = count_ref[0]
    blk = 256
    blocks = seq // blk

    def back(head):
        at_cols = lambda first: pl.ds(pl.multiple_of(first + head * HD, HD), HD)
        for i in range(blocks - 1, -1, -1):
            rows = pl.ds(i * blk, blk)
            span = (i + 1) * blk
            keys = pl.ds(0, span)
            q = space[rows, at_cols(base)]
            g = space[rows, at_cols(gbase)]
            k = space[keys, at_cols(base + hh)]
            lg = jnp.where(
                allowed_block(i * blk, blk, 0, span, count), logistic_block(q, k, seq), 0.0
            )
            w = lg.astype(BF)
            gw = dot(g, space[keys, at_cols(base + 2 * hh)], NT)
            gs = (gw * lg * (1.0 - lg) * HD ** (-0.5)).astype(BF)
            wt[i // 2, :, at_cols((i % 2) * (wide // 2))] = dot(gs, k).astype(BF)
            dk = dot(gs, q, TN)
            dv = dot(w, g, TN)
            if i == blocks - 1:
                dka[...] = dk
                dva[...] = dv
            else:
                dka[keys, :] += dk
                dva[keys, :] += dv
        for i in range(blocks):
            rows = pl.ds(i * blk, blk)
            wt[i // 2, :, at_cols((i % 2) * (wide // 2) + hh)] = dka[rows, :].astype(BF)
            wt[i // 2, :, at_cols((i % 2) * (wide // 2) + 2 * hh)] = dva[rows, :].astype(BF)

    heads = hh // HD
    pl.loop(0, heads // 2)(back)
    gather_lay.forward()
    pl.loop(heads // 2, heads)(back)
    stores = [
        pltpu.make_async_copy(
            wt.at[i // 2, :, pl.ds((i % 2) * (wide // 2), 3 * hh)],
            dq_ref.at[pl.ds(i * blk, blk), :],
            load_s.at[4 + i],
        )
        for i in range(blocks)
    ]
    for cp in stores:
        cp.start()
    stores += line.final(res, rs_ref, rs_s) + [store_gh]
    gather_lay.finish()
    for cp in stores:
        cp.wait()
    line.drain()
    mid.drain()
    lay.drain()


def mid_stage(n_dp, n_mp, ggu, gw, nm, ft, cot, qkv, aw, counts, hid, gain):
    seq, wide = ggu.shape
    hh = qkv.shape[1] // 3
    d = gw.shape[0]
    n, part, chunk = n_dp // 2, seq // n_mp, d // n_dp
    dma = pltpu.SemaphoreType.DMA
    hbm = pl.BlockSpec(memory_space=pl.ANY)
    vm = pl.BlockSpec(memory_space=pltpu.VMEM)
    pieces = PIECES
    return pl.pallas_call(
        functools.partial(mid_kernel, n_dp, n_mp),
        out_shape=[
            jax.ShapeDtypeStruct((pieces, chunk, wide // pieces), BF),
            jax.ShapeDtypeStruct((seq, d), BF),
            jax.ShapeDtypeStruct((seq, d), BF),
            jax.ShapeDtypeStruct((part, d), F32),
            jax.ShapeDtypeStruct((1, d), F32),
            jax.ShapeDtypeStruct((seq, 3 * hh), BF),
        ],
        in_specs=[hbm] * 7 + [pl.BlockSpec(memory_space=pltpu.SMEM), hbm, vm],
        out_specs=[hbm, hbm, hbm, hbm, vm, hbm],
        scratch_shapes=[
            pltpu.VMEM((seq, max(wide, d + 4 * hh)), BF),
            pltpu.VMEM((2, 256, wide), BF),
            dma((2,)),
            pltpu.VMEM((2, seq, chunk), BF),
            dma((2,)),
            pltpu.VMEM((part, d), BF),
            pltpu.VMEM((part, d), F32),
            pltpu.VMEM((part, d), F32),
            pltpu.VMEM((pieces, chunk, wide // pieces), BF),
            dma((pieces,)),
            dma((pieces,)),
            pltpu.VMEM((seq, HD), F32),
            pltpu.VMEM((seq, HD), F32),
            dma((4 + max(d // part, seq // 256),)),
        ]
        + line_sum_scratch(n, pieces, chunk, wide // pieces, 1)
        + quad_sum_scratch(n_mp, part, d // 2)
        + quad_sum_scratch(n_mp, part, d // 2, n_mp // 2)
        + [dma((2, n_mp // 2))]
        + quad_gather_scratch(n_mp, part, d // 2) * 2,
        compiler_params=pltpu.CompilerParams(
            collective_id=4, has_side_effects=True, vmem_limit_bytes=VMEM_LIMIT
        ),
        name="mid_stage",
    )(ggu, gw, nm, ft, cot, qkv, aw, counts, hid, gain)


def last_kernel(
    n_dp,
    n_mp,
    dqkv_hbm,
    aw_hbm,
    nin_hbm,
    low_hbm,
    att_hbm,
    x_hbm,
    gh_hbm,
    gain_ref,
    gmid_ref,
    rs_ref,
    grad_ref,
    gains_ref,
    rhs,
    aw,
    nin,
    low,
    lhs,
    x,
    gh,
    res,
    rs_s,
    loads,
    pout,
    own,
    din,
    uin,
    po_s,
    po_r,
    d_s,
    d_r,
    u_s,
    u_r,
    t,
    r,
    q1,
    q2,
    gown,
    g1,
    g2,
    g3,
    gsum,
    fold_out,
    fold_in,
    fold_s,
    fold_r,
):
    at = Place(n_dp, n_mp)
    hh = att_hbm.shape[1]
    part = t.shape[2]
    chunk = own.shape[2]
    half_cols = t.shape[3]
    copies = [
        pltpu.make_async_copy(src, dst, loads.at[i])
        for i, (src, dst) in enumerate(
            [
                (dqkv_hbm, rhs.at[:, pl.ds(0, 3 * hh)]),
                (aw_hbm.at[:, pl.ds(0, 3 * hh)], aw),
                (nin_hbm, nin),
                (att_hbm, rhs.at[:, pl.ds(3 * hh, hh)]),
                (low_hbm, low),
                (x_hbm.at[part_rows(at, part), :], x),
                (gh_hbm, gh),
            ]
        )
    ]
    for cp in copies:
        cp.start()
    bits = [b for b in (2, 4, 8, 16) if b < n_dp]
    enter(at, [at.fold(b) for b in bits[1:]])
    quad = QuadSum(at, t, r, (q1, q2))
    line = LineSum(at, pout, own, din, uin, (po_s, po_r, d_s, d_r, u_s, u_r), True)
    gather = QuadGather(at, gown, grad_ref, (g1, g2, g3))
    copies[0].wait()
    copies[1].wait()

    d = aw.shape[0]
    fold = fold_out.shape[2]
    per_row = d // fold

    def terms(q):
        rs = pl.ds(pl.multiple_of(q * part, part), part)
        width = 512

        @pl.loop(0, half_cols // width)
        def _(i):
            for half in range(2):
                d0 = pl.multiple_of(half * half_cols + i * width, width)
                v = dot(rhs[rs, 0 : 3 * hh], aw[pl.ds(d0, width), :], NT)
                t[half, q, :, pl.ds(pl.multiple_of(i * width, width), width)] = v.astype(BF)
                u = v * nin[rs, pl.ds(d0, width)].astype(F32)
                gsum[0:1, pl.ds(d0, width)] += jnp.sum(u, axis=0, keepdims=True)

    gsum[...] = jnp.zeros_like(gsum)
    copies[2].wait()
    masks = quad.masks()
    terms(at.quarter(masks[0]))
    quad.offer(masks[0])
    for cp in copies[3:5]:
        cp.wait()
    load_x = copies[5]

    def run(k, core):
        block = 2 * order_of(k, at) + (at.c if core else 1 - at.c)
        cols = pl.ds(pl.multiple_of(block * chunk, chunk), chunk)
        lhs[0] = nin[:, cols].T
        lhs[1] = low[:, cols].T

        def tile(i):
            return dot(lhs[lax.div(i, 3)], rhs[:, pl.ds(pl.multiple_of(i * hh, hh), hh)])

        if core:
            line.mine(k, tile)
        else:
            line.other(k, tile)

    n = at.n
    devs = [at.core] + [at.fold(b) for b in bits] + [at.peer(b) for b in at.bits]

    def fold_copy(b):
        return remote(fold_out.at[b], fold_in.at[b], fold_s.at[b], fold_r.at[b], devs[b])

    def fold_next(b):
        fold_copy(b).wait_recv()
        fold_out[b + 1] = fold_out[b] + fold_in[b]
        if b + 1 < len(devs):
            fold_copy(b + 1).start()

    run(0, 0)
    run(0, 1)
    for mask in masks[1:]:
        terms(at.quarter(mask))
        quad.offer(mask)
    gsum[0:1, :] = gsum[0:1, :] / gain_ref[0:1, :]
    gsum[1:2, :] = gmid_ref[...]
    for i in range(2):
        for j in range(per_row):
            fold_out[0, i * per_row + j] = gsum[i, j * fold : (j + 1) * fold]
    fold_copy(0).start()
    run(1, 0)
    run(1, 1)
    fold_next(0)
    for k in range(2, n):
        run(k, 0)
        run(k, 1)
    quad.turn()
    for b in range(1, len(bits)):
        fold_next(b)
    line.slot(0)
    load_x.wait()
    copies[6].wait()
    fold_next(len(bits))
    step = part // gather.blocks

    def norm(block):
        @pl.loop(0, step // 32)
        def _(b):
            rs = pl.ds(pl.multiple_of(block * step + b * 32, 32), 32)
            v = x[rs, :].astype(F32)
            scale = lax.rsqrt(jnp.mean(v * v, axis=1, keepdims=True) + EPS)
            g = jnp.concatenate([quad.total(0, rs), quad.total(1, rs)], axis=1)
            unit = v * scale
            weighted = g * gain_ref[0:1, :]
            field = scale * (weighted - unit * jnp.mean(weighted * unit, axis=1, keepdims=True))
            total = (gh[rs, :] + field).astype(BF)
            gown[0, rs, :] = total[:, :half_cols]
            gown[1, rs, :] = total[:, half_cols:]

    for block in range(gather.blocks):
        quad.arrive(block)
        norm(block)
        gather.start(block=block)
        if block == 0:
            for b in range(len(bits) + 1, len(devs) - 1):
                fold_next(b)
    for s in range(1, n - 2):
        line.slot(s)
    for block in range(gather.blocks):
        gather.forward(block)
    fold_next(len(devs) - 1)
    for i in range(2):
        for j in range(per_row):
            gsum[i, j * fold : (j + 1) * fold] = fold_out[len(devs), i * per_row + j]
    gains_ref[...] = gsum[:, pl.ds(pl.multiple_of(at.dp * chunk, chunk), chunk)]
    stores = line.final(res, rs_ref, rs_s)
    gather.finish()
    for cp in stores:
        cp.wait()
    line.drain()
    quad.drain()
    for b in range(len(devs)):
        fold_copy(b).wait_send()


def last_stage(n_dp, n_mp, dqkv, aw, nin, low, att, x, gh, gain, gmid):
    seq, hh = att.shape
    d = aw.shape[0]
    n, part, chunk = n_dp // 2, seq // n_mp, d // n_dp
    dma = pltpu.SemaphoreType.DMA
    anyspace = pl.BlockSpec(memory_space=pl.ANY)
    vm = pl.BlockSpec(memory_space=pltpu.VMEM)
    folds = 1 + len([b for b in (1, 2, 4, 8) if b < n_mp]) + len([b for b in (2, 4, 8, 16) if b < n_dp])
    return pl.pallas_call(
        functools.partial(last_kernel, n_dp, n_mp),
        out_shape=[
            jax.ShapeDtypeStruct((4, chunk, hh), BF),
            jax.ShapeDtypeStruct((seq, d), BF),
            jax.ShapeDtypeStruct((8, chunk), F32),
        ],
        in_specs=[anyspace] * 7 + [vm] * 2,
        out_specs=[anyspace, anyspace, vm],
        scratch_shapes=[
            pltpu.VMEM((seq, 4 * hh), BF),
            pltpu.VMEM((d, 3 * hh), BF),
            pltpu.VMEM((seq, d), BF),
            pltpu.VMEM((seq, d), BF),
            pltpu.VMEM((2, chunk, seq), BF),
            pltpu.VMEM((part, d), BF),
            pltpu.VMEM((part, d), F32),
            pltpu.VMEM((4, chunk, hh), BF),
            dma((4,)),
            dma((7,)),
        ]
        + line_sum_scratch(n, 4, chunk, hh)
        + quad_sum_scratch(n_mp, part, d // 2, None, 2)
        + quad_gather_scratch(n_mp, part, d // 2, 2)
        + [
            pltpu.VMEM((8, d), F32),
            pltpu.VMEM((folds + 1, 8, d // 4), F32),
            pltpu.VMEM((folds, 8, d // 4), F32),
            dma((folds,)),
            dma((folds,)),
        ],
        compiler_params=pltpu.CompilerParams(
            collective_id=5, has_side_effects=True, vmem_limit_bytes=VMEM_LIMIT
        ),
        name="last_stage",
    )(dqkv, aw, nin, low, att, x, gh, gain, gmid)


def finish_kernel(
    low_ref,
    lay_ref,
    gu_ref,
    down_ref,
    attn_ref,
    gains_ref,
    lay_out,
    in_out,
    gate_out,
    up_out,
    down_out,
    q_out,
    k_out,
    v_out,
    o_out,
    g1_out,
    g2_out,
):
    lay_out[...] = lay_ref[...]
    in_out[...] = low_ref[...].astype(F32)
    half = gate_out.shape[1]
    gate_out[...] = gu_ref[0, :, :half].astype(F32)
    up_out[...] = gu_ref[0, :, half:].astype(F32)
    step = pl.program_id(0)

    @pl.when(lax.rem(step, 2) == 0)
    def _():
        down_out[...] = down_ref[0].T.astype(F32)

    @pl.when(step == 0)
    def _():
        for i, ref in enumerate((q_out, k_out, v_out)):
            ref[...] = attn_ref[i].astype(F32)
        o_out[...] = attn_ref[3].T.astype(F32)
        g1_out[...] = gains_ref[0]
        g2_out[...] = gains_ref[1]


def finish_stage(low, lay, gu, down, attn, gains):
    seq, d = low.shape
    steps, chunk, wide = gu.shape
    width, hh = down.shape[2], attn.shape[2]
    row = pl.BlockSpec((seq // (2 * steps), d), lambda i: (i, 0))
    fixed = lambda *shape: pl.BlockSpec(shape, lambda i: (0,) * len(shape))
    two = pl.BlockSpec((1, chunk // 2, wide), lambda i: (i // 2, i % 2, 0))
    piece = pl.BlockSpec((1, chunk, width), lambda i: (i // 2, 0, 0))
    cols = pl.BlockSpec((chunk // 2, wide // 2), lambda i: (i % 2, i // 2))
    f32 = lambda *shape: jax.ShapeDtypeStruct(shape, F32)
    return pl.pallas_call(
        finish_kernel,
        grid=(2 * steps,),
        in_specs=[row, row, two, piece, fixed(4, chunk, hh), fixed(*gains.shape)],
        out_specs=[row, row, cols, cols, pl.BlockSpec((width, chunk), lambda i: (i // 2, 0))]
        + [fixed(chunk, hh)] * 3
        + [fixed(hh, chunk)]
        + [fixed(chunk)] * 2,
        out_shape=[
            jax.ShapeDtypeStruct((seq, d), BF),
            f32(seq, d),
            f32(chunk, steps * wide // 2),
            f32(chunk, steps * wide // 2),
            f32(steps * width, chunk),
        ]
        + [f32(chunk, hh)] * 3
        + [f32(hh, chunk)]
        + [f32(chunk)] * 2,
        compiler_params=pltpu.CompilerParams(vmem_limit_bytes=VMEM_LIMIT),
        name="finish_stage",
    )(low, lay, gu, down, attn, gains)


def on_device(
    inputs,
    counts,
    cotangent,
    gain_attn,
    w_query,
    w_key,
    w_value,
    w_output,
    gain_ffn,
    w_gate,
    w_up,
    w_down,
):
    n_dp, n_mp = lax.axis_size("dp"), lax.axis_size("mp")
    attn_w, qkv, attended, normed_in, gains, gu_shard, down_shard, grad_ffn, gu_pre = attn_stage(
        n_dp,
        n_mp,
        counts,
        gain_attn,
        gain_ffn,
        w_query,
        w_key,
        w_value,
        w_output,
        w_gate,
        w_up,
        w_down,
        inputs,
        cotangent,
    )
    gu_w, normed_mid, hidden, gu, inner, down_pre = gate_stage(
        n_dp, n_mp, attended, attn_w, gu_shard, gu_pre, down_shard, inputs, gains
    )
    rs_down, ffn_terms, ggu = down_stage(n_dp, n_mp, inner, gu, grad_ffn, down_shard, down_pre)
    rs_gu, grad_low, layer_out, grad_hidden, g_gain_mid, dqkv = mid_stage(
        n_dp, n_mp, ggu, gu_w, normed_mid, ffn_terms, grad_ffn, qkv, attn_w, counts, hidden, gains
    )
    rs_attn, grad_low_in, g_gains = last_stage(
        n_dp, n_mp, dqkv, attn_w, normed_in, grad_low, attended, inputs, grad_hidden, gains, g_gain_mid
    )
    lay, grad_x, g_gate, g_up, g_down, g_q, g_k, g_v, g_o, g_attn, g_ffn = finish_stage(
        grad_low_in, layer_out, rs_gu, rs_down, rs_attn, g_gains
    )
    return (lay, grad_x, g_attn, g_q, g_k, g_v, g_o, g_ffn, g_gate, g_up, g_down)


def solution(mesh):
    row, both, swapped = P("dp", None), P("dp", "mp"), P("mp", "dp")
    weights = (both, both, both, swapped)
    ffn = (both, both, swapped)
    return jax.shard_map(
        on_device,
        mesh=mesh,
        in_specs=(row, P("dp"), row, P("dp")) + weights + (P("dp"),) + ffn,
        out_specs=(row, row, P("dp")) + weights + (P("dp"),) + ffn,
        check_vma=False,
    )
```

```python
import functools
import math

import jax
import jax.numpy as jnp
from jax import lax
from jax.experimental import pallas as pl
from jax.experimental.pallas import tpu as pltpu
from jax.sharding import PartitionSpec as P

HD = 128
EPS = 1e-06
BF = jnp.bfloat16
F32 = jnp.float32
NT = (((1,), (1,)), ((), ()))
TN = (((0,), (0,)), ((), ()))
NN = (((1,), (0,)), ((), ()))


def dot(a, b, dims=NN):
    return lax.dot_general(a, b, dims, preferred_element_type=F32)


def logistic_block(q, k, seq):
    raw = dot(q, k, NT)
    shifted = math.log(seq) - raw * HD ** (-0.5)
    return 1.0 / (1.0 + jnp.exp(shifted))


def allowed_block(row0, rows, col0, cols, count):
    ri = row0 + lax.broadcasted_iota(jnp.int32, (rows, cols), 0)
    ci = col0 + lax.broadcasted_iota(jnp.int32, (rows, cols), 1)
    return (ci <= ri) & (ci < count)


MESH = pl.DeviceIdType.MESH
VMEM_LIMIT = 60 * 1024 * 1024
PIECES = 4
AHEAD = 1
DOWN_AHEAD = 2


def flipped(index, bit):
    return index + bit - 2 * bit * lax.rem(lax.div(index, bit), 2)


def spread(j, bits):
    return sum(bit for i, bit in enumerate(bits) if j >> i & 1)


class Place:
    def __init__(self, n_dp, n_mp):
        self.n = n_dp // 2
        self.dp = lax.axis_index("dp")
        self.m = lax.axis_index("mp")
        self.p = lax.div(self.dp, 2)
        self.c = lax.rem(self.dp, 2)
        self.above = (self.dp + 2, self.m)
        self.below = (self.dp - 2, self.m)
        self.core = (self.dp + 1 - 2 * self.c, self.m)
        self.bits = [b for b in (1, 2, 4, 8, 16) if b < n_mp]
        self.has_above = self.p < self.n - 1
        self.has_below = self.p > 0

    def fold(self, bit):
        return (flipped(self.dp, bit), self.m)

    def peer(self, bit):
        return (self.dp, flipped(self.m, bit))

    def quarter(self, mask):
        q = self.m
        for bit in self.bits:
            if mask & bit:
                q = flipped(q, bit)
        return q


def signal(dev):
    pl.semaphore_signal(pltpu.get_barrier_semaphore(), inc=1, device_id=dev, device_id_type=MESH)


def enter(at, extra=()):
    always = [at.core] + [at.peer(bit) for bit in at.bits] + list(extra)
    for dev in always:
        signal(dev)

    @pl.when(at.has_above)
    def _():
        signal(at.above)

    @pl.when(at.has_below)
    def _():
        signal(at.below)

    ends = at.has_above.astype(jnp.int32) + at.has_below.astype(jnp.int32)
    pl.semaphore_wait(pltpu.get_barrier_semaphore(), len(always) + ends)


def remote(src, dst, send, recv, dev):
    return pltpu.make_async_remote_copy(
        src_ref=src, dst_ref=dst, send_sem=send, recv_sem=recv, device_id=dev, device_id_type=MESH
    )


def part_rows(at, part):
    return pl.ds(pl.multiple_of(at.m * part, part), part)


def order_of(k, at):
    n, p = at.n, at.p
    if k == n - 1:
        return p
    high = jnp.where(k < p, k, n - 1 - k + p)
    low = jnp.where(k < n - 1 - p, n - 1 - k, k - (n - 1 - p))
    return jnp.where(2 * p >= n, high, low)


class LineSum:
    def __init__(self, at, pout, own, din, uin, sems, paced=False, defer=False):
        self.paced, self.defer = paced, defer
        self.at, self.pout, self.own, self.din, self.uin = at, pout, own, din, uin
        self.po_s, self.po_r, self.d_s, self.d_r, self.u_s, self.u_r = sems
        self.slots, self.pieces = pout.shape[0], own.shape[1]

    def core_copy(self, k, i):
        j = order_of(k, self.at)
        slot = k % self.slots
        return remote(
            self.pout.at[slot, i],
            self.own.at[j, i],
            self.po_s.at[slot, i],
            self.po_r.at[k, i],
            self.at.core,
        )

    def down_copy(self, s, i):
        return remote(
            self.own.at[s, i], self.din.at[s, i], self.d_s.at[s, i], self.d_r.at[s, i], self.at.below
        )

    def up_copy(self, s, i):
        n = self.at.n
        return remote(
            self.own.at[n - 1 - s, i],
            self.uin.at[s, i],
            self.u_s.at[s, i],
            self.u_r.at[s, i],
            self.at.above,
        )

    def other(self, k, tile):
        @pl.loop(0, self.pieces)
        def _(i):
            if k >= self.slots:
                self.core_copy(k - self.slots, i).wait_send()
            self.pout[k % self.slots, i] = tile(i).astype(BF)
            self.core_copy(k, i).start()

    def mine(self, k, tile):
        at = self.at
        j = order_of(k, at)

        @pl.loop(0, self.pieces)
        def _(i):
            value = tile(i)
            self.core_copy(k, i).wait_recv()
            self.own[j, i] = (value + self.own[j, i].astype(F32)).astype(BF)
            if k < (1 if self.paced else at.n - 1):

                @pl.when(at.p == at.n - 1)
                def _():
                    self.down_copy(k, i).start()

                @pl.when(at.p == 0)
                def _():
                    self.up_copy(k, i).start()

    def add(self, dst, src):
        @pl.loop(0, dst.shape[0] // 64)
        def _(b):
            rs = pl.ds(pl.multiple_of(b * 64, 64), 64)
            dst[rs, :] = (dst[rs, :].astype(F32) + src[rs, :].astype(F32)).astype(BF)

    def slot(self, t):
        at = self.at
        n, p = at.n, at.p
        sd = t - (n - 2 - p)
        su = t - (p - 1)

        @pl.loop(0, self.pieces)
        def _(i):
            @pl.when((sd >= 0) & (sd < p) & at.has_above)
            def _():
                self.down_copy(sd, i).wait_recv()
                self.add(self.own.at[sd, i], self.din.at[sd, i])
                pl.when((p > 1) if self.defer else True)(self.down_copy(sd, i).start)

            @pl.when((su >= 0) & (su < n - 1 - p) & at.has_below)
            def _():
                self.up_copy(su, i).wait_recv()
                self.add(self.own.at[n - 1 - su, i], self.uin.at[su, i])
                pl.when((p < n - 2) if self.defer else True)(self.up_copy(su, i).start)

            if self.paced:

                @pl.when(p == n - 1)
                def _():
                    self.down_copy(t, i).wait_send()
                    self.down_copy(t + 1, i).start()

                @pl.when(p == 0)
                def _():
                    self.up_copy(t, i).wait_send()
                    self.up_copy(t + 1, i).start()

    def final(self, out, sink, sems):
        at = self.at
        n, p = at.n, at.p

        @pl.loop(0, self.pieces)
        def _(i):
            inner = at.has_above & at.has_below

            @pl.when(inner if self.defer else at.has_above)
            def _():
                self.down_copy(p, i).wait_recv()

            @pl.when(inner if self.defer else at.has_below)
            def _():
                self.up_copy(n - 1 - p, i).wait_recv()

            def close(parts):
                @pl.loop(0, out.shape[1] // 64)
                def _(b):
                    rs = pl.ds(pl.multiple_of(b * 64, 64), 64)
                    total = self.own[p, i, rs, :].astype(F32)
                    for ref, s in parts:
                        total = total + ref[s, i, rs, :].astype(F32)
                    out[i, rs, :] = total.astype(out.dtype)

            down, up = (self.din, p), (self.uin, n - 1 - p)

            @pl.when(at.has_above & at.has_below)
            def _():
                close([down, up])

            @pl.when(jnp.logical_not(at.has_below))
            def _():
                close([] if self.defer else [down])

            @pl.when(jnp.logical_not(at.has_above))
            def _():
                close([] if self.defer else [up])

            pltpu.make_async_copy(out.at[i], sink.at[i], sems.at[i]).start()

        return [
            pltpu.make_async_copy(out.at[i], sink.at[i], sems.at[i]) for i in range(self.pieces)
        ]

    def drain(self):
        at = self.at
        n, p = at.n, at.p
        for k in range(n - self.slots, n):
            for i in range(self.pieces):
                self.core_copy(k, i).wait_send()
        for s in range(n - 1):
            done = self.paced and s < n - 2

            last = self.defer

            @pl.when((s < p) & (p > 1 if last else at.has_above if done else at.has_below))
            def _():
                for i in range(self.pieces):
                    self.down_copy(s, i).wait_send()

            @pl.when((s < n - 1 - p) & (p < n - 2 if last else at.has_below if done else at.has_above))
            def _():
                for i in range(self.pieces):
                    self.up_copy(s, i).wait_send()


def line_sum_scratch(n, pieces, rows, cols, slots=2):
    dma = pltpu.SemaphoreType.DMA
    return [
        pltpu.VMEM((slots, pieces, rows, cols), BF),
        pltpu.VMEM((n, pieces, rows, cols), BF),
        pltpu.VMEM((n - 1, pieces, rows, cols), BF),
        pltpu.VMEM((n - 1, pieces, rows, cols), BF),
        dma((slots, pieces)),
        dma((n, pieces)),
        dma((n - 1, pieces)),
        dma((n - 1, pieces)),
        dma((n - 1, pieces)),
        dma((n - 1, pieces)),
    ]


class QuadSum:
    def __init__(self, at, t, r, sems):
        self.at, self.t, self.r = at, t, r
        self.s, self.v = sems
        self.blocks = self.s.shape[2]
        self.step = r.shape[2] // self.blocks
        self.order = [at.bits, at.bits[::-1]]
        self.levels = len(at.bits)
        self.seen = set()

    def count(self, k):
        return 1 << (self.levels - 1 - k)

    def slot(self, k, j):
        return sum(self.count(i) for i in range(k)) + j

    def rest(self, half, k):
        return self.order[half][k + 1 :]

    def index(self, half, k, mask):
        rest = self.rest(half, k)
        return self.slot(k, sum(1 << i for i, bit in enumerate(rest) if mask & bit))

    def source(self, half, mask):
        return self.t.at[half, self.at.quarter(mask)]

    def terms(self, half, mask, rs):
        return self.t[half, self.at.quarter(mask), rs, :].astype(F32)

    def split(self, k):
        return self.blocks if k == self.levels - 1 else 1

    def copy(self, half, k, j, block=0):
        bit = self.order[half][k]
        mask = bit + spread(j, self.rest(half, k))
        src = self.source(half, mask) if k == 0 else self.r.at[half, self.index(half, k - 1, mask)]
        at = self.slot(k, j)
        dst = self.r.at[half, at]
        if self.split(k) > 1:
            rows = pl.ds(block * self.step, self.step)
            src, dst = src.at[rows, :], dst.at[rows, :]
        send, recv = self.s.at[half, at, block], self.v.at[half, at, block]
        return remote(src, dst, send, recv, self.at.peer(bit))

    def offer(self, mask, only=(0, 1)):
        for half in only:
            if mask & self.order[half][0]:
                rest = self.rest(half, 0)
                self.copy(half, 0, sum(1 << i for i, b in enumerate(rest) if mask & b)).start()

    def masks(self):
        return sorted(range(1, 2 * self.count(0)), key=lambda m: -bin(m).count("1")) + [0]

    def come(self, half, k, mask, block=0):
        at = self.index(half, k, mask)
        block = min(block, self.split(k) - 1)
        if (half, at, block) not in self.seen:
            self.seen.add((half, at, block))
            self.copy(half, k, at - self.slot(k, 0), block).wait_recv()
        return at

    def turn(self):
        for k in range(1, self.levels):
            for block in range(self.split(k)):
                for half in range(2):
                    for j in range(self.count(k)):
                        self.pass_on(half, k, j, block)

    def pass_on(self, half, k, j, block):
        mask = self.order[half][k] + spread(j, self.rest(half, k))
        got = [self.come(half, i, mask) for i in range(k)]
        rows = self.r.shape[2] // self.split(k)

        @pl.loop(0, rows // 64)
        def _(b):
            rs = pl.ds(pl.multiple_of(block * rows + b * 64, 64), 64)
            total = self.terms(half, mask, rs)
            for i in got:
                total = total + self.r[half, i, rs, :].astype(F32)
            self.r[half, got[-1], rs, :] = total.astype(BF)

        self.copy(half, k, j, block).start()

    def arrive(self, block=0):
        self.got = [
            [self.come(half, k, 0, block) for k in range(self.levels)] for half in range(2)
        ]

    def total(self, half, rs):
        total = self.terms(half, 0, rs)
        for i in self.got[half]:
            total = total + self.r[half, i, rs, :].astype(F32)
        return total

    def drain(self):
        for half in range(2):
            for k in range(self.levels):
                for j in range(self.count(k)):
                    for block in range(self.split(k)):
                        self.copy(half, k, j, block).wait_send()


class QuadSumHbm(QuadSum):
    def __init__(self, at, hbm, t, r, sems):
        super().__init__(at, t, r, sems[:2])
        self.hbm = hbm
        self.loads = [
            pltpu.make_async_copy(
                self.source(half, spread(j, self.rest(half, 0))), t.at[half, j], sems[2].at[half, j]
            )
            for half in range(2)
            for j in range(self.count(0))
        ]

    def source(self, half, mask):
        rows, cols = self.t.shape[2], self.t.shape[3]
        rs = pl.ds(pl.multiple_of(self.at.quarter(mask) * rows, rows), rows)
        return self.hbm.at[rs, pl.ds(half * cols, cols)]

    def terms(self, half, mask, rs):
        return self.t[half, self.index(half, 0, mask), rs, :].astype(F32)


def quad_sum_scratch(mp, rows, cols, parts=None, blocks=1):
    dma = pltpu.SemaphoreType.DMA
    return [
        pltpu.VMEM((2, parts or mp, rows, cols), BF),
        pltpu.VMEM((2, mp - 1, rows, cols), BF),
        dma((2, mp - 1, blocks)),
        dma((2, mp - 1, blocks)),
    ]


class QuadGather:
    def __init__(self, at, own, out, sems):
        self.at, self.own, self.out = at, own, out
        self.s, self.v, self.here = sems
        self.blocks = self.s.shape[2]
        self.order = [at.bits[::-1], at.bits]
        self.levels = len(at.bits)
        self.seen = set()

    def mine(self, half, block):
        step = self.own.shape[1] // self.blocks
        return self.own.at[half, pl.ds(block * step, step), :]

    def spot(self, mask, half, block):
        rows, cols = self.own.shape[1], self.own.shape[2]
        step = rows // self.blocks
        rs = pl.ds(pl.multiple_of(self.at.quarter(mask) * rows + block * step, step), step)
        return self.out.at[rs, pl.ds(half * cols, cols)]

    def copy(self, half, k, j, block):
        mask = spread(j, self.order[half][:k])
        dst = self.spot(mask, half, block)
        src = self.mine(half, block) if j == 0 else dst
        at = (1 << k) - 1 + j
        dev = self.at.peer(self.order[half][k])
        return remote(src, dst, self.s.at[half, at, block], self.v.at[half, at, block], dev)

    def come(self, half, k, j, block):
        if (half, k, j, block) not in self.seen:
            self.seen.add((half, k, j, block))
            self.copy(half, k, j, block).wait_recv()

    def keep(self, half, block):
        return pltpu.make_async_copy(
            self.mine(half, block), self.spot(0, half, block), self.here.at[half, block]
        )

    def start(self, levels=None, block=0):
        for k in range(self.levels) if levels is None else levels:
            for half in range(2):
                self.copy(half, k, 0, block).start()
                if k == 0:
                    self.keep(half, block).start()

    def forward(self, block=0):
        for k in range(1, self.levels):
            for half in range(2):
                for j in range(1, 1 << k):
                    top = j.bit_length() - 1
                    self.come(half, top, j - (1 << top), block)
                    self.copy(half, k, j, block).start()

    def finish(self):
        for half in range(2):
            for block in range(self.blocks):
                for k in range(self.levels):
                    for j in range(1 << k):
                        self.come(half, k, j, block)
                        self.copy(half, k, j, block).wait_send()
                self.keep(half, block).wait()


def quad_gather_scratch(mp, rows, cols, blocks=1):
    dma = pltpu.SemaphoreType.DMA
    return [
        pltpu.VMEM((2, rows, cols), BF),
        dma((2, mp - 1, blocks)),
        dma((2, mp - 1, blocks)),
        dma((2, blocks)),
    ]


class LineGather:
    def __init__(self, at, pieces, shard, spot, sems, pre=0, wide=False):
        self.pre, self.wide = pre, wide
        self.at, self.pieces, self.shard, self.spot = at, pieces, shard, spot
        self.d_s, self.d_r, self.u_s, self.u_r, self.c_s, self.c_r, self.here = sems

    def down_copy(self, h, i, own=False):
        b = 2 * (self.at.p + h) + self.at.c
        dst = self.spot(b, i)
        src = self.shard(i) if own and self.shard else dst
        return remote(src, dst, self.d_s.at[h, i], self.d_r.at[h, i], self.at.below)

    def up_copy(self, h, i, own=False):
        b = 2 * (self.at.p - h) + self.at.c
        dst = self.spot(b, i)
        src = self.shard(i) if own and self.shard else dst
        return remote(src, dst, self.u_s.at[h, i], self.u_r.at[h, i], self.at.above)

    def core_copy(self, z, i, own=False, incoming=False):
        b = 2 * z + (1 - self.at.c if incoming else self.at.c)
        dst = self.spot(b, i)
        src = self.shard(i) if own and self.shard else dst
        return remote(src, dst, self.c_s.at[z, i], self.c_r.at[z, i], self.at.core)

    def keep(self, i):
        at = self.at
        return pltpu.make_async_copy(self.shard(i), self.spot(at.dp, i), self.here.at[i])

    def start(self):
        at = self.at
        down, up = self.late()
        for i in range(self.pre, self.pieces):

            @pl.when(down)
            def _():
                self.down_copy(0, i, True).start()

            @pl.when(up)
            def _():
                self.up_copy(0, i, True).start()

        for i in range(self.pieces):
            self.core_copy(at.p, i, True).start()
            if self.shard:
                self.keep(i).start()

    def late(self):
        at = self.at
        if self.wide:
            return at.p == 1, at.p == at.n - 2
        return at.has_below, at.has_above

    def slot(self, h, i):
        at = self.at
        n, p = at.n, at.p

        @pl.when(p + h < n)
        def _():
            self.down_copy(h - 1, i).wait_recv()

            @pl.when(at.has_below)
            def _():
                self.down_copy(h, i).start()

            self.core_copy(p + h, i).start()

        @pl.when(p - h >= 0)
        def _():
            self.up_copy(h - 1, i).wait_recv()

            @pl.when(at.has_above)
            def _():
                self.up_copy(h, i).start()

            self.core_copy(p - h, i).start()

    def stage(self, h):
        @pl.loop(self.pre if h == 1 else 0, self.pieces)
        def _(i):
            if h == 1 and self.wide:
                self.slot_ends(i)
            else:
                self.slot(h, i)

    def slot_ends(self, i):
        at = self.at

        @pl.when(at.p == 0)
        def _():
            self.down_copy(0, i).wait_recv()
            self.core_copy(1, i).start()

        @pl.when(at.p == at.n - 1)
        def _():
            self.up_copy(0, i).wait_recv()
            self.core_copy(at.n - 2, i).start()

    def early(self, i, above, below):
        at = self.at
        both = at.has_above & at.has_below
        everyone = i < self.pre

        @pl.when(at.has_above if everyone else both)
        def _():
            b = 2 * at.p + 2 + at.c
            dst = self.spot(b, i)

            @pl.when(at.has_below)
            def _():
                remote(above, dst, self.d_s.at[1, i], self.d_r.at[1, i], at.below).start()

            z = at.p + 1
            remote(above, dst, self.c_s.at[z, i], self.c_r.at[z, i], at.core).start()

        @pl.when(at.has_below if everyone else both)
        def _():
            b = 2 * at.p - 2 + at.c
            dst = self.spot(b, i)

            @pl.when(at.has_above)
            def _():
                remote(below, dst, self.u_s.at[1, i], self.u_r.at[1, i], at.above).start()

            z = at.p - 1
            remote(below, dst, self.c_s.at[z, i], self.c_r.at[z, i], at.core).start()

    def ready(self, z, i):
        self.core_copy(z, i, incoming=True).wait_recv()

    def drain(self):
        at = self.at
        n, p = at.n, at.p

        down, up = self.late()

        @pl.loop(0, self.pieces)
        def _(i):
            for h in range(n):
                own = h == 0

                @pl.when((down & (i >= self.pre)) if own else ((p + h < n) & at.has_below))
                def _():
                    self.down_copy(h, i, own).wait_send()

                @pl.when((up & (i >= self.pre)) if own else ((p - h >= 0) & at.has_above))
                def _():
                    self.up_copy(h, i, own).wait_send()

            for z in range(n):
                self.core_copy(z, i).wait_send()


def line_gather_scratch(n, pieces):
    dma = pltpu.SemaphoreType.DMA
    return [dma((n, pieces))] * 6 + [dma((pieces,))]


def rows_spot(out, rows, width):
    def spot(b, i):
        rs = pl.ds(pl.multiple_of(b * rows, rows), rows)
        return out.at[rs, pl.ds(pl.multiple_of(i * width, width), width)]

    return spot


def cols_of(ref, width, base=0):
    return lambda i: ref.at[:, pl.ds(pl.multiple_of(base + i * width, width), width)]


class Presend:
    def __init__(self, at, src, got, sems, narrow):
        s, r = sems
        wide = src.shape[1]
        n, p = at.n, at.p
        self.sends, self.comes = [], []
        for width in sorted({narrow, wide}):
            cols = pl.ds(0, width)
            down = remote(src.at[:, cols], got.at[0, :, cols], s.at[0], r.at[0], at.below)
            up = remote(src.at[:, cols], got.at[1, :, cols], s.at[1], r.at[1], at.above)
            if narrow == wide:
                whens = at.has_below, at.has_above, at.has_above, at.has_below
            elif width == narrow:
                whens = p == 1, p == n - 2, p == 0, p == n - 1
            else:
                inner = at.has_above & at.has_below
                whens = p > 1, p < n - 2, inner, inner
            self.sends += [(whens[0], down), (whens[1], up)]
            self.comes += [(whens[2], down), (whens[3], up)]

    def start(self):
        for when, copy in self.sends:
            pl.when(when)(copy.start)

    def finish(self):
        for when, copy in self.comes:
            pl.when(when)(copy.wait_recv)
        for when, copy in self.sends:
            pl.when(when)(copy.wait_send)


def attend_rows(qkv, out, seq, hh, count, head):
    cols = lambda first: pl.ds(pl.multiple_of(first + head * HD, HD), HD)
    blk = 256
    for i in range(seq // blk):
        rows = pl.ds(i * blk, blk)
        span = (i + 1) * blk
        lg = logistic_block(qkv[rows, cols(0)], qkv[pl.ds(0, span), cols(hh)], seq)
        w = jnp.where(allowed_block(i * blk, blk, 0, span, count), lg, 0.0).astype(BF)
        out[rows, cols(0)] = dot(w, qkv[pl.ds(0, span), cols(2 * hh)]).astype(BF)


def attn_kernel(
    n_dp,
    n_mp,
    count_ref,
    ga_ref,
    gf_ref,
    wq_hbm,
    wk_hbm,
    wv_hbm,
    wo_hbm,
    wg_hbm,
    wu_hbm,
    wd_hbm,
    x_hbm,
    cot_hbm,
    aw_ref,
    qkv_ref,
    att_ref,
    nin_ref,
    gains_ref,
    gush_ref,
    dnsh_ref,
    cotm_ref,
    gpre_ref,
    gains_in,
    w4,
    wo,
    shard,
    x,
    qkv,
    wbuf,
    wgu,
    wd,
    gush,
    dnsh,
    cot,
    load_s,
    wb_s,
    out_s,
    *rest,
):
    at = Place(n_dp, n_mp)
    n = at.n
    chunk, hh = wq_hbm.shape
    seq, d = x.shape
    ff = wgu.shape[2]
    loads = [
        pltpu.make_async_copy(src, dst, load_s.at[i])
        for i, (src, dst) in enumerate(
            [
                (wq_hbm, w4.at[0]),
                (wk_hbm, w4.at[1]),
                (wv_hbm, w4.at[2]),
                (wo_hbm, wo),
                (x_hbm, x),
                (wg_hbm, wgu.at[0]),
                (wu_hbm, wgu.at[1]),
                (wd_hbm, wd),
                (cot_hbm, cot),
            ]
        )
    ]
    for cp in loads:
        cp.start()
    spot = rows_spot(aw_ref, chunk, hh)
    three = LineGather(at, 3, cols_of(shard, hh), spot, rest[0:7])
    last = LineGather(
        at, 1, lambda i: shard.at[:, pl.ds(3 * hh, hh)], lambda b, i: spot(b, 3), rest[7:14]
    )
    small = LineGather(
        at,
        1,
        lambda i: gains_in,
        lambda b, i: gains_ref.at[:, pl.ds(pl.multiple_of(b * chunk, chunk), chunk)],
        rest[14:21],
    )
    for i, ref in enumerate((ga_ref, gf_ref)):
        gains_in[i, :] = ref[...].astype(BF).astype(F32)
    enter(at)
    small.start()
    for i in range(3):
        loads[i].wait()
        shard[:, i * hh : (i + 1) * hh] = w4[i].astype(BF)
    three.start()
    loads[3].wait()
    shard[:, 3 * hh :] = wo[...].T.astype(BF)
    small.slot(1, 0)
    loads[5].wait()
    loads[6].wait()
    half = ff // PIECES

    @pl.loop(0, PIECES)
    def _(i):
        cols = pl.ds(pl.multiple_of(i * half, half), half)
        for k in range(2):
            to = pl.ds(pl.multiple_of((2 * i + k) * half, half), half)
            gush[:, to] = wgu[k, :, cols].astype(BF)

    outs = [pltpu.make_async_copy(gush, gush_ref, out_s.at[0])]
    outs[0].start()
    loads[7].wait()

    @pl.loop(0, ff // 256)
    def _(i):
        rs = pl.ds(pl.multiple_of(i * 256, 256), 256)
        dnsh[:, rs] = wd[rs, :].T.astype(BF)

    outs.append(pltpu.make_async_copy(dnsh, dnsh_ref, out_s.at[2]))
    outs[-1].start()
    loads[8].wait()
    count = count_ref[0]

    @pl.loop(0, seq // 32)
    def _(b):
        rs = pl.ds(pl.multiple_of(b * 32, 32), 32)
        row = b * 32 + lax.broadcasted_iota(jnp.int32, (32, d), 0)
        cot[rs, :] = jnp.where(row < count, cot[rs, :].astype(F32), 0.0).astype(BF)

    outs.append(pltpu.make_async_copy(cot, cotm_ref, out_s.at[3]))
    outs[-1].start()
    for h in range(1, n - 1):
        small.slot(h + 1, 0)
        three.stage(h)
        if h == n - 2:
            last.start()
    small.keep(0).wait()
    for z in range(n):
        small.ready(z, 0)
    loads[4].wait()

    @pl.loop(0, seq // 32)
    def _(b):
        rs = pl.ds(pl.multiple_of(b * 32, 32), 32)
        v = x[rs, :].astype(F32)
        scale = lax.rsqrt(jnp.mean(v * v, axis=1, keepdims=True) + EPS)
        x[rs, :] = (v * scale * gains_ref[0:1, :]).astype(BF)

    outs.append(pltpu.make_async_copy(x, nin_ref, out_s.at[1]))
    outs[-1].start()

    def w_copy(i):
        cols = pl.ds(pl.multiple_of(i * hh, hh), hh)
        return pltpu.make_async_copy(aw_ref.at[:, cols], wbuf.at[i], wb_s.at[i])

    for i in range(3):
        three.slot(n - 1, i)
        three.keep(i).wait()
        for z in range(n):
            three.ready(z, i)
        w_copy(i).start()
        if i == 1:
            last.slot(1, 0)
        w_copy(i).wait()

        @pl.loop(0, seq // 256)
        def _(b):
            rs = pl.ds(pl.multiple_of(b * 256, 256), 256)
            qkv[rs, i * hh : (i + 1) * hh] = dot(x[rs, :], wbuf[i]).astype(BF)

    outs.append(pltpu.make_async_copy(qkv, qkv_ref, out_s.at[4]))
    outs[-1].start()
    for h in range(2, n - 1):
        last.slot(h, 0)
    ahead = Presend(at, gush.at[:, pl.ds(0, 2 * half * AHEAD)], gpre_ref, rest[21:23], 2 * half * AHEAD)
    ahead.start()
    heads = hh // HD

    @pl.loop(0, heads // 2)
    def _(head):
        attend_rows(qkv, att_ref, seq, hh, count, head)

    last.slot(n - 1, 0)

    @pl.loop(heads // 2, heads)
    def _(head):
        attend_rows(qkv, att_ref, seq, hh, count, head)

    last.keep(0).wait()
    for z in range(n):
        last.ready(z, 0)
    for cp in outs:
        cp.wait()
    ahead.finish()
    small.drain()
    three.drain()
    last.drain()


def attn_stage(n_dp, n_mp, counts, ga, gf, wq, wk, wv, wo, wg, wu, wd, x, cot):
    seq, d = x.shape
    chunk, hh = wq.shape
    ff = wg.shape[1]
    n = n_dp // 2
    dma = pltpu.SemaphoreType.DMA
    hbm = pl.BlockSpec(memory_space=pl.ANY)
    vm = pl.BlockSpec(memory_space=pltpu.VMEM)
    shapes = [
        ((d, 4 * hh), BF),
        ((seq, 3 * hh), BF),
        ((seq, hh), BF),
        ((seq, d), BF),
        ((8, d), F32),
        ((chunk, 2 * ff), BF),
        ((chunk, ff), BF),
        ((seq, d), BF),
        ((2, chunk, 2 * ff * AHEAD // PIECES), BF),
    ]
    return pl.pallas_call(
        functools.partial(attn_kernel, n_dp, n_mp),
        out_shape=[jax.ShapeDtypeStruct(*s) for s in shapes],
        in_specs=[pl.BlockSpec(memory_space=pltpu.SMEM), vm, vm] + [hbm] * 9,
        out_specs=[hbm, hbm, vm, hbm, vm, hbm, hbm, hbm, hbm],
        scratch_shapes=[
            pltpu.VMEM((8, chunk), F32),
            pltpu.VMEM((3, chunk, hh), F32),
            pltpu.VMEM((hh, chunk), F32),
            pltpu.VMEM((chunk, 4 * hh), BF),
            pltpu.VMEM((seq, d), BF),
            pltpu.VMEM((seq, 3 * hh), BF),
            pltpu.VMEM((3, d, hh), BF),
            pltpu.VMEM((2, chunk, ff), F32),
            pltpu.VMEM((ff, chunk), F32),
            pltpu.VMEM((chunk, 2 * ff), BF),
            pltpu.VMEM((chunk, ff), BF),
            pltpu.VMEM((seq, d), BF),
            dma((9,)),
            dma((3,)),
            dma((5,)),
        ]
        + line_gather_scratch(n, 3)
        + line_gather_scratch(n, 1) * 2
        + [dma((2,))] * 2,
        compiler_params=pltpu.CompilerParams(
            collective_id=1, has_side_effects=True, vmem_limit_bytes=VMEM_LIMIT
        ),
        name="attn_stage",
    )(counts, ga, gf, wq, wk, wv, wo, wg, wu, wd, x, cot)


def gate_kernel(
    n_dp,
    n_mp,
    att_ref,
    aw_hbm,
    sh_hbm,
    gpre_hbm,
    dnsh_hbm,
    x_hbm,
    gain_ref,
    gw_ref,
    nm_ref,
    hid_hbm,
    gu_ref,
    inner_ref,
    dpre_ref,
    wo,
    gp,
    sh,
    xs,
    hid,
    acc,
    nm,
    wbuf,
    gbuf,
    ibuf,
    gp_s,
    load_s,
    wb_s,
    gb_s,
    ib_s,
    *rest,
):
    at = Place(n_dp, n_mp)
    n = at.n
    quad = QuadSum(at, *rest[0:2], rest[2:4])
    gather_nm = QuadGather(at, rest[4], nm_ref, rest[5:8])
    sems = rest[8:15]
    hh = wo.shape[1]
    part, half_cols = quad.t.shape[2], quad.t.shape[3]
    chunk, wide = sh_hbm.shape
    pieces = sems[6].shape[0]
    width = wide // pieces
    line = LineGather(at, pieces, cols_of(sh, width), rows_spot(gw_ref, chunk, width), sems, AHEAD)

    load_sh = pltpu.make_async_copy(sh_hbm, sh, load_s.at[2])
    load_sh.start()
    load_gp = pltpu.make_async_copy(gpre_hbm, gp, load_s.at[3])
    load_gp.start()
    load = pltpu.make_async_copy(aw_hbm.at[:, pl.ds(3 * hh, hh)], wo, load_s.at[0])
    load.start()
    load_x = pltpu.make_async_copy(x_hbm.at[part_rows(at, part), :], xs, load_s.at[1])
    load_x.start()
    enter(at)
    load_sh.wait()
    line.start()
    load_gp.wait()

    def place(side, i):
        b = at.dp + (2 if side == 0 else -2)
        piece = gp.at[side, :, pl.ds(i * width, width)]
        return pltpu.make_async_copy(piece, line.spot(b, i), gp_s.at[side, i])

    for i in range(AHEAD):
        line.early(i, *[gp.at[side, :, pl.ds(i * width, width)] for side in range(2)])
        pl.when(at.has_above)(place(0, i).start)
        pl.when(at.has_below)(place(1, i).start)
    load.wait()

    def terms(q):
        rs = pl.ds(pl.multiple_of(q * part, part), part)
        for half in range(2):
            w = wo[half * half_cols : (half + 1) * half_cols, :]
            quad.t[half, q] = dot(att_ref[rs, :], w, NT).astype(BF)

    for mask in quad.masks():
        terms(at.quarter(mask))
        quad.offer(mask)
    quad.turn()
    quad.arrive()
    load_x.wait()

    @pl.loop(0, part // 32)
    def _(b):
        rs = pl.ds(pl.multiple_of(b * 32, 32), 32)
        h = xs[rs, :].astype(F32) + jnp.concatenate(
            [quad.total(0, rs), quad.total(1, rs)], axis=1
        )
        hid[rs, :] = h
        scale = lax.rsqrt(jnp.mean(h * h, axis=1, keepdims=True) + EPS)
        res = (h * scale * gain_ref[1:2, :]).astype(BF)
        gather_nm.own[0, rs, :] = res[:, :half_cols]
        gather_nm.own[1, rs, :] = res[:, half_cols:]

    gather_nm.start()
    store_hid = pltpu.make_async_copy(hid, hid_hbm, load_s.at[1])
    store_hid.start()
    line.stage(1)
    gather_nm.forward()
    gather_nm.finish()
    load = pltpu.make_async_copy(nm_ref, nm, load_s.at[0])
    load.start()
    for h in range(2, n - 1):
        line.stage(h)
    load.wait()

    for i in range(AHEAD):
        pl.when(at.has_above)(place(0, i).wait)
        pl.when(at.has_below)(place(1, i).wait)
    ahead = Presend(at, dnsh_hbm, dpre_ref, rest[15:17], width // 2 * DOWN_AHEAD)
    ahead.start()

    pair = 2 * chunk
    near = jnp.where(2 * at.p < n, 0, 1)
    far = jnp.where(2 * at.p < n, n - 1, 0)
    most = (n - 1) * pair
    most_rows = pl.ds(pl.multiple_of(near * pair, pair), most)
    far_rows = pl.ds(pl.multiple_of(far * pair, pair), pair)

    def w_copy(i, slot, rows):
        cols = pl.ds(pl.multiple_of(i * width, width), width)
        return pltpu.make_async_copy(
            gw_ref.at[rows, cols], wbuf.at[slot, rows, :], wb_s.at[slot]
        )

    def first_part(i, slot):
        line.keep(i).wait()

        @pl.loop(0, n - 1)
        def _(z):
            line.ready(near + z, i)

        w_copy(i, slot, most_rows).start()
        w_copy(i, slot, most_rows).wait()

        @pl.loop(0, nm.shape[0] // 256)
        def _(b):
            rs = pl.ds(pl.multiple_of(b * 256, 256), 256)
            acc[rs, :] = dot(nm[rs, most_rows], wbuf[slot, most_rows, :])

    def g_copy(i, slot):
        cols = pl.ds(pl.multiple_of(i * width, width), width)
        return pltpu.make_async_copy(gbuf.at[slot], gu_ref.at[:, cols], gb_s.at[slot])

    def i_copy(i, slot):
        cols = pl.ds(pl.multiple_of(i * (width // 2), width // 2), width // 2)
        return pltpu.make_async_copy(ibuf.at[slot], inner_ref.at[:, cols], ib_s.at[slot])

    @pl.loop(0, pieces)
    def _(i):
        slot = lax.rem(i, 2)
        first_part(i, slot)
        line.slot(n - 1, i)
        line.ready(far, i)
        w_copy(i, slot, far_rows).start()

        @pl.when(i >= 2)
        def _():
            g_copy(i - 2, slot).wait()
            i_copy(i - 2, slot).wait()

        w_copy(i, slot, far_rows).wait()

        @pl.loop(0, nm.shape[0] // 256)
        def _(b):
            rs = pl.ds(pl.multiple_of(b * 256, 256), 256)
            v = (acc[rs, :] + dot(nm[rs, far_rows], wbuf[slot, far_rows, :])).astype(BF)
            gbuf[slot, rs, :] = v
            g = v[:, : width // 2].astype(F32)
            u = v[:, width // 2 :].astype(F32)
            ibuf[slot, rs, :] = (g / (1.0 + jnp.exp(-g)) * u).astype(BF)

        g_copy(i, slot).start()
        i_copy(i, slot).start()

    for i in range(max(0, pieces - 2), pieces):
        g_copy(i, i % 2).wait()
        i_copy(i, i % 2).wait()
    store_hid.wait()
    ahead.finish()
    line.drain()
    quad.drain()


def gate_stage(n_dp, n_mp, att, aw, shard, gpre, dnsh, x, gain):
    seq, hh = att.shape
    d = aw.shape[0]
    chunk, wide = shard.shape
    n, part = n_dp // 2, seq // n_mp
    dma = pltpu.SemaphoreType.DMA
    hbm = pl.BlockSpec(memory_space=pl.ANY)
    vm = pl.BlockSpec(memory_space=pltpu.VMEM)
    width = wide // PIECES
    return pl.pallas_call(
        functools.partial(gate_kernel, n_dp, n_mp),
        out_shape=[
            jax.ShapeDtypeStruct((d, wide), BF),
            jax.ShapeDtypeStruct((seq, d), BF),
            jax.ShapeDtypeStruct((part, d), F32),
            jax.ShapeDtypeStruct((seq, wide), BF),
            jax.ShapeDtypeStruct((seq, wide // 2), BF),
            jax.ShapeDtypeStruct((2, chunk, wide // 2), BF),
        ],
        in_specs=[vm, hbm, hbm, hbm, hbm, hbm, vm],
        out_specs=[hbm] * 6,
        scratch_shapes=[
            pltpu.VMEM((d, hh), BF),
            pltpu.VMEM((2, chunk, width * AHEAD), BF),
            pltpu.VMEM((chunk, wide), BF),
            pltpu.VMEM((part, d), BF),
            pltpu.VMEM((part, d), F32),
            pltpu.VMEM((seq, width), F32),
            pltpu.VMEM((seq, d), BF),
            pltpu.VMEM((2, d, width), BF),
            pltpu.VMEM((2, seq, width), BF),
            pltpu.VMEM((2, seq, width // 2), BF),
            dma((2, AHEAD)),
            dma((4,)),
            dma((2,)),
            dma((2,)),
            dma((2,)),
        ]
        + quad_sum_scratch(n_mp, part, d // 2)
        + quad_gather_scratch(n_mp, part, d // 2)
        + line_gather_scratch(n, PIECES)
        + [dma((2,))] * 2,
        compiler_params=pltpu.CompilerParams(
            collective_id=2, has_side_effects=True, vmem_limit_bytes=VMEM_LIMIT
        ),
        name="gate_stage",
    )(att, aw, shard, gpre, dnsh, x, gain)


def down_kernel(
    n_dp,
    n_mp,
    inner_hbm,
    gu_hbm,
    cot_hbm,
    sh_hbm,
    dpre_hbm,
    rs_ref,
    ft_ref,
    ggu_ref,
    pend_ref,
    inner,
    gu,
    cot,
    dn,
    acc,
    ftb,
    res,
    dp_s,
    load_s,
    cot_s,
    in_s,
    rs_s,
    ft_s,
    dn_s,
    gg_s,
    *rest,
):
    at = Place(n_dp, n_mp)
    n, p = at.n, at.p
    line = LineSum(at, *rest[0:4], rest[4:10], defer=True)
    sems = rest[10:17]
    chunk, ff = sh_hbm.shape
    pieces = sems[6].shape[0]
    width = ff // pieces
    gather = LineGather(at, pieces, None, rows_spot(dn, chunk, width), sems, DOWN_AHEAD, True)
    pair = 2 * chunk
    def cot_copy(k):
        cols = pl.ds(pl.multiple_of(order_of(k, at) * pair, pair), pair)
        return pltpu.make_async_copy(cot_hbm.at[:, cols], cot.at[:, cols], cot_s.at[k])

    def in_copy(i):
        cols = pl.ds(pl.multiple_of(i * width, width), width)
        return pltpu.make_async_copy(inner_hbm.at[:, cols], inner.at[:, cols], in_s.at[i])

    load_gu = pltpu.make_async_copy(gu_hbm, gu, load_s.at[0])
    own = pltpu.make_async_copy(
        sh_hbm, dn.at[pl.ds(pl.multiple_of(at.dp * chunk, chunk), chunk), :], dn_s.at[0]
    )
    own.start()

    inside = at.has_above & at.has_below

    def pre_copy(side, i):
        b = at.dp + (2 if side == 0 else -2)
        piece = dpre_hbm.at[side, :, pl.ds(i * width, width)]
        return pltpu.make_async_copy(piece, gather.spot(b, i), dp_s.at[side, i])

    def pre_whens(i):
        return (at.has_above, at.has_below) if i < DOWN_AHEAD else (inside, inside)

    for i in range(pieces):
        for side in range(2):
            pl.when(pre_whens(i)[side])(pre_copy(side, i).start)
    cot_copy(0).start()
    for i in range(pieces):
        in_copy(i).start()
    for k in range(1, n):
        cot_copy(k).start()
    load_gu.start()
    enter(at)
    own.wait()
    gather.start()
    for i in range(pieces):
        for side in range(2):
            pl.when(pre_whens(i)[side])(pre_copy(side, i).wait)
        gather.early(i, gather.spot(at.dp + 2, i), gather.spot(at.dp - 2, i))

    def run(e):
        k, core = e // 2, e % 2
        block = 2 * order_of(k, at) + (1 - at.c if core == 0 else at.c)
        if core == 0:
            cot_copy(k).wait()
        lhs = cot[:, pl.ds(pl.multiple_of(block * chunk, chunk), chunk)].T

        def tile(i):
            if e == 0:
                in_copy(i).wait()
            return dot(lhs, inner[:, pl.ds(pl.multiple_of(i * width, width), width)])

        if core == 0:
            line.other(k, tile)
        else:
            line.mine(k, tile)

    for e in range(2 * n):
        run(e)

    def ft_copy(z, slot):
        cols = pl.ds(pl.multiple_of(z * pair, pair), pair)
        return pltpu.make_async_copy(ftb.at[slot], ft_ref.at[:, cols], ft_s.at[slot])

    def rows_of(z):
        return pl.ds(pl.multiple_of(z * pair, pair), pair)

    def grads(z, fresh):
        @pl.loop(0, pieces)
        def _(i):
            gather.ready(z, i)

        @pl.loop(0, ff // 512)
        def _(i):
            cols = pl.ds(pl.multiple_of(i * 512, 512), 512)
            v = dot(cot[:, rows_of(z)], dn[rows_of(z), cols])
            acc[:, cols] = v if fresh else acc[:, cols] + v

    def branch(z, fresh):
        if not fresh:
            ft_copy(z, 0).wait()
        ftb[0] = dot(inner[...], dn[rows_of(z), :], NT).astype(BF)
        ft_copy(z, 0).start()

    def blocks(h):
        @pl.when(p + h < n)
        def _():
            grads(p + h, False)
            branch(p + h, False)

        @pl.when(p - h >= 0)
        def _():
            grads(p - h, False)
            branch(p - h, False)

    gather.stage(1)
    grads(p, True)
    branch(p, True)
    line.slot(0)
    if n > 3:
        gather.stage(2)
    load_gu.wait()
    half = width

    def cols_at(i):
        g = pl.ds(pl.multiple_of(i * 2 * half, half), half)
        u = pl.ds(pl.multiple_of(i * 2 * half + half, half), half)
        return g, u, pl.ds(pl.multiple_of(i * half, half), half)

    @pl.loop(0, pieces)
    def _(i):
        gcols, ucols, _ = cols_at(i)

        @pl.loop(0, gu.shape[0] // 64)
        def _(b):
            rs = pl.ds(pl.multiple_of(b * 64, 64), 64)
            g = gu[rs, gcols].astype(F32)
            u = gu[rs, ucols].astype(F32)
            sg = 1.0 / (1.0 + jnp.exp(-g))
            gu[rs, gcols] = (u * sg * (1.0 + g * (1.0 - sg))).astype(BF)
            gu[rs, ucols] = (g * sg).astype(BF)

    blocks(1)
    for h in range(2, n - 1):
        line.slot(h - 1)
        if h + 1 < n - 1:
            gather.stage(h + 1)
        blocks(h)

    gather.stage(n - 1)

    @pl.when(jnp.logical_not(at.has_below))
    def _():
        grads(n - 1, False)

    @pl.when(jnp.logical_not(at.has_above))
    def _():
        grads(0, False)

    def gg_copy(i):
        cols = pl.ds(pl.multiple_of(i * 2 * half, 2 * half), 2 * half)
        return pltpu.make_async_copy(gu.at[:, cols], ggu_ref.at[:, cols], gg_s.at[i])

    @pl.loop(0, pieces)
    def _(i):
        gcols, ucols, acols = cols_at(i)

        @pl.loop(0, gu.shape[0] // 64)
        def _(b):
            rs = pl.ds(pl.multiple_of(b * 64, 64), 64)
            gi = acc[rs, acols]
            gu[rs, gcols] = (gi * gu[rs, gcols].astype(F32)).astype(BF)
            gu[rs, ucols] = (gi * gu[rs, ucols].astype(F32)).astype(BF)

        gg_copy(i).start()

    @pl.when(jnp.logical_not(at.has_below))
    def _():
        branch(n - 1, False)

    @pl.when(jnp.logical_not(at.has_above))
    def _():
        branch(0, False)

    stores = line.final(res, rs_ref, rs_s)
    keep_low = pltpu.make_async_copy(line.own.at[0], pend_ref, dn_s.at[0])
    keep_high = pltpu.make_async_copy(line.own.at[n - 1], pend_ref, dn_s.at[0])
    pl.when(p == 1)(keep_low.start)
    pl.when(p == n - 2)(keep_high.start)
    pl.when((p == 1) | (p == n - 2))(keep_low.wait)
    for i in range(pieces):
        gg_copy(i).wait()
    ft_copy(p, 0).wait()
    for cp in stores:
        cp.wait()
    line.drain()
    gather.drain()


def down_stage(n_dp, n_mp, inner, gu, cot, shard, dpre):
    seq, d = cot.shape
    chunk, ff = shard.shape
    n = n_dp // 2
    dma = pltpu.SemaphoreType.DMA
    hbm = pl.BlockSpec(memory_space=pl.ANY)
    return pl.pallas_call(
        functools.partial(down_kernel, n_dp, n_mp),
        out_shape=[
            jax.ShapeDtypeStruct((PIECES, chunk, ff // PIECES), BF),
            jax.ShapeDtypeStruct((seq, d), BF),
            jax.ShapeDtypeStruct((seq, 2 * ff), BF),
            jax.ShapeDtypeStruct((PIECES, chunk, ff // PIECES), BF),
        ],
        in_specs=[hbm] * 5,
        out_specs=[hbm] * 4,
        scratch_shapes=[
            pltpu.VMEM((seq, ff), BF),
            pltpu.VMEM((seq, 2 * ff), BF),
            pltpu.VMEM((seq, d), BF),
            pltpu.VMEM((d, ff), BF),
            pltpu.VMEM((seq, ff), F32),
            pltpu.VMEM((1, seq, 2 * chunk), BF),
            pltpu.VMEM((PIECES, chunk, ff // PIECES), BF),
            dma((2, PIECES)),
            dma((1,)),
            dma((n,)),
            dma((PIECES,)),
            dma((PIECES,)),
            dma((1,)),
            dma((1,)),
            dma((PIECES,)),
        ]
        + line_sum_scratch(n, PIECES, chunk, ff // PIECES)
        + line_gather_scratch(n, PIECES),
        compiler_params=pltpu.CompilerParams(
            collective_id=3, has_side_effects=True, vmem_limit_bytes=VMEM_LIMIT
        ),
        name="down_stage",
    )(inner, gu, cot, shard, dpre)


def mid_kernel(
    n_dp,
    n_mp,
    ggu_hbm,
    gw_hbm,
    nm_hbm,
    ft_hbm,
    cot_hbm,
    qkv_hbm,
    aw_hbm,
    count_ref,
    hid_hbm,
    gain_ref,
    rs_ref,
    low_ref,
    lay_ref,
    gh_hbm,
    gg_ref,
    dq_ref,
    space,
    wt,
    wt_s,
    nm,
    nm_s,
    cot,
    hid,
    gh,
    res,
    gg_s,
    rs_s,
    dka,
    dva,
    load_s,
    *rest,
):
    at = Place(n_dp, n_mp)
    n = at.n
    line = LineSum(at, *rest[0:4], rest[4:10])
    mid = QuadSum(at, *rest[10:12], rest[12:14])
    lay = QuadSumHbm(at, ft_hbm, *rest[14:16], rest[16:19])
    gather_low = QuadGather(at, rest[19], low_ref, rest[20:23])
    gather_lay = QuadGather(at, rest[23], lay_ref, rest[24:27])
    part, half_cols = mid.t.shape[2], mid.t.shape[3]
    chunk, width = line.own.shape[2], line.own.shape[3]
    pieces = line.pieces
    hh = qkv_hbm.shape[1] // 3
    drows = wt.shape[1]
    tiles = half_cols // drows

    wide = ggu_hbm.shape[1]
    ggu = space.at[:, pl.ds(0, wide)]

    def gg_copy(i):
        cols = pl.ds(pl.multiple_of(i * width, width), width)
        return pltpu.make_async_copy(ggu_hbm.at[:, cols], ggu.at[:, cols], gg_s.at[i])

    load_cot = pltpu.make_async_copy(cot_hbm.at[part_rows(at, part), :], cot, load_s.at[1])

    def nm_copy(e):
        k, core = e // 2, e % 2
        block = 2 * order_of(k, at) + (1 - at.c if core == 0 else at.c)
        cols = pl.ds(pl.multiple_of(block * chunk, chunk), chunk)
        return pltpu.make_async_copy(nm_hbm.at[:, cols], nm.at[e % 2], nm_s.at[e % 2])

    def wt_copy(half, i, slot):
        rows = pl.ds(pl.multiple_of(half * half_cols + i * drows, drows), drows)
        return pltpu.make_async_copy(gw_hbm.at[rows, :], wt.at[slot], wt_s.at[slot])

    nm_copy(0).start()
    for i in range(pieces):
        gg_copy(i).start()
    wt_copy(0, 0, 0).start()
    load_cot.start()
    load_hid = pltpu.make_async_copy(hid_hbm, hid, load_s.at[0])
    load_hid.start()
    for cp in lay.loads:
        cp.start()
    enter(at)
    for mask in lay.masks():
        lay.offer(mask)

    def run(e):
        if e + 1 < 2 * n:
            nm_copy(e + 1).start()
        nm_copy(e).wait()
        lhs = nm[e % 2].T

        def tile(i):
            if e == 0:
                gg_copy(i).wait()
            return dot(lhs, ggu[:, pl.ds(pl.multiple_of(i * width, width), width)])

        if e % 2 == 0:
            line.other(e // 2, tile)
        else:
            line.mine(e // 2, tile)

    def terms(half):
        @pl.loop(0, tiles)
        def _(i):
            slot = lax.rem(i, 2)
            if half == 0:
                nxt = wt_copy(jnp.where(i + 1 < tiles, 0, 1), lax.rem(i + 1, tiles), 1 - slot)
                nxt.start()
            else:

                @pl.when(i + 1 < tiles)
                def _():
                    wt_copy(1, i + 1, 1 - slot).start()

            wt_copy(half, i, slot).wait()
            v = dot(ggu[...], wt[slot], NT).astype(BF)
            cols = pl.ds(pl.multiple_of(i * drows, drows), drows)
            for q in range(n_mp):
                mid.t[half, q, :, cols] = v[q * part : (q + 1) * part]

        for mask in mid.masks():
            mid.offer(mask, (half,))

    run(0)
    run(1)
    terms(0)
    run(2)
    run(3)
    for cp in lay.loads:
        cp.wait()
    lay.turn()
    terms(1)
    for e in range(4, 2 * n):
        run(e)
    lay.arrive()
    load_hid.wait()

    @pl.loop(0, part // 32)
    def _(b):
        rs = pl.ds(pl.multiple_of(b * 32, 32), 32)
        for half in range(2):
            h = hid[rs, pl.ds(half * half_cols, half_cols)]
            gather_lay.own[half, rs, :] = (h + lay.total(half, rs)).astype(BF)

    gather_lay.start([0])
    line.slot(0)
    per = half_cols // hh
    blocks_d = 2 * half_cols // part
    wo_spot = [(e // per // (n_mp // 2), e // per % (n_mp // 2), e % per) for e in range(blocks_d)]
    wo_parts = [
        pltpu.make_async_copy(
            aw_hbm.at[pl.ds(e * part, part), pl.ds(3 * hh, hh)],
            lay.t.at[i, j, :, pl.ds(k * hh, hh)],
            load_s.at[4 + e],
        )
        for e, (i, j, k) in enumerate(wo_spot)
    ]
    for cp in wo_parts:
        cp.start()
    load_qkv = pltpu.make_async_copy(
        qkv_hbm, space.at[:, pl.ds(2 * half_cols, 3 * hh)], load_s.at[2]
    )
    load_qkv.start()
    mid.turn()
    mid.arrive()
    load_cot.wait()
    gg_ref[...] = jnp.zeros_like(gg_ref)

    @pl.loop(0, part // 32)
    def _(b):
        rs = pl.ds(pl.multiple_of(b * 32, 32), 32)
        h = hid[rs, :]
        scale = lax.rsqrt(jnp.mean(h * h, axis=1, keepdims=True) + EPS)
        g = jnp.concatenate([mid.total(0, rs), mid.total(1, rs)], axis=1)
        unit = h * scale
        weighted = g * gain_ref[1:2, :]
        field = scale * (weighted - unit * jnp.mean(weighted * unit, axis=1, keepdims=True))
        out = cot[rs, :].astype(F32) + field
        gh[rs, :] = out
        low = out.astype(BF)
        gather_low.own[0, rs, :] = low[:, :half_cols]
        gather_low.own[1, rs, :] = low[:, half_cols:]
        gg_ref[...] += jnp.sum(g * unit, axis=0, keepdims=True)

    gather_low.start()
    store_gh = pltpu.make_async_copy(gh, gh_hbm, load_s.at[1])
    store_gh.start()
    for s in range(1, n - 2):
        line.slot(s)
    gather_low.forward()
    gather_lay.start(range(1, gather_lay.levels))
    gather_low.finish()
    load_low = pltpu.make_async_copy(low_ref, space.at[:, pl.ds(0, 2 * half_cols)], load_s.at[3])
    load_low.start()
    load_low.wait()
    load_qkv.wait()
    for cp in wo_parts:
        cp.wait()
    seq = space.shape[0]
    base = 2 * half_cols
    gbase = base + 3 * hh

    @pl.loop(0, seq // 256)
    def _(b):
        rs = pl.ds(pl.multiple_of(b * 256, 256), 256)
        total = jnp.zeros((256, hh), F32)
        for e, (i, j, k) in enumerate(wo_spot):
            wo = lay.t[i, j, :, k * hh : (k + 1) * hh]
            total += dot(space[rs, e * part : (e + 1) * part], wo)
        space[rs, gbase : gbase + hh] = total.astype(BF)

    count = count_ref[0]
    blk = 256
    blocks = seq // blk

    def back(head):
        at_cols = lambda first: pl.ds(pl.multiple_of(first + head * HD, HD), HD)
        for i in range(blocks - 1, -1, -1):
            rows = pl.ds(i * blk, blk)
            span = (i + 1) * blk
            keys = pl.ds(0, span)
            q = space[rows, at_cols(base)]
            g = space[rows, at_cols(gbase)]
            k = space[keys, at_cols(base + hh)]
            lg = jnp.where(
                allowed_block(i * blk, blk, 0, span, count), logistic_block(q, k, seq), 0.0
            )
            w = lg.astype(BF)
            gw = dot(g, space[keys, at_cols(base + 2 * hh)], NT)
            gs = (gw * lg * (1.0 - lg) * HD ** (-0.5)).astype(BF)
            wt[i // 2, :, at_cols((i % 2) * (wide // 2))] = dot(gs, k).astype(BF)
            dk = dot(gs, q, TN)
            dv = dot(w, g, TN)
            if i == blocks - 1:
                dka[...] = dk
                dva[...] = dv
            else:
                dka[keys, :] += dk
                dva[keys, :] += dv
        for i in range(blocks):
            rows = pl.ds(i * blk, blk)
            wt[i // 2, :, at_cols((i % 2) * (wide // 2) + hh)] = dka[rows, :].astype(BF)
            wt[i // 2, :, at_cols((i % 2) * (wide // 2) + 2 * hh)] = dva[rows, :].astype(BF)

    heads = hh // HD
    pl.loop(0, heads // 2)(back)
    gather_lay.forward()
    pl.loop(heads // 2, heads)(back)
    stores = [
        pltpu.make_async_copy(
            wt.at[i // 2, :, pl.ds((i % 2) * (wide // 2), 3 * hh)],
            dq_ref.at[pl.ds(i * blk, blk), :],
            load_s.at[4 + i],
        )
        for i in range(blocks)
    ]
    for cp in stores:
        cp.start()
    stores += line.final(res, rs_ref, rs_s) + [store_gh]
    gather_lay.finish()
    for cp in stores:
        cp.wait()
    line.drain()
    mid.drain()
    lay.drain()


def mid_stage(n_dp, n_mp, ggu, gw, nm, ft, cot, qkv, aw, counts, hid, gain):
    seq, wide = ggu.shape
    hh = qkv.shape[1] // 3
    d = gw.shape[0]
    n, part, chunk = n_dp // 2, seq // n_mp, d // n_dp
    dma = pltpu.SemaphoreType.DMA
    hbm = pl.BlockSpec(memory_space=pl.ANY)
    vm = pl.BlockSpec(memory_space=pltpu.VMEM)
    pieces = PIECES
    return pl.pallas_call(
        functools.partial(mid_kernel, n_dp, n_mp),
        out_shape=[
            jax.ShapeDtypeStruct((pieces, chunk, wide // pieces), BF),
            jax.ShapeDtypeStruct((seq, d), BF),
            jax.ShapeDtypeStruct((seq, d), BF),
            jax.ShapeDtypeStruct((part, d), F32),
            jax.ShapeDtypeStruct((1, d), F32),
            jax.ShapeDtypeStruct((seq, 3 * hh), BF),
        ],
        in_specs=[hbm] * 7 + [pl.BlockSpec(memory_space=pltpu.SMEM), hbm, vm],
        out_specs=[hbm, hbm, hbm, hbm, vm, hbm],
        scratch_shapes=[
            pltpu.VMEM((seq, max(wide, d + 4 * hh)), BF),
            pltpu.VMEM((2, 256, wide), BF),
            dma((2,)),
            pltpu.VMEM((2, seq, chunk), BF),
            dma((2,)),
            pltpu.VMEM((part, d), BF),
            pltpu.VMEM((part, d), F32),
            pltpu.VMEM((part, d), F32),
            pltpu.VMEM((pieces, chunk, wide // pieces), BF),
            dma((pieces,)),
            dma((pieces,)),
            pltpu.VMEM((seq, HD), F32),
            pltpu.VMEM((seq, HD), F32),
            dma((4 + max(d // part, seq // 256),)),
        ]
        + line_sum_scratch(n, pieces, chunk, wide // pieces, 1)
        + quad_sum_scratch(n_mp, part, d // 2)
        + quad_sum_scratch(n_mp, part, d // 2, n_mp // 2)
        + [dma((2, n_mp // 2))]
        + quad_gather_scratch(n_mp, part, d // 2) * 2,
        compiler_params=pltpu.CompilerParams(
            collective_id=4, has_side_effects=True, vmem_limit_bytes=VMEM_LIMIT
        ),
        name="mid_stage",
    )(ggu, gw, nm, ft, cot, qkv, aw, counts, hid, gain)


def last_kernel(
    n_dp,
    n_mp,
    dqkv_hbm,
    aw_hbm,
    nin_hbm,
    low_hbm,
    att_hbm,
    x_hbm,
    gh_hbm,
    pend_hbm,
    part_hbm,
    gain_ref,
    gmid_ref,
    rs_ref,
    grad_ref,
    gains_ref,
    rsd_ref,
    rhs,
    aw,
    nin,
    low,
    lhs,
    x,
    gh,
    res,
    rs_s,
    pbuf,
    dbuf,
    pd_s,
    loads,
    pout,
    own,
    din,
    uin,
    po_s,
    po_r,
    d_s,
    d_r,
    u_s,
    u_r,
    t,
    r,
    q1,
    q2,
    gown,
    g1,
    g2,
    g3,
    gsum,
    fold_out,
    fold_in,
    fold_s,
    fold_r,
):
    at = Place(n_dp, n_mp)
    hh = att_hbm.shape[1]
    part = t.shape[2]
    chunk = own.shape[2]
    half_cols = t.shape[3]
    copies = [
        pltpu.make_async_copy(src, dst, loads.at[i])
        for i, (src, dst) in enumerate(
            [
                (dqkv_hbm, rhs.at[:, pl.ds(0, 3 * hh)]),
                (aw_hbm.at[:, pl.ds(0, 3 * hh)], aw),
                (nin_hbm, nin),
                (att_hbm, rhs.at[:, pl.ds(3 * hh, hh)]),
                (low_hbm, low),
                (x_hbm.at[part_rows(at, part), :], x),
                (gh_hbm, gh),
                (part_hbm, dbuf),
            ]
        )
    ]
    for cp in copies:
        cp.start()
    bits = [b for b in (2, 4, 8, 16) if b < n_dp]
    enter(at, [at.fold(b) for b in bits[1:]])
    quad = QuadSum(at, t, r, (q1, q2))
    line = LineSum(at, pout, own, din, uin, (po_s, po_r, d_s, d_r, u_s, u_r), True)
    gather = QuadGather(at, gown, grad_ref, (g1, g2, g3))
    n = at.n
    low_end = remote(pend_hbm, pbuf, pd_s.at[0], pd_s.at[1], at.below)
    high_end = remote(pend_hbm, pbuf, pd_s.at[0], pd_s.at[1], at.above)
    copies[0].wait()
    copies[1].wait()

    d = aw.shape[0]
    fold = fold_out.shape[2]
    per_row = d // fold

    def terms(q):
        rs = pl.ds(pl.multiple_of(q * part, part), part)
        width = 512

        @pl.loop(0, half_cols // width)
        def _(i):
            for half in range(2):
                d0 = pl.multiple_of(half * half_cols + i * width, width)
                v = dot(rhs[rs, 0 : 3 * hh], aw[pl.ds(d0, width), :], NT)
                t[half, q, :, pl.ds(pl.multiple_of(i * width, width), width)] = v.astype(BF)
                u = v * nin[rs, pl.ds(d0, width)].astype(F32)
                gsum[0:1, pl.ds(d0, width)] += jnp.sum(u, axis=0, keepdims=True)

    gsum[...] = jnp.zeros_like(gsum)
    copies[2].wait()
    masks = quad.masks()
    terms(at.quarter(masks[0]))
    quad.offer(masks[0])
    for cp in copies[3:5]:
        cp.wait()
    load_x = copies[5]

    def run(k, core):
        block = 2 * order_of(k, at) + (at.c if core else 1 - at.c)
        cols = pl.ds(pl.multiple_of(block * chunk, chunk), chunk)
        lhs[0] = nin[:, cols].T
        lhs[1] = low[:, cols].T

        def tile(i):
            return dot(lhs[lax.div(i, 3)], rhs[:, pl.ds(pl.multiple_of(i * hh, hh), hh)])

        if core:
            line.mine(k, tile)
        else:
            line.other(k, tile)

    devs = [at.core] + [at.fold(b) for b in bits] + [at.peer(b) for b in at.bits]

    def fold_copy(b):
        return remote(fold_out.at[b], fold_in.at[b], fold_s.at[b], fold_r.at[b], devs[b])

    def fold_next(b):
        fold_copy(b).wait_recv()
        fold_out[b + 1] = fold_out[b] + fold_in[b]
        if b + 1 < len(devs):
            fold_copy(b + 1).start()

    run(0, 0)
    run(0, 1)
    for mask in masks[1:]:
        terms(at.quarter(mask))
        quad.offer(mask)
    gsum[0:1, :] = gsum[0:1, :] / gain_ref[0:1, :]
    gsum[1:2, :] = gmid_ref[...]
    for i in range(2):
        for j in range(per_row):
            fold_out[0, i * per_row + j] = gsum[i, j * fold : (j + 1) * fold]
    fold_copy(0).start()
    run(1, 0)
    run(1, 1)
    fold_next(0)
    for k in range(2, n):
        run(k, 0)
        run(k, 1)
    quad.turn()
    for b in range(1, len(bits)):
        fold_next(b)
    pl.when(at.p == 1)(low_end.start)
    pl.when(at.p == n - 2)(high_end.start)
    line.slot(0)
    load_x.wait()
    copies[6].wait()
    fold_next(len(bits))
    step = part // gather.blocks

    def norm(block):
        @pl.loop(0, step // 32)
        def _(b):
            rs = pl.ds(pl.multiple_of(block * step + b * 32, 32), 32)
            v = x[rs, :].astype(F32)
            scale = lax.rsqrt(jnp.mean(v * v, axis=1, keepdims=True) + EPS)
            g = jnp.concatenate([quad.total(0, rs), quad.total(1, rs)], axis=1)
            unit = v * scale
            weighted = g * gain_ref[0:1, :]
            field = scale * (weighted - unit * jnp.mean(weighted * unit, axis=1, keepdims=True))
            total = (gh[rs, :] + field).astype(BF)
            gown[0, rs, :] = total[:, :half_cols]
            gown[1, rs, :] = total[:, half_cols:]

    for block in range(gather.blocks):
        quad.arrive(block)
        norm(block)
        gather.start(block=block)
        if block == 0:
            for b in range(len(bits) + 1, len(devs) - 1):
                fold_next(b)
    for s in range(1, n - 2):
        line.slot(s)
    for block in range(gather.blocks):
        gather.forward(block)
    fold_next(len(devs) - 1)
    for i in range(2):
        for j in range(per_row):
            gsum[i, j * fold : (j + 1) * fold] = fold_out[len(devs), i * per_row + j]
    gains_ref[...] = gsum[:, pl.ds(pl.multiple_of(at.dp * chunk, chunk), chunk)]
    copies[7].wait()

    @pl.when((at.p == 0) | (at.p == n - 1))
    def _():
        low_end.wait_recv()

        @pl.loop(0, 4)
        def _(i):
            dbuf[i] = (dbuf[i].astype(F32) + pbuf[i].astype(F32)).astype(BF)

    store = pltpu.make_async_copy(dbuf, rsd_ref, pd_s.at[2])
    store.start()
    stores = line.final(res, rs_ref, rs_s) + [store]
    pl.when((at.p == 1) | (at.p == n - 2))(low_end.wait_send)
    gather.finish()
    for cp in stores:
        cp.wait()
    line.drain()
    quad.drain()
    for b in range(len(devs)):
        fold_copy(b).wait_send()


def last_stage(n_dp, n_mp, dqkv, aw, nin, low, att, x, gh, pend, rs_down, gain, gmid):
    seq, hh = att.shape
    d = aw.shape[0]
    n, part, chunk = n_dp // 2, seq // n_mp, d // n_dp
    dma = pltpu.SemaphoreType.DMA
    anyspace = pl.BlockSpec(memory_space=pl.ANY)
    vm = pl.BlockSpec(memory_space=pltpu.VMEM)
    folds = 1 + len([b for b in (1, 2, 4, 8) if b < n_mp]) + len([b for b in (2, 4, 8, 16) if b < n_dp])
    return pl.pallas_call(
        functools.partial(last_kernel, n_dp, n_mp),
        out_shape=[
            jax.ShapeDtypeStruct((4, chunk, hh), BF),
            jax.ShapeDtypeStruct((seq, d), BF),
            jax.ShapeDtypeStruct((8, chunk), F32),
            jax.ShapeDtypeStruct(rs_down.shape, BF),
        ],
        in_specs=[anyspace] * 9 + [vm] * 2,
        out_specs=[anyspace, anyspace, vm, anyspace],
        scratch_shapes=[
            pltpu.VMEM((seq, 4 * hh), BF),
            pltpu.VMEM((d, 3 * hh), BF),
            pltpu.VMEM((seq, d), BF),
            pltpu.VMEM((seq, d), BF),
            pltpu.VMEM((2, chunk, seq), BF),
            pltpu.VMEM((part, d), BF),
            pltpu.VMEM((part, d), F32),
            pltpu.VMEM((4, chunk, hh), BF),
            dma((4,)),
            pltpu.VMEM(rs_down.shape, BF),
            pltpu.VMEM(rs_down.shape, BF),
            dma((3,)),
            dma((8,)),
        ]
        + line_sum_scratch(n, 4, chunk, hh)
        + quad_sum_scratch(n_mp, part, d // 2, None, 2)
        + quad_gather_scratch(n_mp, part, d // 2, 2)
        + [
            pltpu.VMEM((8, d), F32),
            pltpu.VMEM((folds + 1, 8, d // 4), F32),
            pltpu.VMEM((folds, 8, d // 4), F32),
            dma((folds,)),
            dma((folds,)),
        ],
        compiler_params=pltpu.CompilerParams(
            collective_id=5, has_side_effects=True, vmem_limit_bytes=VMEM_LIMIT
        ),
        name="last_stage",
    )(dqkv, aw, nin, low, att, x, gh, pend, rs_down, gain, gmid)


def finish_kernel(
    low_ref,
    lay_ref,
    gu_ref,
    down_ref,
    attn_ref,
    gains_ref,
    lay_out,
    in_out,
    gate_out,
    up_out,
    down_out,
    q_out,
    k_out,
    v_out,
    o_out,
    g1_out,
    g2_out,
):
    lay_out[...] = lay_ref[...]
    in_out[...] = low_ref[...].astype(F32)
    half = gate_out.shape[1]
    gate_out[...] = gu_ref[0, :, :half].astype(F32)
    up_out[...] = gu_ref[0, :, half:].astype(F32)
    step = pl.program_id(0)

    @pl.when(lax.rem(step, 2) == 0)
    def _():
        down_out[...] = down_ref[0].T.astype(F32)

    @pl.when(step == 0)
    def _():
        for i, ref in enumerate((q_out, k_out, v_out)):
            ref[...] = attn_ref[i].astype(F32)
        o_out[...] = attn_ref[3].T.astype(F32)
        g1_out[...] = gains_ref[0]
        g2_out[...] = gains_ref[1]


def finish_stage(low, lay, gu, down, attn, gains):
    seq, d = low.shape
    steps, chunk, wide = gu.shape
    width, hh = down.shape[2], attn.shape[2]
    row = pl.BlockSpec((seq // (2 * steps), d), lambda i: (i, 0))
    fixed = lambda *shape: pl.BlockSpec(shape, lambda i: (0,) * len(shape))
    two = pl.BlockSpec((1, chunk // 2, wide), lambda i: (i // 2, i % 2, 0))
    piece = pl.BlockSpec((1, chunk, width), lambda i: (i // 2, 0, 0))
    cols = pl.BlockSpec((chunk // 2, wide // 2), lambda i: (i % 2, i // 2))
    f32 = lambda *shape: jax.ShapeDtypeStruct(shape, F32)
    return pl.pallas_call(
        finish_kernel,
        grid=(2 * steps,),
        in_specs=[row, row, two, piece, fixed(4, chunk, hh), fixed(*gains.shape)],
        out_specs=[row, row, cols, cols, pl.BlockSpec((width, chunk), lambda i: (i // 2, 0))]
        + [fixed(chunk, hh)] * 3
        + [fixed(hh, chunk)]
        + [fixed(chunk)] * 2,
        out_shape=[
            jax.ShapeDtypeStruct((seq, d), BF),
            f32(seq, d),
            f32(chunk, steps * wide // 2),
            f32(chunk, steps * wide // 2),
            f32(steps * width, chunk),
        ]
        + [f32(chunk, hh)] * 3
        + [f32(hh, chunk)]
        + [f32(chunk)] * 2,
        compiler_params=pltpu.CompilerParams(vmem_limit_bytes=VMEM_LIMIT),
        name="finish_stage",
    )(low, lay, gu, down, attn, gains)


def on_device(
    inputs,
    counts,
    cotangent,
    gain_attn,
    w_query,
    w_key,
    w_value,
    w_output,
    gain_ffn,
    w_gate,
    w_up,
    w_down,
):
    n_dp, n_mp = lax.axis_size("dp"), lax.axis_size("mp")
    attn_w, qkv, attended, normed_in, gains, gu_shard, down_shard, grad_ffn, gu_pre = attn_stage(
        n_dp,
        n_mp,
        counts,
        gain_attn,
        gain_ffn,
        w_query,
        w_key,
        w_value,
        w_output,
        w_gate,
        w_up,
        w_down,
        inputs,
        cotangent,
    )
    gu_w, normed_mid, hidden, gu, inner, down_pre = gate_stage(
        n_dp, n_mp, attended, attn_w, gu_shard, gu_pre, down_shard, inputs, gains
    )
    down_part, ffn_terms, ggu, down_pend = down_stage(n_dp, n_mp, inner, gu, grad_ffn, down_shard, down_pre)
    rs_gu, grad_low, layer_out, grad_hidden, g_gain_mid, dqkv = mid_stage(
        n_dp, n_mp, ggu, gu_w, normed_mid, ffn_terms, grad_ffn, qkv, attn_w, counts, hidden, gains
    )
    rs_attn, grad_low_in, g_gains, rs_down = last_stage(
        n_dp,
        n_mp,
        dqkv,
        attn_w,
        normed_in,
        grad_low,
        attended,
        inputs,
        grad_hidden,
        down_pend,
        down_part,
        gains,
        g_gain_mid,
    )
    lay, grad_x, g_gate, g_up, g_down, g_q, g_k, g_v, g_o, g_attn, g_ffn = finish_stage(
        grad_low_in, layer_out, rs_gu, rs_down, rs_attn, g_gains
    )
    return (lay, grad_x, g_attn, g_q, g_k, g_v, g_o, g_ffn, g_gate, g_up, g_down)


def solution(mesh):
    row, both, swapped = P("dp", None), P("dp", "mp"), P("mp", "dp")
    weights = (both, both, both, swapped)
    ffn = (both, both, swapped)
    return jax.shard_map(
        on_device,
        mesh=mesh,
        in_specs=(row, P("dp"), row, P("dp")) + weights + (P("dp"),) + ffn,
        out_specs=(row, row, P("dp")) + weights + (P("dp"),) + ffn,
        check_vma=False,
    )
```

```python
import functools
import math

import jax
import jax.numpy as jnp
from jax import lax
from jax.experimental import pallas as pl
from jax.experimental.pallas import tpu as pltpu
from jax.sharding import PartitionSpec as P

HD = 128
EPS = 1e-06
BF = jnp.bfloat16
F32 = jnp.float32
NT = (((1,), (1,)), ((), ()))
TN = (((0,), (0,)), ((), ()))
NN = (((1,), (0,)), ((), ()))


def dot(a, b, dims=NN):
    return lax.dot_general(a, b, dims, preferred_element_type=F32)


def logistic_block(q, k, seq):
    raw = dot(q, k, NT)
    shifted = math.log(seq) - raw * HD ** (-0.5)
    return 1.0 / (1.0 + jnp.exp(shifted))


def allowed_block(row0, rows, col0, cols, count):
    ri = row0 + lax.broadcasted_iota(jnp.int32, (rows, cols), 0)
    ci = col0 + lax.broadcasted_iota(jnp.int32, (rows, cols), 1)
    return (ci <= ri) & (ci < count)


MESH = pl.DeviceIdType.MESH
VMEM_LIMIT = 60 * 1024 * 1024
PIECES = 4
AHEAD = 1
DOWN_AHEAD = 2


def flipped(index, bit):
    return index + bit - 2 * bit * lax.rem(lax.div(index, bit), 2)


def spread(j, bits):
    return sum(bit for i, bit in enumerate(bits) if j >> i & 1)


class Place:
    def __init__(self, n_dp, n_mp):
        self.n = n_dp // 2
        self.dp = lax.axis_index("dp")
        self.m = lax.axis_index("mp")
        self.p = lax.div(self.dp, 2)
        self.c = lax.rem(self.dp, 2)
        self.above = (self.dp + 2, self.m)
        self.below = (self.dp - 2, self.m)
        self.core = (self.dp + 1 - 2 * self.c, self.m)
        self.bits = [b for b in (1, 2, 4, 8, 16) if b < n_mp]
        self.has_above = self.p < self.n - 1
        self.has_below = self.p > 0

    def fold(self, bit):
        return (flipped(self.dp, bit), self.m)

    def peer(self, bit):
        return (self.dp, flipped(self.m, bit))

    def quarter(self, mask):
        q = self.m
        for bit in self.bits:
            if mask & bit:
                q = flipped(q, bit)
        return q


def signal(dev):
    pl.semaphore_signal(pltpu.get_barrier_semaphore(), inc=1, device_id=dev, device_id_type=MESH)


def enter(at, extra=()):
    always = [at.core] + [at.peer(bit) for bit in at.bits] + list(extra)
    for dev in always:
        signal(dev)

    @pl.when(at.has_above)
    def _():
        signal(at.above)

    @pl.when(at.has_below)
    def _():
        signal(at.below)

    ends = at.has_above.astype(jnp.int32) + at.has_below.astype(jnp.int32)
    pl.semaphore_wait(pltpu.get_barrier_semaphore(), len(always) + ends)


def remote(src, dst, send, recv, dev):
    return pltpu.make_async_remote_copy(
        src_ref=src, dst_ref=dst, send_sem=send, recv_sem=recv, device_id=dev, device_id_type=MESH
    )


def part_rows(at, part):
    return pl.ds(pl.multiple_of(at.m * part, part), part)


def order_of(k, at):
    n, p = at.n, at.p
    if k == n - 1:
        return p
    high = jnp.where(k < p, k, n - 1 - k + p)
    low = jnp.where(k < n - 1 - p, n - 1 - k, k - (n - 1 - p))
    return jnp.where(2 * p >= n, high, low)


class LineSum:
    def __init__(self, at, pout, own, din, uin, sems, paced=False, defer=False):
        self.paced, self.defer = paced, defer
        self.at, self.pout, self.own, self.din, self.uin = at, pout, own, din, uin
        self.po_s, self.po_r, self.d_s, self.d_r, self.u_s, self.u_r = sems
        self.slots, self.pieces = pout.shape[0], own.shape[1]

    def core_copy(self, k, i):
        j = order_of(k, self.at)
        slot = k % self.slots
        return remote(
            self.pout.at[slot, i],
            self.own.at[j, i],
            self.po_s.at[slot, i],
            self.po_r.at[k, i],
            self.at.core,
        )

    def down_copy(self, s, i):
        return remote(
            self.own.at[s, i], self.din.at[s, i], self.d_s.at[s, i], self.d_r.at[s, i], self.at.below
        )

    def up_copy(self, s, i):
        n = self.at.n
        return remote(
            self.own.at[n - 1 - s, i],
            self.uin.at[s, i],
            self.u_s.at[s, i],
            self.u_r.at[s, i],
            self.at.above,
        )

    def other(self, k, tile):
        @pl.loop(0, self.pieces)
        def _(i):
            if k >= self.slots:
                self.core_copy(k - self.slots, i).wait_send()
            self.pout[k % self.slots, i] = tile(i).astype(BF)
            self.core_copy(k, i).start()

    def mine(self, k, tile):
        at = self.at
        j = order_of(k, at)

        @pl.loop(0, self.pieces)
        def _(i):
            value = tile(i)
            self.core_copy(k, i).wait_recv()
            self.own[j, i] = (value + self.own[j, i].astype(F32)).astype(BF)
            if k < (1 if self.paced else at.n - 1):

                @pl.when(at.p == at.n - 1)
                def _():
                    self.down_copy(k, i).start()

                @pl.when(at.p == 0)
                def _():
                    self.up_copy(k, i).start()

    def add(self, dst, src):
        @pl.loop(0, dst.shape[0] // 64)
        def _(b):
            rs = pl.ds(pl.multiple_of(b * 64, 64), 64)
            dst[rs, :] = (dst[rs, :].astype(F32) + src[rs, :].astype(F32)).astype(BF)

    def slot(self, t, first=0, end=None):
        at = self.at
        n, p = at.n, at.p
        sd = t - (n - 2 - p)
        su = t - (p - 1)

        @pl.loop(first, end or self.pieces)
        def _(i):
            @pl.when((sd >= 0) & (sd < p) & at.has_above)
            def _():
                self.down_copy(sd, i).wait_recv()
                self.add(self.own.at[sd, i], self.din.at[sd, i])
                pl.when((p > 1) if self.defer else True)(self.down_copy(sd, i).start)

            @pl.when((su >= 0) & (su < n - 1 - p) & at.has_below)
            def _():
                self.up_copy(su, i).wait_recv()
                self.add(self.own.at[n - 1 - su, i], self.uin.at[su, i])
                pl.when((p < n - 2) if self.defer else True)(self.up_copy(su, i).start)

            if self.paced:

                @pl.when(p == n - 1)
                def _():
                    self.down_copy(t, i).wait_send()
                    self.down_copy(t + 1, i).start()

                @pl.when(p == 0)
                def _():
                    self.up_copy(t, i).wait_send()
                    self.up_copy(t + 1, i).start()

    def final(self, out, sink, sems):
        at = self.at
        n, p = at.n, at.p

        @pl.loop(0, self.pieces)
        def _(i):
            inner = at.has_above & at.has_below

            @pl.when(inner if self.defer else at.has_above)
            def _():
                self.down_copy(p, i).wait_recv()

            @pl.when(inner if self.defer else at.has_below)
            def _():
                self.up_copy(n - 1 - p, i).wait_recv()

            def close(parts):
                @pl.loop(0, out.shape[1] // 64)
                def _(b):
                    rs = pl.ds(pl.multiple_of(b * 64, 64), 64)
                    total = self.own[p, i, rs, :].astype(F32)
                    for ref, s in parts:
                        total = total + ref[s, i, rs, :].astype(F32)
                    out[i, rs, :] = total.astype(out.dtype)

            down, up = (self.din, p), (self.uin, n - 1 - p)

            @pl.when(at.has_above & at.has_below)
            def _():
                close([down, up])

            @pl.when(jnp.logical_not(at.has_below))
            def _():
                close([] if self.defer else [down])

            @pl.when(jnp.logical_not(at.has_above))
            def _():
                close([] if self.defer else [up])

            pltpu.make_async_copy(out.at[i], sink.at[i], sems.at[i]).start()

        return [
            pltpu.make_async_copy(out.at[i], sink.at[i], sems.at[i]) for i in range(self.pieces)
        ]

    def drain(self):
        at = self.at
        n, p = at.n, at.p
        for k in range(n - self.slots, n):
            for i in range(self.pieces):
                self.core_copy(k, i).wait_send()
        for s in range(n - 1):
            done = self.paced and s < n - 2

            last = self.defer

            @pl.when((s < p) & (p > 1 if last else at.has_above if done else at.has_below))
            def _():
                for i in range(self.pieces):
                    self.down_copy(s, i).wait_send()

            @pl.when((s < n - 1 - p) & (p < n - 2 if last else at.has_below if done else at.has_above))
            def _():
                for i in range(self.pieces):
                    self.up_copy(s, i).wait_send()


def line_sum_scratch(n, pieces, rows, cols, slots=2):
    dma = pltpu.SemaphoreType.DMA
    return [
        pltpu.VMEM((slots, pieces, rows, cols), BF),
        pltpu.VMEM((n, pieces, rows, cols), BF),
        pltpu.VMEM((n - 1, pieces, rows, cols), BF),
        pltpu.VMEM((n - 1, pieces, rows, cols), BF),
        dma((slots, pieces)),
        dma((n, pieces)),
        dma((n - 1, pieces)),
        dma((n - 1, pieces)),
        dma((n - 1, pieces)),
        dma((n - 1, pieces)),
    ]


class QuadSum:
    def __init__(self, at, t, r, sems):
        self.at, self.t, self.r = at, t, r
        self.s, self.v = sems
        self.blocks = self.s.shape[2]
        self.step = r.shape[2] // self.blocks
        self.order = [at.bits, at.bits[::-1]]
        self.levels = len(at.bits)
        self.seen = set()

    def count(self, k):
        return 1 << (self.levels - 1 - k)

    def slot(self, k, j):
        return sum(self.count(i) for i in range(k)) + j

    def rest(self, half, k):
        return self.order[half][k + 1 :]

    def index(self, half, k, mask):
        rest = self.rest(half, k)
        return self.slot(k, sum(1 << i for i, bit in enumerate(rest) if mask & bit))

    def source(self, half, mask):
        return self.t.at[half, self.at.quarter(mask)]

    def terms(self, half, mask, rs):
        return self.t[half, self.at.quarter(mask), rs, :].astype(F32)

    def split(self, k):
        return self.blocks if k == self.levels - 1 else 1

    def copy(self, half, k, j, block=0):
        bit = self.order[half][k]
        mask = bit + spread(j, self.rest(half, k))
        src = self.source(half, mask) if k == 0 else self.r.at[half, self.index(half, k - 1, mask)]
        at = self.slot(k, j)
        dst = self.r.at[half, at]
        if self.split(k) > 1:
            rows = pl.ds(block * self.step, self.step)
            src, dst = src.at[rows, :], dst.at[rows, :]
        send, recv = self.s.at[half, at, block], self.v.at[half, at, block]
        return remote(src, dst, send, recv, self.at.peer(bit))

    def offer(self, mask, only=(0, 1)):
        for half in only:
            if mask & self.order[half][0]:
                rest = self.rest(half, 0)
                self.copy(half, 0, sum(1 << i for i, b in enumerate(rest) if mask & b)).start()

    def masks(self):
        return sorted(range(1, 2 * self.count(0)), key=lambda m: -bin(m).count("1")) + [0]

    def come(self, half, k, mask, block=0):
        at = self.index(half, k, mask)
        block = min(block, self.split(k) - 1)
        if (half, at, block) not in self.seen:
            self.seen.add((half, at, block))
            self.copy(half, k, at - self.slot(k, 0), block).wait_recv()
        return at

    def turn(self):
        for k in range(1, self.levels):
            for block in range(self.split(k)):
                for half in range(2):
                    for j in range(self.count(k)):
                        self.pass_on(half, k, j, block)

    def pass_on(self, half, k, j, block):
        mask = self.order[half][k] + spread(j, self.rest(half, k))
        got = [self.come(half, i, mask) for i in range(k)]
        rows = self.r.shape[2] // self.split(k)

        @pl.loop(0, rows // 64)
        def _(b):
            rs = pl.ds(pl.multiple_of(block * rows + b * 64, 64), 64)
            total = self.terms(half, mask, rs)
            for i in got:
                total = total + self.r[half, i, rs, :].astype(F32)
            self.r[half, got[-1], rs, :] = total.astype(BF)

        self.copy(half, k, j, block).start()

    def arrive(self, block=0):
        self.got = [
            [self.come(half, k, 0, block) for k in range(self.levels)] for half in range(2)
        ]

    def total(self, half, rs):
        total = self.terms(half, 0, rs)
        for i in self.got[half]:
            total = total + self.r[half, i, rs, :].astype(F32)
        return total

    def drain(self):
        for half in range(2):
            for k in range(self.levels):
                for j in range(self.count(k)):
                    for block in range(self.split(k)):
                        self.copy(half, k, j, block).wait_send()


class QuadSumHbm(QuadSum):
    def __init__(self, at, hbm, t, r, sems):
        super().__init__(at, t, r, sems[:2])
        self.hbm = hbm
        self.loads = [
            pltpu.make_async_copy(
                self.source(half, spread(j, self.rest(half, 0))), t.at[half, j], sems[2].at[half, j]
            )
            for half in range(2)
            for j in range(self.count(0))
        ]

    def source(self, half, mask):
        rows, cols = self.t.shape[2], self.t.shape[3]
        rs = pl.ds(pl.multiple_of(self.at.quarter(mask) * rows, rows), rows)
        return self.hbm.at[rs, pl.ds(half * cols, cols)]

    def terms(self, half, mask, rs):
        return self.t[half, self.index(half, 0, mask), rs, :].astype(F32)


def quad_sum_scratch(mp, rows, cols, parts=None, blocks=1):
    dma = pltpu.SemaphoreType.DMA
    return [
        pltpu.VMEM((2, parts or mp, rows, cols), BF),
        pltpu.VMEM((2, mp - 1, rows, cols), BF),
        dma((2, mp - 1, blocks)),
        dma((2, mp - 1, blocks)),
    ]


class QuadGather:
    def __init__(self, at, own, out, sems):
        self.at, self.own, self.out = at, own, out
        self.s, self.v, self.here = sems
        self.blocks = self.s.shape[2]
        self.order = [at.bits[::-1], at.bits]
        self.levels = len(at.bits)
        self.seen = set()

    def mine(self, half, block):
        step = self.own.shape[1] // self.blocks
        return self.own.at[half, pl.ds(block * step, step), :]

    def spot(self, mask, half, block):
        rows, cols = self.own.shape[1], self.own.shape[2]
        step = rows // self.blocks
        rs = pl.ds(pl.multiple_of(self.at.quarter(mask) * rows + block * step, step), step)
        return self.out.at[rs, pl.ds(half * cols, cols)]

    def copy(self, half, k, j, block):
        mask = spread(j, self.order[half][:k])
        dst = self.spot(mask, half, block)
        src = self.mine(half, block) if j == 0 else dst
        at = (1 << k) - 1 + j
        dev = self.at.peer(self.order[half][k])
        return remote(src, dst, self.s.at[half, at, block], self.v.at[half, at, block], dev)

    def come(self, half, k, j, block):
        if (half, k, j, block) not in self.seen:
            self.seen.add((half, k, j, block))
            self.copy(half, k, j, block).wait_recv()

    def keep(self, half, block):
        return pltpu.make_async_copy(
            self.mine(half, block), self.spot(0, half, block), self.here.at[half, block]
        )

    def start(self, levels=None, block=0):
        for k in range(self.levels) if levels is None else levels:
            for half in range(2):
                self.copy(half, k, 0, block).start()
                if k == 0:
                    self.keep(half, block).start()

    def forward(self, block=0):
        for k in range(1, self.levels):
            for half in range(2):
                for j in range(1, 1 << k):
                    top = j.bit_length() - 1
                    self.come(half, top, j - (1 << top), block)
                    self.copy(half, k, j, block).start()

    def finish(self):
        for half in range(2):
            for block in range(self.blocks):
                for k in range(self.levels):
                    for j in range(1 << k):
                        self.come(half, k, j, block)
                        self.copy(half, k, j, block).wait_send()
                self.keep(half, block).wait()


def quad_gather_scratch(mp, rows, cols, blocks=1):
    dma = pltpu.SemaphoreType.DMA
    return [
        pltpu.VMEM((2, rows, cols), BF),
        dma((2, mp - 1, blocks)),
        dma((2, mp - 1, blocks)),
        dma((2, blocks)),
    ]


class LineGather:
    def __init__(self, at, pieces, shard, spot, sems, pre=0, wide=False):
        self.pre, self.wide = pre, wide
        self.at, self.pieces, self.shard, self.spot = at, pieces, shard, spot
        self.d_s, self.d_r, self.u_s, self.u_r, self.c_s, self.c_r, self.here = sems

    def down_copy(self, h, i, own=False):
        b = 2 * (self.at.p + h) + self.at.c
        dst = self.spot(b, i)
        src = self.shard(i) if own and self.shard else dst
        return remote(src, dst, self.d_s.at[h, i], self.d_r.at[h, i], self.at.below)

    def up_copy(self, h, i, own=False):
        b = 2 * (self.at.p - h) + self.at.c
        dst = self.spot(b, i)
        src = self.shard(i) if own and self.shard else dst
        return remote(src, dst, self.u_s.at[h, i], self.u_r.at[h, i], self.at.above)

    def core_copy(self, z, i, own=False, incoming=False):
        b = 2 * z + (1 - self.at.c if incoming else self.at.c)
        dst = self.spot(b, i)
        src = self.shard(i) if own and self.shard else dst
        return remote(src, dst, self.c_s.at[z, i], self.c_r.at[z, i], self.at.core)

    def keep(self, i):
        at = self.at
        return pltpu.make_async_copy(self.shard(i), self.spot(at.dp, i), self.here.at[i])

    def start(self):
        at = self.at
        down, up = self.late()
        for i in range(self.pre, self.pieces):

            @pl.when(down)
            def _():
                self.down_copy(0, i, True).start()

            @pl.when(up)
            def _():
                self.up_copy(0, i, True).start()

        for i in range(self.pieces):
            self.core_copy(at.p, i, True).start()
            if self.shard:
                self.keep(i).start()

    def late(self):
        at = self.at
        if self.wide:
            return at.p == 1, at.p == at.n - 2
        return at.has_below, at.has_above

    def slot(self, h, i):
        at = self.at
        n, p = at.n, at.p

        @pl.when(p + h < n)
        def _():
            self.down_copy(h - 1, i).wait_recv()

            @pl.when(at.has_below)
            def _():
                self.down_copy(h, i).start()

            self.core_copy(p + h, i).start()

        @pl.when(p - h >= 0)
        def _():
            self.up_copy(h - 1, i).wait_recv()

            @pl.when(at.has_above)
            def _():
                self.up_copy(h, i).start()

            self.core_copy(p - h, i).start()

    def stage(self, h):
        @pl.loop(self.pre if h == 1 else 0, self.pieces)
        def _(i):
            if h == 1 and self.wide:
                self.slot_ends(i)
            else:
                self.slot(h, i)

    def slot_ends(self, i):
        at = self.at

        @pl.when(at.p == 0)
        def _():
            self.down_copy(0, i).wait_recv()
            self.core_copy(1, i).start()

        @pl.when(at.p == at.n - 1)
        def _():
            self.up_copy(0, i).wait_recv()
            self.core_copy(at.n - 2, i).start()

    def early(self, i, above, below):
        at = self.at
        both = at.has_above & at.has_below
        everyone = i < self.pre

        @pl.when(at.has_above if everyone else both)
        def _():
            b = 2 * at.p + 2 + at.c
            dst = self.spot(b, i)

            @pl.when(at.has_below)
            def _():
                remote(above, dst, self.d_s.at[1, i], self.d_r.at[1, i], at.below).start()

            z = at.p + 1
            remote(above, dst, self.c_s.at[z, i], self.c_r.at[z, i], at.core).start()

        @pl.when(at.has_below if everyone else both)
        def _():
            b = 2 * at.p - 2 + at.c
            dst = self.spot(b, i)

            @pl.when(at.has_above)
            def _():
                remote(below, dst, self.u_s.at[1, i], self.u_r.at[1, i], at.above).start()

            z = at.p - 1
            remote(below, dst, self.c_s.at[z, i], self.c_r.at[z, i], at.core).start()

    def ready(self, z, i):
        self.core_copy(z, i, incoming=True).wait_recv()

    def drain(self):
        at = self.at
        n, p = at.n, at.p

        down, up = self.late()

        @pl.loop(0, self.pieces)
        def _(i):
            for h in range(n):
                own = h == 0

                @pl.when((down & (i >= self.pre)) if own else ((p + h < n) & at.has_below))
                def _():
                    self.down_copy(h, i, own).wait_send()

                @pl.when((up & (i >= self.pre)) if own else ((p - h >= 0) & at.has_above))
                def _():
                    self.up_copy(h, i, own).wait_send()

            for z in range(n):
                self.core_copy(z, i).wait_send()


def line_gather_scratch(n, pieces):
    dma = pltpu.SemaphoreType.DMA
    return [dma((n, pieces))] * 6 + [dma((pieces,))]


def rows_spot(out, rows, width):
    def spot(b, i):
        rs = pl.ds(pl.multiple_of(b * rows, rows), rows)
        return out.at[rs, pl.ds(pl.multiple_of(i * width, width), width)]

    return spot


def cols_of(ref, width, base=0):
    return lambda i: ref.at[:, pl.ds(pl.multiple_of(base + i * width, width), width)]


class Presend:
    def __init__(self, at, src, got, sems, narrow):
        s, r = sems
        wide = src.shape[1]
        n, p = at.n, at.p
        self.sends, self.comes = [], []
        for width in sorted({narrow, wide}):
            cols = pl.ds(0, width)
            down = remote(src.at[:, cols], got.at[0, :, cols], s.at[0], r.at[0], at.below)
            up = remote(src.at[:, cols], got.at[1, :, cols], s.at[1], r.at[1], at.above)
            if narrow == wide:
                whens = at.has_below, at.has_above, at.has_above, at.has_below
            elif width == narrow:
                whens = p == 1, p == n - 2, p == 0, p == n - 1
            else:
                inner = at.has_above & at.has_below
                whens = p > 1, p < n - 2, inner, inner
            self.sends += [(whens[0], down), (whens[1], up)]
            self.comes += [(whens[2], down), (whens[3], up)]

    def start(self):
        for when, copy in self.sends:
            pl.when(when)(copy.start)

    def finish(self):
        for when, copy in self.comes:
            pl.when(when)(copy.wait_recv)
        for when, copy in self.sends:
            pl.when(when)(copy.wait_send)


def attend_rows(qkv, out, seq, hh, count, head):
    cols = lambda first: pl.ds(pl.multiple_of(first + head * HD, HD), HD)
    blk = 256
    for i in range(seq // blk):
        rows = pl.ds(i * blk, blk)
        span = (i + 1) * blk
        lg = logistic_block(qkv[rows, cols(0)], qkv[pl.ds(0, span), cols(hh)], seq)
        w = jnp.where(allowed_block(i * blk, blk, 0, span, count), lg, 0.0).astype(BF)
        out[rows, cols(0)] = dot(w, qkv[pl.ds(0, span), cols(2 * hh)]).astype(BF)


def attn_kernel(
    n_dp,
    n_mp,
    count_ref,
    ga_ref,
    gf_ref,
    wq_hbm,
    wk_hbm,
    wv_hbm,
    wo_hbm,
    wg_hbm,
    wu_hbm,
    wd_hbm,
    x_hbm,
    cot_hbm,
    aw_ref,
    qkv_ref,
    att_ref,
    nin_ref,
    gains_ref,
    gush_ref,
    dnsh_ref,
    cotm_ref,
    gpre_ref,
    gains_in,
    w4,
    wo,
    shard,
    x,
    qkv,
    wbuf,
    wgu,
    wd,
    gush,
    dnsh,
    cot,
    load_s,
    wb_s,
    out_s,
    *rest,
):
    at = Place(n_dp, n_mp)
    n = at.n
    chunk, hh = wq_hbm.shape
    seq, d = x.shape
    ff = wgu.shape[2]
    loads = [
        pltpu.make_async_copy(src, dst, load_s.at[i])
        for i, (src, dst) in enumerate(
            [
                (wq_hbm, w4.at[0]),
                (wk_hbm, w4.at[1]),
                (wv_hbm, w4.at[2]),
                (wo_hbm, wo),
                (x_hbm, x),
                (wg_hbm, wgu.at[0]),
                (wu_hbm, wgu.at[1]),
                (wd_hbm, wd),
                (cot_hbm, cot),
            ]
        )
    ]
    for cp in loads:
        cp.start()
    spot = rows_spot(aw_ref, chunk, hh)
    three = LineGather(at, 3, cols_of(shard, hh), spot, rest[0:7])
    last = LineGather(
        at, 1, lambda i: shard.at[:, pl.ds(3 * hh, hh)], lambda b, i: spot(b, 3), rest[7:14]
    )
    small = LineGather(
        at,
        1,
        lambda i: gains_in,
        lambda b, i: gains_ref.at[:, pl.ds(pl.multiple_of(b * chunk, chunk), chunk)],
        rest[14:21],
    )
    for i, ref in enumerate((ga_ref, gf_ref)):
        gains_in[i, :] = ref[...].astype(BF).astype(F32)
    enter(at)
    small.start()
    for i in range(3):
        loads[i].wait()
        shard[:, i * hh : (i + 1) * hh] = w4[i].astype(BF)
    three.start()
    loads[3].wait()
    shard[:, 3 * hh :] = wo[...].T.astype(BF)
    small.slot(1, 0)
    loads[5].wait()
    loads[6].wait()
    half = ff // PIECES

    @pl.loop(0, PIECES)
    def _(i):
        cols = pl.ds(pl.multiple_of(i * half, half), half)
        for k in range(2):
            to = pl.ds(pl.multiple_of((2 * i + k) * half, half), half)
            gush[:, to] = wgu[k, :, cols].astype(BF)

    outs = [pltpu.make_async_copy(gush, gush_ref, out_s.at[0])]
    outs[0].start()
    loads[7].wait()

    @pl.loop(0, ff // 256)
    def _(i):
        rs = pl.ds(pl.multiple_of(i * 256, 256), 256)
        dnsh[:, rs] = wd[rs, :].T.astype(BF)

    outs.append(pltpu.make_async_copy(dnsh, dnsh_ref, out_s.at[2]))
    outs[-1].start()
    loads[8].wait()
    count = count_ref[0]

    @pl.loop(0, seq // 32)
    def _(b):
        rs = pl.ds(pl.multiple_of(b * 32, 32), 32)
        row = b * 32 + lax.broadcasted_iota(jnp.int32, (32, d), 0)
        cot[rs, :] = jnp.where(row < count, cot[rs, :].astype(F32), 0.0).astype(BF)

    outs.append(pltpu.make_async_copy(cot, cotm_ref, out_s.at[3]))
    outs[-1].start()
    for h in range(1, n - 1):
        small.slot(h + 1, 0)
        three.stage(h)
        if h == n - 2:
            last.start()
    small.keep(0).wait()
    for z in range(n):
        small.ready(z, 0)
    loads[4].wait()

    @pl.loop(0, seq // 32)
    def _(b):
        rs = pl.ds(pl.multiple_of(b * 32, 32), 32)
        v = x[rs, :].astype(F32)
        scale = lax.rsqrt(jnp.mean(v * v, axis=1, keepdims=True) + EPS)
        x[rs, :] = (v * scale * gains_ref[0:1, :]).astype(BF)

    outs.append(pltpu.make_async_copy(x, nin_ref, out_s.at[1]))
    outs[-1].start()

    def w_copy(i):
        cols = pl.ds(pl.multiple_of(i * hh, hh), hh)
        return pltpu.make_async_copy(aw_ref.at[:, cols], wbuf.at[i], wb_s.at[i])

    for i in range(3):
        three.slot(n - 1, i)
        three.keep(i).wait()
        for z in range(n):
            three.ready(z, i)
        w_copy(i).start()
        if i == 1:
            last.slot(1, 0)
        w_copy(i).wait()

        @pl.loop(0, seq // 256)
        def _(b):
            rs = pl.ds(pl.multiple_of(b * 256, 256), 256)
            qkv[rs, i * hh : (i + 1) * hh] = dot(x[rs, :], wbuf[i]).astype(BF)

    outs.append(pltpu.make_async_copy(qkv, qkv_ref, out_s.at[4]))
    outs[-1].start()
    for h in range(2, n - 1):
        last.slot(h, 0)
    ahead = Presend(at, gush.at[:, pl.ds(0, 2 * half * AHEAD)], gpre_ref, rest[21:23], 2 * half * AHEAD)
    ahead.start()
    heads = hh // HD

    @pl.loop(0, heads // 2)
    def _(head):
        attend_rows(qkv, att_ref, seq, hh, count, head)

    last.slot(n - 1, 0)

    @pl.loop(heads // 2, heads)
    def _(head):
        attend_rows(qkv, att_ref, seq, hh, count, head)

    last.keep(0).wait()
    for z in range(n):
        last.ready(z, 0)
    for cp in outs:
        cp.wait()
    ahead.finish()
    small.drain()
    three.drain()
    last.drain()


def attn_stage(n_dp, n_mp, counts, ga, gf, wq, wk, wv, wo, wg, wu, wd, x, cot):
    seq, d = x.shape
    chunk, hh = wq.shape
    ff = wg.shape[1]
    n = n_dp // 2
    dma = pltpu.SemaphoreType.DMA
    hbm = pl.BlockSpec(memory_space=pl.ANY)
    vm = pl.BlockSpec(memory_space=pltpu.VMEM)
    shapes = [
        ((d, 4 * hh), BF),
        ((seq, 3 * hh), BF),
        ((seq, hh), BF),
        ((seq, d), BF),
        ((8, d), F32),
        ((chunk, 2 * ff), BF),
        ((chunk, ff), BF),
        ((seq, d), BF),
        ((2, chunk, 2 * ff * AHEAD // PIECES), BF),
    ]
    return pl.pallas_call(
        functools.partial(attn_kernel, n_dp, n_mp),
        out_shape=[jax.ShapeDtypeStruct(*s) for s in shapes],
        in_specs=[pl.BlockSpec(memory_space=pltpu.SMEM), vm, vm] + [hbm] * 9,
        out_specs=[hbm, hbm, vm, hbm, vm, hbm, hbm, hbm, hbm],
        scratch_shapes=[
            pltpu.VMEM((8, chunk), F32),
            pltpu.VMEM((3, chunk, hh), F32),
            pltpu.VMEM((hh, chunk), F32),
            pltpu.VMEM((chunk, 4 * hh), BF),
            pltpu.VMEM((seq, d), BF),
            pltpu.VMEM((seq, 3 * hh), BF),
            pltpu.VMEM((3, d, hh), BF),
            pltpu.VMEM((2, chunk, ff), F32),
            pltpu.VMEM((ff, chunk), F32),
            pltpu.VMEM((chunk, 2 * ff), BF),
            pltpu.VMEM((chunk, ff), BF),
            pltpu.VMEM((seq, d), BF),
            dma((9,)),
            dma((3,)),
            dma((5,)),
        ]
        + line_gather_scratch(n, 3)
        + line_gather_scratch(n, 1) * 2
        + [dma((2,))] * 2,
        compiler_params=pltpu.CompilerParams(
            collective_id=1, has_side_effects=True, vmem_limit_bytes=VMEM_LIMIT
        ),
        name="attn_stage",
    )(counts, ga, gf, wq, wk, wv, wo, wg, wu, wd, x, cot)


def gate_kernel(
    n_dp,
    n_mp,
    att_ref,
    aw_hbm,
    sh_hbm,
    gpre_hbm,
    dnsh_hbm,
    x_hbm,
    gain_ref,
    gw_ref,
    nm_ref,
    hid_hbm,
    gu_ref,
    inner_ref,
    dpre_ref,
    wo,
    gp,
    sh,
    xs,
    hid,
    acc,
    nm,
    wbuf,
    gbuf,
    ibuf,
    gp_s,
    load_s,
    wb_s,
    gb_s,
    ib_s,
    *rest,
):
    at = Place(n_dp, n_mp)
    n = at.n
    quad = QuadSum(at, *rest[0:2], rest[2:4])
    gather_nm = QuadGather(at, rest[4], nm_ref, rest[5:8])
    sems = rest[8:15]
    hh = wo.shape[1]
    part, half_cols = quad.t.shape[2], quad.t.shape[3]
    chunk, wide = sh_hbm.shape
    pieces = sems[6].shape[0]
    width = wide // pieces
    line = LineGather(at, pieces, cols_of(sh, width), rows_spot(gw_ref, chunk, width), sems, AHEAD)

    load_sh = pltpu.make_async_copy(sh_hbm, sh, load_s.at[2])
    load_sh.start()
    load_gp = pltpu.make_async_copy(gpre_hbm, gp, load_s.at[3])
    load_gp.start()
    load = pltpu.make_async_copy(aw_hbm.at[:, pl.ds(3 * hh, hh)], wo, load_s.at[0])
    load.start()
    load_x = pltpu.make_async_copy(x_hbm.at[part_rows(at, part), :], xs, load_s.at[1])
    load_x.start()
    enter(at)
    load_sh.wait()
    line.start()
    load_gp.wait()

    def place(side, i):
        b = at.dp + (2 if side == 0 else -2)
        piece = gp.at[side, :, pl.ds(i * width, width)]
        return pltpu.make_async_copy(piece, line.spot(b, i), gp_s.at[side, i])

    for i in range(AHEAD):
        line.early(i, *[gp.at[side, :, pl.ds(i * width, width)] for side in range(2)])
        pl.when(at.has_above)(place(0, i).start)
        pl.when(at.has_below)(place(1, i).start)
    load.wait()

    def terms(q):
        rs = pl.ds(pl.multiple_of(q * part, part), part)
        for half in range(2):
            w = wo[half * half_cols : (half + 1) * half_cols, :]
            quad.t[half, q] = dot(att_ref[rs, :], w, NT).astype(BF)

    for mask in quad.masks():
        terms(at.quarter(mask))
        quad.offer(mask)
    quad.turn()
    quad.arrive()
    load_x.wait()

    @pl.loop(0, part // 32)
    def _(b):
        rs = pl.ds(pl.multiple_of(b * 32, 32), 32)
        h = xs[rs, :].astype(F32) + jnp.concatenate(
            [quad.total(0, rs), quad.total(1, rs)], axis=1
        )
        hid[rs, :] = h
        scale = lax.rsqrt(jnp.mean(h * h, axis=1, keepdims=True) + EPS)
        res = (h * scale * gain_ref[1:2, :]).astype(BF)
        gather_nm.own[0, rs, :] = res[:, :half_cols]
        gather_nm.own[1, rs, :] = res[:, half_cols:]

    gather_nm.start()
    store_hid = pltpu.make_async_copy(hid, hid_hbm, load_s.at[1])
    store_hid.start()
    line.stage(1)
    gather_nm.forward()
    gather_nm.finish()
    load = pltpu.make_async_copy(nm_ref, nm, load_s.at[0])
    load.start()
    for h in range(2, n - 1):
        line.stage(h)
    load.wait()

    for i in range(AHEAD):
        pl.when(at.has_above)(place(0, i).wait)
        pl.when(at.has_below)(place(1, i).wait)
    ahead = Presend(at, dnsh_hbm, dpre_ref, rest[15:17], width // 2 * DOWN_AHEAD)
    ahead.start()

    pair = 2 * chunk
    near = jnp.where(2 * at.p < n, 0, 1)
    far = jnp.where(2 * at.p < n, n - 1, 0)
    most = (n - 1) * pair
    most_rows = pl.ds(pl.multiple_of(near * pair, pair), most)
    far_rows = pl.ds(pl.multiple_of(far * pair, pair), pair)

    def w_copy(i, slot, rows):
        cols = pl.ds(pl.multiple_of(i * width, width), width)
        return pltpu.make_async_copy(
            gw_ref.at[rows, cols], wbuf.at[slot, rows, :], wb_s.at[slot]
        )

    def first_part(i, slot):
        line.keep(i).wait()

        @pl.loop(0, n - 1)
        def _(z):
            line.ready(near + z, i)

        w_copy(i, slot, most_rows).start()
        w_copy(i, slot, most_rows).wait()

        @pl.loop(0, nm.shape[0] // 256)
        def _(b):
            rs = pl.ds(pl.multiple_of(b * 256, 256), 256)
            acc[rs, :] = dot(nm[rs, most_rows], wbuf[slot, most_rows, :])

    def g_copy(i, slot):
        cols = pl.ds(pl.multiple_of(i * width, width), width)
        return pltpu.make_async_copy(gbuf.at[slot], gu_ref.at[:, cols], gb_s.at[slot])

    def i_copy(i, slot):
        cols = pl.ds(pl.multiple_of(i * (width // 2), width // 2), width // 2)
        return pltpu.make_async_copy(ibuf.at[slot], inner_ref.at[:, cols], ib_s.at[slot])

    @pl.loop(0, pieces)
    def _(i):
        slot = lax.rem(i, 2)
        first_part(i, slot)
        line.slot(n - 1, i)
        line.ready(far, i)
        w_copy(i, slot, far_rows).start()

        @pl.when(i >= 2)
        def _():
            g_copy(i - 2, slot).wait()
            i_copy(i - 2, slot).wait()

        w_copy(i, slot, far_rows).wait()

        @pl.loop(0, nm.shape[0] // 256)
        def _(b):
            rs = pl.ds(pl.multiple_of(b * 256, 256), 256)
            v = (acc[rs, :] + dot(nm[rs, far_rows], wbuf[slot, far_rows, :])).astype(BF)
            gbuf[slot, rs, :] = v
            g = v[:, : width // 2].astype(F32)
            u = v[:, width // 2 :].astype(F32)
            ibuf[slot, rs, :] = (g / (1.0 + jnp.exp(-g)) * u).astype(BF)

        g_copy(i, slot).start()
        i_copy(i, slot).start()

    for i in range(max(0, pieces - 2), pieces):
        g_copy(i, i % 2).wait()
        i_copy(i, i % 2).wait()
    store_hid.wait()
    ahead.finish()
    line.drain()
    quad.drain()


def gate_stage(n_dp, n_mp, att, aw, shard, gpre, dnsh, x, gain):
    seq, hh = att.shape
    d = aw.shape[0]
    chunk, wide = shard.shape
    n, part = n_dp // 2, seq // n_mp
    dma = pltpu.SemaphoreType.DMA
    hbm = pl.BlockSpec(memory_space=pl.ANY)
    vm = pl.BlockSpec(memory_space=pltpu.VMEM)
    width = wide // PIECES
    return pl.pallas_call(
        functools.partial(gate_kernel, n_dp, n_mp),
        out_shape=[
            jax.ShapeDtypeStruct((d, wide), BF),
            jax.ShapeDtypeStruct((seq, d), BF),
            jax.ShapeDtypeStruct((part, d), F32),
            jax.ShapeDtypeStruct((seq, wide), BF),
            jax.ShapeDtypeStruct((seq, wide // 2), BF),
            jax.ShapeDtypeStruct((2, chunk, wide // 2), BF),
        ],
        in_specs=[vm, hbm, hbm, hbm, hbm, hbm, vm],
        out_specs=[hbm] * 6,
        scratch_shapes=[
            pltpu.VMEM((d, hh), BF),
            pltpu.VMEM((2, chunk, width * AHEAD), BF),
            pltpu.VMEM((chunk, wide), BF),
            pltpu.VMEM((part, d), BF),
            pltpu.VMEM((part, d), F32),
            pltpu.VMEM((seq, width), F32),
            pltpu.VMEM((seq, d), BF),
            pltpu.VMEM((2, d, width), BF),
            pltpu.VMEM((2, seq, width), BF),
            pltpu.VMEM((2, seq, width // 2), BF),
            dma((2, AHEAD)),
            dma((4,)),
            dma((2,)),
            dma((2,)),
            dma((2,)),
        ]
        + quad_sum_scratch(n_mp, part, d // 2)
        + quad_gather_scratch(n_mp, part, d // 2)
        + line_gather_scratch(n, PIECES)
        + [dma((2,))] * 2,
        compiler_params=pltpu.CompilerParams(
            collective_id=2, has_side_effects=True, vmem_limit_bytes=VMEM_LIMIT
        ),
        name="gate_stage",
    )(att, aw, shard, gpre, dnsh, x, gain)


def down_kernel(
    n_dp,
    n_mp,
    inner_hbm,
    gu_hbm,
    cot_hbm,
    sh_hbm,
    dpre_hbm,
    rs_ref,
    ft_ref,
    ggu_ref,
    pend_ref,
    inner,
    gu,
    cot,
    dn,
    acc,
    ftb,
    res,
    dp_s,
    load_s,
    cot_s,
    in_s,
    rs_s,
    ft_s,
    dn_s,
    gg_s,
    *rest,
):
    at = Place(n_dp, n_mp)
    n, p = at.n, at.p
    line = LineSum(at, *rest[0:4], rest[4:10], defer=True)
    sems = rest[10:17]
    chunk, ff = sh_hbm.shape
    pieces = sems[6].shape[0]
    width = ff // pieces
    gather = LineGather(at, pieces, None, rows_spot(dn, chunk, width), sems, DOWN_AHEAD, True)
    pair = 2 * chunk
    def cot_copy(k):
        cols = pl.ds(pl.multiple_of(order_of(k, at) * pair, pair), pair)
        return pltpu.make_async_copy(cot_hbm.at[:, cols], cot.at[:, cols], cot_s.at[k])

    def in_copy(i):
        cols = pl.ds(pl.multiple_of(i * width, width), width)
        return pltpu.make_async_copy(inner_hbm.at[:, cols], inner.at[:, cols], in_s.at[i])

    load_gu = pltpu.make_async_copy(gu_hbm, gu, load_s.at[0])
    own = pltpu.make_async_copy(
        sh_hbm, dn.at[pl.ds(pl.multiple_of(at.dp * chunk, chunk), chunk), :], dn_s.at[0]
    )
    own.start()

    inside = at.has_above & at.has_below

    def pre_copy(side, i):
        b = at.dp + (2 if side == 0 else -2)
        piece = dpre_hbm.at[side, :, pl.ds(i * width, width)]
        return pltpu.make_async_copy(piece, gather.spot(b, i), dp_s.at[side, i])

    def pre_whens(i):
        return (at.has_above, at.has_below) if i < DOWN_AHEAD else (inside, inside)

    for i in range(pieces):
        for side in range(2):
            pl.when(pre_whens(i)[side])(pre_copy(side, i).start)
    cot_copy(0).start()
    for i in range(pieces):
        in_copy(i).start()
    for k in range(1, n):
        cot_copy(k).start()
    load_gu.start()
    enter(at)
    own.wait()
    gather.start()
    for i in range(pieces):
        for side in range(2):
            pl.when(pre_whens(i)[side])(pre_copy(side, i).wait)
        gather.early(i, gather.spot(at.dp + 2, i), gather.spot(at.dp - 2, i))

    def run(e):
        k, core = e // 2, e % 2
        block = 2 * order_of(k, at) + (1 - at.c if core == 0 else at.c)
        if core == 0:
            cot_copy(k).wait()
        lhs = cot[:, pl.ds(pl.multiple_of(block * chunk, chunk), chunk)].T

        def tile(i):
            if e == 0:
                in_copy(i).wait()
            return dot(lhs, inner[:, pl.ds(pl.multiple_of(i * width, width), width)])

        if core == 0:
            line.other(k, tile)
        else:
            line.mine(k, tile)

    for e in range(2 * n):
        run(e)

    def ft_copy(z, slot):
        cols = pl.ds(pl.multiple_of(z * pair, pair), pair)
        return pltpu.make_async_copy(ftb.at[slot], ft_ref.at[:, cols], ft_s.at[slot])

    def rows_of(z):
        return pl.ds(pl.multiple_of(z * pair, pair), pair)

    def grads(z, fresh):
        @pl.loop(0, pieces)
        def _(i):
            gather.ready(z, i)

        @pl.loop(0, ff // 512)
        def _(i):
            cols = pl.ds(pl.multiple_of(i * 512, 512), 512)
            v = dot(cot[:, rows_of(z)], dn[rows_of(z), cols])
            acc[:, cols] = v if fresh else acc[:, cols] + v

    def branch(z, fresh):
        if not fresh:
            ft_copy(z, 0).wait()
        ftb[0] = dot(inner[...], dn[rows_of(z), :], NT).astype(BF)
        ft_copy(z, 0).start()

    def blocks(h):
        @pl.when(p + h < n)
        def _():
            grads(p + h, False)
            branch(p + h, False)

        @pl.when(p - h >= 0)
        def _():
            grads(p - h, False)
            branch(p - h, False)

    gather.stage(1)
    grads(p, True)
    branch(p, True)
    line.slot(0)
    if n > 3:
        gather.stage(2)
    load_gu.wait()
    half = width

    def cols_at(i):
        g = pl.ds(pl.multiple_of(i * 2 * half, half), half)
        u = pl.ds(pl.multiple_of(i * 2 * half + half, half), half)
        return g, u, pl.ds(pl.multiple_of(i * half, half), half)

    @pl.loop(0, pieces)
    def _(i):
        gcols, ucols, _ = cols_at(i)

        @pl.loop(0, gu.shape[0] // 64)
        def _(b):
            rs = pl.ds(pl.multiple_of(b * 64, 64), 64)
            g = gu[rs, gcols].astype(F32)
            u = gu[rs, ucols].astype(F32)
            sg = 1.0 / (1.0 + jnp.exp(-g))
            gu[rs, gcols] = (u * sg * (1.0 + g * (1.0 - sg))).astype(BF)
            gu[rs, ucols] = (g * sg).astype(BF)

    blocks(1)
    for h in range(2, n - 1):
        line.slot(h - 1)
        if h + 1 < n - 1:
            gather.stage(h + 1)
        blocks(h)

    gather.stage(n - 1)

    @pl.when(jnp.logical_not(at.has_below))
    def _():
        grads(n - 1, False)

    @pl.when(jnp.logical_not(at.has_above))
    def _():
        grads(0, False)

    def gg_copy(i):
        cols = pl.ds(pl.multiple_of(i * 2 * half, 2 * half), 2 * half)
        return pltpu.make_async_copy(gu.at[:, cols], ggu_ref.at[:, cols], gg_s.at[i])

    @pl.loop(0, pieces)
    def _(i):
        gcols, ucols, acols = cols_at(i)

        @pl.loop(0, gu.shape[0] // 64)
        def _(b):
            rs = pl.ds(pl.multiple_of(b * 64, 64), 64)
            gi = acc[rs, acols]
            gu[rs, gcols] = (gi * gu[rs, gcols].astype(F32)).astype(BF)
            gu[rs, ucols] = (gi * gu[rs, ucols].astype(F32)).astype(BF)

        gg_copy(i).start()

    @pl.when(jnp.logical_not(at.has_below))
    def _():
        branch(n - 1, False)

    @pl.when(jnp.logical_not(at.has_above))
    def _():
        branch(0, False)

    stores = line.final(res, rs_ref, rs_s)
    keep_low = pltpu.make_async_copy(line.own.at[0], pend_ref, dn_s.at[0])
    keep_high = pltpu.make_async_copy(line.own.at[n - 1], pend_ref, dn_s.at[0])
    pl.when(p == 1)(keep_low.start)
    pl.when(p == n - 2)(keep_high.start)
    pl.when((p == 1) | (p == n - 2))(keep_low.wait)
    for i in range(pieces):
        gg_copy(i).wait()
    ft_copy(p, 0).wait()
    for cp in stores:
        cp.wait()
    line.drain()
    gather.drain()


def down_stage(n_dp, n_mp, inner, gu, cot, shard, dpre):
    seq, d = cot.shape
    chunk, ff = shard.shape
    n = n_dp // 2
    dma = pltpu.SemaphoreType.DMA
    hbm = pl.BlockSpec(memory_space=pl.ANY)
    return pl.pallas_call(
        functools.partial(down_kernel, n_dp, n_mp),
        out_shape=[
            jax.ShapeDtypeStruct((PIECES, chunk, ff // PIECES), BF),
            jax.ShapeDtypeStruct((seq, d), BF),
            jax.ShapeDtypeStruct((seq, 2 * ff), BF),
            jax.ShapeDtypeStruct((PIECES, chunk, ff // PIECES), BF),
        ],
        in_specs=[hbm] * 5,
        out_specs=[hbm] * 4,
        scratch_shapes=[
            pltpu.VMEM((seq, ff), BF),
            pltpu.VMEM((seq, 2 * ff), BF),
            pltpu.VMEM((seq, d), BF),
            pltpu.VMEM((d, ff), BF),
            pltpu.VMEM((seq, ff), F32),
            pltpu.VMEM((1, seq, 2 * chunk), BF),
            pltpu.VMEM((PIECES, chunk, ff // PIECES), BF),
            dma((2, PIECES)),
            dma((1,)),
            dma((n,)),
            dma((PIECES,)),
            dma((PIECES,)),
            dma((1,)),
            dma((1,)),
            dma((PIECES,)),
        ]
        + line_sum_scratch(n, PIECES, chunk, ff // PIECES)
        + line_gather_scratch(n, PIECES),
        compiler_params=pltpu.CompilerParams(
            collective_id=3, has_side_effects=True, vmem_limit_bytes=VMEM_LIMIT
        ),
        name="down_stage",
    )(inner, gu, cot, shard, dpre)


def mid_kernel(
    n_dp,
    n_mp,
    ggu_hbm,
    gw_hbm,
    nm_hbm,
    ft_hbm,
    cot_hbm,
    qkv_hbm,
    aw_hbm,
    count_ref,
    hid_hbm,
    gain_ref,
    rs_ref,
    low_ref,
    lay_ref,
    gh_hbm,
    gg_ref,
    dq_ref,
    space,
    wt,
    wt_s,
    nm,
    nm_s,
    cot,
    hid,
    gh,
    res,
    gg_s,
    rs_s,
    dka,
    dva,
    load_s,
    *rest,
):
    at = Place(n_dp, n_mp)
    n = at.n
    line = LineSum(at, *rest[0:4], rest[4:10])
    mid = QuadSum(at, *rest[10:12], rest[12:14])
    lay = QuadSumHbm(at, ft_hbm, *rest[14:16], rest[16:19])
    gather_low = QuadGather(at, rest[19], low_ref, rest[20:23])
    gather_lay = QuadGather(at, rest[23], lay_ref, rest[24:27])
    part, half_cols = mid.t.shape[2], mid.t.shape[3]
    chunk, width = line.own.shape[2], line.own.shape[3]
    pieces = line.pieces
    hh = qkv_hbm.shape[1] // 3
    drows = wt.shape[1]
    tiles = half_cols // drows

    wide = ggu_hbm.shape[1]
    ggu = space.at[:, pl.ds(0, wide)]

    def gg_copy(i):
        cols = pl.ds(pl.multiple_of(i * width, width), width)
        return pltpu.make_async_copy(ggu_hbm.at[:, cols], ggu.at[:, cols], gg_s.at[i])

    load_cot = pltpu.make_async_copy(cot_hbm.at[part_rows(at, part), :], cot, load_s.at[1])

    def nm_copy(e):
        k, core = e // 2, e % 2
        block = 2 * order_of(k, at) + (1 - at.c if core == 0 else at.c)
        cols = pl.ds(pl.multiple_of(block * chunk, chunk), chunk)
        return pltpu.make_async_copy(nm_hbm.at[:, cols], nm.at[e % 2], nm_s.at[e % 2])

    def wt_copy(half, i, slot):
        rows = pl.ds(pl.multiple_of(half * half_cols + i * drows, drows), drows)
        return pltpu.make_async_copy(gw_hbm.at[rows, :], wt.at[slot], wt_s.at[slot])

    nm_copy(0).start()
    for i in range(pieces):
        gg_copy(i).start()
    wt_copy(0, 0, 0).start()
    load_cot.start()
    load_hid = pltpu.make_async_copy(hid_hbm, hid, load_s.at[0])
    load_hid.start()
    for cp in lay.loads:
        cp.start()
    enter(at)
    for mask in lay.masks():
        lay.offer(mask)

    def run(e):
        if e + 1 < 2 * n:
            nm_copy(e + 1).start()
        nm_copy(e).wait()
        lhs = nm[e % 2].T

        def tile(i):
            if e == 0:
                gg_copy(i).wait()
            return dot(lhs, ggu[:, pl.ds(pl.multiple_of(i * width, width), width)])

        if e % 2 == 0:
            line.other(e // 2, tile)
        else:
            line.mine(e // 2, tile)

    def terms(half):
        @pl.loop(0, tiles)
        def _(i):
            slot = lax.rem(i, 2)
            if half == 0:
                nxt = wt_copy(jnp.where(i + 1 < tiles, 0, 1), lax.rem(i + 1, tiles), 1 - slot)
                nxt.start()
            else:

                @pl.when(i + 1 < tiles)
                def _():
                    wt_copy(1, i + 1, 1 - slot).start()

            wt_copy(half, i, slot).wait()
            v = dot(ggu[...], wt[slot], NT).astype(BF)
            cols = pl.ds(pl.multiple_of(i * drows, drows), drows)
            for q in range(n_mp):
                mid.t[half, q, :, cols] = v[q * part : (q + 1) * part]

        for mask in mid.masks():
            mid.offer(mask, (half,))

    run(0)
    run(1)
    terms(0)
    run(2)
    run(3)
    for cp in lay.loads:
        cp.wait()
    lay.turn()
    line.slot(0, 0, 2)
    terms(1)
    line.slot(0, 2, 3)
    for e in range(4, 2 * n):
        run(e)
    lay.arrive()
    load_hid.wait()

    @pl.loop(0, part // 32)
    def _(b):
        rs = pl.ds(pl.multiple_of(b * 32, 32), 32)
        for half in range(2):
            h = hid[rs, pl.ds(half * half_cols, half_cols)]
            gather_lay.own[half, rs, :] = (h + lay.total(half, rs)).astype(BF)

    gather_lay.start([0])
    line.slot(0, 3)
    per = half_cols // hh
    blocks_d = 2 * half_cols // part
    wo_spot = [(e // per // (n_mp // 2), e // per % (n_mp // 2), e % per) for e in range(blocks_d)]
    wo_parts = [
        pltpu.make_async_copy(
            aw_hbm.at[pl.ds(e * part, part), pl.ds(3 * hh, hh)],
            lay.t.at[i, j, :, pl.ds(k * hh, hh)],
            load_s.at[4 + e],
        )
        for e, (i, j, k) in enumerate(wo_spot)
    ]
    for cp in wo_parts:
        cp.start()
    load_qkv = pltpu.make_async_copy(
        qkv_hbm, space.at[:, pl.ds(2 * half_cols, 3 * hh)], load_s.at[2]
    )
    load_qkv.start()
    mid.turn()
    mid.arrive()
    load_cot.wait()
    gg_ref[...] = jnp.zeros_like(gg_ref)

    @pl.loop(0, part // 32)
    def _(b):
        rs = pl.ds(pl.multiple_of(b * 32, 32), 32)
        h = hid[rs, :]
        scale = lax.rsqrt(jnp.mean(h * h, axis=1, keepdims=True) + EPS)
        g = jnp.concatenate([mid.total(0, rs), mid.total(1, rs)], axis=1)
        unit = h * scale
        weighted = g * gain_ref[1:2, :]
        field = scale * (weighted - unit * jnp.mean(weighted * unit, axis=1, keepdims=True))
        out = cot[rs, :].astype(F32) + field
        gh[rs, :] = out
        low = out.astype(BF)
        gather_low.own[0, rs, :] = low[:, :half_cols]
        gather_low.own[1, rs, :] = low[:, half_cols:]
        gg_ref[...] += jnp.sum(g * unit, axis=0, keepdims=True)

    gather_low.start()
    store_gh = pltpu.make_async_copy(gh, gh_hbm, load_s.at[1])
    store_gh.start()
    for s in range(1, n - 2):
        line.slot(s)
    gather_low.forward()
    gather_lay.start(range(1, gather_lay.levels))
    gather_lay.forward()
    gather_low.finish()
    load_low = pltpu.make_async_copy(low_ref, space.at[:, pl.ds(0, 2 * half_cols)], load_s.at[3])
    load_low.start()
    load_low.wait()
    load_qkv.wait()
    for cp in wo_parts:
        cp.wait()
    seq = space.shape[0]
    base = 2 * half_cols
    gbase = base + 3 * hh

    @pl.loop(0, seq // 256)
    def _(b):
        rs = pl.ds(pl.multiple_of(b * 256, 256), 256)
        total = jnp.zeros((256, hh), F32)
        for e, (i, j, k) in enumerate(wo_spot):
            wo = lay.t[i, j, :, k * hh : (k + 1) * hh]
            total += dot(space[rs, e * part : (e + 1) * part], wo)
        space[rs, gbase : gbase + hh] = total.astype(BF)

    count = count_ref[0]
    blk = 256
    blocks = seq // blk

    def back(head):
        at_cols = lambda first: pl.ds(pl.multiple_of(first + head * HD, HD), HD)
        for i in range(blocks - 1, -1, -1):
            rows = pl.ds(i * blk, blk)
            span = (i + 1) * blk
            keys = pl.ds(0, span)
            q = space[rows, at_cols(base)]
            g = space[rows, at_cols(gbase)]
            k = space[keys, at_cols(base + hh)]
            lg = jnp.where(
                allowed_block(i * blk, blk, 0, span, count), logistic_block(q, k, seq), 0.0
            )
            w = lg.astype(BF)
            gw = dot(g, space[keys, at_cols(base + 2 * hh)], NT)
            gs = (gw * lg * (1.0 - lg) * HD ** (-0.5)).astype(BF)
            wt[i // 2, :, at_cols((i % 2) * (wide // 2))] = dot(gs, k).astype(BF)
            dk = dot(gs, q, TN)
            dv = dot(w, g, TN)
            if i == blocks - 1:
                dka[...] = dk
                dva[...] = dv
            else:
                dka[keys, :] += dk
                dva[keys, :] += dv
        for i in range(blocks):
            rows = pl.ds(i * blk, blk)
            wt[i // 2, :, at_cols((i % 2) * (wide // 2) + hh)] = dka[rows, :].astype(BF)
            wt[i // 2, :, at_cols((i % 2) * (wide // 2) + 2 * hh)] = dva[rows, :].astype(BF)

    heads = hh // HD
    pl.loop(0, heads)(back)
    stores = [
        pltpu.make_async_copy(
            wt.at[i // 2, :, pl.ds((i % 2) * (wide // 2), 3 * hh)],
            dq_ref.at[pl.ds(i * blk, blk), :],
            load_s.at[4 + i],
        )
        for i in range(blocks)
    ]
    for cp in stores:
        cp.start()
    stores += line.final(res, rs_ref, rs_s) + [store_gh]
    gather_lay.finish()
    for cp in stores:
        cp.wait()
    line.drain()
    mid.drain()
    lay.drain()


def mid_stage(n_dp, n_mp, ggu, gw, nm, ft, cot, qkv, aw, counts, hid, gain):
    seq, wide = ggu.shape
    hh = qkv.shape[1] // 3
    d = gw.shape[0]
    n, part, chunk = n_dp // 2, seq // n_mp, d // n_dp
    dma = pltpu.SemaphoreType.DMA
    hbm = pl.BlockSpec(memory_space=pl.ANY)
    vm = pl.BlockSpec(memory_space=pltpu.VMEM)
    pieces = PIECES
    return pl.pallas_call(
        functools.partial(mid_kernel, n_dp, n_mp),
        out_shape=[
            jax.ShapeDtypeStruct((pieces, chunk, wide // pieces), BF),
            jax.ShapeDtypeStruct((seq, d), BF),
            jax.ShapeDtypeStruct((seq, d), BF),
            jax.ShapeDtypeStruct((part, d), F32),
            jax.ShapeDtypeStruct((1, d), F32),
            jax.ShapeDtypeStruct((seq, 3 * hh), BF),
        ],
        in_specs=[hbm] * 7 + [pl.BlockSpec(memory_space=pltpu.SMEM), hbm, vm],
        out_specs=[hbm, hbm, hbm, hbm, vm, hbm],
        scratch_shapes=[
            pltpu.VMEM((seq, max(wide, d + 4 * hh)), BF),
            pltpu.VMEM((2, 256, wide), BF),
            dma((2,)),
            pltpu.VMEM((2, seq, chunk), BF),
            dma((2,)),
            pltpu.VMEM((part, d), BF),
            pltpu.VMEM((part, d), F32),
            pltpu.VMEM((part, d), F32),
            pltpu.VMEM((pieces, chunk, wide // pieces), BF),
            dma((pieces,)),
            dma((pieces,)),
            pltpu.VMEM((seq, HD), F32),
            pltpu.VMEM((seq, HD), F32),
            dma((4 + max(d // part, seq // 256),)),
        ]
        + line_sum_scratch(n, pieces, chunk, wide // pieces, 1)
        + quad_sum_scratch(n_mp, part, d // 2)
        + quad_sum_scratch(n_mp, part, d // 2, n_mp // 2)
        + [dma((2, n_mp // 2))]
        + quad_gather_scratch(n_mp, part, d // 2) * 2,
        compiler_params=pltpu.CompilerParams(
            collective_id=4, has_side_effects=True, vmem_limit_bytes=VMEM_LIMIT
        ),
        name="mid_stage",
    )(ggu, gw, nm, ft, cot, qkv, aw, counts, hid, gain)


def last_kernel(
    n_dp,
    n_mp,
    dqkv_hbm,
    aw_hbm,
    nin_hbm,
    low_hbm,
    att_hbm,
    x_hbm,
    gh_hbm,
    pend_hbm,
    part_hbm,
    gain_ref,
    gmid_ref,
    rs_ref,
    grad_ref,
    gains_ref,
    rsd_ref,
    rhs,
    aw,
    nin,
    low,
    lhs,
    x,
    gh,
    res,
    rs_s,
    pbuf,
    dbuf,
    pd_s,
    loads,
    pout,
    own,
    din,
    uin,
    po_s,
    po_r,
    d_s,
    d_r,
    u_s,
    u_r,
    t,
    r,
    q1,
    q2,
    gown,
    g1,
    g2,
    g3,
    gsum,
    fold_out,
    fold_in,
    fold_s,
    fold_r,
):
    at = Place(n_dp, n_mp)
    hh = att_hbm.shape[1]
    part = t.shape[2]
    chunk = own.shape[2]
    half_cols = t.shape[3]
    copies = [
        pltpu.make_async_copy(src, dst, loads.at[i])
        for i, (src, dst) in enumerate(
            [
                (dqkv_hbm, rhs.at[:, pl.ds(0, 3 * hh)]),
                (aw_hbm.at[:, pl.ds(0, 3 * hh)], aw),
                (nin_hbm, nin),
                (att_hbm, rhs.at[:, pl.ds(3 * hh, hh)]),
                (low_hbm, low),
                (x_hbm.at[part_rows(at, part), :], x),
                (gh_hbm, gh),
                (part_hbm, dbuf),
            ]
        )
    ]
    for cp in copies:
        cp.start()
    bits = [b for b in (2, 4, 8, 16) if b < n_dp]
    enter(at, [at.fold(b) for b in bits[1:]])
    quad = QuadSum(at, t, r, (q1, q2))
    line = LineSum(at, pout, own, din, uin, (po_s, po_r, d_s, d_r, u_s, u_r), True)
    gather = QuadGather(at, gown, grad_ref, (g1, g2, g3))
    n = at.n
    low_end = remote(pend_hbm, pbuf, pd_s.at[0], pd_s.at[1], at.below)
    high_end = remote(pend_hbm, pbuf, pd_s.at[0], pd_s.at[1], at.above)
    copies[0].wait()
    copies[1].wait()

    d = aw.shape[0]
    fold = fold_out.shape[2]
    per_row = d // fold

    def terms(q):
        rs = pl.ds(pl.multiple_of(q * part, part), part)
        width = 512

        @pl.loop(0, half_cols // width)
        def _(i):
            for half in range(2):
                d0 = pl.multiple_of(half * half_cols + i * width, width)
                v = dot(rhs[rs, 0 : 3 * hh], aw[pl.ds(d0, width), :], NT)
                t[half, q, :, pl.ds(pl.multiple_of(i * width, width), width)] = v.astype(BF)
                u = v * nin[rs, pl.ds(d0, width)].astype(F32)
                gsum[0:1, pl.ds(d0, width)] += jnp.sum(u, axis=0, keepdims=True)

    gsum[...] = jnp.zeros_like(gsum)
    copies[2].wait()
    masks = quad.masks()
    terms(at.quarter(masks[0]))
    quad.offer(masks[0])
    for cp in copies[3:5]:
        cp.wait()
    load_x = copies[5]

    def run(k, core):
        block = 2 * order_of(k, at) + (at.c if core else 1 - at.c)
        cols = pl.ds(pl.multiple_of(block * chunk, chunk), chunk)
        lhs[0] = nin[:, cols].T
        lhs[1] = low[:, cols].T

        def tile(i):
            return dot(lhs[lax.div(i, 3)], rhs[:, pl.ds(pl.multiple_of(i * hh, hh), hh)])

        if core:
            line.mine(k, tile)
        else:
            line.other(k, tile)

    devs = [at.core] + [at.fold(b) for b in bits] + [at.peer(b) for b in at.bits]

    def fold_copy(b):
        return remote(fold_out.at[b], fold_in.at[b], fold_s.at[b], fold_r.at[b], devs[b])

    def fold_next(b):
        fold_copy(b).wait_recv()
        fold_out[b + 1] = fold_out[b] + fold_in[b]
        if b + 1 < len(devs):
            fold_copy(b + 1).start()

    run(0, 0)
    run(0, 1)
    for mask in masks[1:]:
        terms(at.quarter(mask))
        quad.offer(mask)
    gsum[0:1, :] = gsum[0:1, :] / gain_ref[0:1, :]
    gsum[1:2, :] = gmid_ref[...]
    for i in range(2):
        for j in range(per_row):
            fold_out[0, i * per_row + j] = gsum[i, j * fold : (j + 1) * fold]
    fold_copy(0).start()
    run(1, 0)
    run(1, 1)
    fold_next(0)
    for k in range(2, n):
        run(k, 0)
        run(k, 1)
    quad.turn()
    for b in range(1, len(bits)):
        fold_next(b)
    pl.when(at.p == 1)(low_end.start)
    pl.when(at.p == n - 2)(high_end.start)
    line.slot(0)
    load_x.wait()
    copies[6].wait()
    fold_next(len(bits))
    step = part // gather.blocks

    def norm(block):
        @pl.loop(0, step // 32)
        def _(b):
            rs = pl.ds(pl.multiple_of(block * step + b * 32, 32), 32)
            v = x[rs, :].astype(F32)
            scale = lax.rsqrt(jnp.mean(v * v, axis=1, keepdims=True) + EPS)
            g = jnp.concatenate([quad.total(0, rs), quad.total(1, rs)], axis=1)
            unit = v * scale
            weighted = g * gain_ref[0:1, :]
            field = scale * (weighted - unit * jnp.mean(weighted * unit, axis=1, keepdims=True))
            total = (gh[rs, :] + field).astype(BF)
            gown[0, rs, :] = total[:, :half_cols]
            gown[1, rs, :] = total[:, half_cols:]

    for block in range(gather.blocks):
        quad.arrive(block)
        norm(block)
        gather.start(block=block)
        if block == 0:
            for b in range(len(bits) + 1, len(devs) - 1):
                fold_next(b)
    for s in range(1, n - 2):
        line.slot(s)
    for block in range(gather.blocks):
        gather.forward(block)
    fold_next(len(devs) - 1)
    for i in range(2):
        for j in range(per_row):
            gsum[i, j * fold : (j + 1) * fold] = fold_out[len(devs), i * per_row + j]
    gains_ref[...] = gsum[:, pl.ds(pl.multiple_of(at.dp * chunk, chunk), chunk)]
    copies[7].wait()

    @pl.when((at.p == 0) | (at.p == n - 1))
    def _():
        low_end.wait_recv()

        @pl.loop(0, 4)
        def _(i):
            dbuf[i] = (dbuf[i].astype(F32) + pbuf[i].astype(F32)).astype(BF)

    store = pltpu.make_async_copy(dbuf, rsd_ref, pd_s.at[2])
    store.start()
    stores = line.final(res, rs_ref, rs_s) + [store]
    pl.when((at.p == 1) | (at.p == n - 2))(low_end.wait_send)
    gather.finish()
    for cp in stores:
        cp.wait()
    line.drain()
    quad.drain()
    for b in range(len(devs)):
        fold_copy(b).wait_send()


def last_stage(n_dp, n_mp, dqkv, aw, nin, low, att, x, gh, pend, rs_down, gain, gmid):
    seq, hh = att.shape
    d = aw.shape[0]
    n, part, chunk = n_dp // 2, seq // n_mp, d // n_dp
    dma = pltpu.SemaphoreType.DMA
    anyspace = pl.BlockSpec(memory_space=pl.ANY)
    vm = pl.BlockSpec(memory_space=pltpu.VMEM)
    folds = 1 + len([b for b in (1, 2, 4, 8) if b < n_mp]) + len([b for b in (2, 4, 8, 16) if b < n_dp])
    return pl.pallas_call(
        functools.partial(last_kernel, n_dp, n_mp),
        out_shape=[
            jax.ShapeDtypeStruct((4, chunk, hh), BF),
            jax.ShapeDtypeStruct((seq, d), BF),
            jax.ShapeDtypeStruct((8, chunk), F32),
            jax.ShapeDtypeStruct(rs_down.shape, BF),
        ],
        in_specs=[anyspace] * 9 + [vm] * 2,
        out_specs=[anyspace, anyspace, vm, anyspace],
        scratch_shapes=[
            pltpu.VMEM((seq, 4 * hh), BF),
            pltpu.VMEM((d, 3 * hh), BF),
            pltpu.VMEM((seq, d), BF),
            pltpu.VMEM((seq, d), BF),
            pltpu.VMEM((2, chunk, seq), BF),
            pltpu.VMEM((part, d), BF),
            pltpu.VMEM((part, d), F32),
            pltpu.VMEM((4, chunk, hh), BF),
            dma((4,)),
            pltpu.VMEM(rs_down.shape, BF),
            pltpu.VMEM(rs_down.shape, BF),
            dma((3,)),
            dma((8,)),
        ]
        + line_sum_scratch(n, 4, chunk, hh)
        + quad_sum_scratch(n_mp, part, d // 2, None, 2)
        + quad_gather_scratch(n_mp, part, d // 2, 2)
        + [
            pltpu.VMEM((8, d), F32),
            pltpu.VMEM((folds + 1, 8, d // 4), F32),
            pltpu.VMEM((folds, 8, d // 4), F32),
            dma((folds,)),
            dma((folds,)),
        ],
        compiler_params=pltpu.CompilerParams(
            collective_id=5, has_side_effects=True, vmem_limit_bytes=VMEM_LIMIT
        ),
        name="last_stage",
    )(dqkv, aw, nin, low, att, x, gh, pend, rs_down, gain, gmid)


def finish_kernel(
    low_ref,
    lay_ref,
    gu_ref,
    down_ref,
    attn_ref,
    gains_ref,
    lay_out,
    in_out,
    gate_out,
    up_out,
    down_out,
    q_out,
    k_out,
    v_out,
    o_out,
    g1_out,
    g2_out,
):
    lay_out[...] = lay_ref[...]
    in_out[...] = low_ref[...].astype(F32)
    half = gate_out.shape[1]
    gate_out[...] = gu_ref[0, :, :half].astype(F32)
    up_out[...] = gu_ref[0, :, half:].astype(F32)
    step = pl.program_id(0)

    @pl.when(lax.rem(step, 2) == 0)
    def _():
        down_out[...] = down_ref[0].T.astype(F32)

    @pl.when(step == 0)
    def _():
        for i, ref in enumerate((q_out, k_out, v_out)):
            ref[...] = attn_ref[i].astype(F32)
        o_out[...] = attn_ref[3].T.astype(F32)
        g1_out[...] = gains_ref[0]
        g2_out[...] = gains_ref[1]


def finish_stage(low, lay, gu, down, attn, gains):
    seq, d = low.shape
    steps, chunk, wide = gu.shape
    width, hh = down.shape[2], attn.shape[2]
    row = pl.BlockSpec((seq // (2 * steps), d), lambda i: (i, 0))
    fixed = lambda *shape: pl.BlockSpec(shape, lambda i: (0,) * len(shape))
    two = pl.BlockSpec((1, chunk // 2, wide), lambda i: (i // 2, i % 2, 0))
    piece = pl.BlockSpec((1, chunk, width), lambda i: (i // 2, 0, 0))
    cols = pl.BlockSpec((chunk // 2, wide // 2), lambda i: (i % 2, i // 2))
    f32 = lambda *shape: jax.ShapeDtypeStruct(shape, F32)
    return pl.pallas_call(
        finish_kernel,
        grid=(2 * steps,),
        in_specs=[row, row, two, piece, fixed(4, chunk, hh), fixed(*gains.shape)],
        out_specs=[row, row, cols, cols, pl.BlockSpec((width, chunk), lambda i: (i // 2, 0))]
        + [fixed(chunk, hh)] * 3
        + [fixed(hh, chunk)]
        + [fixed(chunk)] * 2,
        out_shape=[
            jax.ShapeDtypeStruct((seq, d), BF),
            f32(seq, d),
            f32(chunk, steps * wide // 2),
            f32(chunk, steps * wide // 2),
            f32(steps * width, chunk),
        ]
        + [f32(chunk, hh)] * 3
        + [f32(hh, chunk)]
        + [f32(chunk)] * 2,
        compiler_params=pltpu.CompilerParams(vmem_limit_bytes=VMEM_LIMIT),
        name="finish_stage",
    )(low, lay, gu, down, attn, gains)


def on_device(
    inputs,
    counts,
    cotangent,
    gain_attn,
    w_query,
    w_key,
    w_value,
    w_output,
    gain_ffn,
    w_gate,
    w_up,
    w_down,
):
    n_dp, n_mp = lax.axis_size("dp"), lax.axis_size("mp")
    attn_w, qkv, attended, normed_in, gains, gu_shard, down_shard, grad_ffn, gu_pre = attn_stage(
        n_dp,
        n_mp,
        counts,
        gain_attn,
        gain_ffn,
        w_query,
        w_key,
        w_value,
        w_output,
        w_gate,
        w_up,
        w_down,
        inputs,
        cotangent,
    )
    gu_w, normed_mid, hidden, gu, inner, down_pre = gate_stage(
        n_dp, n_mp, attended, attn_w, gu_shard, gu_pre, down_shard, inputs, gains
    )
    down_part, ffn_terms, ggu, down_pend = down_stage(n_dp, n_mp, inner, gu, grad_ffn, down_shard, down_pre)
    rs_gu, grad_low, layer_out, grad_hidden, g_gain_mid, dqkv = mid_stage(
        n_dp, n_mp, ggu, gu_w, normed_mid, ffn_terms, grad_ffn, qkv, attn_w, counts, hidden, gains
    )
    rs_attn, grad_low_in, g_gains, rs_down = last_stage(
        n_dp,
        n_mp,
        dqkv,
        attn_w,
        normed_in,
        grad_low,
        attended,
        inputs,
        grad_hidden,
        down_pend,
        down_part,
        gains,
        g_gain_mid,
    )
    lay, grad_x, g_gate, g_up, g_down, g_q, g_k, g_v, g_o, g_attn, g_ffn = finish_stage(
        grad_low_in, layer_out, rs_gu, rs_down, rs_attn, g_gains
    )
    return (lay, grad_x, g_attn, g_q, g_k, g_v, g_o, g_ffn, g_gate, g_up, g_down)


def solution(mesh):
    row, both, swapped = P("dp", None), P("dp", "mp"), P("mp", "dp")
    weights = (both, both, both, swapped)
    ffn = (both, both, swapped)
    return jax.shard_map(
        on_device,
        mesh=mesh,
        in_specs=(row, P("dp"), row, P("dp")) + weights + (P("dp"),) + ffn,
        out_specs=(row, row, P("dp")) + weights + (P("dp"),) + ffn,
        check_vma=False,
    )
```

```python
import functools
import math

import jax
import jax.numpy as jnp
from jax import lax
from jax.experimental import pallas as pl
from jax.experimental.pallas import tpu as pltpu
from jax.sharding import PartitionSpec as P

HD = 128
EPS = 1e-06
BF = jnp.bfloat16
F32 = jnp.float32
NT = (((1,), (1,)), ((), ()))
TN = (((0,), (0,)), ((), ()))
NN = (((1,), (0,)), ((), ()))


def dot(a, b, dims=NN):
    return lax.dot_general(a, b, dims, preferred_element_type=F32)


def logistic_block(q, k, seq):
    raw = dot(q, k, NT)
    shifted = math.log(seq) - raw * HD ** (-0.5)
    return 1.0 / (1.0 + jnp.exp(shifted))


def allowed_block(row0, rows, col0, cols, count):
    ri = row0 + lax.broadcasted_iota(jnp.int32, (rows, cols), 0)
    ci = col0 + lax.broadcasted_iota(jnp.int32, (rows, cols), 1)
    return (ci <= ri) & (ci < count)


MESH = pl.DeviceIdType.MESH
VMEM_LIMIT = 60 * 1024 * 1024
PIECES = 4
AHEAD = 1
DOWN_AHEAD = 2


def flipped(index, bit):
    return index + bit - 2 * bit * lax.rem(lax.div(index, bit), 2)


def spread(j, bits):
    return sum(bit for i, bit in enumerate(bits) if j >> i & 1)


class Place:
    def __init__(self, n_dp, n_mp):
        self.n = n_dp // 2
        self.dp = lax.axis_index("dp")
        self.m = lax.axis_index("mp")
        self.p = lax.div(self.dp, 2)
        self.c = lax.rem(self.dp, 2)
        self.above = (self.dp + 2, self.m)
        self.below = (self.dp - 2, self.m)
        self.core = (self.dp + 1 - 2 * self.c, self.m)
        self.bits = [b for b in (1, 2, 4, 8, 16) if b < n_mp]
        self.has_above = self.p < self.n - 1
        self.has_below = self.p > 0

    def fold(self, bit):
        return (flipped(self.dp, bit), self.m)

    def peer(self, bit):
        return (self.dp, flipped(self.m, bit))

    def quarter(self, mask):
        q = self.m
        for bit in self.bits:
            if mask & bit:
                q = flipped(q, bit)
        return q


def signal(dev):
    pl.semaphore_signal(pltpu.get_barrier_semaphore(), inc=1, device_id=dev, device_id_type=MESH)


def enter(at, extra=()):
    always = [at.core] + [at.peer(bit) for bit in at.bits] + list(extra)
    for dev in always:
        signal(dev)

    @pl.when(at.has_above)
    def _():
        signal(at.above)

    @pl.when(at.has_below)
    def _():
        signal(at.below)

    ends = at.has_above.astype(jnp.int32) + at.has_below.astype(jnp.int32)
    pl.semaphore_wait(pltpu.get_barrier_semaphore(), len(always) + ends)


def remote(src, dst, send, recv, dev):
    return pltpu.make_async_remote_copy(
        src_ref=src, dst_ref=dst, send_sem=send, recv_sem=recv, device_id=dev, device_id_type=MESH
    )


def part_rows(at, part):
    return pl.ds(pl.multiple_of(at.m * part, part), part)


def order_of(k, at):
    n, p = at.n, at.p
    if k == n - 1:
        return p
    high = jnp.where(k < p, k, n - 1 - k + p)
    low = jnp.where(k < n - 1 - p, n - 1 - k, k - (n - 1 - p))
    return jnp.where(2 * p >= n, high, low)


class LineSum:
    def __init__(self, at, pout, own, din, uin, sems, paced=False, defer=False):
        self.paced, self.defer = paced, defer
        self.at, self.pout, self.own, self.din, self.uin = at, pout, own, din, uin
        self.po_s, self.po_r, self.d_s, self.d_r, self.u_s, self.u_r = sems
        self.slots, self.pieces = pout.shape[0], own.shape[1]

    def core_copy(self, k, i):
        j = order_of(k, self.at)
        slot = k % self.slots
        return remote(
            self.pout.at[slot, i],
            self.own.at[j, i],
            self.po_s.at[slot, i],
            self.po_r.at[k, i],
            self.at.core,
        )

    def down_copy(self, s, i):
        return remote(
            self.own.at[s, i], self.din.at[s, i], self.d_s.at[s, i], self.d_r.at[s, i], self.at.below
        )

    def up_copy(self, s, i):
        n = self.at.n
        return remote(
            self.own.at[n - 1 - s, i],
            self.uin.at[s, i],
            self.u_s.at[s, i],
            self.u_r.at[s, i],
            self.at.above,
        )

    def other(self, k, tile):
        @pl.loop(0, self.pieces)
        def _(i):
            if k >= self.slots:
                self.core_copy(k - self.slots, i).wait_send()
            self.pout[k % self.slots, i] = tile(i).astype(BF)
            self.core_copy(k, i).start()

    def mine(self, k, tile):
        at = self.at
        j = order_of(k, at)

        @pl.loop(0, self.pieces)
        def _(i):
            value = tile(i)
            self.core_copy(k, i).wait_recv()
            self.own[j, i] = (value + self.own[j, i].astype(F32)).astype(BF)
            if k < (1 if self.paced else at.n - 1):

                @pl.when(at.p == at.n - 1)
                def _():
                    self.down_copy(k, i).start()

                @pl.when(at.p == 0)
                def _():
                    self.up_copy(k, i).start()

    def add(self, dst, src):
        @pl.loop(0, dst.shape[0] // 64)
        def _(b):
            rs = pl.ds(pl.multiple_of(b * 64, 64), 64)
            dst[rs, :] = (dst[rs, :].astype(F32) + src[rs, :].astype(F32)).astype(BF)

    def slot(self, t, first=0, end=None):
        at = self.at
        n, p = at.n, at.p
        sd = t - (n - 2 - p)
        su = t - (p - 1)

        @pl.loop(first, end or self.pieces)
        def _(i):
            @pl.when((sd >= 0) & (sd < p) & at.has_above)
            def _():
                self.down_copy(sd, i).wait_recv()
                self.add(self.own.at[sd, i], self.din.at[sd, i])
                pl.when((p > 1) if self.defer else True)(self.down_copy(sd, i).start)

            @pl.when((su >= 0) & (su < n - 1 - p) & at.has_below)
            def _():
                self.up_copy(su, i).wait_recv()
                self.add(self.own.at[n - 1 - su, i], self.uin.at[su, i])
                pl.when((p < n - 2) if self.defer else True)(self.up_copy(su, i).start)

            if self.paced:

                @pl.when(p == n - 1)
                def _():
                    self.down_copy(t, i).wait_send()
                    self.down_copy(t + 1, i).start()

                @pl.when(p == 0)
                def _():
                    self.up_copy(t, i).wait_send()
                    self.up_copy(t + 1, i).start()

    def final(self, out, sink, sems):
        at = self.at
        n, p = at.n, at.p

        @pl.loop(0, self.pieces)
        def _(i):
            inner = at.has_above & at.has_below

            @pl.when(inner if self.defer else at.has_above)
            def _():
                self.down_copy(p, i).wait_recv()

            @pl.when(inner if self.defer else at.has_below)
            def _():
                self.up_copy(n - 1 - p, i).wait_recv()

            def close(parts):
                @pl.loop(0, out.shape[1] // 64)
                def _(b):
                    rs = pl.ds(pl.multiple_of(b * 64, 64), 64)
                    total = self.own[p, i, rs, :].astype(F32)
                    for ref, s in parts:
                        total = total + ref[s, i, rs, :].astype(F32)
                    out[i, rs, :] = total.astype(out.dtype)

            down, up = (self.din, p), (self.uin, n - 1 - p)

            @pl.when(at.has_above & at.has_below)
            def _():
                close([down, up])

            @pl.when(jnp.logical_not(at.has_below))
            def _():
                close([] if self.defer else [down])

            @pl.when(jnp.logical_not(at.has_above))
            def _():
                close([] if self.defer else [up])

            pltpu.make_async_copy(out.at[i], sink.at[i], sems.at[i]).start()

        return [
            pltpu.make_async_copy(out.at[i], sink.at[i], sems.at[i]) for i in range(self.pieces)
        ]

    def drain(self):
        at = self.at
        n, p = at.n, at.p
        for k in range(n - self.slots, n):
            for i in range(self.pieces):
                self.core_copy(k, i).wait_send()
        for s in range(n - 1):
            done = self.paced and s < n - 2

            last = self.defer

            @pl.when((s < p) & (p > 1 if last else at.has_above if done else at.has_below))
            def _():
                for i in range(self.pieces):
                    self.down_copy(s, i).wait_send()

            @pl.when((s < n - 1 - p) & (p < n - 2 if last else at.has_below if done else at.has_above))
            def _():
                for i in range(self.pieces):
                    self.up_copy(s, i).wait_send()


def line_sum_scratch(n, pieces, rows, cols, slots=2):
    dma = pltpu.SemaphoreType.DMA
    return [
        pltpu.VMEM((slots, pieces, rows, cols), BF),
        pltpu.VMEM((n, pieces, rows, cols), BF),
        pltpu.VMEM((n - 1, pieces, rows, cols), BF),
        pltpu.VMEM((n - 1, pieces, rows, cols), BF),
        dma((slots, pieces)),
        dma((n, pieces)),
        dma((n - 1, pieces)),
        dma((n - 1, pieces)),
        dma((n - 1, pieces)),
        dma((n - 1, pieces)),
    ]


class QuadSum:
    def __init__(self, at, t, r, sems):
        self.at, self.t, self.r = at, t, r
        self.s, self.v = sems
        self.blocks = self.s.shape[2]
        self.step = r.shape[2] // self.blocks
        self.order = [at.bits, at.bits[::-1]]
        self.levels = len(at.bits)
        self.seen = set()

    def count(self, k):
        return 1 << (self.levels - 1 - k)

    def slot(self, k, j):
        return sum(self.count(i) for i in range(k)) + j

    def rest(self, half, k):
        return self.order[half][k + 1 :]

    def index(self, half, k, mask):
        rest = self.rest(half, k)
        return self.slot(k, sum(1 << i for i, bit in enumerate(rest) if mask & bit))

    def source(self, half, mask):
        return self.t.at[half, self.at.quarter(mask)]

    def terms(self, half, mask, rs):
        return self.t[half, self.at.quarter(mask), rs, :].astype(F32)

    def split(self, k):
        return self.blocks if k == self.levels - 1 else 1

    def copy(self, half, k, j, block=0):
        bit = self.order[half][k]
        mask = bit + spread(j, self.rest(half, k))
        src = self.source(half, mask) if k == 0 else self.r.at[half, self.index(half, k - 1, mask)]
        at = self.slot(k, j)
        dst = self.r.at[half, at]
        if self.split(k) > 1:
            rows = pl.ds(block * self.step, self.step)
            src, dst = src.at[rows, :], dst.at[rows, :]
        send, recv = self.s.at[half, at, block], self.v.at[half, at, block]
        return remote(src, dst, send, recv, self.at.peer(bit))

    def offer(self, mask, only=(0, 1)):
        for half in only:
            if mask & self.order[half][0]:
                rest = self.rest(half, 0)
                self.copy(half, 0, sum(1 << i for i, b in enumerate(rest) if mask & b)).start()

    def masks(self):
        return sorted(range(1, 2 * self.count(0)), key=lambda m: -bin(m).count("1")) + [0]

    def come(self, half, k, mask, block=0):
        at = self.index(half, k, mask)
        block = min(block, self.split(k) - 1)
        if (half, at, block) not in self.seen:
            self.seen.add((half, at, block))
            self.copy(half, k, at - self.slot(k, 0), block).wait_recv()
        return at

    def turn(self):
        for k in range(1, self.levels):
            for block in range(self.split(k)):
                for half in range(2):
                    for j in range(self.count(k)):
                        self.pass_on(half, k, j, block)

    def pass_on(self, half, k, j, block):
        mask = self.order[half][k] + spread(j, self.rest(half, k))
        got = [self.come(half, i, mask) for i in range(k)]
        rows = self.r.shape[2] // self.split(k)

        @pl.loop(0, rows // 64)
        def _(b):
            rs = pl.ds(pl.multiple_of(block * rows + b * 64, 64), 64)
            total = self.terms(half, mask, rs)
            for i in got:
                total = total + self.r[half, i, rs, :].astype(F32)
            self.r[half, got[-1], rs, :] = total.astype(BF)

        self.copy(half, k, j, block).start()

    def arrive(self, block=0):
        self.got = [
            [self.come(half, k, 0, block) for k in range(self.levels)] for half in range(2)
        ]

    def total(self, half, rs):
        total = self.terms(half, 0, rs)
        for i in self.got[half]:
            total = total + self.r[half, i, rs, :].astype(F32)
        return total

    def drain(self):
        for half in range(2):
            for k in range(self.levels):
                for j in range(self.count(k)):
                    for block in range(self.split(k)):
                        self.copy(half, k, j, block).wait_send()


class QuadSumHbm(QuadSum):
    def __init__(self, at, hbm, t, r, sems):
        super().__init__(at, t, r, sems[:2])
        self.hbm = hbm
        self.loads = [
            pltpu.make_async_copy(
                self.source(half, spread(j, self.rest(half, 0))), t.at[half, j], sems[2].at[half, j]
            )
            for half in range(2)
            for j in range(self.count(0))
        ]

    def source(self, half, mask):
        rows, cols = self.t.shape[2], self.t.shape[3]
        rs = pl.ds(pl.multiple_of(self.at.quarter(mask) * rows, rows), rows)
        return self.hbm.at[rs, pl.ds(half * cols, cols)]

    def terms(self, half, mask, rs):
        return self.t[half, self.index(half, 0, mask), rs, :].astype(F32)


def quad_sum_scratch(mp, rows, cols, parts=None, blocks=1):
    dma = pltpu.SemaphoreType.DMA
    return [
        pltpu.VMEM((2, parts or mp, rows, cols), BF),
        pltpu.VMEM((2, mp - 1, rows, cols), BF),
        dma((2, mp - 1, blocks)),
        dma((2, mp - 1, blocks)),
    ]


class QuadGather:
    def __init__(self, at, own, out, sems):
        self.at, self.own, self.out = at, own, out
        self.s, self.v, self.here = sems
        self.blocks = self.s.shape[2]
        self.order = [at.bits[::-1], at.bits]
        self.levels = len(at.bits)
        self.seen = set()

    def mine(self, half, block):
        step = self.own.shape[1] // self.blocks
        return self.own.at[half, pl.ds(block * step, step), :]

    def spot(self, mask, half, block):
        rows, cols = self.own.shape[1], self.own.shape[2]
        step = rows // self.blocks
        rs = pl.ds(pl.multiple_of(self.at.quarter(mask) * rows + block * step, step), step)
        return self.out.at[rs, pl.ds(half * cols, cols)]

    def copy(self, half, k, j, block):
        mask = spread(j, self.order[half][:k])
        dst = self.spot(mask, half, block)
        src = self.mine(half, block) if j == 0 else dst
        at = (1 << k) - 1 + j
        dev = self.at.peer(self.order[half][k])
        return remote(src, dst, self.s.at[half, at, block], self.v.at[half, at, block], dev)

    def come(self, half, k, j, block):
        if (half, k, j, block) not in self.seen:
            self.seen.add((half, k, j, block))
            self.copy(half, k, j, block).wait_recv()

    def keep(self, half, block):
        return pltpu.make_async_copy(
            self.mine(half, block), self.spot(0, half, block), self.here.at[half, block]
        )

    def start(self, levels=None, block=0):
        for k in range(self.levels) if levels is None else levels:
            for half in range(2):
                self.copy(half, k, 0, block).start()
                if k == 0:
                    self.keep(half, block).start()

    def forward(self, block=0):
        for k in range(1, self.levels):
            for half in range(2):
                for j in range(1, 1 << k):
                    top = j.bit_length() - 1
                    self.come(half, top, j - (1 << top), block)
                    self.copy(half, k, j, block).start()

    def finish(self):
        for half in range(2):
            for block in range(self.blocks):
                for k in range(self.levels):
                    for j in range(1 << k):
                        self.come(half, k, j, block)
                        self.copy(half, k, j, block).wait_send()
                self.keep(half, block).wait()


def quad_gather_scratch(mp, rows, cols, blocks=1):
    dma = pltpu.SemaphoreType.DMA
    return [
        pltpu.VMEM((2, rows, cols), BF),
        dma((2, mp - 1, blocks)),
        dma((2, mp - 1, blocks)),
        dma((2, blocks)),
    ]


class LineGather:
    def __init__(self, at, pieces, shard, spot, sems, pre=0, wide=False):
        self.pre, self.wide = pre, wide
        self.at, self.pieces, self.shard, self.spot = at, pieces, shard, spot
        self.d_s, self.d_r, self.u_s, self.u_r, self.c_s, self.c_r, self.here = sems

    def down_copy(self, h, i, own=False):
        b = 2 * (self.at.p + h) + self.at.c
        dst = self.spot(b, i)
        src = self.shard(i) if own and self.shard else dst
        return remote(src, dst, self.d_s.at[h, i], self.d_r.at[h, i], self.at.below)

    def up_copy(self, h, i, own=False):
        b = 2 * (self.at.p - h) + self.at.c
        dst = self.spot(b, i)
        src = self.shard(i) if own and self.shard else dst
        return remote(src, dst, self.u_s.at[h, i], self.u_r.at[h, i], self.at.above)

    def core_copy(self, z, i, own=False, incoming=False):
        b = 2 * z + (1 - self.at.c if incoming else self.at.c)
        dst = self.spot(b, i)
        src = self.shard(i) if own and self.shard else dst
        return remote(src, dst, self.c_s.at[z, i], self.c_r.at[z, i], self.at.core)

    def keep(self, i):
        at = self.at
        return pltpu.make_async_copy(self.shard(i), self.spot(at.dp, i), self.here.at[i])

    def start(self):
        at = self.at
        down, up = self.late()
        for i in range(self.pre, self.pieces):

            @pl.when(down)
            def _():
                self.down_copy(0, i, True).start()

            @pl.when(up)
            def _():
                self.up_copy(0, i, True).start()

        for i in range(self.pieces):
            self.core_copy(at.p, i, True).start()
            if self.shard:
                self.keep(i).start()

    def late(self):
        at = self.at
        if self.wide:
            return at.p == 1, at.p == at.n - 2
        return at.has_below, at.has_above

    def slot(self, h, i):
        at = self.at
        n, p = at.n, at.p

        @pl.when(p + h < n)
        def _():
            self.down_copy(h - 1, i).wait_recv()

            @pl.when(at.has_below)
            def _():
                self.down_copy(h, i).start()

            self.core_copy(p + h, i).start()

        @pl.when(p - h >= 0)
        def _():
            self.up_copy(h - 1, i).wait_recv()

            @pl.when(at.has_above)
            def _():
                self.up_copy(h, i).start()

            self.core_copy(p - h, i).start()

    def stage(self, h):
        @pl.loop(self.pre if h == 1 else 0, self.pieces)
        def _(i):
            if h == 1 and self.wide:
                self.slot_ends(i)
            else:
                self.slot(h, i)

    def slot_ends(self, i):
        at = self.at

        @pl.when(at.p == 0)
        def _():
            self.down_copy(0, i).wait_recv()
            self.core_copy(1, i).start()

        @pl.when(at.p == at.n - 1)
        def _():
            self.up_copy(0, i).wait_recv()
            self.core_copy(at.n - 2, i).start()

    def early(self, i, above, below):
        at = self.at
        both = at.has_above & at.has_below
        everyone = i < self.pre

        @pl.when(at.has_above if everyone else both)
        def _():
            b = 2 * at.p + 2 + at.c
            dst = self.spot(b, i)

            @pl.when(at.has_below)
            def _():
                remote(above, dst, self.d_s.at[1, i], self.d_r.at[1, i], at.below).start()

            z = at.p + 1
            remote(above, dst, self.c_s.at[z, i], self.c_r.at[z, i], at.core).start()

        @pl.when(at.has_below if everyone else both)
        def _():
            b = 2 * at.p - 2 + at.c
            dst = self.spot(b, i)

            @pl.when(at.has_above)
            def _():
                remote(below, dst, self.u_s.at[1, i], self.u_r.at[1, i], at.above).start()

            z = at.p - 1
            remote(below, dst, self.c_s.at[z, i], self.c_r.at[z, i], at.core).start()

    def ready(self, z, i):
        self.core_copy(z, i, incoming=True).wait_recv()

    def drain(self):
        at = self.at
        n, p = at.n, at.p

        down, up = self.late()

        @pl.loop(0, self.pieces)
        def _(i):
            for h in range(n):
                own = h == 0

                @pl.when((down & (i >= self.pre)) if own else ((p + h < n) & at.has_below))
                def _():
                    self.down_copy(h, i, own).wait_send()

                @pl.when((up & (i >= self.pre)) if own else ((p - h >= 0) & at.has_above))
                def _():
                    self.up_copy(h, i, own).wait_send()

            for z in range(n):
                self.core_copy(z, i).wait_send()


def line_gather_scratch(n, pieces):
    dma = pltpu.SemaphoreType.DMA
    return [dma((n, pieces))] * 6 + [dma((pieces,))]


def rows_spot(out, rows, width):
    def spot(b, i):
        rs = pl.ds(pl.multiple_of(b * rows, rows), rows)
        return out.at[rs, pl.ds(pl.multiple_of(i * width, width), width)]

    return spot


def cols_of(ref, width, base=0):
    return lambda i: ref.at[:, pl.ds(pl.multiple_of(base + i * width, width), width)]


class Presend:
    def __init__(self, at, src, got, sems, narrow):
        s, r = sems
        wide = src.shape[1]
        n, p = at.n, at.p
        self.sends, self.comes = [], []
        for width in sorted({narrow, wide}):
            cols = pl.ds(0, width)
            down = remote(src.at[:, cols], got.at[0, :, cols], s.at[0], r.at[0], at.below)
            up = remote(src.at[:, cols], got.at[1, :, cols], s.at[1], r.at[1], at.above)
            if narrow == wide:
                whens = at.has_below, at.has_above, at.has_above, at.has_below
            elif width == narrow:
                whens = p == 1, p == n - 2, p == 0, p == n - 1
            else:
                inner = at.has_above & at.has_below
                whens = p > 1, p < n - 2, inner, inner
            self.sends += [(whens[0], down), (whens[1], up)]
            self.comes += [(whens[2], down), (whens[3], up)]

    def start(self):
        for when, copy in self.sends:
            pl.when(when)(copy.start)

    def finish(self):
        for when, copy in self.comes:
            pl.when(when)(copy.wait_recv)
        for when, copy in self.sends:
            pl.when(when)(copy.wait_send)


def attend_rows(qkv, out, seq, hh, count, head):
    cols = lambda first: pl.ds(pl.multiple_of(first + head * HD, HD), HD)
    blk = 256
    for i in range(seq // blk):
        rows = pl.ds(i * blk, blk)
        span = (i + 1) * blk
        lg = logistic_block(qkv[rows, cols(0)], qkv[pl.ds(0, span), cols(hh)], seq)
        w = jnp.where(allowed_block(i * blk, blk, 0, span, count), lg, 0.0).astype(BF)
        out[rows, cols(0)] = dot(w, qkv[pl.ds(0, span), cols(2 * hh)]).astype(BF)


def attn_kernel(
    n_dp,
    n_mp,
    count_ref,
    ga_ref,
    gf_ref,
    wq_hbm,
    wk_hbm,
    wv_hbm,
    wo_hbm,
    wg_hbm,
    wu_hbm,
    wd_hbm,
    x_hbm,
    cot_hbm,
    aw_ref,
    qkv_ref,
    att_ref,
    nin_ref,
    gains_ref,
    gush_ref,
    dnsh_ref,
    cotm_ref,
    gpre_ref,
    gains_in,
    w4,
    wo,
    shard,
    x,
    qkv,
    wbuf,
    wgu,
    wd,
    gush,
    dnsh,
    cot,
    load_s,
    wb_s,
    out_s,
    *rest,
):
    at = Place(n_dp, n_mp)
    n = at.n
    chunk, hh = wq_hbm.shape
    seq, d = x.shape
    ff = wgu.shape[2]
    loads = [
        pltpu.make_async_copy(src, dst, load_s.at[i])
        for i, (src, dst) in enumerate(
            [
                (wq_hbm, w4.at[0]),
                (wk_hbm, w4.at[1]),
                (wv_hbm, w4.at[2]),
                (wo_hbm, wo),
                (x_hbm, x),
                (wg_hbm, wgu.at[0]),
                (wu_hbm, wgu.at[1]),
                (wd_hbm, wd),
                (cot_hbm, cot),
            ]
        )
    ]
    for cp in loads:
        cp.start()
    spot = rows_spot(aw_ref, chunk, hh)
    three = LineGather(at, 3, cols_of(shard, hh), spot, rest[0:7])
    last = LineGather(
        at, 1, lambda i: shard.at[:, pl.ds(3 * hh, hh)], lambda b, i: spot(b, 3), rest[7:14]
    )
    small = LineGather(
        at,
        1,
        lambda i: gains_in,
        lambda b, i: gains_ref.at[:, pl.ds(pl.multiple_of(b * chunk, chunk), chunk)],
        rest[14:21],
    )
    for i, ref in enumerate((ga_ref, gf_ref)):
        gains_in[i, :] = ref[...].astype(BF).astype(F32)
    enter(at)
    small.start()
    for i in range(3):
        loads[i].wait()
        shard[:, i * hh : (i + 1) * hh] = w4[i].astype(BF)
    three.start()
    loads[3].wait()
    shard[:, 3 * hh :] = wo[...].T.astype(BF)
    small.slot(1, 0)
    loads[5].wait()
    loads[6].wait()
    half = ff // PIECES

    @pl.loop(0, PIECES)
    def _(i):
        cols = pl.ds(pl.multiple_of(i * half, half), half)
        for k in range(2):
            to = pl.ds(pl.multiple_of((2 * i + k) * half, half), half)
            gush[:, to] = wgu[k, :, cols].astype(BF)

    outs = [pltpu.make_async_copy(gush, gush_ref, out_s.at[0])]
    outs[0].start()
    loads[7].wait()

    @pl.loop(0, ff // 256)
    def _(i):
        rs = pl.ds(pl.multiple_of(i * 256, 256), 256)
        dnsh[:, rs] = wd[rs, :].T.astype(BF)

    outs.append(pltpu.make_async_copy(dnsh, dnsh_ref, out_s.at[2]))
    outs[-1].start()
    loads[8].wait()
    count = count_ref[0]

    @pl.loop(0, seq // 32)
    def _(b):
        rs = pl.ds(pl.multiple_of(b * 32, 32), 32)
        row = b * 32 + lax.broadcasted_iota(jnp.int32, (32, d), 0)
        cot[rs, :] = jnp.where(row < count, cot[rs, :].astype(F32), 0.0).astype(BF)

    outs.append(pltpu.make_async_copy(cot, cotm_ref, out_s.at[3]))
    outs[-1].start()
    for h in range(1, n - 1):
        small.slot(h + 1, 0)
        three.stage(h)
        if h == n - 2:
            last.start()
    small.keep(0).wait()
    for z in range(n):
        small.ready(z, 0)
    loads[4].wait()

    @pl.loop(0, seq // 32)
    def _(b):
        rs = pl.ds(pl.multiple_of(b * 32, 32), 32)
        v = x[rs, :].astype(F32)
        scale = lax.rsqrt(jnp.mean(v * v, axis=1, keepdims=True) + EPS)
        x[rs, :] = (v * scale * gains_ref[0:1, :]).astype(BF)

    outs.append(pltpu.make_async_copy(x, nin_ref, out_s.at[1]))
    outs[-1].start()

    def w_copy(i):
        cols = pl.ds(pl.multiple_of(i * hh, hh), hh)
        return pltpu.make_async_copy(aw_ref.at[:, cols], wbuf.at[i], wb_s.at[i])

    for i in range(3):
        three.slot(n - 1, i)
        three.keep(i).wait()
        for z in range(n):
            three.ready(z, i)
        w_copy(i).start()
        if i == 1:
            last.slot(1, 0)
        w_copy(i).wait()

        @pl.loop(0, seq // 256)
        def _(b):
            rs = pl.ds(pl.multiple_of(b * 256, 256), 256)
            qkv[rs, i * hh : (i + 1) * hh] = dot(x[rs, :], wbuf[i]).astype(BF)

    outs.append(pltpu.make_async_copy(qkv, qkv_ref, out_s.at[4]))
    outs[-1].start()
    for h in range(2, n - 1):
        last.slot(h, 0)
    ahead = Presend(at, gush.at[:, pl.ds(0, 2 * half * AHEAD)], gpre_ref, rest[21:23], 2 * half * AHEAD)
    ahead.start()
    heads = hh // HD

    @pl.loop(0, heads // 2)
    def _(head):
        attend_rows(qkv, att_ref, seq, hh, count, head)

    last.slot(n - 1, 0)

    @pl.loop(heads // 2, heads)
    def _(head):
        attend_rows(qkv, att_ref, seq, hh, count, head)

    last.keep(0).wait()
    for z in range(n):
        last.ready(z, 0)
    for cp in outs:
        cp.wait()
    ahead.finish()
    small.drain()
    three.drain()
    last.drain()


def attn_stage(n_dp, n_mp, counts, ga, gf, wq, wk, wv, wo, wg, wu, wd, x, cot):
    seq, d = x.shape
    chunk, hh = wq.shape
    ff = wg.shape[1]
    n = n_dp // 2
    dma = pltpu.SemaphoreType.DMA
    hbm = pl.BlockSpec(memory_space=pl.ANY)
    vm = pl.BlockSpec(memory_space=pltpu.VMEM)
    shapes = [
        ((d, 4 * hh), BF),
        ((seq, 3 * hh), BF),
        ((seq, hh), BF),
        ((seq, d), BF),
        ((8, d), F32),
        ((chunk, 2 * ff), BF),
        ((chunk, ff), BF),
        ((seq, d), BF),
        ((2, chunk, 2 * ff * AHEAD // PIECES), BF),
    ]
    return pl.pallas_call(
        functools.partial(attn_kernel, n_dp, n_mp),
        out_shape=[jax.ShapeDtypeStruct(*s) for s in shapes],
        in_specs=[pl.BlockSpec(memory_space=pltpu.SMEM), vm, vm] + [hbm] * 9,
        out_specs=[hbm, hbm, vm, hbm, vm, hbm, hbm, hbm, hbm],
        scratch_shapes=[
            pltpu.VMEM((8, chunk), F32),
            pltpu.VMEM((3, chunk, hh), F32),
            pltpu.VMEM((hh, chunk), F32),
            pltpu.VMEM((chunk, 4 * hh), BF),
            pltpu.VMEM((seq, d), BF),
            pltpu.VMEM((seq, 3 * hh), BF),
            pltpu.VMEM((3, d, hh), BF),
            pltpu.VMEM((2, chunk, ff), F32),
            pltpu.VMEM((ff, chunk), F32),
            pltpu.VMEM((chunk, 2 * ff), BF),
            pltpu.VMEM((chunk, ff), BF),
            pltpu.VMEM((seq, d), BF),
            dma((9,)),
            dma((3,)),
            dma((5,)),
        ]
        + line_gather_scratch(n, 3)
        + line_gather_scratch(n, 1) * 2
        + [dma((2,))] * 2,
        compiler_params=pltpu.CompilerParams(
            collective_id=1, has_side_effects=True, vmem_limit_bytes=VMEM_LIMIT
        ),
        name="attn_stage",
    )(counts, ga, gf, wq, wk, wv, wo, wg, wu, wd, x, cot)


def gate_kernel(
    n_dp,
    n_mp,
    att_ref,
    aw_hbm,
    sh_hbm,
    gpre_hbm,
    dnsh_hbm,
    x_hbm,
    gain_ref,
    gw_ref,
    nm_ref,
    hid_hbm,
    gu_ref,
    inner_ref,
    dpre_ref,
    wo,
    gp,
    sh,
    xs,
    hid,
    acc,
    nm,
    wbuf,
    gbuf,
    ibuf,
    gp_s,
    load_s,
    wb_s,
    gb_s,
    ib_s,
    *rest,
):
    at = Place(n_dp, n_mp)
    n = at.n
    quad = QuadSum(at, *rest[0:2], rest[2:4])
    gather_nm = QuadGather(at, rest[4], nm_ref, rest[5:8])
    sems = rest[8:15]
    hh = wo.shape[1]
    part, half_cols = quad.t.shape[2], quad.t.shape[3]
    chunk, wide = sh_hbm.shape
    pieces = sems[6].shape[0]
    width = wide // pieces
    line = LineGather(at, pieces, cols_of(sh, width), rows_spot(gw_ref, chunk, width), sems, AHEAD)

    load_sh = pltpu.make_async_copy(sh_hbm, sh, load_s.at[2])
    load_sh.start()
    load_gp = pltpu.make_async_copy(gpre_hbm, gp, load_s.at[3])
    load_gp.start()
    load = pltpu.make_async_copy(aw_hbm.at[:, pl.ds(3 * hh, hh)], wo, load_s.at[0])
    load.start()
    load_x = pltpu.make_async_copy(x_hbm.at[part_rows(at, part), :], xs, load_s.at[1])
    load_x.start()
    enter(at)
    load_sh.wait()
    line.start()
    load_gp.wait()

    def place(side, i):
        b = at.dp + (2 if side == 0 else -2)
        piece = gp.at[side, :, pl.ds(i * width, width)]
        return pltpu.make_async_copy(piece, line.spot(b, i), gp_s.at[side, i])

    for i in range(AHEAD):
        line.early(i, *[gp.at[side, :, pl.ds(i * width, width)] for side in range(2)])
        pl.when(at.has_above)(place(0, i).start)
        pl.when(at.has_below)(place(1, i).start)
    load.wait()

    def terms(q):
        rs = pl.ds(pl.multiple_of(q * part, part), part)
        for half in range(2):
            w = wo[half * half_cols : (half + 1) * half_cols, :]
            quad.t[half, q] = dot(att_ref[rs, :], w, NT).astype(BF)

    for mask in quad.masks():
        terms(at.quarter(mask))
        quad.offer(mask)
    quad.turn()
    quad.arrive()
    load_x.wait()

    @pl.loop(0, part // 32)
    def _(b):
        rs = pl.ds(pl.multiple_of(b * 32, 32), 32)
        h = xs[rs, :].astype(F32) + jnp.concatenate(
            [quad.total(0, rs), quad.total(1, rs)], axis=1
        )
        hid[rs, :] = h
        scale = lax.rsqrt(jnp.mean(h * h, axis=1, keepdims=True) + EPS)
        res = (h * scale * gain_ref[1:2, :]).astype(BF)
        gather_nm.own[0, rs, :] = res[:, :half_cols]
        gather_nm.own[1, rs, :] = res[:, half_cols:]

    gather_nm.start()
    store_hid = pltpu.make_async_copy(hid, hid_hbm, load_s.at[1])
    store_hid.start()
    line.stage(1)
    gather_nm.forward()
    gather_nm.finish()
    load = pltpu.make_async_copy(nm_ref, nm, load_s.at[0])
    load.start()
    for h in range(2, n - 1):
        line.stage(h)
    load.wait()

    for i in range(AHEAD):
        pl.when(at.has_above)(place(0, i).wait)
        pl.when(at.has_below)(place(1, i).wait)
    ahead = Presend(at, dnsh_hbm, dpre_ref, rest[15:17], width // 2 * DOWN_AHEAD)
    ahead.start()

    pair = 2 * chunk
    near = jnp.where(2 * at.p < n, 0, 1)
    far = jnp.where(2 * at.p < n, n - 1, 0)
    most = (n - 1) * pair
    most_rows = pl.ds(pl.multiple_of(near * pair, pair), most)
    far_rows = pl.ds(pl.multiple_of(far * pair, pair), pair)

    def w_copy(i, slot, rows):
        cols = pl.ds(pl.multiple_of(i * width, width), width)
        return pltpu.make_async_copy(
            gw_ref.at[rows, cols], wbuf.at[slot, rows, :], wb_s.at[slot]
        )

    def first_part(i, slot):
        line.keep(i).wait()

        @pl.loop(0, n - 1)
        def _(z):
            line.ready(near + z, i)

        w_copy(i, slot, most_rows).start()
        w_copy(i, slot, most_rows).wait()

        @pl.loop(0, nm.shape[0] // 256)
        def _(b):
            rs = pl.ds(pl.multiple_of(b * 256, 256), 256)
            acc[rs, :] = dot(nm[rs, most_rows], wbuf[slot, most_rows, :])

    def g_copy(i, slot):
        cols = pl.ds(pl.multiple_of(i * width, width), width)
        return pltpu.make_async_copy(gbuf.at[slot], gu_ref.at[:, cols], gb_s.at[slot])

    def i_copy(i, slot):
        cols = pl.ds(pl.multiple_of(i * (width // 2), width // 2), width // 2)
        return pltpu.make_async_copy(ibuf.at[slot], inner_ref.at[:, cols], ib_s.at[slot])

    @pl.loop(0, pieces)
    def _(i):
        slot = lax.rem(i, 2)
        first_part(i, slot)
        line.slot(n - 1, i)
        line.ready(far, i)
        w_copy(i, slot, far_rows).start()

        @pl.when(i >= 2)
        def _():
            g_copy(i - 2, slot).wait()
            i_copy(i - 2, slot).wait()

        w_copy(i, slot, far_rows).wait()

        @pl.loop(0, nm.shape[0] // 256)
        def _(b):
            rs = pl.ds(pl.multiple_of(b * 256, 256), 256)
            v = (acc[rs, :] + dot(nm[rs, far_rows], wbuf[slot, far_rows, :])).astype(BF)
            gbuf[slot, rs, :] = v
            g = v[:, : width // 2].astype(F32)
            u = v[:, width // 2 :].astype(F32)
            ibuf[slot, rs, :] = (g / (1.0 + jnp.exp(-g)) * u).astype(BF)

        g_copy(i, slot).start()
        i_copy(i, slot).start()

    for i in range(max(0, pieces - 2), pieces):
        g_copy(i, i % 2).wait()
        i_copy(i, i % 2).wait()
    store_hid.wait()
    ahead.finish()
    line.drain()
    quad.drain()


def gate_stage(n_dp, n_mp, att, aw, shard, gpre, dnsh, x, gain):
    seq, hh = att.shape
    d = aw.shape[0]
    chunk, wide = shard.shape
    n, part = n_dp // 2, seq // n_mp
    dma = pltpu.SemaphoreType.DMA
    hbm = pl.BlockSpec(memory_space=pl.ANY)
    vm = pl.BlockSpec(memory_space=pltpu.VMEM)
    width = wide // PIECES
    return pl.pallas_call(
        functools.partial(gate_kernel, n_dp, n_mp),
        out_shape=[
            jax.ShapeDtypeStruct((d, wide), BF),
            jax.ShapeDtypeStruct((seq, d), BF),
            jax.ShapeDtypeStruct((part, d), F32),
            jax.ShapeDtypeStruct((seq, wide), BF),
            jax.ShapeDtypeStruct((seq, wide // 2), BF),
            jax.ShapeDtypeStruct((2, chunk, wide // 2), BF),
        ],
        in_specs=[vm, hbm, hbm, hbm, hbm, hbm, vm],
        out_specs=[hbm] * 6,
        scratch_shapes=[
            pltpu.VMEM((d, hh), BF),
            pltpu.VMEM((2, chunk, width * AHEAD), BF),
            pltpu.VMEM((chunk, wide), BF),
            pltpu.VMEM((part, d), BF),
            pltpu.VMEM((part, d), F32),
            pltpu.VMEM((seq, width), F32),
            pltpu.VMEM((seq, d), BF),
            pltpu.VMEM((2, d, width), BF),
            pltpu.VMEM((2, seq, width), BF),
            pltpu.VMEM((2, seq, width // 2), BF),
            dma((2, AHEAD)),
            dma((4,)),
            dma((2,)),
            dma((2,)),
            dma((2,)),
        ]
        + quad_sum_scratch(n_mp, part, d // 2)
        + quad_gather_scratch(n_mp, part, d // 2)
        + line_gather_scratch(n, PIECES)
        + [dma((2,))] * 2,
        compiler_params=pltpu.CompilerParams(
            collective_id=2, has_side_effects=True, vmem_limit_bytes=VMEM_LIMIT
        ),
        name="gate_stage",
    )(att, aw, shard, gpre, dnsh, x, gain)


def down_kernel(
    n_dp,
    n_mp,
    inner_hbm,
    gu_hbm,
    cot_hbm,
    sh_hbm,
    dpre_hbm,
    rs_ref,
    ft_ref,
    ggu_ref,
    pend_ref,
    inner,
    gu,
    cot,
    dn,
    acc,
    ftb,
    res,
    dp_s,
    load_s,
    cot_s,
    in_s,
    rs_s,
    ft_s,
    dn_s,
    gg_s,
    *rest,
):
    at = Place(n_dp, n_mp)
    n, p = at.n, at.p
    line = LineSum(at, *rest[0:4], rest[4:10], defer=True)
    sems = rest[10:17]
    chunk, ff = sh_hbm.shape
    pieces = sems[6].shape[0]
    width = ff // pieces
    gather = LineGather(at, pieces, None, rows_spot(dn, chunk, width), sems, DOWN_AHEAD, True)
    pair = 2 * chunk
    def cot_copy(k):
        cols = pl.ds(pl.multiple_of(order_of(k, at) * pair, pair), pair)
        return pltpu.make_async_copy(cot_hbm.at[:, cols], cot.at[:, cols], cot_s.at[k])

    def in_copy(i):
        cols = pl.ds(pl.multiple_of(i * width, width), width)
        return pltpu.make_async_copy(inner_hbm.at[:, cols], inner.at[:, cols], in_s.at[i])

    load_gu = pltpu.make_async_copy(gu_hbm, gu, load_s.at[0])
    own = pltpu.make_async_copy(
        sh_hbm, dn.at[pl.ds(pl.multiple_of(at.dp * chunk, chunk), chunk), :], dn_s.at[0]
    )
    own.start()

    inside = at.has_above & at.has_below

    def pre_copy(side, i):
        b = at.dp + (2 if side == 0 else -2)
        piece = dpre_hbm.at[side, :, pl.ds(i * width, width)]
        return pltpu.make_async_copy(piece, gather.spot(b, i), dp_s.at[side, i])

    def pre_whens(i):
        return (at.has_above, at.has_below) if i < DOWN_AHEAD else (inside, inside)

    for i in range(pieces):
        for side in range(2):
            pl.when(pre_whens(i)[side])(pre_copy(side, i).start)
    cot_copy(0).start()
    for i in range(pieces):
        in_copy(i).start()
    for k in range(1, n):
        cot_copy(k).start()
    load_gu.start()
    enter(at)
    own.wait()
    gather.start()
    for i in range(pieces):
        for side in range(2):
            pl.when(pre_whens(i)[side])(pre_copy(side, i).wait)
        gather.early(i, gather.spot(at.dp + 2, i), gather.spot(at.dp - 2, i))

    def run(e):
        k, core = e // 2, e % 2
        block = 2 * order_of(k, at) + (1 - at.c if core == 0 else at.c)
        if core == 0:
            cot_copy(k).wait()
        lhs = cot[:, pl.ds(pl.multiple_of(block * chunk, chunk), chunk)].T

        def tile(i):
            if e == 0:
                in_copy(i).wait()
            return dot(lhs, inner[:, pl.ds(pl.multiple_of(i * width, width), width)])

        if core == 0:
            line.other(k, tile)
        else:
            line.mine(k, tile)

    for e in range(2 * n):
        run(e)

    def ft_copy(z, slot):
        cols = pl.ds(pl.multiple_of(z * pair, pair), pair)
        return pltpu.make_async_copy(ftb.at[slot], ft_ref.at[:, cols], ft_s.at[slot])

    def rows_of(z):
        return pl.ds(pl.multiple_of(z * pair, pair), pair)

    def grads(z, fresh):
        @pl.loop(0, pieces)
        def _(i):
            gather.ready(z, i)

        @pl.loop(0, ff // 512)
        def _(i):
            cols = pl.ds(pl.multiple_of(i * 512, 512), 512)
            v = dot(cot[:, rows_of(z)], dn[rows_of(z), cols])
            acc[:, cols] = v if fresh else acc[:, cols] + v

    def branch(z, fresh):
        if not fresh:
            ft_copy(z, 0).wait()
        ftb[0] = dot(inner[...], dn[rows_of(z), :], NT).astype(BF)
        ft_copy(z, 0).start()

    def blocks(h):
        @pl.when(p + h < n)
        def _():
            grads(p + h, False)
            branch(p + h, False)

        @pl.when(p - h >= 0)
        def _():
            grads(p - h, False)
            branch(p - h, False)

    gather.stage(1)
    grads(p, True)
    branch(p, True)
    line.slot(0)
    if n > 3:
        gather.stage(2)
    load_gu.wait()
    half = width

    def cols_at(i):
        g = pl.ds(pl.multiple_of(i * 2 * half, half), half)
        u = pl.ds(pl.multiple_of(i * 2 * half + half, half), half)
        return g, u, pl.ds(pl.multiple_of(i * half, half), half)

    @pl.loop(0, pieces)
    def _(i):
        gcols, ucols, _ = cols_at(i)

        @pl.loop(0, gu.shape[0] // 64)
        def _(b):
            rs = pl.ds(pl.multiple_of(b * 64, 64), 64)
            g = gu[rs, gcols].astype(F32)
            u = gu[rs, ucols].astype(F32)
            sg = 1.0 / (1.0 + jnp.exp(-g))
            gu[rs, gcols] = (u * sg * (1.0 + g * (1.0 - sg))).astype(BF)
            gu[rs, ucols] = (g * sg).astype(BF)

    blocks(1)
    for h in range(2, n - 1):
        line.slot(h - 1)
        if h + 1 < n - 1:
            gather.stage(h + 1)
        blocks(h)

    gather.stage(n - 1)

    @pl.when(jnp.logical_not(at.has_below))
    def _():
        grads(n - 1, False)

    @pl.when(jnp.logical_not(at.has_above))
    def _():
        grads(0, False)

    def gg_copy(i):
        cols = pl.ds(pl.multiple_of(i * 2 * half, 2 * half), 2 * half)
        return pltpu.make_async_copy(gu.at[:, cols], ggu_ref.at[:, cols], gg_s.at[i])

    @pl.loop(0, pieces)
    def _(i):
        gcols, ucols, acols = cols_at(i)

        @pl.loop(0, gu.shape[0] // 64)
        def _(b):
            rs = pl.ds(pl.multiple_of(b * 64, 64), 64)
            gi = acc[rs, acols]
            gu[rs, gcols] = (gi * gu[rs, gcols].astype(F32)).astype(BF)
            gu[rs, ucols] = (gi * gu[rs, ucols].astype(F32)).astype(BF)

        gg_copy(i).start()

    @pl.when(jnp.logical_not(at.has_below))
    def _():
        branch(n - 1, False)

    @pl.when(jnp.logical_not(at.has_above))
    def _():
        branch(0, False)

    stores = line.final(res, rs_ref, rs_s)
    keep_low = pltpu.make_async_copy(line.own.at[0], pend_ref, dn_s.at[0])
    keep_high = pltpu.make_async_copy(line.own.at[n - 1], pend_ref, dn_s.at[0])
    pl.when(p == 1)(keep_low.start)
    pl.when(p == n - 2)(keep_high.start)
    pl.when((p == 1) | (p == n - 2))(keep_low.wait)
    for i in range(pieces):
        gg_copy(i).wait()
    ft_copy(p, 0).wait()
    for cp in stores:
        cp.wait()
    line.drain()
    gather.drain()


def down_stage(n_dp, n_mp, inner, gu, cot, shard, dpre):
    seq, d = cot.shape
    chunk, ff = shard.shape
    n = n_dp // 2
    dma = pltpu.SemaphoreType.DMA
    hbm = pl.BlockSpec(memory_space=pl.ANY)
    return pl.pallas_call(
        functools.partial(down_kernel, n_dp, n_mp),
        out_shape=[
            jax.ShapeDtypeStruct((PIECES, chunk, ff // PIECES), BF),
            jax.ShapeDtypeStruct((seq, d), BF),
            jax.ShapeDtypeStruct((seq, 2 * ff), BF),
            jax.ShapeDtypeStruct((PIECES, chunk, ff // PIECES), BF),
        ],
        in_specs=[hbm] * 5,
        out_specs=[hbm] * 4,
        scratch_shapes=[
            pltpu.VMEM((seq, ff), BF),
            pltpu.VMEM((seq, 2 * ff), BF),
            pltpu.VMEM((seq, d), BF),
            pltpu.VMEM((d, ff), BF),
            pltpu.VMEM((seq, ff), F32),
            pltpu.VMEM((1, seq, 2 * chunk), BF),
            pltpu.VMEM((PIECES, chunk, ff // PIECES), BF),
            dma((2, PIECES)),
            dma((1,)),
            dma((n,)),
            dma((PIECES,)),
            dma((PIECES,)),
            dma((1,)),
            dma((1,)),
            dma((PIECES,)),
        ]
        + line_sum_scratch(n, PIECES, chunk, ff // PIECES)
        + line_gather_scratch(n, PIECES),
        compiler_params=pltpu.CompilerParams(
            collective_id=3, has_side_effects=True, vmem_limit_bytes=VMEM_LIMIT
        ),
        name="down_stage",
    )(inner, gu, cot, shard, dpre)


def mid_kernel(
    n_dp,
    n_mp,
    ggu_hbm,
    gw_hbm,
    nm_hbm,
    ft_hbm,
    cot_hbm,
    qkv_hbm,
    aw_hbm,
    count_ref,
    hid_hbm,
    gain_ref,
    rs_ref,
    low_ref,
    lay_ref,
    gh_hbm,
    gg_ref,
    dq_ref,
    space,
    wt,
    wt_s,
    nm,
    nm_s,
    cot,
    hid,
    gh,
    res,
    gg_s,
    rs_s,
    dka,
    dva,
    load_s,
    *rest,
):
    at = Place(n_dp, n_mp)
    n = at.n
    line = LineSum(at, *rest[0:4], rest[4:10])
    mid = QuadSum(at, *rest[10:12], rest[12:14])
    lay = QuadSumHbm(at, ft_hbm, *rest[14:16], rest[16:19])
    gather_low = QuadGather(at, rest[19], low_ref, rest[20:23])
    gather_lay = QuadGather(at, rest[23], lay_ref, rest[24:27])
    part, half_cols = mid.t.shape[2], mid.t.shape[3]
    chunk, width = line.own.shape[2], line.own.shape[3]
    pieces = line.pieces
    hh = qkv_hbm.shape[1] // 3
    drows = wt.shape[1]
    tiles = half_cols // drows

    wide = ggu_hbm.shape[1]
    ggu = space.at[:, pl.ds(0, wide)]

    def gg_copy(i):
        cols = pl.ds(pl.multiple_of(i * width, width), width)
        return pltpu.make_async_copy(ggu_hbm.at[:, cols], ggu.at[:, cols], gg_s.at[i])

    load_cot = pltpu.make_async_copy(cot_hbm.at[part_rows(at, part), :], cot, load_s.at[1])

    def nm_copy(e):
        k, core = e // 2, e % 2
        block = 2 * order_of(k, at) + (1 - at.c if core == 0 else at.c)
        cols = pl.ds(pl.multiple_of(block * chunk, chunk), chunk)
        return pltpu.make_async_copy(nm_hbm.at[:, cols], nm.at[e % 2], nm_s.at[e % 2])

    def wt_copy(half, i, slot):
        rows = pl.ds(pl.multiple_of(half * half_cols + i * drows, drows), drows)
        return pltpu.make_async_copy(gw_hbm.at[rows, :], wt.at[slot], wt_s.at[slot])

    nm_copy(0).start()
    for i in range(pieces):
        gg_copy(i).start()
    wt_copy(0, 0, 0).start()
    load_cot.start()
    load_hid = pltpu.make_async_copy(hid_hbm, hid, load_s.at[0])
    load_hid.start()
    for cp in lay.loads:
        cp.start()
    enter(at)
    for mask in lay.masks():
        lay.offer(mask)

    def run(e):
        if e + 1 < 2 * n:
            nm_copy(e + 1).start()
        nm_copy(e).wait()
        lhs = nm[e % 2].T

        def tile(i):
            if e == 0:
                gg_copy(i).wait()
            return dot(lhs, ggu[:, pl.ds(pl.multiple_of(i * width, width), width)])

        if e % 2 == 0:
            line.other(e // 2, tile)
        else:
            line.mine(e // 2, tile)

    def terms(half):
        @pl.loop(0, tiles)
        def _(i):
            slot = lax.rem(i, 2)
            if half == 0:
                nxt = wt_copy(jnp.where(i + 1 < tiles, 0, 1), lax.rem(i + 1, tiles), 1 - slot)
                nxt.start()
            else:

                @pl.when(i + 1 < tiles)
                def _():
                    wt_copy(1, i + 1, 1 - slot).start()

            wt_copy(half, i, slot).wait()
            v = dot(ggu[...], wt[slot], NT).astype(BF)
            cols = pl.ds(pl.multiple_of(i * drows, drows), drows)
            for q in range(n_mp):
                mid.t[half, q, :, cols] = v[q * part : (q + 1) * part]

        for mask in mid.masks():
            mid.offer(mask, (half,))

    run(0)
    run(1)
    terms(0)
    run(2)
    run(3)
    for cp in lay.loads:
        cp.wait()
    lay.turn()
    line.slot(0, 0, 2)
    terms(1)
    line.slot(0, 2, 3)
    for e in range(4, 2 * n):
        run(e)
    lay.arrive()
    load_hid.wait()

    @pl.loop(0, part // 32)
    def _(b):
        rs = pl.ds(pl.multiple_of(b * 32, 32), 32)
        for half in range(2):
            h = hid[rs, pl.ds(half * half_cols, half_cols)]
            gather_lay.own[half, rs, :] = (h + lay.total(half, rs)).astype(BF)

    gather_lay.start([0])
    line.slot(0, 3)
    per = half_cols // hh
    blocks_d = 2 * half_cols // part
    wo_spot = [(e // per // (n_mp // 2), e // per % (n_mp // 2), e % per) for e in range(blocks_d)]
    wo_parts = [
        pltpu.make_async_copy(
            aw_hbm.at[pl.ds(e * part, part), pl.ds(3 * hh, hh)],
            lay.t.at[i, j, :, pl.ds(k * hh, hh)],
            load_s.at[4 + e],
        )
        for e, (i, j, k) in enumerate(wo_spot)
    ]
    for cp in wo_parts:
        cp.start()
    load_qkv = pltpu.make_async_copy(
        qkv_hbm, space.at[:, pl.ds(2 * half_cols, 3 * hh)], load_s.at[2]
    )
    load_qkv.start()
    mid.turn()
    mid.arrive()
    load_cot.wait()
    gg_ref[...] = jnp.zeros_like(gg_ref)

    @pl.loop(0, part // 32)
    def _(b):
        rs = pl.ds(pl.multiple_of(b * 32, 32), 32)
        h = hid[rs, :]
        scale = lax.rsqrt(jnp.mean(h * h, axis=1, keepdims=True) + EPS)
        g = jnp.concatenate([mid.total(0, rs), mid.total(1, rs)], axis=1)
        unit = h * scale
        weighted = g * gain_ref[1:2, :]
        field = scale * (weighted - unit * jnp.mean(weighted * unit, axis=1, keepdims=True))
        out = cot[rs, :].astype(F32) + field
        gh[rs, :] = out
        low = out.astype(BF)
        gather_low.own[0, rs, :] = low[:, :half_cols]
        gather_low.own[1, rs, :] = low[:, half_cols:]
        gg_ref[...] += jnp.sum(g * unit, axis=0, keepdims=True)

    gather_low.start()
    store_gh = pltpu.make_async_copy(gh, gh_hbm, load_s.at[1])
    store_gh.start()
    for s in range(1, n - 2):
        line.slot(s)
    gather_low.forward()
    gather_lay.start(range(1, gather_lay.levels))
    gather_lay.forward()
    gather_low.finish()
    load_low = pltpu.make_async_copy(low_ref, space.at[:, pl.ds(0, 2 * half_cols)], load_s.at[3])
    load_low.start()
    load_low.wait()
    load_qkv.wait()
    for cp in wo_parts:
        cp.wait()
    seq = space.shape[0]
    base = 2 * half_cols
    gbase = base + 3 * hh

    @pl.loop(0, seq // 256)
    def _(b):
        rs = pl.ds(pl.multiple_of(b * 256, 256), 256)
        total = jnp.zeros((256, hh), F32)
        for e, (i, j, k) in enumerate(wo_spot):
            wo = lay.t[i, j, :, k * hh : (k + 1) * hh]
            total += dot(space[rs, e * part : (e + 1) * part], wo)
        space[rs, gbase : gbase + hh] = total.astype(BF)

    count = count_ref[0]
    blk = 256
    blocks = seq // blk

    def back(head):
        at_cols = lambda first: pl.ds(pl.multiple_of(first + head * HD, HD), HD)
        for i in range(blocks - 1, -1, -1):
            rows = pl.ds(i * blk, blk)
            span = (i + 1) * blk
            keys = pl.ds(0, span)
            q = space[rows, at_cols(base)]
            g = space[rows, at_cols(gbase)]
            k = space[keys, at_cols(base + hh)]
            lg = jnp.where(
                allowed_block(i * blk, blk, 0, span, count), logistic_block(q, k, seq), 0.0
            )
            w = lg.astype(BF)
            gw = dot(g, space[keys, at_cols(base + 2 * hh)], NT)
            gs = (gw * lg * (1.0 - lg) * HD ** (-0.5)).astype(BF)
            wt[i // 2, :, at_cols((i % 2) * (wide // 2))] = dot(gs, k).astype(BF)
            dk = dot(gs, q, TN)
            dv = dot(w, g, TN)
            if i == blocks - 1:
                dka[...] = dk
                dva[...] = dv
            else:
                dka[keys, :] += dk
                dva[keys, :] += dv
        for i in range(blocks):
            rows = pl.ds(i * blk, blk)
            wt[i // 2, :, at_cols((i % 2) * (wide // 2) + hh)] = dka[rows, :].astype(BF)
            wt[i // 2, :, at_cols((i % 2) * (wide // 2) + 2 * hh)] = dva[rows, :].astype(BF)

    heads = hh // HD
    pl.loop(0, heads)(back)
    stores = [
        pltpu.make_async_copy(
            wt.at[i // 2, :, pl.ds((i % 2) * (wide // 2), 3 * hh)],
            dq_ref.at[pl.ds(i * blk, blk), :],
            load_s.at[4 + i],
        )
        for i in range(blocks)
    ]
    for cp in stores:
        cp.start()
    stores += line.final(res, rs_ref, rs_s) + [store_gh]
    gather_lay.finish()
    for cp in stores:
        cp.wait()
    line.drain()
    mid.drain()
    lay.drain()


def mid_stage(n_dp, n_mp, ggu, gw, nm, ft, cot, qkv, aw, counts, hid, gain):
    seq, wide = ggu.shape
    hh = qkv.shape[1] // 3
    d = gw.shape[0]
    n, part, chunk = n_dp // 2, seq // n_mp, d // n_dp
    dma = pltpu.SemaphoreType.DMA
    hbm = pl.BlockSpec(memory_space=pl.ANY)
    vm = pl.BlockSpec(memory_space=pltpu.VMEM)
    pieces = PIECES
    return pl.pallas_call(
        functools.partial(mid_kernel, n_dp, n_mp),
        out_shape=[
            jax.ShapeDtypeStruct((pieces, chunk, wide // pieces), BF),
            jax.ShapeDtypeStruct((seq, d), BF),
            jax.ShapeDtypeStruct((seq, d), BF),
            jax.ShapeDtypeStruct((part, d), F32),
            jax.ShapeDtypeStruct((1, d), F32),
            jax.ShapeDtypeStruct((seq, 3 * hh), BF),
        ],
        in_specs=[hbm] * 7 + [pl.BlockSpec(memory_space=pltpu.SMEM), hbm, vm],
        out_specs=[hbm, hbm, hbm, hbm, vm, hbm],
        scratch_shapes=[
            pltpu.VMEM((seq, max(wide, d + 4 * hh)), BF),
            pltpu.VMEM((2, 256, wide), BF),
            dma((2,)),
            pltpu.VMEM((2, seq, chunk), BF),
            dma((2,)),
            pltpu.VMEM((part, d), BF),
            pltpu.VMEM((part, d), F32),
            pltpu.VMEM((part, d), F32),
            pltpu.VMEM((pieces, chunk, wide // pieces), BF),
            dma((pieces,)),
            dma((pieces,)),
            pltpu.VMEM((seq, HD), F32),
            pltpu.VMEM((seq, HD), F32),
            dma((4 + max(d // part, seq // 256),)),
        ]
        + line_sum_scratch(n, pieces, chunk, wide // pieces, 1)
        + quad_sum_scratch(n_mp, part, d // 2)
        + quad_sum_scratch(n_mp, part, d // 2, n_mp // 2)
        + [dma((2, n_mp // 2))]
        + quad_gather_scratch(n_mp, part, d // 2) * 2,
        compiler_params=pltpu.CompilerParams(
            collective_id=4, has_side_effects=True, vmem_limit_bytes=VMEM_LIMIT
        ),
        name="mid_stage",
    )(ggu, gw, nm, ft, cot, qkv, aw, counts, hid, gain)


def last_kernel(
    n_dp,
    n_mp,
    dqkv_hbm,
    aw_hbm,
    nin_hbm,
    low_hbm,
    att_hbm,
    x_hbm,
    gh_hbm,
    pend_hbm,
    part_hbm,
    gain_ref,
    gmid_ref,
    rs_ref,
    grad_ref,
    gains_ref,
    rsd_ref,
    rhs,
    aw,
    nin,
    low,
    lhs,
    x,
    gh,
    res,
    rs_s,
    pbuf,
    dbuf,
    pd_s,
    loads,
    pout,
    own,
    din,
    uin,
    po_s,
    po_r,
    d_s,
    d_r,
    u_s,
    u_r,
    t,
    r,
    q1,
    q2,
    gown,
    g1,
    g2,
    g3,
    gsum,
    fold_out,
    fold_in,
    fold_s,
    fold_r,
):
    at = Place(n_dp, n_mp)
    hh = att_hbm.shape[1]
    part = t.shape[2]
    chunk = own.shape[2]
    half_cols = t.shape[3]
    copies = [
        pltpu.make_async_copy(src, dst, loads.at[i])
        for i, (src, dst) in enumerate(
            [
                (dqkv_hbm, rhs.at[:, pl.ds(0, 3 * hh)]),
                (aw_hbm.at[:, pl.ds(0, 3 * hh)], aw),
                (nin_hbm, nin),
                (att_hbm, rhs.at[:, pl.ds(3 * hh, hh)]),
                (low_hbm, low),
                (x_hbm.at[part_rows(at, part), :], x),
                (gh_hbm, gh),
                (part_hbm, dbuf),
            ]
        )
    ]
    for cp in copies:
        cp.start()
    bits = [b for b in (2, 4, 8, 16) if b < n_dp]
    enter(at, [at.fold(b) for b in bits[1:]])
    quad = QuadSum(at, t, r, (q1, q2))
    line = LineSum(at, pout, own, din, uin, (po_s, po_r, d_s, d_r, u_s, u_r), True)
    gather = QuadGather(at, gown, grad_ref, (g1, g2, g3))
    n = at.n
    low_end = remote(pend_hbm, pbuf, pd_s.at[0], pd_s.at[1], at.below)
    high_end = remote(pend_hbm, pbuf, pd_s.at[0], pd_s.at[1], at.above)
    copies[0].wait()
    copies[1].wait()

    d = aw.shape[0]
    fold = fold_out.shape[2]
    per_row = d // fold

    def terms(q, gains=True):
        rs = pl.ds(pl.multiple_of(q * part, part), part)
        width = 512

        @pl.loop(0, half_cols // width)
        def _(i):
            for half in range(2):
                d0 = pl.multiple_of(half * half_cols + i * width, width)
                v = dot(rhs[rs, 0 : 3 * hh], aw[pl.ds(d0, width), :], NT)
                t[half, q, :, pl.ds(pl.multiple_of(i * width, width), width)] = v.astype(BF)
                if gains:
                    u = v * nin[rs, pl.ds(d0, width)].astype(F32)
                    gsum[0:1, pl.ds(d0, width)] += jnp.sum(u, axis=0, keepdims=True)

    masks = quad.masks()
    terms(at.quarter(masks[0]), False)
    quad.offer(masks[0])
    copies[2].wait()
    for cp in copies[3:5]:
        cp.wait()
    load_x = copies[5]

    def run(k, core):
        block = 2 * order_of(k, at) + (at.c if core else 1 - at.c)
        cols = pl.ds(pl.multiple_of(block * chunk, chunk), chunk)
        lhs[0] = nin[:, cols].T
        lhs[1] = low[:, cols].T

        def tile(i):
            return dot(lhs[lax.div(i, 3)], rhs[:, pl.ds(pl.multiple_of(i * hh, hh), hh)])

        if core:
            line.mine(k, tile)
        else:
            line.other(k, tile)

    devs = [at.core] + [at.fold(b) for b in bits] + [at.peer(b) for b in at.bits]

    def fold_copy(b):
        return remote(fold_out.at[b], fold_in.at[b], fold_s.at[b], fold_r.at[b], devs[b])

    def fold_next(b):
        fold_copy(b).wait_recv()
        fold_out[b + 1] = fold_out[b] + fold_in[b]
        if b + 1 < len(devs):
            fold_copy(b + 1).start()

    run(0, 0)
    run(0, 1)
    first = pl.ds(pl.multiple_of(at.quarter(masks[0]) * part, part), part)
    for half in range(2):
        cols = slice(half * half_cols, (half + 1) * half_cols)
        u = t[half, at.quarter(masks[0])].astype(F32) * nin[first, cols].astype(F32)
        gsum[0:1, cols] = jnp.sum(u, axis=0, keepdims=True)
    for mask in masks[1:]:
        terms(at.quarter(mask))
        quad.offer(mask)
    gsum[0:1, :] = gsum[0:1, :] / gain_ref[0:1, :]
    gsum[1:2, :] = gmid_ref[...]
    for i in range(2):
        for j in range(per_row):
            fold_out[0, i * per_row + j] = gsum[i, j * fold : (j + 1) * fold]
    fold_copy(0).start()
    run(1, 0)
    run(1, 1)
    fold_next(0)
    for k in range(2, n):
        run(k, 0)
        run(k, 1)
    quad.turn()
    for b in range(1, len(bits)):
        fold_next(b)
    pl.when(at.p == 1)(low_end.start)
    pl.when(at.p == n - 2)(high_end.start)
    line.slot(0)
    load_x.wait()
    copies[6].wait()
    fold_next(len(bits))
    step = part // gather.blocks

    def norm(block):
        @pl.loop(0, step // 32)
        def _(b):
            rs = pl.ds(pl.multiple_of(block * step + b * 32, 32), 32)
            v = x[rs, :].astype(F32)
            scale = lax.rsqrt(jnp.mean(v * v, axis=1, keepdims=True) + EPS)
            g = jnp.concatenate([quad.total(0, rs), quad.total(1, rs)], axis=1)
            unit = v * scale
            weighted = g * gain_ref[0:1, :]
            field = scale * (weighted - unit * jnp.mean(weighted * unit, axis=1, keepdims=True))
            total = (gh[rs, :] + field).astype(BF)
            gown[0, rs, :] = total[:, :half_cols]
            gown[1, rs, :] = total[:, half_cols:]

    for block in range(gather.blocks):
        quad.arrive(block)
        norm(block)
        gather.start(block=block)
        if block == 0:
            for b in range(len(bits) + 1, len(devs) - 1):
                fold_next(b)
    for s in range(1, n - 2):
        line.slot(s)
    for block in range(gather.blocks):
        gather.forward(block)
    fold_next(len(devs) - 1)
    for i in range(2):
        for j in range(per_row):
            gsum[i, j * fold : (j + 1) * fold] = fold_out[len(devs), i * per_row + j]
    gains_ref[...] = gsum[:, pl.ds(pl.multiple_of(at.dp * chunk, chunk), chunk)]
    copies[7].wait()

    @pl.when((at.p == 0) | (at.p == n - 1))
    def _():
        low_end.wait_recv()

        @pl.loop(0, 4)
        def _(i):
            dbuf[i] = (dbuf[i].astype(F32) + pbuf[i].astype(F32)).astype(BF)

    store = pltpu.make_async_copy(dbuf, rsd_ref, pd_s.at[2])
    store.start()
    stores = line.final(res, rs_ref, rs_s) + [store]
    pl.when((at.p == 1) | (at.p == n - 2))(low_end.wait_send)
    gather.finish()
    for cp in stores:
        cp.wait()
    line.drain()
    quad.drain()
    for b in range(len(devs)):
        fold_copy(b).wait_send()


def last_stage(n_dp, n_mp, dqkv, aw, nin, low, att, x, gh, pend, rs_down, gain, gmid):
    seq, hh = att.shape
    d = aw.shape[0]
    n, part, chunk = n_dp // 2, seq // n_mp, d // n_dp
    dma = pltpu.SemaphoreType.DMA
    anyspace = pl.BlockSpec(memory_space=pl.ANY)
    vm = pl.BlockSpec(memory_space=pltpu.VMEM)
    folds = 1 + len([b for b in (1, 2, 4, 8) if b < n_mp]) + len([b for b in (2, 4, 8, 16) if b < n_dp])
    return pl.pallas_call(
        functools.partial(last_kernel, n_dp, n_mp),
        out_shape=[
            jax.ShapeDtypeStruct((4, chunk, hh), BF),
            jax.ShapeDtypeStruct((seq, d), BF),
            jax.ShapeDtypeStruct((8, chunk), F32),
            jax.ShapeDtypeStruct(rs_down.shape, BF),
        ],
        in_specs=[anyspace] * 9 + [vm] * 2,
        out_specs=[anyspace, anyspace, vm, anyspace],
        scratch_shapes=[
            pltpu.VMEM((seq, 4 * hh), BF),
            pltpu.VMEM((d, 3 * hh), BF),
            pltpu.VMEM((seq, d), BF),
            pltpu.VMEM((seq, d), BF),
            pltpu.VMEM((2, chunk, seq), BF),
            pltpu.VMEM((part, d), BF),
            pltpu.VMEM((part, d), F32),
            pltpu.VMEM((4, chunk, hh), BF),
            dma((4,)),
            pltpu.VMEM(rs_down.shape, BF),
            pltpu.VMEM(rs_down.shape, BF),
            dma((3,)),
            dma((8,)),
        ]
        + line_sum_scratch(n, 4, chunk, hh)
        + quad_sum_scratch(n_mp, part, d // 2, None, 2)
        + quad_gather_scratch(n_mp, part, d // 2, 2)
        + [
            pltpu.VMEM((8, d), F32),
            pltpu.VMEM((folds + 1, 8, d // 4), F32),
            pltpu.VMEM((folds, 8, d // 4), F32),
            dma((folds,)),
            dma((folds,)),
        ],
        compiler_params=pltpu.CompilerParams(
            collective_id=5, has_side_effects=True, vmem_limit_bytes=VMEM_LIMIT
        ),
        name="last_stage",
    )(dqkv, aw, nin, low, att, x, gh, pend, rs_down, gain, gmid)


def finish_kernel(
    low_ref,
    lay_ref,
    gu_ref,
    down_ref,
    attn_ref,
    gains_ref,
    lay_out,
    in_out,
    gate_out,
    up_out,
    down_out,
    q_out,
    k_out,
    v_out,
    o_out,
    g1_out,
    g2_out,
):
    lay_out[...] = lay_ref[...]
    in_out[...] = low_ref[...].astype(F32)
    half = gate_out.shape[1]
    gate_out[...] = gu_ref[0, :, :half].astype(F32)
    up_out[...] = gu_ref[0, :, half:].astype(F32)
    down_out[...] = down_ref[0].T.astype(F32)

    @pl.when(pl.program_id(0) == 0)
    def _():
        for i, ref in enumerate((q_out, k_out, v_out)):
            ref[...] = attn_ref[i].astype(F32)
        o_out[...] = attn_ref[3].T.astype(F32)
        g1_out[...] = gains_ref[0]
        g2_out[...] = gains_ref[1]


def finish_stage(low, lay, gu, down, attn, gains):
    seq, d = low.shape
    steps, chunk, wide = gu.shape
    width, hh = down.shape[2], attn.shape[2]
    row = pl.BlockSpec((seq // steps, d), lambda i: (i, 0))
    fixed = lambda *shape: pl.BlockSpec(shape, lambda i: (0,) * len(shape))
    piece = lambda w: pl.BlockSpec((1, chunk, w), lambda i: (i, 0, 0))
    cols = pl.BlockSpec((chunk, wide // 2), lambda i: (0, i))
    f32 = lambda *shape: jax.ShapeDtypeStruct(shape, F32)
    return pl.pallas_call(
        finish_kernel,
        grid=(steps,),
        in_specs=[row, row, piece(wide), piece(width), fixed(4, chunk, hh), fixed(*gains.shape)],
        out_specs=[row, row, cols, cols, pl.BlockSpec((width, chunk), lambda i: (i, 0))]
        + [fixed(chunk, hh)] * 3
        + [fixed(hh, chunk)]
        + [fixed(chunk)] * 2,
        out_shape=[
            jax.ShapeDtypeStruct((seq, d), BF),
            f32(seq, d),
            f32(chunk, steps * wide // 2),
            f32(chunk, steps * wide // 2),
            f32(steps * width, chunk),
        ]
        + [f32(chunk, hh)] * 3
        + [f32(hh, chunk)]
        + [f32(chunk)] * 2,
        compiler_params=pltpu.CompilerParams(vmem_limit_bytes=VMEM_LIMIT),
        name="finish_stage",
    )(low, lay, gu, down, attn, gains)


def on_device(
    inputs,
    counts,
    cotangent,
    gain_attn,
    w_query,
    w_key,
    w_value,
    w_output,
    gain_ffn,
    w_gate,
    w_up,
    w_down,
):
    n_dp, n_mp = lax.axis_size("dp"), lax.axis_size("mp")
    attn_w, qkv, attended, normed_in, gains, gu_shard, down_shard, grad_ffn, gu_pre = attn_stage(
        n_dp,
        n_mp,
        counts,
        gain_attn,
        gain_ffn,
        w_query,
        w_key,
        w_value,
        w_output,
        w_gate,
        w_up,
        w_down,
        inputs,
        cotangent,
    )
    gu_w, normed_mid, hidden, gu, inner, down_pre = gate_stage(
        n_dp, n_mp, attended, attn_w, gu_shard, gu_pre, down_shard, inputs, gains
    )
    down_part, ffn_terms, ggu, down_pend = down_stage(n_dp, n_mp, inner, gu, grad_ffn, down_shard, down_pre)
    rs_gu, grad_low, layer_out, grad_hidden, g_gain_mid, dqkv = mid_stage(
        n_dp, n_mp, ggu, gu_w, normed_mid, ffn_terms, grad_ffn, qkv, attn_w, counts, hidden, gains
    )
    rs_attn, grad_low_in, g_gains, rs_down = last_stage(
        n_dp,
        n_mp,
        dqkv,
        attn_w,
        normed_in,
        grad_low,
        attended,
        inputs,
        grad_hidden,
        down_pend,
        down_part,
        gains,
        g_gain_mid,
    )
    lay, grad_x, g_gate, g_up, g_down, g_q, g_k, g_v, g_o, g_attn, g_ffn = finish_stage(
        grad_low_in, layer_out, rs_gu, rs_down, rs_attn, g_gains
    )
    return (lay, grad_x, g_attn, g_q, g_k, g_v, g_o, g_ffn, g_gate, g_up, g_down)


def solution(mesh):
    row, both, swapped = P("dp", None), P("dp", "mp"), P("mp", "dp")
    weights = (both, both, both, swapped)
    ffn = (both, both, swapped)
    return jax.shard_map(
        on_device,
        mesh=mesh,
        in_specs=(row, P("dp"), row, P("dp")) + weights + (P("dp"),) + ffn,
        out_specs=(row, row, P("dp")) + weights + (P("dp"),) + ffn,
        check_vma=False,
    )
```
